32 devices in a mesh: seq: 2 (over x), tp: 16 (over z, y, core).
Axes of the slice: x: 2, y: 2, z: 4, core: 2. Of those that a mesh axis runs over, the one named last changes fastest.
Arguments:
- text_states: bfloat16 [8192, 768], P(('seq', 'tp')), may hold values from -6 to 6
- visual_maps: bfloat16 [1024, 256], P(('seq', 'tp'))
- text_boxes: int32 [2, 8192], P(None, ('seq', 'tp')), may hold values from 0 to 999
- text_lengths: int32 [16], replicated, may hold values from 64 to 512, as said below
- qkv_weight: bfloat16 [2, 3, 768, 768], replicated, may hold values from -0.21875 to 0.21875
- out_weight: bfloat16 [2, 768, 768], replicated, may hold values from -2.5 to 2.5
- attn_bias: float32 [2, 3, 768], replicated, may hold values from -3 to 3
- ffn_in: bfloat16 [2, 3072, 768], P(None, 'tp'), may hold values from -0.21875 to 0.21875
- ffn_in_bias: bfloat16 [2, 3072], P(None, 'tp'), may hold values from -3 to 3
- ffn_out: bfloat16 [2, 3072, 768], P(None, 'tp'), may hold values from -0.109375 to 0.109375
- ffn_out_bias: float32 [2, 768], replicated, may hold values from -3 to 3
- norm_gain: float32 [2, 2, 768], replicated, may hold values from 0.25 to 1.75
- norm_shift: float32 [2, 2, 768], replicated, may hold values from -3 to 3
- bias_table: float32 [160, 12], replicated, may hold values from -3 to 3
- vis_weight: bfloat16 [256, 768], replicated, may hold values from -0.375 to 0.375
- vis_bias: float32 [768], replicated, may hold values from -3 to 3
- bn_gain: float32 [256], replicated, may hold values from 0.25 to 1.75
- bn_shift: float32 [256], replicated, may hold values from -3 to 3
- cotangent: bfloat16 [9216, 768], P(('seq', 'tp')), may hold values from -6 to 6
Outputs:
- out_states: bfloat16 [9216, 768], P(('seq', 'tp'))
- grad_text: float32 [8192, 768], P(('seq', 'tp'))
- grad_maps: float32 [1024, 256], P(('seq', 'tp'))
- grad_qkv: float32 [2, 3, 768, 768], P(None, None, 'tp')
- grad_out_weight: float32 [2, 768, 768], P(None, 'tp')
- grad_attn_bias: float32 [2, 3, 768], replicated
- grad_ffn_in: float32 [2, 3072, 768], P(None, 'tp')
- grad_ffn_in_bias: float32 [2, 3072], P(None, 'tp')
- grad_ffn_out: float32 [2, 3072, 768], P(None, 'tp')
- grad_ffn_out_bias: float32 [2, 768], replicated
- grad_norm_gain: float32 [2, 2, 768], replicated
- grad_norm_shift: float32 [2, 2, 768], replicated
- grad_bias_table: float32 [160, 12], replicated
- grad_vis_weight: float32 [256, 768], replicated
- grad_vis_bias: float32 [768], replicated
- grad_bn_gain: float32 [256], replicated
- grad_bn_shift: float32 [256], replicated
The draws below stay inside these ranges and needn't reach their ends.
Inputs may be any that keep to these rules, and one draw needn't show every extreme that they name: `text_lengths`: some page has all 512 text slots used.
All inputs are finite; a program needn't handle non-finite values.
Results may differ from the reference program's by a relative error of at most 0.035.
Values may be sent and summed in bfloat16 or wider, within the bound.
No kernel may reach another device: no remote copies, remote signals or barrier semaphores. Data moves between devices by JAX's collectives and lax.ppermute only.
A program may use at most 256 MiB of HBM per device.

```python
import jax
import jax.numpy as jnp
from jax import lax

D = 768
HEADS = 12
HEAD_DIM = 64
FF = 3072
CHANNELS = 256
TEXT_LEN = 512
VIS_TOK = 49
VIS_SLOTS = 64
POS_BINS = 32
BOX_BINS = 64
LAYERS = 2
PAIR_PAGES = 1
PAGES = 16
TEXT_ROWS = 8192
VIS_ROWS = 1024
TOKENS = 9216
BUCKETS = 160
N_SEQ = 2
N_TP = 16


def draw_visual_maps(key, part):
    key = jax.random.fold_in(key, 11)
    row_key, chan_key, base_key, mean_key = jax.random.split(key, 4)
    row_index = jnp.arange(VIS_ROWS, dtype=jnp.int32)
    block_index = row_index // (VIS_SLOTS // 2)
    page_index = block_index // PAIR_PAGES // 2 * PAIR_PAGES + block_index % PAIR_PAGES
    page_scale = 1.0 + 2.0 * page_index.astype(jnp.float32) / max(PAGES - 1, 1)
    row_scale = jnp.exp(jax.random.uniform(row_key, (VIS_ROWS, 1), jnp.float32, 0.0, 2.3026))
    chan_scale = jnp.exp(jax.random.uniform(chan_key, (1, CHANNELS), jnp.float32, 0.0, 2.3026))
    base_values = jax.random.normal(base_key, (VIS_ROWS, CHANNELS), jnp.float32) + 0.3 * jax.random.normal(mean_key, (1, CHANNELS), jnp.float32)
    return (page_scale[:, None] * row_scale * chan_scale * base_values).astype(jnp.bfloat16)


def draw_text_lengths(key, part):
    key = jax.random.fold_in(key, 23)
    draw_key, pick_key = jax.random.split(key)
    lengths = jax.random.randint(draw_key, (PAGES,), TEXT_LEN // 8, TEXT_LEN + 1, jnp.int32)
    chosen = jax.random.randint(pick_key, (), 0, PAGES, jnp.int32)
    return jnp.where(jnp.arange(PAGES, dtype=jnp.int32) == chosen, TEXT_LEN, lengths)


def place_ends(entries, stream_key, least, high):
    longest = entries.shape.index(max(entries.shape))
    spots = []
    for shift in (0, 1):
        where = [jax.random.randint(jax.random.fold_in(stream_key, axis), (), 0, length) for axis, length in enumerate(entries.shape)]
        where[longest] = (where[longest] + shift) % entries.shape[longest]
        spots.append(tuple(where))
    return entries.at[spots[0]].set(least).at[spots[1]].set(high)


def shard_levels(own_key, extent, shards, low, largest):
    gain = 1.0
    for position, blocks in shards:
        steps = jax.random.uniform(jax.random.fold_in(jax.random.fold_in(own_key, 6), position), (blocks,), jnp.float32, low / len(shards), largest / len(shards))
        gain = gain * jnp.repeat(jnp.exp(steps), extent[position] // blocks).reshape((-1,) + (1,) * (len(extent) - 1 - position))
    return gain


def scatter_about(key, extent, width, limit, pieces=(), held_as=jnp.bfloat16):
    drawn = jax.random.normal(key, extent, jnp.float32) * width
    if len(pieces) > 0:
        drawn = shard_levels(key, extent, pieces, -0.22, 0.18) * drawn
    return jnp.clip(drawn, min=-limit, max=limit).astype(held_as)


def setup_inputs(seed: int = 0) -> dict:
    splits = jax.random.split(jax.random.key(seed), 20)
    return {
        "text_states": scatter_about(splits[0], (TEXT_ROWS, D), 1.0, 6.0, ((0, 32),)),
        "visual_maps": draw_visual_maps(jax.random.fold_in(splits[19], 71), 0),
        "text_boxes": place_ends(jax.random.randint(splits[2], (2, TEXT_ROWS), 0, 1000), jax.random.fold_in(splits[2], 1), 0, 999).astype(jnp.int32),
        "text_lengths": draw_text_lengths(jax.random.fold_in(splits[19], 71), 0),
        "qkv_weight": scatter_about(splits[4], (LAYERS, 3, D, D), D ** -0.5, 0.21875),
        "out_weight": scatter_about(splits[5], (LAYERS, D, D), (max(1, 4 * D // TEXT_LEN)) ** -0.5, 2.5),
        "attn_bias": scatter_about(splits[6], (LAYERS, 3, D), 0.5, 3.0, (), jnp.float32),
        "ffn_in": scatter_about(splits[7], (LAYERS, FF, D), D ** -0.5, 0.21875, ((1, 16),)),
        "ffn_in_bias": scatter_about(splits[8], (LAYERS, FF), 0.5, 3.0, ((1, 16),)),
        "ffn_out": scatter_about(splits[9], (LAYERS, FF, D), FF ** -0.5, 0.109375, ((1, 16),)),
        "ffn_out_bias": scatter_about(splits[10], (LAYERS, D), 0.5, 3.0, (), jnp.float32),
        "norm_gain": jnp.clip(1.0 + 0.15 * jax.random.normal(splits[11], (LAYERS, 2, D), jnp.float32), 0.25, 1.75),
        "norm_shift": scatter_about(splits[12], (LAYERS, 2, D), 0.5, 3.0, (), jnp.float32),
        "bias_table": scatter_about(splits[13], (BUCKETS, HEADS), 0.5, 3.0, (), jnp.float32),
        "vis_weight": scatter_about(splits[14], (CHANNELS, D), CHANNELS ** -0.5, 0.375),
        "vis_bias": scatter_about(splits[15], (D,), 0.5, 3.0, (), jnp.float32),
        "bn_gain": jnp.clip(1.0 + 0.15 * jax.random.normal(splits[16], (CHANNELS,), jnp.float32), 0.25, 1.75),
        "bn_shift": scatter_about(splits[17], (CHANNELS,), 0.5, 3.0, (), jnp.float32),
        "cotangent": scatter_about(splits[18], (TOKENS, D), 1.0, 6.0, ((0, 32),)),
    }


@jax.custom_vjp
def low(v):
    return lax.optimization_barrier(v.astype(jnp.bfloat16)).astype(jnp.float32)

@jax.custom_vjp
def low_back(v):
    return v

def low_keep(v):
    return (low(v), None)

def low_pass(kept, grad):
    return (grad,)

def back_keep(v):
    return (v, None)

def back_low(kept, grad):
    return (low(grad),)
low.defvjp(low_keep, low_pass)
low_back.defvjp(back_keep, back_low)
highest = lax.Precision.HIGHEST
box_step = 16
grid_pitch = 143
grid_width = 7
norm_epsilon = 1e-05
masked_score = -1000000000.0

def layer_norm(values, gain_row, shift_row):
    center = values - lax.optimization_barrier(jnp.mean(values, axis=-1, keepdims=True))
    spread = lax.optimization_barrier(jnp.mean(center * center, axis=-1, keepdims=True))
    return center * lax.rsqrt(spread + norm_epsilon) * gain_row + shift_row

def half_meta(boxes_half, length, half_index):
    text_count = boxes_half.shape[-1]
    slot_count = VIS_SLOTS // 2
    text_place = half_index * text_count + jnp.arange(text_count, dtype=jnp.int32)
    slot_place = half_index * slot_count + jnp.arange(slot_count, dtype=jnp.int32)
    places = jnp.concatenate([text_place, slot_place])
    grid_x = slot_place % grid_width * grid_pitch + 71
    grid_y = slot_place // grid_width * grid_pitch + 71
    coord_x = jnp.concatenate([boxes_half[0], grid_x])
    coord_y = jnp.concatenate([boxes_half[1], grid_y])
    usable = jnp.concatenate([text_place < length, slot_place < VIS_TOK])
    return (places, coord_x, coord_y, usable)

def bucket_codes(query_meta, key_meta):
    pos_half = POS_BINS // 2
    box_half = BOX_BINS // 2
    near_code = jnp.clip(key_meta[0][None, :] - query_meta[0][:, None], -pos_half, pos_half - 1) + pos_half
    across = jnp.clip((key_meta[1][None, :] - query_meta[1][:, None]) // box_step, -box_half, box_half - 1) + box_half + POS_BINS
    down_code = jnp.clip((key_meta[2][None, :] - query_meta[2][:, None]) // box_step, -box_half, box_half - 1) + box_half + POS_BINS + BOX_BINS
    return (near_code, across, down_code)

def layer_forward(states, score_bias, usable, layer_index, weights):
    qkv_weight, out_weight, attn_bias, ffn_in, ffn_in_bias, ffn_out, ffn_out_bias, norm_gain, norm_shift = weights
    row_total = states.shape[0]
    inverse_root = HEAD_DIM ** (-0.5)
    rounded = low(states)
    query_states = low_back(low(jnp.dot(rounded, qkv_weight[layer_index, 0], precision=highest) + attn_bias[layer_index, 0]))
    key_states = low_back(low(jnp.dot(rounded, qkv_weight[layer_index, 1], precision=highest)))
    value_states = low_back(low(jnp.dot(rounded, qkv_weight[layer_index, 2], precision=highest) + attn_bias[layer_index, 1]))
    query_heads = query_states.reshape(row_total, HEADS, HEAD_DIM)
    key_heads = key_states.reshape(row_total, HEADS, HEAD_DIM)
    value_heads = value_states.reshape(row_total, HEADS, HEAD_DIM)
    scores = jnp.einsum('qhd,khd->hqk', query_heads, key_heads, precision=highest) * inverse_root + score_bias
    scores = jnp.where(usable[None, None, :], low_back(scores), masked_score)
    soft_weights = low(jax.nn.softmax(scores, axis=-1))
    context = jnp.einsum('hqk,khd->qhd', soft_weights, value_heads, precision=highest).reshape(row_total, D)
    context = low_back(low(context))
    attended = low_back(jnp.dot(context, out_weight[layer_index], precision=highest) + attn_bias[layer_index, 2])
    normed = layer_norm(states + attended, norm_gain[layer_index, 0], norm_shift[layer_index, 0])
    hidden = low_back(jnp.dot(low(normed), ffn_in[layer_index].T, precision=highest) + ffn_in_bias[layer_index])
    activated = low(jax.nn.gelu(hidden, approximate=False))
    branch = low_back(jnp.dot(activated, ffn_out[layer_index], precision=highest) + ffn_out_bias[layer_index])
    return layer_norm(normed + branch, norm_gain[layer_index, 1], norm_shift[layer_index, 1])

def page_forward(page_states, page_meta, weights, bias_table):
    near_code, across, down_code = bucket_codes(page_meta, page_meta)
    score_bias = jnp.transpose(bias_table[near_code] + bias_table[across] + bias_table[down_code], (2, 0, 1))
    states = page_states
    for layer_index in range(LAYERS):
        states = layer_forward(states, score_bias, page_meta[3], layer_index, weights)
    return states

def reference(text_states, visual_maps, text_boxes, text_lengths, qkv_weight, out_weight, attn_bias, ffn_in, ffn_in_bias, ffn_out, ffn_out_bias, norm_gain, norm_shift, bias_table, vis_weight, vis_bias, bn_gain, bn_shift, cotangent):
    pair_total = N_SEQ * N_TP // 2
    text_half = TEXT_LEN // 2
    slot_half = VIS_SLOTS // 2
    page_rows = text_half + slot_half

    def to_pages(values, block_rows):
        shaped = values.reshape((pair_total, 2, PAIR_PAGES, block_rows) + values.shape[1:])
        return jnp.swapaxes(shaped, 1, 2).reshape((PAGES, 2, block_rows) + values.shape[1:])

    def from_pages(values, block_rows):
        shaped = values.reshape((pair_total, PAIR_PAGES, 2, block_rows) + values.shape[3:])
        return jnp.swapaxes(shaped, 1, 2).reshape((pair_total * 2 * PAIR_PAGES * block_rows,) + values.shape[3:])
    row_slot = jnp.arange(VIS_ROWS, dtype=jnp.int32)
    half_of_row = row_slot // (slot_half * PAIR_PAGES) % 2
    slot_valid = half_of_row * slot_half + row_slot % slot_half < VIS_TOK
    page_boxes = to_pages(text_boxes.T, text_half)

    def page_meta(boxes_page, length):
        front_part = half_meta(boxes_page[0].T, length, 0)
        back_part = half_meta(boxes_page[1].T, length, 1)
        return tuple((jnp.concatenate([front_piece, back_piece]) for front_piece, back_piece in zip(front_part, back_part)))
    metas = jax.vmap(page_meta)(page_boxes, text_lengths)

    def forward(text_float, maps_float, qkv_float, outw_float, attn_b, in_float, in_b, out_ffn, out_b, gains, shifts, table_float, vis_w, vis_b, bn_g, bn_s):
        slot_mask = slot_valid[:, None]
        count_cells = PAGES * VIS_TOK
        channel_mean = lax.optimization_barrier(jnp.sum(jnp.where(slot_mask, maps_float, 0.0), axis=0)) / count_cells
        channel_square = lax.optimization_barrier(jnp.sum(jnp.where(slot_mask, maps_float * maps_float, 0.0), axis=0)) / count_cells
        inverse_std = lax.rsqrt(channel_square - channel_mean * channel_mean + norm_epsilon)
        normalized = jnp.where(slot_mask, (maps_float - channel_mean) * inverse_std * bn_g + bn_s, 0.0)
        visual_tokens = low_back(jnp.dot(low(normalized), vis_w, precision=highest) + vis_b)
        page_states = jnp.concatenate([to_pages(text_float, text_half), to_pages(visual_tokens, slot_half)], axis=2)
        page_states = page_states.reshape(PAGES, 2 * page_rows, D)
        weights = (qkv_float, outw_float, attn_b, in_float, in_b, out_ffn, out_b, gains, shifts)

        def run_page(block_item):
            return page_forward(block_item[0], block_item[1:], weights, table_float)
        outputs = lax.map(jax.checkpoint(run_page), (page_states,) + metas)
        return from_pages(outputs.reshape(PAGES, 2, page_rows, D), page_rows)
    float_args = tuple((array.astype(jnp.float32) for array in (text_states, visual_maps, qkv_weight, out_weight, attn_bias, ffn_in, ffn_in_bias, ffn_out, ffn_out_bias, norm_gain, norm_shift, bias_table, vis_weight, vis_bias, bn_gain, bn_shift)))
    outputs, pullback = jax.vjp(forward, *float_args)
    gradients = pullback(cotangent.astype(jnp.float32))
    return (outputs.astype(jnp.bfloat16), gradients[0], gradients[1], gradients[2], gradients[3], gradients[4], gradients[5], gradients[6], gradients[7], gradients[8], gradients[9], gradients[10], gradients[11], gradients[12], gradients[13], gradients[14], gradients[15])
```

```python
import jax
import jax.numpy as jnp
import numpy as np
from jax import lax
from jax.experimental import pallas as pl
from jax.experimental.pallas import tpu as pltpu
from jax.sharding import PartitionSpec as P

HEADS = 12
HEAD_DIM = 64
VIS_TOK = 49
VIS_SLOTS = 64
POS_BINS = 32
BOX_BINS = 64
LAYERS = 2
BUCKETS = POS_BINS + 2 * BOX_BINS

HALF_TEXT = 256
HALF_SLOTS = VIS_SLOTS // 2
ROWS = HALF_TEXT + HALF_SLOTS
KEYS = 640
PAIRS = HEADS // 2
LANES = 128
norm_epsilon = 1e-05
NEVER = -1e30
bf16 = jnp.bfloat16
f32 = jnp.float32
MIB = 1 << 20


def mesh_bits(axis):
    return (lax.axis_size(axis) - 1).bit_length()


def flipped(block, axis, bit):
    count = lax.axis_size(axis)
    return lax.ppermute(block, axis, [(i, i ^ (1 << bit)) for i in range(count)])


def total_over_all(value):
    for axis in ("tp", "seq"):
        for bit in range(mesh_bits(axis)):
            value = value + flipped(value, axis, bit)
    return value


def add_low(left, right):
    return (left.astype(f32) + right.astype(f32)).astype(bf16)


def scatter_sum(keep, send, order):
    bits = mesh_bits("tp")
    part = add_low(keep, flipped(send, "tp", 0))
    shape = part.shape[1:]
    part = part.reshape((2,) * (bits - 1) + shape)
    left = list(range(1, bits))
    for bit in order(bits):
        axis = len(left) - 1 - left.index(bit)
        low = lax.index_in_dim(part, 0, axis, keepdims=False)
        high = lax.index_in_dim(part, 1, axis, keepdims=False)
        part = add_low(low, flipped(high, "tp", bit))
        left.remove(bit)
    for bit in range(mesh_bits("seq")):
        part = add_low(part, flipped(part, "seq", bit))
    return part.astype(f32)


def low_first(bits):
    return list(range(1, bits))


def high_first(bits):
    return list(range(2, bits)) + [1]


def page_places(half, length, own_boxes, other_boxes):
    def slots(width, first, second):
        lane = lax.broadcasted_iota(jnp.int32, (1, width), 1)
        place = jnp.where(lane < HALF_SLOTS, first + lane, second + lane - HALF_SLOTS)
        place = jnp.where(lane < VIS_SLOTS, place, VIS_SLOTS - 1)
        row = (place * 37) >> 8
        return place, 71 + 143 * (place - 7 * row), 71 + 143 * row

    text = lax.broadcasted_iota(jnp.int32, (1, HALF_TEXT), 1)
    own_text = half * HALF_TEXT + text
    other_text = (1 - half) * HALF_TEXT + text
    slot = slots(LANES, half * HALF_SLOTS, (1 - half) * HALF_SLOTS)
    lane = lax.broadcasted_iota(jnp.int32, (1, LANES), 1)
    slot_used = jnp.where((slot[0] < VIS_TOK) & (lane < VIS_SLOTS), 1, 0)
    keys = (
        jnp.concatenate([own_text, other_text, slot[0]], axis=1),
        jnp.concatenate([own_boxes[0:1], other_boxes[0:1], slot[1]], axis=1),
        jnp.concatenate([own_boxes[1:2], other_boxes[1:2], slot[2]], axis=1),
        jnp.concatenate(
            [
                jnp.where(own_text < length, 1, 0),
                jnp.where(other_text < length, 1, 0),
                slot_used,
            ],
            axis=1,
        ),
    )
    queries = (
        jnp.concatenate([own_text, slot[0]], axis=1),
        jnp.concatenate([own_boxes[0:1], slot[1]], axis=1),
        jnp.concatenate([own_boxes[1:2], slot[2]], axis=1),
    )
    return keys, queries


def as_columns(rows):
    stacked = jnp.concatenate(list(rows) + [rows[0]] * (8 - len(rows)), axis=0)
    turned = jnp.transpose(stacked.astype(f32), (1, 0)).astype(jnp.int32)
    return [turned[:ROWS, i : i + 1] for i in range(len(rows))]


def bias_kernel(facts, own_boxes, other_boxes, table_a, table_b, out, near_s, across_s, down_s):
    @pl.when(pl.program_id(0) == 0)
    def _():
        keys, queries = page_places(facts[0], facts[1], own_boxes[...], other_boxes[...])
        place, x, y = as_columns(queries)
        near_s[...] = jnp.clip(keys[0] - place, -16, 15) + 16
        across_s[...] = jnp.clip((keys[1] - x) >> 4, -32, 31) + 64
        down_s[...] = jnp.where(
            keys[3] > 0, jnp.clip((keys[2] - y) >> 4, -32, 31) + 32, BOX_BINS
        )

    a = jnp.broadcast_to(table_a[0, 0:1, :], (ROWS, LANES))
    b = jnp.broadcast_to(table_b[0, 0:1, :], (ROWS, LANES))
    for tile in range(KEYS // LANES):
        span = slice(tile * LANES, (tile + 1) * LANES)

        def look(table, codes):
            return jnp.take_along_axis(table, codes, axis=1, mode="promise_in_bounds")

        out[0, :, span] = (
            look(a, near_s[:, span]) + look(a, across_s[:, span]) + look(b, down_s[:, span])
        )


def make_bias(facts, own_boxes, other_boxes, bias_table):
    columns = bias_table.T
    table_a = jnp.pad(columns[:, : POS_BINS + BOX_BINS], ((0, 0), (0, LANES - POS_BINS - BOX_BINS)))
    table_b = jnp.pad(
        columns[:, POS_BINS + BOX_BINS :],
        ((0, 0), (0, LANES - BOX_BINS)),
        constant_values=NEVER,
    )
    spread = lambda t: jnp.broadcast_to(t[:, None, :], (HEADS, 8, LANES))
    whole = lambda h, facts: (0, 0)
    return pl.pallas_call(
        bias_kernel,
        out_shape=jax.ShapeDtypeStruct((HEADS, ROWS, KEYS), f32),
        grid_spec=pltpu.PrefetchScalarGridSpec(
            num_scalar_prefetch=1,
            grid=(HEADS,),
            in_specs=[
                pl.BlockSpec((2, HALF_TEXT), whole),
                pl.BlockSpec((2, HALF_TEXT), whole),
                pl.BlockSpec((1, 8, LANES), lambda h, facts: (h, 0, 0)),
                pl.BlockSpec((1, 8, LANES), lambda h, facts: (h, 0, 0)),
            ],
            out_specs=pl.BlockSpec((1, ROWS, KEYS), lambda h, facts: (h, 0, 0)),
            scratch_shapes=[pltpu.VMEM((ROWS, KEYS), jnp.int32)] * 3,
        ),
        compiler_params=pltpu.CompilerParams(vmem_limit_bytes=24 * MIB),
        cost_estimate=pl.CostEstimate(
            flops=40 * HEADS * ROWS * KEYS,
            bytes_accessed=4 * HEADS * ROWS * KEYS,
            transcendentals=0,
        ),
        name="score_bias",
    )(facts, own_boxes, other_boxes, spread(table_a), spread(table_b))


def table_kernel(facts, own_boxes, other_boxes, ds_a, ds_b, out, right, left, band, cx, cy, high):
    @pl.when(pl.program_id(0) == 0)
    def _():
        keys, queries = page_places(facts[0], facts[1], own_boxes[...], other_boxes[...])
        place, x, y = as_columns(queries)
        diff = keys[0] - place
        band[...] = jnp.where((diff >= -16) & (diff <= 15), 1.0, 0.0).astype(bf16)
        high[...] = jnp.where(diff > 15, 1.0, 0.0).astype(bf16)
        cx[...] = jnp.where((keys[1] & 15) < (x & 15), 1.0, 0.0).astype(bf16)
        cy[...] = jnp.where((keys[2] & 15) < (y & 15), 1.0, 0.0).astype(bf16)
        row = lax.broadcasted_iota(jnp.int32, (64, KEYS), 0)
        key_hot = [
            jnp.where((63 - row) == (code & 63), 1.0, 0.0)
            for code in (keys[1] >> 4, keys[2] >> 4, keys[0])
        ]
        key_hot.append(jnp.zeros((64, KEYS), f32))
        right[...] = jnp.transpose(jnp.concatenate(key_hot, axis=0), (1, 0)).astype(bf16)
        row = lax.broadcasted_iota(jnp.int32, (64, 384), 0)
        query_hot = [
            jnp.where(row == queries[1] >> 4, 1.0, 0.0),
            jnp.where(row == queries[2] >> 4, 1.0, 0.0),
            jnp.where(row[:32] + 64 == queries[2] >> 4, 1.0, 0.0),
            jnp.where(row == (queries[0] & 63), 1.0, 0.0),
        ]
        left[...] = jnp.concatenate(query_hot, axis=0)[:, :ROWS].astype(bf16)

    total = (ds_a[0].astype(f32) + ds_b[0].astype(f32)).astype(bf16)
    hot = right[...]
    query_hot = left[...]

    def fold(values, columns, rows):
        inner = jnp.dot(values, hot[:, columns], preferred_element_type=f32).astype(bf16)
        return jnp.dot(query_hot[rows], inner, preferred_element_type=f32)

    plain = fold(total, slice(0, 128), slice(0, 160))
    by_x = fold(total * cx[...], slice(0, 128), slice(0, 64))
    by_y = fold(total * cy[...], slice(0, 128), slice(64, 160))
    near = fold(total * band[...], slice(128, 256), slice(160, 224))

    def diagonals(square):
        lane = lax.broadcasted_iota(jnp.int32, square.shape, 1)
        square = jnp.where(lane < 64, square, 0.0)
        turned = pltpu.roll(square, 0, axis=1, stride=1, stride_axis=0)
        return jnp.sum(turned, axis=0, keepdims=True)

    def second(square):
        return pltpu.roll(square, 64, axis=1)

    above = jnp.sum((total * high[...]).astype(f32), axis=0, keepdims=True)
    above = sum(above[:, t * LANES : (t + 1) * LANES] for t in range(KEYS // LANES))
    out[0] = jnp.concatenate(
        [
            diagonals(plain[:64]),
            diagonals(by_x),
            diagonals(second(plain[64:128])),
            diagonals(second(by_y[:64])),
            diagonals(near),
            above,
            diagonals(second(plain[128:])),
            diagonals(second(by_y[64:])),
        ],
        axis=0,
    )


def table_bins():
    bins = np.zeros((8, LANES, BUCKETS), np.float32)
    for c in range(127):
        diff = 63 - c
        for kind, base in ((0, POS_BINS), (1, POS_BINS + BOX_BINS)):
            here = base + 32 + min(max(diff, -32), 31)
            below = base + 32 + min(max(diff - 1, -32), 31)
            bins[2 * kind, c, here] += 1
            bins[2 * kind + 1, c, below] += 1
            bins[2 * kind + 1, c, here] -= 1
        far = -1 - c
        bins[6, c, 128 + max(far, -32)] += 1
        bins[7, c, 128 + max(far - 1, -32)] += 1
        bins[7, c, 128 + max(far, -32)] -= 1
        near = (diff + 32) % 64 - 32
        if -16 <= near <= 15:
            bins[4, c, near + 16] += 1
        bins[0, c, 0] += 1
        bins[4, c, 0] -= 1
    bins[5, :, 31] += 1
    bins[5, :, 0] -= 1
    return bins


def make_table_grad(facts, own_boxes, other_boxes, ds_a, ds_b):
    whole = lambda h, facts: (0, 0)
    head = pl.BlockSpec((1, ROWS, KEYS), lambda h, facts: (h, 0, 0))
    folded = pl.pallas_call(
        table_kernel,
        out_shape=jax.ShapeDtypeStruct((HEADS, 8, LANES), f32),
        grid_spec=pltpu.PrefetchScalarGridSpec(
            num_scalar_prefetch=1,
            grid=(HEADS,),
            in_specs=[
                pl.BlockSpec((2, HALF_TEXT), whole),
                pl.BlockSpec((2, HALF_TEXT), whole),
                head,
                head,
            ],
            out_specs=pl.BlockSpec((1, 8, LANES), lambda h, facts: (h, 0, 0)),
            scratch_shapes=[
                pltpu.VMEM((KEYS, 256), bf16),
                pltpu.VMEM((224, ROWS), bf16),
                pltpu.VMEM((ROWS, KEYS), bf16),
                pltpu.VMEM((ROWS, KEYS), bf16),
                pltpu.VMEM((ROWS, KEYS), bf16),
                pltpu.VMEM((ROWS, KEYS), bf16),
            ],
        ),
        compiler_params=pltpu.CompilerParams(vmem_limit_bytes=24 * MIB),
        cost_estimate=pl.CostEstimate(
            flops=HEADS * 2 * 4 * ROWS * KEYS * 256,
            bytes_accessed=4 * HEADS * ROWS * KEYS,
            transcendentals=0,
        ),
        name="table_grad",
    )(facts, own_boxes, other_boxes, ds_a, ds_b)
    bins = jnp.asarray(table_bins()).reshape(8 * LANES, BUCKETS)
    return lax.dot_general(
        bins,
        folded.reshape(HEADS, 8 * LANES),
        (((0,), (1,)), ((), ())),
        precision=lax.Precision.HIGHEST,
        preferred_element_type=f32,
    )


def whole_page(own, other):
    return jnp.concatenate(
        [
            own[:HALF_TEXT],
            other[:HALF_TEXT],
            own[HALF_TEXT:],
            other[HALF_TEXT:],
            jnp.zeros((KEYS - 2 * ROWS, own.shape[1]), own.dtype),
        ],
        axis=0,
    )


def page_split(both):
    mid = 2 * HALF_TEXT
    own = jnp.concatenate([both[:HALF_TEXT], both[mid : mid + HALF_SLOTS]], axis=0)
    other = jnp.concatenate(
        [both[HALF_TEXT:mid], both[mid + HALF_SLOTS : mid + VIS_SLOTS]], axis=0
    )
    return own, other


def nt_dot(left, right):
    return lax.dot_general(left, right, (((1,), (1,)), ((), ())), preferred_element_type=f32)


def tn_dot(left, right):
    return lax.dot_general(left, right, (((0,), (0,)), ((), ())), preferred_element_type=f32)


def attend_kernel(q_ref, ko, kp, vo, vp, bias, ctx, soft):
    q = q_ref[...] * jnp.asarray(HEAD_DIM**-0.5, bf16)
    keys = whole_page(ko[...], kp[...])
    values = whole_page(vo[...], vp[...])
    first = lax.broadcasted_iota(jnp.int32, (ROWS, LANES), 1) < HEAD_DIM
    parts = []
    for head in range(2):
        mine = jnp.where(first if head == 0 else ~first, q, jnp.zeros_like(q))
        scores = nt_dot(mine, keys) + bias[head]
        raised = jnp.exp(scores - jnp.max(scores, axis=1, keepdims=True))
        weights = (raised * (1.0 / jnp.sum(raised, axis=1, keepdims=True))).astype(bf16)
        soft[head] = weights
        parts.append(jnp.dot(weights, values, preferred_element_type=f32))
    ctx[...] = jnp.where(first, parts[0], parts[1]).astype(bf16)


def attend(q, ko, kp, vo, vp, bias):
    slab = pl.BlockSpec((ROWS, LANES), lambda p: (0, p))
    heads = pl.BlockSpec((2, ROWS, KEYS), lambda p: (p, 0, 0))
    return pl.pallas_call(
        attend_kernel,
        grid=(PAIRS,),
        in_specs=[slab] * 5 + [heads],
        out_specs=[slab, heads],
        out_shape=[
            jax.ShapeDtypeStruct(q.shape, bf16),
            jax.ShapeDtypeStruct((HEADS, ROWS, KEYS), bf16),
        ],
        compiler_params=pltpu.CompilerParams(vmem_limit_bytes=32 * MIB),
        cost_estimate=pl.CostEstimate(
            flops=HEADS * 4 * ROWS * KEYS * 256,
            bytes_accessed=6 * HEADS * ROWS * KEYS,
            transcendentals=HEADS * ROWS * KEYS,
        ),
        name="attend",
    )(q, ko, kp, vo, vp, bias)


def attend_back_kernel(q_ref, ko, kp, vo, vp, dc_ref, soft, dq, ds, dk_own, dk_other, dv_own, dv_other):
    scale = HEAD_DIM**-0.5
    q = q_ref[...]
    dc = dc_ref[...]
    keys = whole_page(ko[...], kp[...])
    values = whole_page(vo[...], vp[...])
    first = lax.broadcasted_iota(jnp.int32, (ROWS, LANES), 1) < HEAD_DIM
    q_turned = jnp.transpose(q.astype(f32), (1, 0)).astype(bf16)
    dc_turned = jnp.transpose(dc.astype(f32), (1, 0)).astype(bf16)
    dq_parts, dk_parts, dv_parts = [], [], []
    for head in range(2):
        span = slice(head * HEAD_DIM, (head + 1) * HEAD_DIM)
        mine = jnp.where(first if head == 0 else ~first, dc, jnp.zeros_like(dc))
        weights = soft[head]
        weights_f = weights.astype(f32)
        flow = nt_dot(mine, values)
        share = jnp.sum(weights_f * flow, axis=1, keepdims=True)
        score_grad = (weights_f * (flow - share)).astype(bf16)
        ds[head] = score_grad
        dq_parts.append(jnp.dot(score_grad, keys, preferred_element_type=f32))
        dk_parts.append(jnp.dot(q_turned[span], score_grad, preferred_element_type=f32))
        dv_parts.append(jnp.dot(dc_turned[span], weights, preferred_element_type=f32))
    dq[...] = (jnp.where(first, dq_parts[0], dq_parts[1]) * scale).astype(bf16)
    own, other = page_split(jnp.transpose(jnp.concatenate(dk_parts, axis=0) * scale, (1, 0)))
    dk_own[...] = own
    dk_other[...] = other.astype(bf16)
    own, other = page_split(jnp.transpose(jnp.concatenate(dv_parts, axis=0), (1, 0)))
    dv_own[...] = own
    dv_other[...] = other.astype(bf16)


def attend_back(q, ko, kp, vo, vp, dctx, soft):
    slab = pl.BlockSpec((ROWS, LANES), lambda p: (0, p))
    heads = pl.BlockSpec((2, ROWS, KEYS), lambda p: (p, 0, 0))
    low = jax.ShapeDtypeStruct(q.shape, bf16)
    wide = jax.ShapeDtypeStruct(q.shape, f32)
    return pl.pallas_call(
        attend_back_kernel,
        grid=(PAIRS,),
        in_specs=[slab] * 6 + [heads],
        out_specs=[slab, heads] + [slab] * 4,
        out_shape=[
            low,
            jax.ShapeDtypeStruct((HEADS, ROWS, KEYS), bf16),
            wide,
            low,
            wide,
            low,
        ],
        compiler_params=pltpu.CompilerParams(vmem_limit_bytes=32 * MIB),
        cost_estimate=pl.CostEstimate(
            flops=HEADS * 8 * ROWS * KEYS * 256,
            bytes_accessed=4 * HEADS * ROWS * KEYS,
            transcendentals=0,
        ),
        name="attend_back",
    )(q, ko, kp, vo, vp, dctx, soft)


def ffn_kernel(me, x_ref, own_w, mate_w, bias, act, slope, branch):
    step = pl.program_id(0)
    width = x_ref.shape[1]
    x = x_ref[...]

    @pl.when(step == 0)
    def _():
        branch[...] = jnp.zeros_like(branch)

    total = None
    for index, block in enumerate((own_w, mate_w)):
        weights = block[0]
        hidden = nt_dot(x, weights[:, :width]) + bias[pl.ds(me[0] ^ (2 * step + index), 1), :]
        half_cdf = 0.5 + 0.5 * lax.erf(hidden * 0.5**0.5)
        low = (hidden * half_cdf).astype(bf16)
        act[index] = low
        density = jnp.exp(hidden * hidden * -0.5) * (1.0 / (2.0 * np.pi) ** 0.5)
        slope[index] = (half_cdf + hidden * density).astype(bf16)
        term = jnp.dot(low, weights[:, width:], preferred_element_type=f32)
        total = term if total is None else total + term
    branch[...] += total


def ffn(me, layer, x, gathered, bias, units):
    groups = bias.shape[0]
    rows, width = x.shape
    whole = lambda i, me: (0, 0)
    pick = lambda which: pl.BlockSpec(
        (1, units, 2 * width), lambda i, me: (me[0] ^ (2 * i + which), layer, 0)
    )
    kept = pl.BlockSpec((2, rows, units), lambda i, me: (i, 0, 0))
    kept_shape = jax.ShapeDtypeStruct((groups, rows, units), bf16)
    return pl.pallas_call(
        ffn_kernel,
        out_shape=[kept_shape, kept_shape, jax.ShapeDtypeStruct((rows, width), f32)],
        grid_spec=pltpu.PrefetchScalarGridSpec(
            num_scalar_prefetch=1,
            grid=(groups // 2,),
            in_specs=[
                pl.BlockSpec((rows, width), whole),
                pick(0),
                pick(1),
                pl.BlockSpec(bias.shape, whole),
            ],
            out_specs=[kept, kept, pl.BlockSpec((rows, width), whole)],
        ),
        compiler_params=pltpu.CompilerParams(vmem_limit_bytes=32 * MIB),
        cost_estimate=pl.CostEstimate(
            flops=4 * rows * width * groups * units,
            bytes_accessed=4 * groups * units * (width + rows),
            transcendentals=2 * rows * groups * units,
        ),
        name="feed_forward",
    )(me, x, gathered, gathered, bias)


def ffn_back_kernel(me, x_ref, dy_ref, own_w, mate_w, act, slope, keep, send, bias_grad, dx):
    step = pl.program_id(0)
    width = x_ref.shape[1]
    x = x_ref[...]
    dy = dy_ref[...]

    @pl.when(step == 0)
    def _():
        dx[...] = jnp.zeros_like(dx)

    total = None
    for index, (block, out) in enumerate(((own_w, keep), (mate_w, send))):
        weights = block[0]
        flow = nt_dot(dy, weights[:, width:])
        grad = (flow * slope[index].astype(f32)).astype(bf16)
        bias_grad[index] = jnp.broadcast_to(
            jnp.sum(grad.astype(f32), axis=0, keepdims=True), bias_grad.shape[1:]
        )
        term = jnp.dot(grad, weights[:, :width], preferred_element_type=f32)
        total = term if total is None else total + term
        out[0, :, :width] = tn_dot(grad, x).astype(bf16)
        out[0, :, width:] = tn_dot(act[index], dy).astype(bf16)
    dx[...] += total


def ffn_back(me, layer, x, dy, gathered, act, slope):
    groups, rows, units = act.shape
    width = x.shape[1]
    whole = lambda i, me: (0, 0)
    pick = lambda which: pl.BlockSpec(
        (1, units, 2 * width), lambda i, me: (me[0] ^ (2 * i + which), layer, 0)
    )
    kept = pl.BlockSpec((2, rows, units), lambda i, me: (i, 0, 0))
    grads = pl.BlockSpec((1, units, 2 * width), lambda i, me: (i, 0, 0))
    grads_shape = jax.ShapeDtypeStruct((groups // 2, units, 2 * width), bf16)
    return pl.pallas_call(
        ffn_back_kernel,
        out_shape=[
            grads_shape,
            grads_shape,
            jax.ShapeDtypeStruct((groups, 8, units), f32),
            jax.ShapeDtypeStruct((rows, width), f32),
        ],
        grid_spec=pltpu.PrefetchScalarGridSpec(
            num_scalar_prefetch=1,
            grid=(groups // 2,),
            in_specs=[
                pl.BlockSpec((rows, width), whole),
                pl.BlockSpec((rows, width), whole),
                pick(0),
                pick(1),
                kept,
                kept,
            ],
            out_specs=[
                grads,
                grads,
                pl.BlockSpec((2, 8, units), lambda i, me: (i, 0, 0)),
                pl.BlockSpec((rows, width), whole),
            ],
        ),
        compiler_params=pltpu.CompilerParams(vmem_limit_bytes=32 * MIB),
        cost_estimate=pl.CostEstimate(
            flops=8 * rows * width * groups * units,
            bytes_accessed=4 * groups * units * (2 * width + rows),
            transcendentals=0,
        ),
        name="feed_forward_back",
    )(me, x, dy, gathered, gathered, act, slope)


def projection_kernel(me, x_ref, ctx_ref, dq, dk, dv, da, keep, send, whole_s):
    groups = 2 * keep.shape[0]
    rows = keep.shape[1]
    width = x_ref.shape[1]
    for index, (left, right) in enumerate(
        ((x_ref, dq), (x_ref, dk), (x_ref, dv), (ctx_ref, da))
    ):
        whole_s[...] = tn_dot(left[...], right[...])
        span = slice(index * width, (index + 1) * width)
        for place in range(groups):
            start = pl.multiple_of((me[0] ^ place) * rows, 8)
            target = keep if place % 2 == 0 else send
            target[place // 2, :, span] = whole_s[pl.ds(start, rows), :].astype(bf16)


def projection_grads(me, x, ctx, dq, dk, dv, da, groups):
    width = x.shape[1]
    vmem = pl.BlockSpec(memory_space=pltpu.VMEM)
    shape = jax.ShapeDtypeStruct((groups // 2, width // groups, 4 * width), bf16)
    return pl.pallas_call(
        projection_kernel,
        out_shape=[shape, shape],
        in_specs=[pl.BlockSpec(memory_space=pltpu.SMEM)] + [vmem] * 6,
        out_specs=[vmem, vmem],
        scratch_shapes=[pltpu.VMEM((width, width), f32)],
        compiler_params=pltpu.CompilerParams(vmem_limit_bytes=32 * MIB),
        cost_estimate=pl.CostEstimate(
            flops=8 * x.shape[0] * width * width,
            bytes_accessed=8 * width * width,
            transcendentals=0,
        ),
        name="projection_grads",
    )(me, x, ctx, dq, dk, dv, da)


def layer_norm(values, gain_row, shift_row):
    center = values - jnp.mean(values, axis=-1, keepdims=True)
    spread = jnp.mean(center * center, axis=-1, keepdims=True)
    return center * lax.rsqrt(spread + norm_epsilon) * gain_row + shift_row


def body(
    text_states,
    visual_maps,
    text_boxes,
    text_lengths,
    qkv_weight,
    out_weight,
    attn_bias,
    ffn_in,
    ffn_in_bias,
    ffn_out,
    ffn_out_bias,
    norm_gain,
    norm_shift,
    bias_table,
    vis_weight,
    vis_bias,
    bn_gain,
    bn_shift,
    cotangent,
):
    tp_index = lax.axis_index("tp")
    tp_size = lax.axis_size("tp")
    half = tp_index % 2
    page = (lax.axis_index("seq") * tp_size + tp_index) // 2
    me = tp_index.astype(jnp.int32).reshape(1)
    units = ffn_in.shape[1]
    width = text_states.shape[1]
    text_rows = text_states.shape[0]

    bias_rows = jnp.pad(ffn_in_bias, ((0, 16 - LAYERS), (0, 2 * width - units)))
    packed = jnp.concatenate(
        [
            jnp.concatenate([ffn_in, ffn_out], axis=2).reshape(LAYERS * units, 2 * width),
            bias_rows,
        ],
        axis=0,
    )
    gathered = lax.all_gather(packed, "tp", axis=0)
    hidden_bias = gathered[:, LAYERS * units : LAYERS * units + LAYERS, :units].astype(f32)

    other_boxes = flipped(text_boxes, "tp", 0)
    length = lax.dynamic_index_in_dim(text_lengths, page, 0, keepdims=False)
    facts = jnp.stack([half.astype(jnp.int32), length])
    score_bias = make_bias(facts, text_boxes, other_boxes, bias_table)

    count_cells = text_lengths.shape[0] * VIS_TOK
    maps_float = visual_maps.astype(f32)
    slot_place = half * HALF_SLOTS + jnp.arange(HALF_SLOTS, dtype=jnp.int32)
    slot_mask = (slot_place < VIS_TOK)[:, None]
    masked_maps = jnp.where(slot_mask, maps_float, 0.0)
    sums = total_over_all(
        jnp.stack([jnp.sum(masked_maps, axis=0), jnp.sum(masked_maps * masked_maps, axis=0)])
    )
    channel_mean = sums[0] / count_cells
    inverse_std = lax.rsqrt(sums[1] / count_cells - channel_mean * channel_mean + norm_epsilon)
    centered_hat = jnp.where(slot_mask, (maps_float - channel_mean) * inverse_std, 0.0)
    normal_low = jnp.where(slot_mask, centered_hat * bn_gain + bn_shift, 0.0).astype(bf16)
    visual_tokens = jnp.dot(normal_low, vis_weight, preferred_element_type=f32) + vis_bias
    states = jnp.concatenate([text_states.astype(f32), visual_tokens], axis=0)

    saved = []
    for layer in range(LAYERS):
        rounded = states.astype(bf16)
        project = lambda index: jnp.dot(
            rounded, qkv_weight[layer, index], preferred_element_type=f32
        )
        key_value = jnp.concatenate(
            [project(1).astype(bf16), (project(2) + attn_bias[layer, 1]).astype(bf16)], axis=1
        )
        other_key_value = flipped(key_value, "tp", 0)
        query = (project(0) + attn_bias[layer, 0]).astype(bf16)
        parts = (
            query,
            key_value[:, :width],
            other_key_value[:, :width],
            key_value[:, width:],
            other_key_value[:, width:],
        )
        context, soft = attend(*parts, score_bias)
        attended = (
            jnp.dot(context, out_weight[layer], preferred_element_type=f32) + attn_bias[layer, 2]
        )
        residual_one = states + attended
        normed = layer_norm(residual_one, norm_gain[layer, 0], norm_shift[layer, 0])
        normed_low = normed.astype(bf16)
        act, slope, branch = ffn(
            me, layer, normed_low, gathered, hidden_bias[:, layer], units
        )
        residual_two = normed + (branch + ffn_out_bias[layer])
        states = layer_norm(residual_two, norm_gain[layer, 1], norm_shift[layer, 1])
        saved.append((rounded, parts, soft, context, residual_one, normed_low, residual_two, act, slope))
    out_states = states.astype(bf16)

    gradient = cotangent.astype(f32)
    bias_grads = [None] * LAYERS
    bout_grads = [None] * LAYERS
    bin_grads = [None] * LAYERS
    gain_grads = [None] * LAYERS
    shift_grads = [None] * LAYERS
    ffn_shards = [None] * LAYERS
    projection_shards = [None] * LAYERS
    score_grads = [None] * LAYERS
    for layer in reversed(range(LAYERS)):
        rounded, parts, soft, context, residual_one, normed_low, residual_two, act, slope = saved[layer]
        grad_two, gain_two, shift_two = jax.vjp(
            layer_norm, residual_two, norm_gain[layer, 1], norm_shift[layer, 1]
        )[1](gradient)
        branch_grad = grad_two.astype(bf16)
        bout_grads[layer] = jnp.sum(branch_grad.astype(f32), axis=0)
        keep, send, bin_part, normed_grad = ffn_back(
            me, layer, normed_low, branch_grad, gathered, act, slope
        )
        bin_grads[layer] = bin_part[:, 0]
        ffn_shards[layer] = scatter_sum(keep, send, low_first)
        grad_one, gain_one, shift_one = jax.vjp(
            layer_norm, residual_one, norm_gain[layer, 0], norm_shift[layer, 0]
        )[1](grad_two + normed_grad)
        gain_grads[layer] = jnp.stack([gain_one, gain_two])
        shift_grads[layer] = jnp.stack([shift_one, shift_two])
        attended_grad = grad_one.astype(bf16)
        context_grad = nt_dot(attended_grad, out_weight[layer]).astype(bf16)
        query_grad, score_grads[layer], dk_own, dk_other, dv_own, dv_other = attend_back(
            *parts, context_grad, soft
        )
        back = flipped(jnp.concatenate([dk_other, dv_other], axis=1), "tp", 0)
        key_grad = (dk_own + back[:, :width].astype(f32)).astype(bf16)
        value_grad = (dv_own + back[:, width:].astype(f32)).astype(bf16)
        bias_grads[layer] = jnp.stack(
            [
                jnp.sum(query_grad.astype(f32), axis=0),
                jnp.sum(value_grad.astype(f32), axis=0),
                jnp.sum(attended_grad.astype(f32), axis=0),
            ]
        )
        gradient = grad_one + (
            nt_dot(query_grad, qkv_weight[layer, 0])
            + nt_dot(key_grad, qkv_weight[layer, 1])
            + nt_dot(value_grad, qkv_weight[layer, 2])
        )
        keep, send = projection_grads(
            me, rounded, context, query_grad, key_grad, value_grad, attended_grad, tp_size
        )
        projection_shards[layer] = scatter_sum(keep, send, high_first)

    table_grad = make_table_grad(facts, text_boxes, other_boxes, score_grads[0], score_grads[1])
    grad_text = gradient[:text_rows]
    token_grad = gradient[text_rows:].astype(bf16)
    vis_weight_grad = total_over_all(tn_dot(normal_low, token_grad).astype(bf16)).astype(f32)
    normal_grad = jnp.where(slot_mask, nt_dot(token_grad, vis_weight), 0.0)

    small = [
        jnp.stack(bias_grads).reshape(-1),
        jnp.stack(bout_grads).reshape(-1),
        jnp.stack(gain_grads).reshape(-1),
        jnp.stack(shift_grads).reshape(-1),
        table_grad.reshape(-1),
        jnp.sum(token_grad.astype(f32), axis=0),
        jnp.sum(normal_grad * centered_hat, axis=0),
        jnp.sum(normal_grad, axis=0),
        jnp.take(jnp.stack(bin_grads, axis=1), tp_index ^ jnp.arange(tp_size), axis=0).reshape(-1),
    ]
    sizes = [part.size for part in small]
    flat = jnp.concatenate(small)
    flat = jnp.pad(flat, (0, -flat.size % 1024)).reshape(-1, 128)
    flat = total_over_all(flat).reshape(-1)
    found = []
    start = 0
    for size in sizes:
        found.append(flat[start : start + size])
        start += size
    bias_total, bout_total, gain_total, shift_total, table_total, visb_total = found[:6]
    bn_gain_grad, bn_shift_grad, bin_total = found[6:]
    bin_total = lax.dynamic_index_in_dim(
        bin_total.reshape(tp_size, LAYERS, units), tp_index, 0, keepdims=False
    )
    grad_maps = jnp.where(
        slot_mask,
        inverse_std
        * (
            normal_grad * bn_gain
            - bn_gain * bn_shift_grad / count_cells
            - centered_hat * (bn_gain * bn_gain_grad / count_cells)
        ),
        0.0,
    )
    projections = jnp.stack(projection_shards).reshape(LAYERS, -1, 4, width)
    ffn_total = jnp.stack(ffn_shards)
    return (
        out_states,
        grad_text,
        grad_maps,
        projections[:, :, :3].transpose(0, 2, 1, 3),
        projections[:, :, 3],
        bias_total.reshape(attn_bias.shape),
        ffn_total[:, :, :width],
        bin_total,
        ffn_total[:, :, width:],
        bout_total.reshape(ffn_out_bias.shape),
        gain_total.reshape(norm_gain.shape),
        shift_total.reshape(norm_shift.shape),
        table_total.reshape(bias_table.shape),
        vis_weight_grad,
        visb_total,
        bn_gain_grad,
        bn_shift_grad,
    )


def solution(mesh):
    rows = P(("seq", "tp"), None)
    units = P(None, "tp", None)
    return jax.shard_map(
        body,
        mesh=mesh,
        in_specs=(
            rows,
            rows,
            P(None, ("seq", "tp")),
            P(),
            P(),
            P(),
            P(),
            units,
            P(None, "tp"),
            units,
            P(),
            P(),
            P(),
            P(),
            P(),
            P(),
            P(),
            P(),
            rows,
        ),
        out_specs=(
            rows,
            rows,
            rows,
            P(None, None, "tp", None),
            units,
            P(),
            units,
            P(None, "tp"),
            units,
            P(),
            P(),
            P(),
            P(),
            P(),
            P(),
            P(),
            P(),
        ),
        check_vma=False,
    )
```

```python
import functools

import jax
import jax.numpy as jnp
import numpy as np
from jax import lax
from jax.experimental import pallas as pl
from jax.experimental.pallas import tpu as pltpu
from jax.sharding import PartitionSpec as P

HEADS = 12
HEAD_DIM = 64
VIS_TOK = 49
VIS_SLOTS = 64
POS_BINS = 32
BOX_BINS = 64
LAYERS = 2
BUCKETS = POS_BINS + 2 * BOX_BINS

HALF_TEXT = 256
HALF_SLOTS = VIS_SLOTS // 2
ROWS = HALF_TEXT + HALF_SLOTS
KEYS = 640
PAIRS = HEADS // 2
LANES = 128
norm_epsilon = 1e-05
NEVER = -1e30
bf16 = jnp.bfloat16
f32 = jnp.float32
MIB = 1 << 20
brief = pl.CostEstimate(flops=1, bytes_accessed=1, transcendentals=0)


def mesh_bits(axis):
    return (lax.axis_size(axis) - 1).bit_length()


def flipped(block, axis, bit):
    count = lax.axis_size(axis)
    return lax.ppermute(block, axis, [(i, i ^ (1 << bit)) for i in range(count)])


def total_over_all(value):
    for axis in ("tp", "seq"):
        for bit in range(mesh_bits(axis)):
            value = value + flipped(value, axis, bit)
    return value


def add_low(left, right):
    return (left.astype(f32) + right.astype(f32)).astype(bf16)


def tied(values, after):
    return lax.optimization_barrier((tuple(values), tuple(after)))[0]


class Reducer:
    def __init__(self, left, right, steps):
        self.bits = [bit for bit in reversed(range(1, mesh_bits("tp")))]
        shape = (2,) * len(self.bits) + left.shape[1:]
        self.left = left.reshape(shape)
        self.right = right.reshape(shape)
        self.steps = list(steps) + [("all", bit) for bit in range(1, mesh_bits("seq"))]

    def step(self, *after):
        if after:
            self.left, self.right = tied((self.left, self.right), after)
        what = self.steps.pop(0)
        if isinstance(what, tuple):
            self.left = add_low(self.left, self.right)
            self.right = flipped(self.left, "seq", what[1])
            return
        axis = self.bits.index(what)
        self.bits.remove(what)
        pick = lambda block, which: lax.index_in_dim(block, which, axis, keepdims=False)
        going = add_low(pick(self.left, 1), pick(self.right, 1))
        self.left, self.right = (
            add_low(pick(self.left, 0), pick(self.right, 0)),
            flipped(going, "tp", what),
        )

    def finish(self):
        while self.steps:
            self.step()
        mine = add_low(self.left, self.right)
        other = flipped(mine, "seq", 0)
        first = lax.axis_index("seq") % 2 == 0
        both = (jnp.where(first, mine, other), jnp.where(first, other, mine))
        return jnp.concatenate(both, axis=-1).astype(f32)


class Gather:
    def __init__(self, value):
        self.left = value
        self.right = None
        self.steps = list(range(mesh_bits("seq")))

    def step(self, *after):
        if self.right is not None:
            self.left = add_low(self.left, self.right)
        if after:
            (self.left,) = tied((self.left,), after)
        self.right = flipped(self.left, "seq", self.steps.pop(0))

    def finish(self):
        while self.steps:
            self.step()
        return self.left.astype(f32) + self.right.astype(f32)


def over_chips(value):
    count = lax.axis_size("tp")
    groups = [list(range(core, count, 2)) for core in range(2)]
    return lax.psum_scatter(value, "tp", scatter_dimension=0, axis_index_groups=groups)


def low_first():
    return list(range(1, mesh_bits("tp")))


def high_first():
    return list(range(2, mesh_bits("tp"))) + [1]


def page_places(half, length, own_boxes, other_boxes):
    def slots(width, first, second):
        lane = lax.broadcasted_iota(jnp.int32, (1, width), 1)
        place = jnp.where(lane < HALF_SLOTS, first + lane, second + lane - HALF_SLOTS)
        place = jnp.where(lane < VIS_SLOTS, place, VIS_SLOTS - 1)
        row = (place * 37) >> 8
        return place, 71 + 143 * (place - 7 * row), 71 + 143 * row

    text = lax.broadcasted_iota(jnp.int32, (1, HALF_TEXT), 1)
    own_text = half * HALF_TEXT + text
    other_text = (1 - half) * HALF_TEXT + text
    slot = slots(LANES, half * HALF_SLOTS, (1 - half) * HALF_SLOTS)
    lane = lax.broadcasted_iota(jnp.int32, (1, LANES), 1)
    slot_used = jnp.where((slot[0] < VIS_TOK) & (lane < VIS_SLOTS), 1, 0)
    keys = (
        jnp.concatenate([own_text, other_text, slot[0]], axis=1),
        jnp.concatenate([own_boxes[0:1], other_boxes[0:1], slot[1]], axis=1),
        jnp.concatenate([own_boxes[1:2], other_boxes[1:2], slot[2]], axis=1),
        jnp.concatenate(
            [
                jnp.where(own_text < length, 1, 0),
                jnp.where(other_text < length, 1, 0),
                slot_used,
            ],
            axis=1,
        ),
    )
    queries = (
        jnp.concatenate([own_text, slot[0]], axis=1),
        jnp.concatenate([own_boxes[0:1], slot[1]], axis=1),
        jnp.concatenate([own_boxes[1:2], slot[2]], axis=1),
    )
    return keys, queries


def as_columns(rows):
    stacked = jnp.concatenate(list(rows) + [rows[0]] * (8 - len(rows)), axis=0)
    turned = jnp.transpose(stacked.astype(f32), (1, 0)).astype(jnp.int32)
    return [turned[:ROWS, i : i + 1] for i in range(len(rows))]


def bias_kernel(facts, own_boxes, other_boxes, table_a, table_b, out, near_s, across_s, down_s):
    @pl.when(pl.program_id(0) == 0)
    def _():
        keys, queries = page_places(facts[0], facts[1], own_boxes[...], other_boxes[...])
        place, x, y = as_columns(queries)
        near_s[...] = jnp.clip(keys[0] - place, -16, 15) + 16
        across_s[...] = jnp.clip((keys[1] - x) >> 4, -32, 31) + 64
        down_s[...] = jnp.where(
            keys[3] > 0, jnp.clip((keys[2] - y) >> 4, -32, 31) + 32, BOX_BINS
        )

    a = jnp.broadcast_to(table_a[0, 0:1, :], (ROWS, LANES))
    b = jnp.broadcast_to(table_b[0, 0:1, :], (ROWS, LANES))
    for tile in range(KEYS // LANES):
        span = slice(tile * LANES, (tile + 1) * LANES)

        def look(table, codes):
            return jnp.take_along_axis(table, codes, axis=1, mode="promise_in_bounds")

        out[0, :, span] = (
            look(a, near_s[:, span]) + look(a, across_s[:, span]) + look(b, down_s[:, span])
        )


def make_bias(facts, own_boxes, other_boxes, bias_table):
    columns = bias_table.T
    table_a = jnp.pad(columns[:, : POS_BINS + BOX_BINS], ((0, 0), (0, LANES - POS_BINS - BOX_BINS)))
    table_b = jnp.pad(
        columns[:, POS_BINS + BOX_BINS :],
        ((0, 0), (0, LANES - BOX_BINS)),
        constant_values=NEVER,
    )
    spread = lambda t: jnp.broadcast_to(t[:, None, :], (HEADS, 8, LANES))
    whole = lambda h, facts: (0, 0)
    return pl.pallas_call(
        bias_kernel,
        out_shape=jax.ShapeDtypeStruct((HEADS, ROWS, KEYS), f32),
        grid_spec=pltpu.PrefetchScalarGridSpec(
            num_scalar_prefetch=1,
            grid=(HEADS,),
            in_specs=[
                pl.BlockSpec((2, HALF_TEXT), whole),
                pl.BlockSpec((2, HALF_TEXT), whole),
                pl.BlockSpec((1, 8, LANES), lambda h, facts: (h, 0, 0)),
                pl.BlockSpec((1, 8, LANES), lambda h, facts: (h, 0, 0)),
            ],
            out_specs=pl.BlockSpec((1, ROWS, KEYS), lambda h, facts: (h, 0, 0)),
            scratch_shapes=[pltpu.VMEM((ROWS, KEYS), jnp.int32)] * 3,
        ),
        compiler_params=pltpu.CompilerParams(vmem_limit_bytes=50 * MIB),
        cost_estimate=brief,
        name="score_bias",
    )(facts, own_boxes, other_boxes, spread(table_a), spread(table_b))


def table_kernel(facts, own_boxes, other_boxes, ds_a, ds_b, *rest):
    out, right, left, band, cx, cy, high = rest[-7:]

    @pl.when(pl.program_id(0) == 0)
    def _():
        keys, queries = page_places(facts[0], facts[1], own_boxes[...], other_boxes[...])
        place, x, y = as_columns(queries)
        diff = keys[0] - place
        band[...] = jnp.where((diff >= -16) & (diff <= 15), 1.0, 0.0).astype(bf16)
        high[...] = jnp.where(diff > 15, 1.0, 0.0).astype(bf16)
        cx[...] = jnp.where((keys[1] & 15) < (x & 15), 1.0, 0.0).astype(bf16)
        cy[...] = jnp.where((keys[2] & 15) < (y & 15), 1.0, 0.0).astype(bf16)
        row = lax.broadcasted_iota(jnp.int32, (64, KEYS), 0)
        key_hot = [
            jnp.where((63 - row) == (code & 63), 1.0, 0.0)
            for code in (keys[1] >> 4, keys[2] >> 4, keys[0])
        ]
        key_hot.append(jnp.zeros((64, KEYS), f32))
        right[...] = jnp.transpose(jnp.concatenate(key_hot, axis=0), (1, 0)).astype(bf16)
        row = lax.broadcasted_iota(jnp.int32, (64, 384), 0)
        query_hot = [
            jnp.where(row == queries[1] >> 4, 1.0, 0.0),
            jnp.where(row == queries[2] >> 4, 1.0, 0.0),
            jnp.where(row[:32] + 64 == queries[2] >> 4, 1.0, 0.0),
            jnp.where(row == (queries[0] & 63), 1.0, 0.0),
        ]
        left[...] = jnp.concatenate(query_hot, axis=0)[:, :ROWS].astype(bf16)

    total = (ds_a[0].astype(f32) + ds_b[0].astype(f32)).astype(bf16)
    hot = right[...]
    query_hot = left[...]

    def fold(values, columns, rows):
        inner = jnp.dot(values, hot[:, columns], preferred_element_type=f32).astype(bf16)
        return jnp.dot(query_hot[rows], inner, preferred_element_type=f32)

    plain = fold(total, slice(0, 128), slice(0, 160))
    by_x = fold(total * cx[...], slice(0, 128), slice(0, 64))
    by_y = fold(total * cy[...], slice(0, 128), slice(64, 160))
    near = fold(total * band[...], slice(128, 256), slice(160, 224))

    def diagonals(square):
        lane = lax.broadcasted_iota(jnp.int32, square.shape, 1)
        square = jnp.where(lane < 64, square, 0.0)
        turned = pltpu.roll(square, 0, axis=1, stride=1, stride_axis=0)
        return jnp.sum(turned, axis=0, keepdims=True)

    def second(square):
        return pltpu.roll(square, 64, axis=1)

    above = jnp.sum((total * high[...]).astype(f32), axis=0, keepdims=True)
    above = sum(above[:, t * LANES : (t + 1) * LANES] for t in range(KEYS // LANES))
    out[0] = jnp.concatenate(
        [
            diagonals(plain[:64]),
            diagonals(by_x),
            diagonals(second(plain[64:128])),
            diagonals(second(by_y[:64])),
            diagonals(near),
            above,
            diagonals(second(plain[128:])),
            diagonals(second(by_y[64:])),
        ],
        axis=0,
    )


def table_bins():
    bins = np.zeros((8, LANES, BUCKETS), np.float32)
    for c in range(127):
        diff = 63 - c
        for kind, base in ((0, POS_BINS), (1, POS_BINS + BOX_BINS)):
            here = base + 32 + min(max(diff, -32), 31)
            below = base + 32 + min(max(diff - 1, -32), 31)
            bins[2 * kind, c, here] += 1
            bins[2 * kind + 1, c, below] += 1
            bins[2 * kind + 1, c, here] -= 1
        far = -1 - c
        bins[6, c, 128 + max(far, -32)] += 1
        bins[7, c, 128 + max(far - 1, -32)] += 1
        bins[7, c, 128 + max(far, -32)] -= 1
        near = (diff + 32) % 64 - 32
        if -16 <= near <= 15:
            bins[4, c, near + 16] += 1
        bins[0, c, 0] += 1
        bins[4, c, 0] -= 1
    bins[5, :, 31] += 1
    bins[5, :, 0] -= 1
    return bins


def fold_table(facts, own_boxes, other_boxes, ds_a, ds_b, part, parts, after=()):
    whole = lambda h, facts: (0, 0)
    count = HEADS // parts
    head = pl.BlockSpec((1, ROWS, KEYS), lambda h, facts: (h + part * count, 0, 0))
    return pl.pallas_call(
        table_kernel,
        out_shape=jax.ShapeDtypeStruct((count, 8, LANES), f32),
        grid_spec=pltpu.PrefetchScalarGridSpec(
            num_scalar_prefetch=1,
            grid=(count,),
            in_specs=[
                pl.BlockSpec((2, HALF_TEXT), whole),
                pl.BlockSpec((2, HALF_TEXT), whole),
                head,
                head,
            ]
            + [pl.BlockSpec(memory_space=pl.ANY)] * len(after),
            out_specs=pl.BlockSpec((1, 8, LANES), lambda h, facts: (h, 0, 0)),
            scratch_shapes=[
                pltpu.VMEM((KEYS, 256), bf16),
                pltpu.VMEM((224, ROWS), bf16),
                pltpu.VMEM((ROWS, KEYS), bf16),
                pltpu.VMEM((ROWS, KEYS), bf16),
                pltpu.VMEM((ROWS, KEYS), bf16),
                pltpu.VMEM((ROWS, KEYS), bf16),
            ],
        ),
        compiler_params=pltpu.CompilerParams(vmem_limit_bytes=50 * MIB),
        cost_estimate=brief,
        name="table_grad",
    )(facts, own_boxes, other_boxes, ds_a, ds_b, *after)


def table_grad_of(folded):
    bins = jnp.asarray(table_bins()).reshape(8 * LANES, BUCKETS)
    return lax.dot_general(
        bins,
        folded.reshape(HEADS, 8 * LANES),
        (((0,), (1,)), ((), ())),
        precision=lax.Precision.HIGHEST,
        preferred_element_type=f32,
    )


def whole_page(own, other):
    return jnp.concatenate(
        [
            own[:HALF_TEXT],
            other[:HALF_TEXT],
            own[HALF_TEXT:],
            other[HALF_TEXT:],
            jnp.zeros((KEYS - 2 * ROWS, own.shape[1]), own.dtype),
        ],
        axis=0,
    )


def page_split(both):
    mid = 2 * HALF_TEXT
    own = jnp.concatenate([both[:HALF_TEXT], both[mid : mid + HALF_SLOTS]], axis=0)
    other = jnp.concatenate(
        [both[HALF_TEXT:mid], both[mid + HALF_SLOTS : mid + VIS_SLOTS]], axis=0
    )
    return own, other


def nt_dot(left, right):
    return lax.dot_general(left, right, (((1,), (1,)), ((), ())), preferred_element_type=f32)


def tn_dot(left, right):
    return lax.dot_general(left, right, (((0,), (0,)), ((), ())), preferred_element_type=f32)


def centred(values):
    center = values - jnp.mean(values, axis=1, keepdims=True)
    spread = jnp.mean(center * center, axis=1, keepdims=True)
    rate = lax.rsqrt(spread + norm_epsilon)
    return center * rate, rate


def norm_back(grad, values, gain_row):
    hat, rate = centred(values)
    scaled = grad * gain_row
    mean = jnp.mean(scaled, axis=1, keepdims=True)
    along = jnp.mean(scaled * hat, axis=1, keepdims=True)
    column = lambda block: jnp.sum(block, axis=0, keepdims=True)
    return rate * (scaled - mean - hat * along), column(grad * hat), column(grad)


def attend_kernel(
    layer,
    q_ref,
    ko,
    kp,
    vo,
    vp,
    bias,
    x_ref,
    weight,
    attn_bias,
    gain,
    shift,
    soft,
    pair,
    residual,
    normed,
):
    step = pl.program_id(0)
    q = q_ref[...] * jnp.asarray(HEAD_DIM**-0.5, bf16)
    keys = whole_page(ko[...], kp[...])
    values = whole_page(vo[...], vp[...])
    first = lax.broadcasted_iota(jnp.int32, (ROWS, LANES), 1) < HEAD_DIM
    parts = []
    for head in range(2):
        mine = jnp.where(first if head == 0 else ~first, q, jnp.zeros_like(q))
        scores = nt_dot(mine, keys) + bias[head]
        raised = jnp.exp(scores - jnp.max(scores, axis=1, keepdims=True))
        weights = (raised * (1.0 / jnp.sum(raised, axis=1, keepdims=True))).astype(bf16)
        soft[head] = weights
        parts.append(jnp.dot(weights, values, preferred_element_type=f32))
    slab = pl.ds(pl.multiple_of(step * LANES, LANES), LANES)
    pair[0, :, slab] = jnp.where(first, parts[0], parts[1]).astype(bf16)

    @pl.when(step == PAIRS - 1)
    def _():
        attended = jnp.dot(pair[0], weight[0], preferred_element_type=f32)
        summed = x_ref[...] + (attended + attn_bias[layer, 2:3, :])
        residual[...] = summed
        out = centred(summed)[0] * gain[layer, 0:1, :] + shift[layer, 0:1, :]
        normed[...] = out
        pair[1] = out.astype(bf16)


def full(array):
    return pl.BlockSpec(array.shape, lambda *at: (0,) * array.ndim)


def attend(layer, q, kv, other_kv, bias, x, out_weight, attn_bias, gain, shift):
    rows, width = q.shape
    slab = pl.BlockSpec((ROWS, LANES), lambda p: (0, p))
    second = pl.BlockSpec((ROWS, LANES), lambda p: (0, p + PAIRS))
    heads = pl.BlockSpec((2, ROWS, KEYS), lambda p: (p, 0, 0))
    whole = pl.BlockSpec((rows, width), lambda p: (0, 0))
    wide = jax.ShapeDtypeStruct((rows, width), f32)
    low = jax.ShapeDtypeStruct((2, rows, width), bf16)
    return pl.pallas_call(
        functools.partial(attend_kernel, layer),
        grid=(PAIRS,),
        in_specs=[
            slab,
            slab,
            slab,
            second,
            second,
            heads,
            whole,
            pl.BlockSpec((1, width, width), lambda p: (layer, 0, 0)),
            full(attn_bias),
            full(gain),
            full(shift),
        ],
        out_specs=[
            heads,
            pl.BlockSpec((2, rows, width), lambda p: (0, 0, 0)),
            whole,
            whole,
        ],
        out_shape=[jax.ShapeDtypeStruct((HEADS, ROWS, KEYS), bf16), low, wide, wide],
        compiler_params=pltpu.CompilerParams(vmem_limit_bytes=50 * MIB),
        cost_estimate=brief,
        name="attend",
    )(q, kv, other_kv, kv, other_kv, bias, x, out_weight, attn_bias, gain, shift)


def attend_back_kernel(q_ref, ko, kp, vo, vp, dc_ref, soft, *rest):
    ds, grads = rest[-2:]
    scale = HEAD_DIM**-0.5
    q = q_ref[...]
    dc = dc_ref[...]
    keys = whole_page(ko[...], kp[...])
    values = whole_page(vo[...], vp[...])
    first = lax.broadcasted_iota(jnp.int32, (ROWS, LANES), 1) < HEAD_DIM
    q_turned = jnp.transpose(q.astype(f32), (1, 0)).astype(bf16)
    dc_turned = jnp.transpose(dc.astype(f32), (1, 0)).astype(bf16)
    dq_parts, dk_parts, dv_parts = [], [], []
    for head in range(2):
        span = slice(head * HEAD_DIM, (head + 1) * HEAD_DIM)
        mine = jnp.where(first if head == 0 else ~first, dc, jnp.zeros_like(dc))
        weights = soft[head]
        weights_f = weights.astype(f32)
        flow = nt_dot(mine, values)
        share = jnp.sum(weights_f * flow, axis=1, keepdims=True)
        score_grad = (weights_f * (flow - share)).astype(bf16)
        ds[head] = score_grad
        dq_parts.append(jnp.dot(score_grad, keys, preferred_element_type=f32))
        dk_parts.append(jnp.dot(q_turned[span], score_grad, preferred_element_type=f32))
        dv_parts.append(jnp.dot(dc_turned[span], weights, preferred_element_type=f32))
    grads[0] = (jnp.where(first, dq_parts[0], dq_parts[1]) * scale).astype(bf16)
    own, other = page_split(jnp.transpose(jnp.concatenate(dk_parts, axis=0) * scale, (1, 0)))
    grads[1] = own.astype(bf16)
    grads[2] = other.astype(bf16)
    own, other = page_split(jnp.transpose(jnp.concatenate(dv_parts, axis=0), (1, 0)))
    grads[3] = own.astype(bf16)
    grads[4] = other.astype(bf16)


def attend_back(q, kv, other_kv, dctx, soft, after=()):
    slab = pl.BlockSpec((ROWS, LANES), lambda p: (0, p))
    second = pl.BlockSpec((ROWS, LANES), lambda p: (0, p + PAIRS))
    heads = pl.BlockSpec((2, ROWS, KEYS), lambda p: (p, 0, 0))
    return pl.pallas_call(
        attend_back_kernel,
        grid=(PAIRS,),
        in_specs=[slab, slab, slab, second, second, slab, heads]
        + [pl.BlockSpec(memory_space=pl.ANY)] * len(after),
        out_specs=[heads, pl.BlockSpec((5, ROWS, LANES), lambda p: (0, 0, p))],
        out_shape=[
            jax.ShapeDtypeStruct((HEADS, ROWS, KEYS), bf16),
            jax.ShapeDtypeStruct((5,) + q.shape, bf16),
        ],
        compiler_params=pltpu.CompilerParams(vmem_limit_bytes=50 * MIB),
        cost_estimate=brief,
        name="attend_back",
    )(q, kv, other_kv, kv, other_kv, dctx, soft, *after)


def ffn_kernel(layer, more, me, x_ref, own_w, mate_w, bias, n_ref, out_bias, gain, shift, *rest):
    step = pl.program_id(0)
    width = x_ref.shape[1]
    units = own_w.shape[1]
    own_act, mate_act, slope, residual = rest[-7 if more else -5 :][:4]
    x = x_ref[...]

    total = None
    for index, (block, act) in enumerate(((own_w, own_act), (mate_w, mate_act))):
        weights = block[0]
        row = bias[pl.ds(me[0] ^ (2 * step + index), 1), layer, :units]
        hidden = nt_dot(x, weights[:, :width]) + row.astype(f32)
        half_cdf = 0.5 + 0.5 * lax.erf(hidden * 0.5**0.5)
        low = (hidden * half_cdf).astype(bf16)
        act[0] = low
        density = jnp.exp(hidden * hidden * -0.5) * (1.0 / (2.0 * np.pi) ** 0.5)
        slope[index] = (half_cdf + hidden * density).astype(bf16)
        term = jnp.dot(low, weights[:, width:], preferred_element_type=f32)
        total = term if total is None else total + term

    @pl.when(step == 0)
    def _():
        residual[...] = n_ref[...] + out_bias[layer : layer + 1, :] + total

    @pl.when(step > 0)
    def _():
        residual[...] += total

    @pl.when(step == pl.num_programs(0) - 1)
    def _():
        states = centred(residual[...])[0] * gain[layer, 1:2, :] + shift[layer, 1:2, :]
        rounded = states.astype(bf16)
        if more:
            weight, attn_bias = rest[:2]
            wide, query, shared = rest[-3:]
            wide[...] = states
            project = lambda index: jnp.dot(
                rounded, weight[0, index], preferred_element_type=f32
            )
            query[...] = (project(0) + attn_bias[layer + 1, 0:1, :]).astype(bf16)
            shared[:, :width] = project(1).astype(bf16)
            shared[:, width : 2 * width] = (
                project(2) + attn_bias[layer + 1, 1:2, :]
            ).astype(bf16)
            shared[:, 2 * width :] = rounded
        else:
            rest[-1][...] = rounded


def ffn(me, layer, pair, n, gathered, units, out_bias, gain, shift, qkv_weight, attn_bias):
    groups = gathered.shape[0]
    rows, width = n.shape
    more = layer < LAYERS - 1
    whole = pl.BlockSpec((rows, width), lambda i, me: (0, 0))
    pick = lambda which: pl.BlockSpec(
        (1, units, 2 * width), lambda i, me: (me[0] ^ (2 * i + which), layer, 0)
    )
    kept = pl.BlockSpec((2, rows, units), lambda i, me: (i, 0, 0))
    kept_shape = jax.ShapeDtypeStruct((groups, rows, units), bf16)
    wide = jax.ShapeDtypeStruct((rows, width), f32)
    low = jax.ShapeDtypeStruct((rows, width), bf16)
    half_act = pl.BlockSpec((1, rows, units), lambda i, me: (i, 0, 0))
    half_shape = jax.ShapeDtypeStruct((groups // 2, rows, units), bf16)
    inputs = [pair, gathered, gathered, gathered, n, out_bias, gain, shift]
    in_specs = [
        pl.BlockSpec((None, rows, width), lambda i, me: (1, 0, 0)),
        pick(0),
        pick(1),
        pl.BlockSpec(
            (groups, 16, 2 * width), lambda i, me: (0, LAYERS * units // 16, 0)
        ),
        whole,
        full(out_bias),
        full(gain),
        full(shift),
    ]
    out_specs = [half_act, half_act, kept, whole]
    out_shape = [half_shape, half_shape, kept_shape, wide]
    if more:
        inputs += [qkv_weight, attn_bias]
        in_specs += [
            pl.BlockSpec((1, 3, width, width), lambda i, me: (layer + 1, 0, 0, 0)),
            full(attn_bias),
        ]
        out_specs += [whole, whole, pl.BlockSpec((rows, 3 * width), lambda i, me: (0, 0))]
        out_shape += [wide, low, jax.ShapeDtypeStruct((rows, 3 * width), bf16)]
    else:
        out_specs += [whole]
        out_shape += [low]
    return pl.pallas_call(
        functools.partial(ffn_kernel, layer, more),
        out_shape=out_shape,
        grid_spec=pltpu.PrefetchScalarGridSpec(
            num_scalar_prefetch=1, grid=(groups // 2,), in_specs=in_specs, out_specs=out_specs
        ),
        compiler_params=pltpu.CompilerParams(vmem_limit_bytes=50 * MIB),
        cost_estimate=brief,
        name="feed_forward",
    )(me, *inputs)


def ffn_back_kernel(
    layer,
    me,
    grad_ref,
    r2_ref,
    r1_ref,
    own_w,
    mate_w,
    slope,
    gain,
    out_weight,
    own_dh,
    mate_dh,
    low_grads,
    bias_grad,
    sums,
    dx,
    dctx,
    total_s,
):
    step = pl.program_id(0)
    width = r2_ref.shape[1]
    column = lambda block: jnp.sum(block, axis=0, keepdims=True)

    @pl.when(step == 0)
    def _():
        grad, gain_grad, shift_grad = norm_back(
            grad_ref[...].astype(f32), r2_ref[...], gain[layer, 1:2, :]
        )
        low = grad.astype(bf16)
        total_s[...] = grad
        low_grads[0] = low
        sums[0:1, :] = gain_grad
        sums[1:2, :] = shift_grad
        sums[2:3, :] = column(low.astype(f32))

    dy = low_grads[0]
    total = None
    for index, (block, dh) in enumerate(((own_w, own_dh), (mate_w, mate_dh))):
        weights = block[0]
        flow = nt_dot(dy, weights[:, width:])
        grad = (flow * slope[index].astype(f32)).astype(bf16)
        dh[0] = grad
        bias_grad[index] = jnp.broadcast_to(column(grad.astype(f32)), bias_grad.shape[1:])
        term = jnp.dot(grad, weights[:, :width], preferred_element_type=f32)
        total = term if total is None else total + term
    total_s[...] += total

    @pl.when(step == pl.num_programs(0) - 1)
    def _():
        grad, gain_grad, shift_grad = norm_back(total_s[...], r1_ref[...], gain[layer, 0:1, :])
        low = grad.astype(bf16)
        dx[...] = grad
        low_grads[1] = low
        dctx[...] = nt_dot(low, out_weight[0]).astype(bf16)
        sums[3:4, :] = gain_grad
        sums[4:5, :] = shift_grad
        sums[5:6, :] = column(low.astype(f32))
        sums[6:8, :] = jnp.zeros((2, width), f32)


def ffn_back(me, layer, grad, r2, r1, gathered, slope, gain, out_weight):
    groups, rows, units = slope.shape
    width = r2.shape[1]
    whole = pl.BlockSpec((rows, width), lambda i, me: (0, 0))
    pick = lambda which: pl.BlockSpec(
        (1, units, 2 * width), lambda i, me: (me[0] ^ (2 * i + which), layer, 0)
    )
    half = pl.BlockSpec((1, rows, units), lambda i, me: (i, 0, 0))
    half_shape = jax.ShapeDtypeStruct((groups // 2, rows, units), bf16)
    return pl.pallas_call(
        functools.partial(ffn_back_kernel, layer),
        out_shape=[
            half_shape,
            half_shape,
            jax.ShapeDtypeStruct((2, rows, width), bf16),
            jax.ShapeDtypeStruct((groups, 8, units), f32),
            jax.ShapeDtypeStruct((8, width), f32),
            jax.ShapeDtypeStruct((rows, width), f32),
            jax.ShapeDtypeStruct((rows, width), bf16),
        ],
        grid_spec=pltpu.PrefetchScalarGridSpec(
            num_scalar_prefetch=1,
            grid=(groups // 2,),
            in_specs=[
                whole,
                whole,
                whole,
                pick(0),
                pick(1),
                pl.BlockSpec((2, rows, units), lambda i, me: (i, 0, 0)),
                full(gain),
                pl.BlockSpec((1, width, width), lambda i, me: (layer, 0, 0)),
            ],
            out_specs=[
                half,
                half,
                pl.BlockSpec((2, rows, width), lambda i, me: (0, 0, 0)),
                pl.BlockSpec((2, 8, units), lambda i, me: (i, 0, 0)),
                pl.BlockSpec((8, width), lambda i, me: (0, 0)),
                whole,
                whole,
            ],
            scratch_shapes=[pltpu.VMEM((rows, width), f32)],
        ),
        compiler_params=pltpu.CompilerParams(vmem_limit_bytes=50 * MIB),
        cost_estimate=brief,
        name="feed_forward_back",
    )(me, grad, r2, r1, gathered, gathered, slope, gain, out_weight)


def ffn_grads_kernel(me, n, n_mate, dy, dy_mate, dh, dh_mate, act, act_mate, *rest):
    main, keep, send, n_s, dy_s = rest[-5:]
    rows, width = n.shape
    part = keep.shape[-1]

    @pl.when(pl.program_id(0) == 0)
    def _():
        for target, own, mate in ((n_s, n, n_mate), (dy_s, dy, dy_mate)):
            target[:rows] = own[...]
            target[rows:] = mate[...]

    both = lambda own, mate: jnp.concatenate([own[0], mate[0]], axis=0)
    into = tn_dot(both(dh, dh_mate), n_s[...])
    out = tn_dot(both(act, act_mate), dy_s[...])
    first = main.shape[-1] - width
    main[0, :, :width] = into.astype(bf16)
    main[0, :, width:] = out[:, :first].astype(bf16)
    low = out[:, first : first + part].astype(bf16)
    high = out[:, first + part :].astype(bf16)
    turn = me[1] % 2 == 0
    keep[0] = jnp.where(turn, low, high)
    send[0] = jnp.where(turn, high, low)


def ffn_grads(me, pair, pair_mate, low_grads, low_grads_mate, dh, dh_mate, act, act_mate, after=()):
    groups, rows, units = dh.shape
    width = pair.shape[2]
    part = width // 3
    row_block = lambda which: pl.BlockSpec((None, rows, width), lambda i, me: (which, 0, 0))
    hidden = pl.BlockSpec((1, rows, units), lambda i, me: (i, 0, 0))
    halves = pl.BlockSpec((1, units, part), lambda i, me: (i, 0, 0))
    halves_shape = jax.ShapeDtypeStruct((groups, units, part), bf16)
    return pl.pallas_call(
        ffn_grads_kernel,
        out_shape=[
            jax.ShapeDtypeStruct((groups, units, 2 * width - 2 * part), bf16),
            halves_shape,
            halves_shape,
        ],
        grid_spec=pltpu.PrefetchScalarGridSpec(
            num_scalar_prefetch=1,
            grid=(groups,),
            in_specs=[row_block(1), row_block(1), row_block(0), row_block(0)]
            + [hidden] * 4
            + [pl.BlockSpec(memory_space=pl.ANY)] * len(after),
            out_specs=[
                pl.BlockSpec(
                    (1, units, 2 * width - 2 * part), lambda i, me: ((me[0] >> 1) ^ i, 0, 0)
                ),
                halves,
                halves,
            ],
            scratch_shapes=[pltpu.VMEM((2 * rows, width), bf16)] * 2,
        ),
        compiler_params=pltpu.CompilerParams(vmem_limit_bytes=50 * MIB),
        cost_estimate=brief,
        name="feed_forward_grads",
    )(
        me,
        pair,
        pair_mate,
        low_grads,
        low_grads_mate,
        dh,
        dh_mate,
        act,
        act_mate,
        *after,
    )


def projection_kernel(
    me, x, x_mate, ctx, ctx_mate, own, mate, da, da_mate, dr_ref, weight, *rest
):
    keep, send, dx, sums, whole_s, left_s, right_s = rest[-7:]
    step = pl.program_id(0)
    chips, shard, width = keep.shape
    rows = x.shape[0]
    column = lambda block: jnp.sum(block.astype(f32), axis=0, keepdims=True)

    @pl.when(step == 0)
    def _():
        dx[...] = dr_ref[...]
        left_s[:rows] = x[...]
        left_s[rows:] = x_mate[...]
        right_s[:rows] = own[0]
        right_s[rows:] = mate[0]
        sums[0:1, :] = column(own[0])
        sums[2:8, :] = jnp.zeros((6, width), f32)

    for index in (1, 2):

        @pl.when(step == index)
        def _():
            right_s[:rows] = add_low(own[2 * index - 1], mate[2 * index])
            right_s[rows:] = add_low(mate[2 * index - 1], own[2 * index])

    @pl.when(step == 2)
    def _():
        sums[1:2, :] = column(right_s[:rows])

    @pl.when(step < 3)
    def _():
        dx[...] += nt_dot(right_s[:rows], weight[0, 0])

    @pl.when(step == 3)
    def _():
        left_s[:rows] = ctx[...]
        left_s[rows:] = ctx_mate[...]
        right_s[:rows] = da[...]
        right_s[rows:] = da_mate[...]

    whole_s[...] = tn_dot(left_s[...], right_s[...])

    def put(target):
        for place in range(chips):
            start = pl.multiple_of((me[0] ^ (2 * place)) * shard, 8)
            target[place] = whole_s[pl.ds(start, shard), :].astype(bf16)

    mine = step // 2 == me[1] % 2
    pl.when(mine)(lambda: put(keep))
    pl.when(jnp.logical_not(mine))(lambda: put(send))


def projection_grads(
    me, layer, shared, shared_mate, pair, pair_mate, own, mate, low, low_mate, dr, weight, after=()
):
    rows, width = dr.shape
    groups = lax.axis_size("tp")
    shard = width // groups
    whole = pl.BlockSpec((rows, width), lambda t, me: (0, 0))
    x_block = pl.BlockSpec((rows, width), lambda t, me: (0, 2))
    layered = lambda which: pl.BlockSpec((None, rows, width), lambda t, me: (which, 0, 0))
    shape = jax.ShapeDtypeStruct((groups // 2, shard, 2 * width), bf16)
    turned = lambda t, first: jnp.clip(t - 2 * first, 0, 1)
    return pl.pallas_call(
        projection_kernel,
        out_shape=[
            shape,
            shape,
            jax.ShapeDtypeStruct((rows, width), f32),
            jax.ShapeDtypeStruct((8, width), f32),
        ],
        grid_spec=pltpu.PrefetchScalarGridSpec(
            num_scalar_prefetch=1,
            grid=(4,),
            in_specs=[
                x_block,
                x_block,
                layered(0),
                layered(0),
                full(own),
                full(mate),
                layered(1),
                layered(1),
                whole,
                pl.BlockSpec(
                    (1, 1, width, width), lambda t, me: (layer, jnp.minimum(t, 2), 0, 0)
                ),
            ]
            + [pl.BlockSpec(memory_space=pl.ANY)] * len(after),
            out_specs=[
                pl.BlockSpec(
                    (groups // 2, shard, width), lambda t, me: (0, 0, turned(t, me[1] % 2))
                ),
                pl.BlockSpec(
                    (groups // 2, shard, width), lambda t, me: (0, 0, turned(t, 1 - me[1] % 2))
                ),
                whole,
                pl.BlockSpec((8, width), lambda t, me: (0, 0)),
            ],
            scratch_shapes=[
                pltpu.VMEM((width, width), f32),
                pltpu.VMEM((2 * rows, width), bf16),
                pltpu.VMEM((2 * rows, width), bf16),
            ],
        ),
        compiler_params=pltpu.CompilerParams(vmem_limit_bytes=50 * MIB),
        cost_estimate=brief,
        name="projection_grads",
    )(
        me,
        shared,
        shared_mate,
        pair,
        pair_mate,
        own,
        mate,
        low,
        low_mate,
        dr,
        weight,
        *after,
    )


def body(
    text_states,
    visual_maps,
    text_boxes,
    text_lengths,
    qkv_weight,
    out_weight,
    attn_bias,
    ffn_in,
    ffn_in_bias,
    ffn_out,
    ffn_out_bias,
    norm_gain,
    norm_shift,
    bias_table,
    vis_weight,
    vis_bias,
    bn_gain,
    bn_shift,
    cotangent,
):
    tp_index = lax.axis_index("tp")
    tp_size = lax.axis_size("tp")
    half = tp_index % 2
    page = (lax.axis_index("seq") * tp_size + tp_index) // 2
    me = jnp.stack([tp_index, lax.axis_index("seq")]).astype(jnp.int32)
    units = ffn_in.shape[1]
    width = text_states.shape[1]
    text_rows = text_states.shape[0]

    bias_rows = jnp.pad(ffn_in_bias, ((0, 16 - LAYERS), (0, 2 * width - units)))
    packed = jnp.concatenate(
        [
            jnp.concatenate([ffn_in, ffn_out], axis=2).reshape(LAYERS * units, 2 * width),
            bias_rows,
        ],
        axis=0,
    )
    gathered = lax.all_gather(packed, "tp", axis=0)

    other_boxes = flipped(text_boxes, "tp", 0)
    length = lax.dynamic_index_in_dim(text_lengths, page, 0, keepdims=False)
    facts = jnp.stack([half.astype(jnp.int32), length])
    score_bias = make_bias(facts, text_boxes, other_boxes, bias_table)

    count_cells = text_lengths.shape[0] * VIS_TOK
    maps_float = visual_maps.astype(f32)
    slot_place = half * HALF_SLOTS + jnp.arange(HALF_SLOTS, dtype=jnp.int32)
    slot_mask = (slot_place < VIS_TOK)[:, None]
    masked_maps = jnp.where(slot_mask, maps_float, 0.0)
    sums = total_over_all(
        jnp.stack([jnp.sum(masked_maps, axis=0), jnp.sum(masked_maps * masked_maps, axis=0)])
    )
    channel_mean = sums[0] / count_cells
    inverse_std = lax.rsqrt(sums[1] / count_cells - channel_mean * channel_mean + norm_epsilon)
    centered_hat = jnp.where(slot_mask, (maps_float - channel_mean) * inverse_std, 0.0)
    normal_low = jnp.where(slot_mask, centered_hat * bn_gain + bn_shift, 0.0).astype(bf16)
    visual_tokens = jnp.dot(normal_low, vis_weight, preferred_element_type=f32) + vis_bias
    states = jnp.concatenate([text_states.astype(f32), visual_tokens], axis=0)

    rounded = states.astype(bf16)
    project = lambda index: jnp.dot(rounded, qkv_weight[0, index], preferred_element_type=f32)
    shared = jnp.concatenate(
        [project(1).astype(bf16), (project(2) + attn_bias[0, 1]).astype(bf16), rounded], axis=1
    )
    query = (project(0) + attn_bias[0, 0]).astype(bf16)
    saved = []
    for layer in range(LAYERS):
        shared_mate = flipped(shared, "tp", 0)
        parts = (query, shared, shared_mate)
        soft, pair, residual_one, normed = attend(
            layer, *parts, score_bias, states, out_weight, attn_bias, norm_gain, norm_shift
        )
        act, act_send, slope, residual_two, *onwards = ffn(
            me,
            layer,
            pair,
            normed,
            gathered,
            units,
            ffn_out_bias,
            norm_gain,
            norm_shift,
            qkv_weight,
            attn_bias,
        )
        mates = (flipped(pair, "tp", 0), flipped(act_send, "tp", 0))
        saved.append((parts, soft, pair, residual_one, residual_two, act, slope, mates))
        if layer < LAYERS - 1:
            states, query, shared = onwards
    out_states = onwards[0]

    gradient = cotangent
    norm_sums = [None] * LAYERS
    projection_rows = [None] * LAYERS
    bin_grads = [None] * LAYERS
    score_grads = [None] * LAYERS
    projection_sums = [None] * LAYERS
    ffn_sums = [None] * LAYERS
    ffn_main = [None] * LAYERS
    moving = []

    def begin(sums):
        moving.append(sums)
        return sums

    def onward(values):
        values = tied(values, [sums.right for sums in moving])
        for sums in list(moving):
            if sums.steps:
                sums.step(values[0])
            else:
                moving.remove(sums)
        return values

    for layer in reversed(range(LAYERS)):
        last = layer == LAYERS - 1
        parts, soft, pair, residual_one, residual_two, act, slope, mates = saved[layer]
        dh, dh_send, low, bin_part, norm_sums[layer], grad_one, context_grad = ffn_back(
            me, layer, gradient, residual_two, residual_one, gathered, slope, norm_gain, out_weight
        )
        bin_grads[layer] = bin_part[:, 0]
        dh_mate, low_mate = flipped(dh_send, "tp", 0), flipped(low, "tp", 0)
        if not last:
            context_grad, dh, dh_mate, low_mate = onward((context_grad, dh, dh_mate, low_mate))
        main, keep, send = ffn_grads(me, pair, mates[0], low, low_mate, dh, dh_mate, act, mates[1])
        ffn_main[layer] = over_chips(main)
        came = flipped(send, "seq", 0)
        score_grads[layer], grads = attend_back(*parts, context_grad, soft, after=(keep,))
        grads, keep, came = onward((grads, keep, came))
        grads_mate = flipped(grads, "tp", 0)
        ffn_sums[layer] = begin(Reducer(keep, came, low_first()))
        ffn_sums[layer].step()
        keep, send, gradient, projection_rows[layer] = projection_grads(
            me,
            layer,
            parts[1],
            parts[2],
            pair,
            mates[0],
            grads,
            grads_mate,
            low,
            low_mate,
            grad_one,
            qkv_weight,
            after=[sums.left for sums in moving],
        )
        gradient, keep, send = onward((gradient, keep, send))
        came = flipped(send, "seq", 0)
        if last:
            projection_sums[layer] = begin(Reducer(keep, came, low_first()))

    token_grad = gradient[text_rows:].astype(bf16)
    vis_sum = tn_dot(normal_low, token_grad).astype(bf16)
    fold = functools.partial(fold_table, facts, text_boxes, other_boxes, *score_grads, parts=2)
    first_fold = fold(0, after=[sums.left for sums in moving])
    first_fold, vis_sum, keep, came = onward((first_fold, vis_sum, keep, came))
    projection_sums[0] = begin(Reducer(keep, came, low_first()))
    projection_sums[0].step()
    mid = vis_sum.shape[0] // 2
    pick = lambda which: jnp.where(half == which, vis_sum[:mid], vis_sum[mid:])
    vis_sum = add_low(pick(0), flipped(pick(1), "tp", 0))
    vis_moving = flipped(vis_sum, "tp", 1)
    second_fold = fold(1, after=[first_fold] + [sums.left for sums in moving] + [vis_sum])
    second_fold, vis_moving, *ffn_main = onward((second_fold, vis_moving, *ffn_main))
    vis_sum = add_low(vis_sum, vis_moving)
    for axis, bits in (("tp", range(2, mesh_bits("tp"))), ("seq", range(mesh_bits("seq")))):
        for bit in bits:
            vis_sum = add_low(vis_sum, flipped(vis_sum, axis, bit))
    vis_mate = flipped(vis_sum, "tp", 0)
    vis_weight_grad = jnp.concatenate(
        [
            jnp.where(half == 0, vis_sum, vis_mate),
            jnp.where(half == 0, vis_mate, vis_sum),
        ],
        axis=0,
    ).astype(f32)
    table_grad = table_grad_of(jnp.concatenate([first_fold, second_fold], axis=0))
    grad_text = gradient[:text_rows]
    normal_grad = jnp.where(slot_mask, nt_dot(token_grad, vis_weight), 0.0)

    small = [
        jnp.stack(norm_sums).reshape(-1),
        jnp.stack([rows[:2] for rows in projection_rows]).reshape(-1),
        table_grad.reshape(-1),
        jnp.sum(token_grad.astype(f32), axis=0),
        jnp.sum(normal_grad * centered_hat, axis=0),
        jnp.sum(normal_grad, axis=0),
        jnp.take(
            jnp.stack(bin_grads), tp_index ^ jnp.arange(tp_size), axis=1
        ).reshape(-1),
    ]
    sizes = [part.size for part in small]
    flat = jnp.concatenate(small)
    flat = jnp.pad(flat, (0, -flat.size % 1024)).reshape(-1, 128)
    flat = total_over_all(flat).reshape(-1)
    found = []
    start = 0
    for size in sizes:
        found.append(flat[start : start + size])
        start += size
    norm_total = found[0].reshape(LAYERS, 8, width)
    projection_total = found[1].reshape(LAYERS, 2, width)
    table_total, visb_total, bn_gain_grad, bn_shift_grad = found[2:6]
    bin_total = lax.dynamic_index_in_dim(
        found[6].reshape(LAYERS, tp_size, units), tp_index, 1, keepdims=False
    )
    grad_maps = jnp.where(
        slot_mask,
        inverse_std
        * (
            normal_grad * bn_gain
            - bn_gain * bn_shift_grad / count_cells
            - centered_hat * (bn_gain * bn_gain_grad / count_cells)
        ),
        0.0,
    )
    projections = jnp.stack([sums.finish() for sums in projection_sums])
    projections = projections.reshape(LAYERS, -1, 4, width)
    ffn_total = jnp.stack(
        [
            jnp.concatenate([Gather(main).finish(), sums.finish()], axis=1)
            for main, sums in zip(ffn_main, ffn_sums)
        ]
    )
    return (
        out_states,
        grad_text,
        grad_maps,
        projections[:, :, :3].transpose(0, 2, 1, 3),
        projections[:, :, 3],
        jnp.concatenate([projection_total, norm_total[:, 5:6]], axis=1),
        ffn_total[:, :, :width],
        bin_total,
        ffn_total[:, :, width:],
        norm_total[:, 2],
        jnp.stack([norm_total[:, 3], norm_total[:, 0]], axis=1),
        jnp.stack([norm_total[:, 4], norm_total[:, 1]], axis=1),
        table_total.reshape(bias_table.shape),
        vis_weight_grad,
        visb_total,
        bn_gain_grad,
        bn_shift_grad,
    )


def solution(mesh):
    rows = P(("seq", "tp"), None)
    units = P(None, "tp", None)
    return jax.shard_map(
        body,
        mesh=mesh,
        in_specs=(
            rows,
            rows,
            P(None, ("seq", "tp")),
            P(),
            P(),
            P(),
            P(),
            units,
            P(None, "tp"),
            units,
            P(),
            P(),
            P(),
            P(),
            P(),
            P(),
            P(),
            P(),
            rows,
        ),
        out_specs=(
            rows,
            rows,
            rows,
            P(None, None, "tp", None),
            units,
            P(),
            units,
            P(None, "tp"),
            units,
            P(),
            P(),
            P(),
            P(),
            P(),
            P(),
            P(),
            P(),
        ),
        check_vma=False,
    )
```

```python
import functools

import jax
import jax.numpy as jnp
import numpy as np
from jax import lax
from jax.experimental import pallas as pl
from jax.experimental.pallas import tpu as pltpu
from jax.sharding import PartitionSpec as P

HEADS = 12
HEAD_DIM = 64
VIS_TOK = 49
VIS_SLOTS = 64
POS_BINS = 32
BOX_BINS = 64
LAYERS = 2
BUCKETS = POS_BINS + 2 * BOX_BINS

HALF_TEXT = 256
HALF_SLOTS = VIS_SLOTS // 2
ROWS = HALF_TEXT + HALF_SLOTS
KEYS = 640
PAIRS = HEADS // 2
LANES = 128
FOLDS = 2
BLOCKS = 4
HALF = BLOCKS // 2
norm_epsilon = 1e-05
NEVER = -1e30
bf16 = jnp.bfloat16
f32 = jnp.float32
MIB = 1 << 20
brief = pl.CostEstimate(flops=1, bytes_accessed=1, transcendentals=0)


def mesh_bits(axis):
    return (lax.axis_size(axis) - 1).bit_length()


def flipped(block, axis, bit):
    count = lax.axis_size(axis)
    return lax.ppermute(block, axis, [(i, i ^ (1 << bit)) for i in range(count)])


def total_over_all(value):
    for axis in ("tp", "seq"):
        for bit in range(mesh_bits(axis)):
            value = value + flipped(value, axis, bit)
    return value


def add_low(left, right):
    return (left.astype(f32) + right.astype(f32)).astype(bf16)


def tied(values, after):
    return lax.optimization_barrier((tuple(values), tuple(after)))[0]


class Shards:
    def __init__(self, near_keep, near_send, seq_keep, seq_send):
        self.near = near_keep
        self.seq = seq_keep
        self.near_came = flipped(near_send, "tp", 1)
        self.seq_came = flipped(seq_send, "seq", 0)

    def underway(self):
        return [self.near_came, self.seq_came]

    def second(self, *after):
        near, near_came, seq, seq_came = tied(
            (self.near, self.near_came, self.seq, self.seq_came), after
        )
        turn = lax.axis_index("seq") % 2
        middle = near.shape[-1] // 2
        pick = lambda block, which: jnp.where(
            turn == which, block[..., :middle], block[..., middle:]
        )
        self.near = add_low(pick(near, 0), pick(near_came, 0))
        self.near_came = flipped(add_low(pick(near, 1), pick(near_came, 1)), "seq", 0)
        far = seq.shape[0] // 2
        self.seq = add_low(seq[:far], seq_came[:far])
        self.seq_came = flipped(add_low(seq[far:], seq_came[far:]), "tp", 1)

    def scatter(self, *after):
        near, near_came, seq, seq_came = tied(
            (self.near, self.near_came, self.seq, self.seq_came), after
        )
        both = jnp.concatenate([add_low(near, near_came), add_low(seq, seq_came)], axis=1)
        count = lax.axis_size("tp")
        groups = [list(range(first, count, 4)) for first in range(4)]
        self.shard = lax.psum_scatter(both, "tp", scatter_dimension=0, axis_index_groups=groups)

    def halve(self, *after):
        near, near_came, seq, seq_came = tied(
            (self.near, self.near_came, self.seq, self.seq_came), after
        )
        bit = mesh_bits("tp") - (near.shape[0] - 1).bit_length()
        pick = lambda block, which: block.reshape((-1, 2) + block.shape[1:])[:, which]
        add = lambda which: jnp.concatenate(
            [
                add_low(pick(near, which), pick(near_came, which)),
                add_low(pick(seq, which), pick(seq_came, which)),
            ],
            axis=1,
        )
        self.shard, self.came = add(0), flipped(add(1), "tp", bit)
        self.bit = bit + 1

    def halve_more(self, *after):
        shard, came = tied((self.shard, self.came), after)
        if shard.shape[0] == 1:
            self.shard = add_low(shard, came)[0]
            return
        pick = lambda block, which: block.reshape((-1, 2) + block.shape[1:])[:, which]
        self.shard = add_low(pick(shard, 0), pick(came, 0))
        self.came = flipped(add_low(pick(shard, 1), pick(came, 1)), "tp", self.bit)
        self.bit += 1

    def join(self, *after):
        (shard,) = tied((self.shard,), after)
        for bit in range(1, mesh_bits("seq")):
            shard = add_low(shard, flipped(shard, "seq", bit))
        self.shard = shard
        self.other = flipped(shard, "seq", 0)


class Tree:
    def __init__(self, value, ways, join=None, add=add_low):
        self.lefts = [value]
        self.rights = []
        self.steps = list(ways) + ([join] if join else [])
        self.add = add

    def step(self, *after):
        if after:
            both = tied(self.lefts + self.rights, after)
            self.lefts, self.rights = list(both[:1]), list(both[1:])
        if self.rights:
            self.lefts = [self.add(self.lefts[0], self.rights[0])]
        self.rights = [flipped(self.lefts[0], *self.steps.pop(0))]

    def result(self):
        return self.lefts[0], self.rights[0]


def page_places(half, length, own_boxes, other_boxes):
    def slots(width, first, second):
        lane = lax.broadcasted_iota(jnp.int32, (1, width), 1)
        place = jnp.where(lane < HALF_SLOTS, first + lane, second + lane - HALF_SLOTS)
        place = jnp.where(lane < VIS_SLOTS, place, VIS_SLOTS - 1)
        row = (place * 37) >> 8
        return place, 71 + 143 * (place - 7 * row), 71 + 143 * row

    text = lax.broadcasted_iota(jnp.int32, (1, HALF_TEXT), 1)
    own_text = half * HALF_TEXT + text
    other_text = (1 - half) * HALF_TEXT + text
    slot = slots(LANES, half * HALF_SLOTS, (1 - half) * HALF_SLOTS)
    lane = lax.broadcasted_iota(jnp.int32, (1, LANES), 1)
    slot_used = jnp.where((slot[0] < VIS_TOK) & (lane < VIS_SLOTS), 1, 0)
    keys = (
        jnp.concatenate([own_text, other_text, slot[0]], axis=1),
        jnp.concatenate([own_boxes[0:1], other_boxes[0:1], slot[1]], axis=1),
        jnp.concatenate([own_boxes[1:2], other_boxes[1:2], slot[2]], axis=1),
        jnp.concatenate(
            [
                jnp.where(own_text < length, 1, 0),
                jnp.where(other_text < length, 1, 0),
                slot_used,
            ],
            axis=1,
        ),
    )
    queries = (
        jnp.concatenate([own_text, slot[0]], axis=1),
        jnp.concatenate([own_boxes[0:1], slot[1]], axis=1),
        jnp.concatenate([own_boxes[1:2], slot[2]], axis=1),
    )
    return keys, queries


def as_columns(rows):
    stacked = jnp.concatenate(list(rows) + [rows[0]] * (8 - len(rows)), axis=0)
    turned = jnp.transpose(stacked.astype(f32), (1, 0)).astype(jnp.int32)
    return [turned[:ROWS, i : i + 1] for i in range(len(rows))]


def bias_kernel(facts, own_boxes, other_boxes, table_a, table_b, out, near_s, across_s, down_s):
    @pl.when(pl.program_id(0) == 0)
    def _():
        keys, queries = page_places(facts[0], facts[1], own_boxes[...], other_boxes[...])
        place, x, y = as_columns(queries)
        near_s[...] = jnp.clip(keys[0] - place, -16, 15) + 16
        across_s[...] = jnp.clip((keys[1] - x) >> 4, -32, 31) + 64
        down_s[...] = jnp.where(
            keys[3] > 0, jnp.clip((keys[2] - y) >> 4, -32, 31) + 32, BOX_BINS
        )

    a = jnp.broadcast_to(table_a[0, 0:1, :], (ROWS, LANES))
    b = jnp.broadcast_to(table_b[0, 0:1, :], (ROWS, LANES))
    for tile in range(KEYS // LANES):
        span = slice(tile * LANES, (tile + 1) * LANES)

        def look(table, codes):
            return jnp.take_along_axis(table, codes, axis=1, mode="promise_in_bounds")

        out[0, :, span] = (
            look(a, near_s[:, span]) + look(a, across_s[:, span]) + look(b, down_s[:, span])
        )


def make_bias(facts, own_boxes, other_boxes, bias_table):
    columns = bias_table.T
    table_a = jnp.pad(columns[:, : POS_BINS + BOX_BINS], ((0, 0), (0, LANES - POS_BINS - BOX_BINS)))
    table_b = jnp.pad(
        columns[:, POS_BINS + BOX_BINS :],
        ((0, 0), (0, LANES - BOX_BINS)),
        constant_values=NEVER,
    )
    spread = lambda t: jnp.broadcast_to(t[:, None, :], (HEADS, 8, LANES))
    whole = lambda h, facts: (0, 0)
    return pl.pallas_call(
        bias_kernel,
        out_shape=jax.ShapeDtypeStruct((HEADS, ROWS, KEYS), f32),
        grid_spec=pltpu.PrefetchScalarGridSpec(
            num_scalar_prefetch=1,
            grid=(HEADS,),
            in_specs=[
                pl.BlockSpec((2, HALF_TEXT), whole),
                pl.BlockSpec((2, HALF_TEXT), whole),
                pl.BlockSpec((1, 8, LANES), lambda h, facts: (h, 0, 0)),
                pl.BlockSpec((1, 8, LANES), lambda h, facts: (h, 0, 0)),
            ],
            out_specs=pl.BlockSpec((1, ROWS, KEYS), lambda h, facts: (h, 0, 0)),
            scratch_shapes=[pltpu.VMEM((ROWS, KEYS), jnp.int32)] * 3,
        ),
        compiler_params=pltpu.CompilerParams(vmem_limit_bytes=50 * MIB),
        cost_estimate=brief,
        name="score_bias",
    )(facts, own_boxes, other_boxes, spread(table_a), spread(table_b))


def pairs_kernel(facts, own_boxes, other_boxes, right, left, masks):
    keys, queries = page_places(facts[0], facts[1], own_boxes[...], other_boxes[...])
    place, x, y = as_columns(queries)
    diff = keys[0] - place
    for index, holds in enumerate(
        (
            (diff >= -16) & (diff <= 15),
            (keys[1] & 15) < (x & 15),
            (keys[2] & 15) < (y & 15),
            diff > 15,
        )
    ):
        masks[index] = jnp.where(holds, 1.0, 0.0).astype(bf16)
    row = lax.broadcasted_iota(jnp.int32, (64, KEYS), 0)
    key_hot = [
        jnp.where((63 - row) == (code & 63), 1.0, 0.0)
        for code in (keys[1] >> 4, keys[2] >> 4, keys[0])
    ]
    key_hot.append(jnp.zeros((64, KEYS), f32))
    right[...] = jnp.transpose(jnp.concatenate(key_hot, axis=0), (1, 0)).astype(bf16)
    row = lax.broadcasted_iota(jnp.int32, (64, 384), 0)
    query_hot = [
        jnp.where(row == queries[1] >> 4, 1.0, 0.0),
        jnp.where(row == queries[2] >> 4, 1.0, 0.0),
        jnp.where(row[:32] + 64 == queries[2] >> 4, 1.0, 0.0),
        jnp.where(row == (queries[0] & 63), 1.0, 0.0),
    ]
    left[...] = jnp.concatenate(query_hot, axis=0)[:, :ROWS].astype(bf16)


def page_pairs(facts, own_boxes, other_boxes):
    vmem = pl.BlockSpec(memory_space=pltpu.VMEM)
    return pl.pallas_call(
        pairs_kernel,
        in_specs=[pl.BlockSpec(memory_space=pltpu.SMEM), vmem, vmem],
        out_specs=[vmem] * 3,
        out_shape=[
            jax.ShapeDtypeStruct((KEYS, 256), bf16),
            jax.ShapeDtypeStruct((224, ROWS), bf16),
            jax.ShapeDtypeStruct((4, ROWS, KEYS), bf16),
        ],
        compiler_params=pltpu.CompilerParams(vmem_limit_bytes=24 * MIB),
        cost_estimate=brief,
        name="page_pairs",
    )(facts, own_boxes, other_boxes)


def table_kernel(right, left, masks, ds_a, ds_b, *rest):
    out = rest[-1]
    total = (ds_a[0].astype(f32) + ds_b[0].astype(f32)).astype(bf16)
    hot = right[...]
    query_hot = left[...]

    def fold(values, columns, rows):
        inner = jnp.dot(values, hot[:, columns], preferred_element_type=f32).astype(bf16)
        return jnp.dot(query_hot[rows], inner, preferred_element_type=f32)

    plain = fold(total, slice(0, 128), slice(0, 160))
    near = fold(total * masks[0], slice(128, 256), slice(160, 224))
    by_x = fold(total * masks[1], slice(0, 128), slice(0, 64))
    by_y = fold(total * masks[2], slice(0, 128), slice(64, 160))

    def diagonals(square):
        lane = lax.broadcasted_iota(jnp.int32, square.shape, 1)
        square = jnp.where(lane < 64, square, 0.0)
        turned = pltpu.roll(square, 0, axis=1, stride=1, stride_axis=0)
        return jnp.sum(turned, axis=0, keepdims=True)

    def second(square):
        return pltpu.roll(square, 64, axis=1)

    above = jnp.sum((total * masks[3]).astype(f32), axis=0, keepdims=True)
    above = sum(above[:, t * LANES : (t + 1) * LANES] for t in range(KEYS // LANES))
    out[0] = jnp.concatenate(
        [
            diagonals(plain[:64]),
            diagonals(by_x),
            diagonals(second(plain[64:128])),
            diagonals(second(by_y[:64])),
            diagonals(near),
            above,
            diagonals(second(plain[128:])),
            diagonals(second(by_y[64:])),
        ],
        axis=0,
    )


def table_bins():
    bins = np.zeros((8, LANES, BUCKETS), np.float32)
    for c in range(127):
        diff = 63 - c
        for kind, base in ((0, POS_BINS), (1, POS_BINS + BOX_BINS)):
            here = base + 32 + min(max(diff, -32), 31)
            below = base + 32 + min(max(diff - 1, -32), 31)
            bins[2 * kind, c, here] += 1
            bins[2 * kind + 1, c, below] += 1
            bins[2 * kind + 1, c, here] -= 1
        far = -1 - c
        bins[6, c, 128 + max(far, -32)] += 1
        bins[7, c, 128 + max(far - 1, -32)] += 1
        bins[7, c, 128 + max(far, -32)] -= 1
        near = (diff + 32) % 64 - 32
        if -16 <= near <= 15:
            bins[4, c, near + 16] += 1
        bins[0, c, 0] += 1
        bins[4, c, 0] -= 1
    bins[5, :, 31] += 1
    bins[5, :, 0] -= 1
    return bins


def fold_table(pairs, ds_a, ds_b, part, parts, after=()):
    count = HEADS // parts
    head = pl.BlockSpec((1, ROWS, KEYS), lambda h: (h + part * count, 0, 0))
    return pl.pallas_call(
        table_kernel,
        out_shape=jax.ShapeDtypeStruct((count, 8, LANES), f32),
        grid=(count,),
        in_specs=[full(array) for array in pairs]
        + [head, head]
        + [pl.BlockSpec(memory_space=pl.ANY)] * len(after),
        out_specs=pl.BlockSpec((1, 8, LANES), lambda h: (h, 0, 0)),
        compiler_params=pltpu.CompilerParams(vmem_limit_bytes=58 * MIB),
        cost_estimate=brief,
        name="table_grad",
    )(*pairs, ds_a, ds_b, *after)


def visual_kernel(half, grad_ref, normal_low, hat, weight, keep, send, normal_grad, sums):
    rows = normal_low.shape[0]
    column = lambda block: jnp.sum(block, axis=0, keepdims=True)
    token_grad = grad_ref[...].astype(bf16)
    whole = tn_dot(normal_low[...], token_grad)
    mid = whole.shape[0] // 2
    first = half[0] == 0
    keep[...] = jnp.where(first, whole[:mid], whole[mid:]).astype(bf16)
    send[...] = jnp.where(first, whole[mid:], whole[:mid]).astype(bf16)
    place = half[0] * rows + lax.broadcasted_iota(jnp.int32, (rows, 1), 0)
    grad = jnp.where(place < VIS_TOK, nt_dot(token_grad, weight[...]), 0.0)
    normal_grad[...] = grad
    total = column(token_grad.astype(f32))
    put_row(sums, 0, total)
    at = total.shape[1] // LANES
    count = grad.shape[1] // LANES
    put_row(sums.at[at : at + count], 0, column(grad * hat[...]))
    put_row(sums.at[at + count : at + 2 * count], 0, column(grad))


def visual_back(half, gradient, normal_low, hat, weight):
    slots, channels = normal_low.shape
    width = weight.shape[1]
    return pl.pallas_call(
        visual_kernel,
        grid_spec=pltpu.PrefetchScalarGridSpec(
            num_scalar_prefetch=1,
            grid=(1,),
            in_specs=[
                pl.BlockSpec(
                    (slots, width), lambda i, half: (gradient.shape[0] // slots - 1, 0)
                ),
                full(normal_low),
                full(hat),
                full(weight),
            ],
            out_specs=[
                pl.BlockSpec((channels // 2, width), lambda i, half: (0, 0)),
                pl.BlockSpec((channels // 2, width), lambda i, half: (0, 0)),
                pl.BlockSpec((slots, channels), lambda i, half: (0, 0)),
                pl.BlockSpec(((width + 2 * channels) // LANES, LANES), lambda i, half: (0, 0)),
            ],
        ),
        out_shape=[
            jax.ShapeDtypeStruct((channels // 2, width), bf16),
            jax.ShapeDtypeStruct((channels // 2, width), bf16),
            jax.ShapeDtypeStruct((slots, channels), f32),
            jax.ShapeDtypeStruct(((width + 2 * channels) // LANES, LANES), f32),
        ],
        cost_estimate=brief,
        name="visual_back",
    )(half, gradient, normal_low, hat, weight)


def join_kernel(*refs):
    out = refs[-1]
    out[...] = jnp.zeros_like(out)
    at = 0
    for ref in refs[:-1]:
        values = ref[...]
        if len(values.shape) == 3 and values.shape[1] > 1:
            for head in range(values.shape[0]):
                out[at : at + values.shape[1], :] = values[head]
                at += values.shape[1]
        elif len(values.shape) == 3:
            for group in range(values.shape[0]):
                for start in range(0, values.shape[2], LANES):
                    size = min(LANES, values.shape[2] - start)
                    out[at : at + 1, :size] = ref[group, :, start : start + size]
                    at += 1
        else:
            out[at : at + values.shape[0], :] = values
            at += values.shape[0]


def bin_rows(units):
    return -(-units // LANES)


def join(parts):
    rows = 0
    for part in parts:
        if part.ndim == 3 and part.shape[1] == 1:
            rows += part.shape[0] * bin_rows(part.shape[2])
        else:
            rows += part.size // LANES
    vmem = pl.BlockSpec(memory_space=pltpu.VMEM)
    return pl.pallas_call(
        join_kernel,
        out_shape=jax.ShapeDtypeStruct((rows, LANES), f32),
        in_specs=[vmem] * len(parts),
        out_specs=vmem,
        cost_estimate=brief,
        name="join",
    )(*parts)


def split_kernel(
    sizes,
    count,
    me,
    left,
    right,
    bins,
    normal_grad,
    hat,
    inverse_std,
    bn_gain,
    attn,
    out_bias,
    gain,
    shift,
    table,
    vis_bias,
    gain_grad,
    shift_grad,
    hidden_bias,
    maps,
    total,
):
    total[...] = left[...] + right[...]
    units = hidden_bias.shape[1]
    width = out_bias.shape[1]
    channels = gain_grad.shape[1]
    starts = [0]
    for size in sizes:
        starts.append(starts[-1] + size)

    def take(start, index, wide):
        per = wide // LANES
        begin = start + index * per
        return jnp.concatenate([total[begin + i : begin + i + 1, :] for i in range(per)], axis=1)

    for layer in range(LAYERS):
        norm = functools.partial(take, starts[layer])
        gain[layer, 1:2, :] = norm(0, width)
        shift[layer, 1:2, :] = norm(1, width)
        out_bias[layer : layer + 1, :] = norm(2, width)
        gain[layer, 0:1, :] = norm(3, width)
        shift[layer, 0:1, :] = norm(4, width)
        attn[2, layer : layer + 1, :] = norm(5, width)
        rows = functools.partial(take, starts[LAYERS + layer])
        attn[0, layer : layer + 1, :] = rows(0, width)
        attn[1, layer : layer + 1, :] = rows(1, width)
        per = bin_rows(units)
        begin = starts[2 * LAYERS + layer] + me[0] * per
        for part in range(per):
            span = min(LANES, units - part * LANES)
            hidden_bias[layer : layer + 1, part * LANES : part * LANES + span] = total[
                pl.ds(begin + part, 1), :span
            ]
    at = starts[3 * LAYERS]
    vis_bias[...] = total[at : at + width // LANES, :]
    at += width // LANES
    by_gain = take(at, 0, channels)
    by_shift = take(at, 1, channels)
    gain_grad[...] = by_gain
    shift_grad[...] = by_shift
    scale = inverse_std[...] * bn_gain[...]
    slots = normal_grad.shape[0]
    place = (me[0] & 1) * slots + lax.broadcasted_iota(jnp.int32, (slots, 1), 0)
    maps[...] = jnp.where(
        place < VIS_TOK,
        scale * (normal_grad[...] - by_shift / count - hat[...] * (by_gain / count)),
        0.0,
    )
    at = starts[3 * LAYERS + 1]
    folded = jnp.zeros((16, BUCKETS), f32)
    for kind in range(8):
        rows = jnp.concatenate(
            [total[at + 8 * head + kind : at + 8 * head + kind + 1, :] for head in range(HEADS)]
            + [jnp.zeros((16 - HEADS, LANES), f32)],
            axis=0,
        )
        high = rows.astype(bf16)
        middle = (rows - high.astype(f32)).astype(bf16)
        low = (rows - high.astype(f32) - middle.astype(f32)).astype(bf16)
        for part in (high, middle, low):
            folded = folded + nt_dot(part, bins[kind])
    table[...] = folded[:HEADS]


def split(me, left, right, sizes, count, normal_grad, hat, inverse_std, bn_gain, units, width):
    slots, channels = normal_grad.shape
    bins = jnp.asarray(table_bins().transpose(0, 2, 1), bf16)
    row = lambda value: value.reshape(1, -1)
    vmem = pl.BlockSpec(memory_space=pltpu.VMEM)
    shape = lambda *size: jax.ShapeDtypeStruct(size, f32)
    return pl.pallas_call(
        functools.partial(split_kernel, sizes, count),
        in_specs=[pl.BlockSpec(memory_space=pltpu.SMEM)] + [vmem] * 7,
        out_specs=[vmem] * 10,
        out_shape=[
            shape(3, LAYERS, width),
            shape(LAYERS, width),
            shape(LAYERS, 2, width),
            shape(LAYERS, 2, width),
            shape(HEADS, BUCKETS),
            shape(width // LANES, LANES),
            shape(1, channels),
            shape(1, channels),
            shape(LAYERS, units),
            shape(slots, channels),
        ],
        scratch_shapes=[pltpu.VMEM(left.shape, f32)],
        cost_estimate=brief,
        name="split",
    )(me, left, right, bins, normal_grad, hat, row(inverse_std), row(bn_gain))


def whole_page(own, other):
    return jnp.concatenate(
        [
            own[:HALF_TEXT],
            other[:HALF_TEXT],
            own[HALF_TEXT:],
            other[HALF_TEXT:],
            jnp.zeros((KEYS - 2 * ROWS, own.shape[1]), own.dtype),
        ],
        axis=0,
    )


def page_split(both):
    mid = 2 * HALF_TEXT
    own = jnp.concatenate([both[:HALF_TEXT], both[mid : mid + HALF_SLOTS]], axis=0)
    other = jnp.concatenate(
        [both[HALF_TEXT:mid], both[mid + HALF_SLOTS : mid + VIS_SLOTS]], axis=0
    )
    return own, other


def nt_dot(left, right):
    return lax.dot_general(left, right, (((1,), (1,)), ((), ())), preferred_element_type=f32)


def tn_dot(left, right):
    return lax.dot_general(left, right, (((0,), (0,)), ((), ())), preferred_element_type=f32)


def put_row(target, index, row):
    count = row.shape[1] // LANES
    for part in range(count):
        at = index * count + part
        target[at : at + 1, :] = row[:, part * LANES : (part + 1) * LANES]


def centred(values):
    center = values - jnp.mean(values, axis=1, keepdims=True)
    spread = jnp.mean(center * center, axis=1, keepdims=True)
    rate = lax.rsqrt(spread + norm_epsilon)
    return center * rate, rate


def norm_back(grad, values, gain_row):
    hat, rate = centred(values)
    scaled = grad * gain_row
    mean = jnp.mean(scaled, axis=1, keepdims=True)
    along = jnp.mean(scaled * hat, axis=1, keepdims=True)
    column = lambda block: jnp.sum(block, axis=0, keepdims=True)
    return rate * (scaled - mean - hat * along), column(grad * hat), column(grad)


def attend_kernel(
    layer,
    q_ref,
    ko,
    kp,
    vo,
    vp,
    bias,
    x_ref,
    weight,
    attn_bias,
    gain,
    shift,
    soft,
    pair,
    residual,
    normed,
):
    step = pl.program_id(0)
    q = q_ref[...] * jnp.asarray(HEAD_DIM**-0.5, bf16)
    keys = whole_page(ko[...], kp[...])
    values = whole_page(vo[...], vp[...])
    first = lax.broadcasted_iota(jnp.int32, (ROWS, LANES), 1) < HEAD_DIM
    parts = []
    for head in range(2):
        mine = jnp.where(first if head == 0 else ~first, q, jnp.zeros_like(q))
        scores = nt_dot(mine, keys) + bias[head]
        raised = jnp.exp(scores - jnp.max(scores, axis=1, keepdims=True))
        weights = (raised * (1.0 / jnp.sum(raised, axis=1, keepdims=True))).astype(bf16)
        soft[head] = weights
        parts.append(jnp.dot(weights, values, preferred_element_type=f32))
    slab = pl.ds(pl.multiple_of(step * LANES, LANES), LANES)
    pair[0, :, slab] = jnp.where(first, parts[0], parts[1]).astype(bf16)

    @pl.when(step == PAIRS - 1)
    def _():
        attended = jnp.dot(pair[0], weight[0], preferred_element_type=f32)
        summed = x_ref[...] + (attended + attn_bias[layer, 2:3, :])
        residual[...] = summed
        out = centred(summed)[0] * gain[layer, 0:1, :] + shift[layer, 0:1, :]
        normed[...] = out
        pair[1] = out.astype(bf16)


def full(array):
    return pl.BlockSpec(array.shape, lambda *at: (0,) * array.ndim)


def attend(layer, q, kv, other_kv, bias, x, out_weight, attn_bias, gain, shift):
    rows, width = q.shape
    slab = pl.BlockSpec((ROWS, LANES), lambda p: (0, p))
    second = pl.BlockSpec((ROWS, LANES), lambda p: (0, p + PAIRS))
    heads = pl.BlockSpec((2, ROWS, KEYS), lambda p: (p, 0, 0))
    whole = pl.BlockSpec((rows, width), lambda p: (0, 0))
    wide = jax.ShapeDtypeStruct((rows, width), f32)
    low = jax.ShapeDtypeStruct((2, rows, width), bf16)
    return pl.pallas_call(
        functools.partial(attend_kernel, layer),
        grid=(PAIRS,),
        in_specs=[
            slab,
            slab,
            slab,
            second,
            second,
            heads,
            whole,
            pl.BlockSpec((1, width, width), lambda p: (layer, 0, 0)),
            full(attn_bias),
            full(gain),
            full(shift),
        ],
        out_specs=[
            heads,
            pl.BlockSpec((2, rows, width), lambda p: (0, 0, 0)),
            whole,
            whole,
        ],
        out_shape=[jax.ShapeDtypeStruct((HEADS, ROWS, KEYS), bf16), low, wide, wide],
        compiler_params=pltpu.CompilerParams(vmem_limit_bytes=50 * MIB),
        cost_estimate=brief,
        name="attend",
    )(q, kv, other_kv, kv, other_kv, bias, x, out_weight, attn_bias, gain, shift)


def attend_back_kernel(q_ref, ko, kp, vo, vp, dc_ref, soft, *rest):
    ds, *grads = rest[-6:]
    scale = HEAD_DIM**-0.5
    q = q_ref[...]
    dc = dc_ref[...]
    keys = whole_page(ko[...], kp[...])
    values = whole_page(vo[...], vp[...])
    first = lax.broadcasted_iota(jnp.int32, (ROWS, LANES), 1) < HEAD_DIM
    q_turned = jnp.transpose(q.astype(f32), (1, 0)).astype(bf16)
    dc_turned = jnp.transpose(dc.astype(f32), (1, 0)).astype(bf16)
    dq_parts, dk_parts, dv_parts = [], [], []
    for head in range(2):
        span = slice(head * HEAD_DIM, (head + 1) * HEAD_DIM)
        mine = jnp.where(first if head == 0 else ~first, dc, jnp.zeros_like(dc))
        weights = soft[head]
        weights_f = weights.astype(f32)
        flow = nt_dot(mine, values)
        share = jnp.sum(weights_f * flow, axis=1, keepdims=True)
        score_grad = (weights_f * (flow - share)).astype(bf16)
        ds[head] = score_grad
        dq_parts.append(jnp.dot(score_grad, keys, preferred_element_type=f32))
        dk_parts.append(jnp.dot(q_turned[span], score_grad, preferred_element_type=f32))
        dv_parts.append(jnp.dot(dc_turned[span], weights, preferred_element_type=f32))
    grads[0][...] = (jnp.where(first, dq_parts[0], dq_parts[1]) * scale).astype(bf16)
    own, other = page_split(jnp.transpose(jnp.concatenate(dk_parts, axis=0) * scale, (1, 0)))
    grads[1][...] = own.astype(bf16)
    grads[2][...] = other.astype(bf16)
    own, other = page_split(jnp.transpose(jnp.concatenate(dv_parts, axis=0), (1, 0)))
    grads[3][...] = own.astype(bf16)
    grads[4][...] = other.astype(bf16)


def attend_back(q, kv, other_kv, dctx, soft, after=()):
    slab = pl.BlockSpec((ROWS, LANES), lambda p: (0, p))
    second = pl.BlockSpec((ROWS, LANES), lambda p: (0, p + PAIRS))
    heads = pl.BlockSpec((2, ROWS, KEYS), lambda p: (p, 0, 0))
    return pl.pallas_call(
        attend_back_kernel,
        grid=(PAIRS,),
        in_specs=[slab, slab, slab, second, second, slab, heads]
        + [pl.BlockSpec(memory_space=pl.ANY)] * len(after),
        out_specs=[heads] + [slab] * 5,
        out_shape=[
            jax.ShapeDtypeStruct((HEADS, ROWS, KEYS), bf16),
        ]
        + [jax.ShapeDtypeStruct(q.shape, bf16)] * 5,
        compiler_params=pltpu.CompilerParams(vmem_limit_bytes=50 * MIB),
        cost_estimate=brief,
        name="attend_back",
    )(q, kv, other_kv, kv, other_kv, dctx, soft, *after)


def ffn_kernel(layer, more, me, x_ref, *refs):
    step = pl.program_id(0)
    width = x_ref.shape[1]
    blocks, (bias, n_ref, out_bias, gain, shift), rest = refs[:BLOCKS], refs[BLOCKS:][:5], refs[BLOCKS + 5 :]
    units = blocks[0].shape[1]
    own_act, mate_act, slope, residual = rest[-7 if more else -5 :][:4]
    x = x_ref[...]

    total = None
    for index, block in enumerate(blocks):
        weights = block[0]
        row = bias[pl.ds(me[0] ^ (BLOCKS * step + index), 1), layer, :units]
        hidden = nt_dot(x, weights[:, :width]) + row.astype(f32)
        half_cdf = 0.5 + 0.5 * lax.erf(hidden * 0.5**0.5)
        low = (hidden * half_cdf).astype(bf16)
        (mate_act if index % 2 else own_act)[index // 2] = low
        density = jnp.exp(hidden * hidden * -0.5) * (1.0 / (2.0 * np.pi) ** 0.5)
        slope[index] = (half_cdf + hidden * density).astype(bf16)
        term = jnp.dot(low, weights[:, width:], preferred_element_type=f32)
        total = term if total is None else total + term

    @pl.when(step == 0)
    def _():
        residual[...] = n_ref[...] + out_bias[layer : layer + 1, :] + total

    @pl.when(step > 0)
    def _():
        residual[...] += total

    @pl.when(step == pl.num_programs(0) - 1)
    def _():
        states = centred(residual[...])[0] * gain[layer, 1:2, :] + shift[layer, 1:2, :]
        rounded = states.astype(bf16)
        if more:
            weight, attn_bias = rest[:2]
            wide, query, shared = rest[-3:]
            wide[...] = states
            project = lambda index: jnp.dot(
                rounded, weight[0, index], preferred_element_type=f32
            )
            query[...] = (project(0) + attn_bias[layer + 1, 0:1, :]).astype(bf16)
            shared[:, :width] = project(1).astype(bf16)
            shared[:, width : 2 * width] = (
                project(2) + attn_bias[layer + 1, 1:2, :]
            ).astype(bf16)
            shared[:, 2 * width :] = rounded
        else:
            rest[-1][...] = rounded


def weight_blocks(layer, units, width):
    pick = lambda which: pl.BlockSpec(
        (1, units, 2 * width), lambda i, me: (me[0] ^ (BLOCKS * i + which), layer, 0)
    )
    return [pick(which) for which in range(BLOCKS)]


def ffn(me, layer, pair, n, gathered, units, out_bias, gain, shift, qkv_weight, attn_bias):
    groups = gathered.shape[0]
    rows, width = n.shape
    more = layer < LAYERS - 1
    whole = pl.BlockSpec((rows, width), lambda i, me: (0, 0))
    kept = pl.BlockSpec((BLOCKS, rows, units), lambda i, me: (i, 0, 0))
    kept_shape = jax.ShapeDtypeStruct((groups, rows, units), bf16)
    wide = jax.ShapeDtypeStruct((rows, width), f32)
    low = jax.ShapeDtypeStruct((rows, width), bf16)
    half_act = pl.BlockSpec((HALF, rows, units), lambda i, me: (i, 0, 0))
    half_shape = jax.ShapeDtypeStruct((groups // 2, rows, units), bf16)
    inputs = [pair] + [gathered] * (BLOCKS + 1) + [n, out_bias, gain, shift]
    in_specs = [
        pl.BlockSpec((None, rows, width), lambda i, me: (1, 0, 0)),
        *weight_blocks(layer, units, width),
        pl.BlockSpec(
            (groups, 16, 2 * width), lambda i, me: (0, LAYERS * units // 16, 0)
        ),
        whole,
        full(out_bias),
        full(gain),
        full(shift),
    ]
    out_specs = [half_act, half_act, kept, whole]
    out_shape = [half_shape, half_shape, kept_shape, wide]
    if more:
        inputs += [qkv_weight, attn_bias]
        in_specs += [
            pl.BlockSpec((1, 3, width, width), lambda i, me: (layer + 1, 0, 0, 0)),
            full(attn_bias),
        ]
        out_specs += [whole, whole, pl.BlockSpec((rows, 3 * width), lambda i, me: (0, 0))]
        out_shape += [wide, low, jax.ShapeDtypeStruct((rows, 3 * width), bf16)]
    else:
        out_specs += [whole]
        out_shape += [low]
    return pl.pallas_call(
        functools.partial(ffn_kernel, layer, more),
        out_shape=out_shape,
        grid_spec=pltpu.PrefetchScalarGridSpec(
            num_scalar_prefetch=1, grid=(groups // BLOCKS,), in_specs=in_specs, out_specs=out_specs
        ),
        compiler_params=pltpu.CompilerParams(vmem_limit_bytes=50 * MIB),
        cost_estimate=brief,
        name="feed_forward",
    )(me, *inputs)


def ffn_back_kernel(layer, me, grad_ref, r2_ref, r1_ref, *refs):
    blocks, (slope, gain, out_weight), rest = refs[:BLOCKS], refs[BLOCKS:][:3], refs[BLOCKS + 3 :]
    own_dh, mate_dh, low_grads, bias_grad, sums, dx, dctx, total_s = rest
    step = pl.program_id(0)
    width = r2_ref.shape[1]
    column = lambda block: jnp.sum(block, axis=0, keepdims=True)

    @pl.when(step == 0)
    def _():
        grad, gain_grad, shift_grad = norm_back(
            grad_ref[...].astype(f32), r2_ref[...], gain[layer, 1:2, :]
        )
        low = grad.astype(bf16)
        total_s[...] = grad
        low_grads[0] = low
        put_row(sums, 0, gain_grad)
        put_row(sums, 1, shift_grad)
        put_row(sums, 2, column(low.astype(f32)))

    dy = low_grads[0]
    total = None
    for index, block in enumerate(blocks):
        weights = block[0]
        flow = nt_dot(dy, weights[:, width:])
        grad = (flow * slope[index].astype(f32)).astype(bf16)
        (mate_dh if index % 2 else own_dh)[index // 2] = grad
        bias_grad[index ^ (me[0] & (BLOCKS - 1))] = column(grad.astype(f32))
        term = jnp.dot(grad, weights[:, :width], preferred_element_type=f32)
        total = term if total is None else total + term
    total_s[...] += total

    @pl.when(step == pl.num_programs(0) - 1)
    def _():
        grad, gain_grad, shift_grad = norm_back(total_s[...], r1_ref[...], gain[layer, 0:1, :])
        low = grad.astype(bf16)
        dx[...] = grad
        low_grads[1] = low
        dctx[...] = nt_dot(low, out_weight[0]).astype(bf16)
        put_row(sums, 3, gain_grad)
        put_row(sums, 4, shift_grad)
        put_row(sums, 5, column(low.astype(f32)))


def ffn_back(me, layer, grad, r2, r1, gathered, slope, gain, out_weight):
    groups, rows, units = slope.shape
    width = r2.shape[1]
    whole = pl.BlockSpec((rows, width), lambda i, me: (0, 0))
    half = pl.BlockSpec((HALF, rows, units), lambda i, me: (i, 0, 0))
    half_shape = jax.ShapeDtypeStruct((groups // 2, rows, units), bf16)
    return pl.pallas_call(
        functools.partial(ffn_back_kernel, layer),
        out_shape=[
            half_shape,
            half_shape,
            jax.ShapeDtypeStruct((2, rows, width), bf16),
            jax.ShapeDtypeStruct((groups, 1, units), f32),
            jax.ShapeDtypeStruct((6 * width // LANES, LANES), f32),
            jax.ShapeDtypeStruct((rows, width), f32),
            jax.ShapeDtypeStruct((rows, width), bf16),
        ],
        grid_spec=pltpu.PrefetchScalarGridSpec(
            num_scalar_prefetch=1,
            grid=(groups // BLOCKS,),
            in_specs=[
                whole,
                whole,
                whole,
                *weight_blocks(layer, units, width),
                pl.BlockSpec((BLOCKS, rows, units), lambda i, me: (i, 0, 0)),
                full(gain),
                pl.BlockSpec((1, width, width), lambda i, me: (layer, 0, 0)),
            ],
            out_specs=[
                half,
                half,
                pl.BlockSpec((2, rows, width), lambda i, me: (0, 0, 0)),
                pl.BlockSpec((BLOCKS, 1, units), lambda i, me: (me[0] // BLOCKS ^ i, 0, 0)),
                pl.BlockSpec((6 * width // LANES, LANES), lambda i, me: (0, 0)),
                whole,
                whole,
            ],
            scratch_shapes=[pltpu.VMEM((rows, width), f32)],
        ),
        compiler_params=pltpu.CompilerParams(vmem_limit_bytes=50 * MIB),
        cost_estimate=brief,
        name="feed_forward_back",
    )(me, grad, r2, r1, *[gathered] * BLOCKS, slope, gain, out_weight)


def ffn_grads_kernel(me, n, n_mate, dy, dy_mate, dh, dh_mate, act, act_mate, *rest):
    near_keep, near_send, seq_keep, seq_send, n_s, dy_s = rest[-6:]
    rows, width = n.shape
    step = pl.program_id(0)
    near = step < pl.num_programs(0) // 2

    @pl.when(step == 0)
    def _():
        for target, own, mate in ((n_s, n, n_mate), (dy_s, dy, dy_mate)):
            target[:rows] = own[...]
            target[rows:] = mate[...]

    both = lambda own, mate: jnp.concatenate([own[0], mate[0]], axis=0)
    into = tn_dot(both(dh, dh_mate), n_s[...]).astype(bf16)

    @pl.when(near)
    def _():
        near_keep[0] = into

    @pl.when(jnp.logical_not(near))
    def _():
        near_send[0] = into

    out = tn_dot(both(act, act_mate), dy_s[...]).astype(bf16)
    turn = me[1] % 2 == 0
    seq_keep[0] = jnp.where(turn, out[:, : width // 2], out[:, width // 2 :])
    seq_send[0] = jnp.where(turn, out[:, width // 2 :], out[:, : width // 2])


def ffn_grads(me, pair, pair_mate, low_grads, low_grads_mate, dh, dh_mate, act, act_mate):
    groups, rows, units = dh.shape
    width = pair.shape[2]
    far = groups // 2
    row_block = lambda which: pl.BlockSpec((None, rows, width), lambda i, me: (which, 0, 0))
    hidden = pl.BlockSpec((1, rows, units), lambda i, me: ((i % far) * 2 + i // far, 0, 0))
    place = lambda i, me: (me[0] >> 2) ^ i
    near_shape = jax.ShapeDtypeStruct((far, units, width), bf16)
    seq_shape = jax.ShapeDtypeStruct((groups, units, width // 2), bf16)
    seq_block = pl.BlockSpec(
        (1, units, width // 2), lambda i, me: (i // far * far + place(i % far, me), 0, 0)
    )
    return pl.pallas_call(
        ffn_grads_kernel,
        out_shape=[near_shape, near_shape, seq_shape, seq_shape],
        grid_spec=pltpu.PrefetchScalarGridSpec(
            num_scalar_prefetch=1,
            grid=(groups,),
            in_specs=[row_block(1), row_block(1), row_block(0), row_block(0)] + [hidden] * 4,
            out_specs=[
                pl.BlockSpec(
                    (1, units, width), lambda i, me: (place(jnp.minimum(i, far - 1), me), 0, 0)
                ),
                pl.BlockSpec(
                    (1, units, width), lambda i, me: (place(jnp.maximum(i - far, 0), me), 0, 0)
                ),
                seq_block,
                seq_block,
            ],
            scratch_shapes=[pltpu.VMEM((2 * rows, width), bf16)] * 2,
        ),
        compiler_params=pltpu.CompilerParams(vmem_limit_bytes=50 * MIB),
        cost_estimate=brief,
        name="feed_forward_grads",
    )(me, pair, pair_mate, low_grads, low_grads_mate, dh, dh_mate, act, act_mate)


def projection_kernel(by_distance, me, x, x_mate, ctx, ctx_mate, *refs):
    own, mate, refs = refs[:5], refs[5:10], refs[10:]
    da, da_mate, dr_ref, weight = refs[:4]
    near_keep, near_send, seq_keep, seq_send, dx, sums, turned_s, left_s, right_s, shards_s = refs[-10:]
    step = pl.program_id(0)
    far, shard = near_keep.shape[:2]
    rows, width = x.shape
    column = lambda block: jnp.sum(block.astype(f32), axis=0, keepdims=True)

    def place_of(place, near):
        far_place = (me[0] >> 2) ^ place if by_distance else place
        return far_place * 4 + ((me[0] & 3) ^ (2 * near))

    def pick_left(first, second):
        for index, block in enumerate((first, second)):
            turned_s[...] = jnp.transpose(block[...].astype(f32), (1, 0))
            for near in range(2):
                for place in range(far):
                    start = pl.multiple_of(place_of(place, near) * shard, 8)
                    at = (near * far + place) * shard
                    left_s[index, at : at + shard, :] = turned_s[pl.ds(start, shard), :]

    @pl.when(step == 0)
    def _():
        dx[...] = dr_ref[...]
        pick_left(x, x_mate)
        right_s[0] = own[0][...]
        right_s[1] = mate[0][...]
        put_row(sums, 0, column(own[0][...]))

    for index in (1, 2):

        @pl.when(step == index)
        def _():
            right_s[0] = add_low(own[2 * index - 1][...], mate[2 * index][...])
            right_s[1] = add_low(mate[2 * index - 1][...], own[2 * index][...])

    @pl.when(step == 2)
    def _():
        put_row(sums, 1, column(right_s[0]))

    @pl.when(step < 3)
    def _():
        dx[...] += nt_dot(right_s[0], weight[0, 0])

    @pl.when(step == 3)
    def _():
        pick_left(ctx, ctx_mate)
        right_s[0] = da[...]
        right_s[1] = da_mate[...]

    shards_s[...] = sum(
        jnp.dot(left_s[index].astype(bf16), right_s[index], preferred_element_type=f32)
        for index in range(2)
    )

    def put(target, first, near, columns):
        for place in range(far):
            at = (near * far + place) * shard
            target[first + place, :, columns] = shards_s[at : at + shard, :].astype(bf16)

    for index in range(2):

        @pl.when(step == index)
        def _():
            columns = slice(index * width, (index + 1) * width)
            put(near_keep, 0, 0, columns)
            put(near_send, 0, 1, columns)

    def put_seq(target):
        put(target, 0, 0, slice(None))
        put(target, far, 1, slice(None))

    mine = step - 2 == me[1] % 2
    pl.when((step >= 2) & mine)(lambda: put_seq(seq_keep))
    pl.when((step >= 2) & jnp.logical_not(mine))(lambda: put_seq(seq_send))


def projection_grads(
    by_distance,
    me,
    layer,
    shared,
    shared_mate,
    pair,
    pair_mate,
    own,
    mate,
    low,
    low_mate,
    dr,
    weight,
    after=(),
):
    rows, width = dr.shape
    groups = lax.axis_size("tp")
    shard = width // groups
    whole = pl.BlockSpec((rows, width), lambda t, me: (0, 0))
    x_block = pl.BlockSpec((rows, width), lambda t, me: (0, 2))
    layered = lambda which: pl.BlockSpec((None, rows, width), lambda t, me: (which, 0, 0))
    near_shape = jax.ShapeDtypeStruct((groups // 4, shard, 2 * width), bf16)
    near_block = pl.BlockSpec(near_shape.shape, lambda t, me: (0, 0, 0))
    seq_shape = jax.ShapeDtypeStruct((groups // 2, shard, width), bf16)
    seq_block = pl.BlockSpec(seq_shape.shape, lambda t, me: (0, 0, 0))
    return pl.pallas_call(
        functools.partial(projection_kernel, by_distance),
        out_shape=[near_shape, near_shape, seq_shape, seq_shape]
        + [
            jax.ShapeDtypeStruct((rows, width), f32),
            jax.ShapeDtypeStruct((2 * width // LANES, LANES), f32),
        ],
        grid_spec=pltpu.PrefetchScalarGridSpec(
            num_scalar_prefetch=1,
            grid=(4,),
            in_specs=[
                x_block,
                x_block,
                layered(0),
                layered(0),
                *[whole] * 10,
                layered(1),
                layered(1),
                whole,
                pl.BlockSpec(
                    (1, 1, width, width), lambda t, me: (layer, jnp.minimum(t, 2), 0, 0)
                ),
            ]
            + [pl.BlockSpec(memory_space=pl.ANY)] * len(after),
            out_specs=[near_block, near_block, seq_block, seq_block]
            + [
                whole,
                pl.BlockSpec((2 * width // LANES, LANES), lambda t, me: (0, 0)),
            ],
            scratch_shapes=[
                pltpu.VMEM((width, rows), f32),
                pltpu.VMEM((2, width // 2, rows), f32),
                pltpu.VMEM((2, rows, width), bf16),
                pltpu.VMEM((width // 2, width), f32),
            ],
        ),
        compiler_params=pltpu.CompilerParams(vmem_limit_bytes=50 * MIB),
        cost_estimate=brief,
        name="projection_grads",
    )(
        me,
        shared,
        shared_mate,
        pair,
        pair_mate,
        *own,
        *mate,
        low,
        low_mate,
        dr,
        weight,
        *after,
    )


def ordered(turn, mine, other):
    return jnp.where(turn, mine, other), jnp.where(turn, other, mine)


def projection_out_kernel(me, *refs):
    qkv, out = refs[-2:]
    shard, width = out.shape[1:]
    for layer in range(LAYERS):
        mine, other = refs[2 * layer : 2 * layer + 2]
        first, second = ordered(me[1] % 2 == 0, mine[...], other[...])
        low, high = first[:shard].astype(f32), second[:shard].astype(f32)
        qkv[layer, 0] = low
        qkv[layer, 1] = high
        qkv[layer, 2] = first[shard:].astype(f32)
        out[layer] = second[shard:].astype(f32)


def ffn_out_kernel(me, *refs):
    into, out = refs[-2:]
    units, width = out.shape[1:]
    for layer in range(LAYERS):
        mine, other = refs[2 * layer : 2 * layer + 2]
        for index, part in enumerate(ordered(me[1] % 2 == 0, mine[...], other[...])):
            columns = slice(index * (width // 2), (index + 1) * (width // 2))
            into[layer, :, columns] = part[:units].astype(f32)
            out[layer, :, columns] = part[units:].astype(f32)


def write_out(kernel, name, me, parts, shapes):
    vmem = pl.BlockSpec(memory_space=pltpu.VMEM)
    return pl.pallas_call(
        kernel,
        in_specs=[pl.BlockSpec(memory_space=pltpu.SMEM)] + [vmem] * len(parts),
        out_specs=[vmem] * len(shapes),
        out_shape=[jax.ShapeDtypeStruct(shape, f32) for shape in shapes],
        compiler_params=pltpu.CompilerParams(vmem_limit_bytes=24 * MIB),
        cost_estimate=brief,
        name=name,
    )(me, *parts)


def body(
    text_states,
    visual_maps,
    text_boxes,
    text_lengths,
    qkv_weight,
    out_weight,
    attn_bias,
    ffn_in,
    ffn_in_bias,
    ffn_out,
    ffn_out_bias,
    norm_gain,
    norm_shift,
    bias_table,
    vis_weight,
    vis_bias,
    bn_gain,
    bn_shift,
    cotangent,
):
    tp_index = lax.axis_index("tp")
    tp_size = lax.axis_size("tp")
    half = tp_index % 2
    page = (lax.axis_index("seq") * tp_size + tp_index) // 2
    me = jnp.stack([tp_index, lax.axis_index("seq")]).astype(jnp.int32)
    units = ffn_in.shape[1]
    width = text_states.shape[1]
    text_rows = text_states.shape[0]

    bias_rows = jnp.pad(ffn_in_bias, ((0, 16 - LAYERS), (0, 2 * width - units)))
    packed = jnp.concatenate(
        [
            jnp.concatenate([ffn_in, ffn_out], axis=2).reshape(LAYERS * units, 2 * width),
            bias_rows,
        ],
        axis=0,
    )
    gathered = lax.all_gather(packed, "tp", axis=0)

    other_boxes = flipped(text_boxes, "tp", 0)
    length = lax.dynamic_index_in_dim(text_lengths, page, 0, keepdims=False)
    facts = jnp.stack([half.astype(jnp.int32), length])
    score_bias = make_bias(facts, text_boxes, other_boxes, bias_table)

    count_cells = text_lengths.shape[0] * VIS_TOK
    maps_float = visual_maps.astype(f32)
    slot_place = half * HALF_SLOTS + jnp.arange(HALF_SLOTS, dtype=jnp.int32)
    slot_mask = (slot_place < VIS_TOK)[:, None]
    masked_maps = jnp.where(slot_mask, maps_float, 0.0)
    sums = total_over_all(
        jnp.stack([jnp.sum(masked_maps, axis=0), jnp.sum(masked_maps * masked_maps, axis=0)])
    )
    channel_mean = sums[0] / count_cells
    inverse_std = lax.rsqrt(sums[1] / count_cells - channel_mean * channel_mean + norm_epsilon)
    centered_hat = jnp.where(slot_mask, (maps_float - channel_mean) * inverse_std, 0.0)
    normal_low = jnp.where(slot_mask, centered_hat * bn_gain + bn_shift, 0.0).astype(bf16)
    visual_tokens = jnp.dot(normal_low, vis_weight, preferred_element_type=f32) + vis_bias
    states = jnp.concatenate([text_states.astype(f32), visual_tokens], axis=0)

    rounded = states.astype(bf16)
    project = lambda index: jnp.dot(rounded, qkv_weight[0, index], preferred_element_type=f32)
    shared = jnp.concatenate(
        [project(1).astype(bf16), (project(2) + attn_bias[0, 1]).astype(bf16), rounded], axis=1
    )
    query = (project(0) + attn_bias[0, 0]).astype(bf16)
    saved = []
    for layer in range(LAYERS):
        shared_mate = flipped(shared, "tp", 0)
        parts = (query, shared, shared_mate)
        soft, pair, residual_one, normed = attend(
            layer, *parts, score_bias, states, out_weight, attn_bias, norm_gain, norm_shift
        )
        if layer == 0:
            pairs = page_pairs(facts, text_boxes, other_boxes)
            normed, *pairs = tied((normed, *pairs), ())
        act, act_send, slope, residual_two, *onwards = ffn(
            me,
            layer,
            pair,
            normed,
            gathered,
            units,
            ffn_out_bias,
            norm_gain,
            norm_shift,
            qkv_weight,
            attn_bias,
        )
        mates = (flipped(pair, "tp", 0), flipped(act_send, "tp", 0))
        saved.append((parts, soft, pair, residual_one, residual_two, act, slope, mates))
        if layer < LAYERS - 1:
            states, query, shared = onwards
    out_states = onwards[0]

    gradient = cotangent
    norm_sums = [None] * LAYERS
    projection_rows = [None] * LAYERS
    bin_grads = [None] * LAYERS
    score_grads = [None] * LAYERS
    projections = [None] * LAYERS
    ffns = [None] * LAYERS
    for layer in reversed(range(LAYERS)):
        last = layer == LAYERS - 1
        parts, soft, pair, residual_one, residual_two, act, slope, mates = saved[layer]
        dh, dh_send, low, bin_grads[layer], norm_sums[layer], grad_one, context_grad = ffn_back(
            me, layer, gradient, residual_two, residual_one, gathered, slope, norm_gain, out_weight
        )
        if not last:
            context_grad, dh_send = tied((context_grad, dh_send), ffns[-1].underway())
            ffns[-1].second(context_grad)
        dh_mate, low_mate = flipped(dh_send, "tp", 0), flipped(low, "tp", 0)
        score_grads[layer], *grads = attend_back(*parts, context_grad, soft)
        (dh, dh_mate, low_mate, pair_mate, act_mate), grads = (
            tied((dh, dh_mate, low_mate, *mates), grads[:1]),
            tied(grads, (dh_mate, low_mate, *mates)),
        )
        grads_mate = [flipped(part, "tp", 0) for part in grads]
        weights = ffn_grads(me, pair, pair_mate, low, low_mate, dh, dh_mate, act, act_mate)
        if not last:
            weights = tied(weights, projections[-1].underway() + ffns[-1].underway())
            projections[-1].second(weights[0])
            ffns[-1].scatter(weights[0])
        ffns[layer] = Shards(*weights)
        *weights, gradient, projection_rows[layer] = projection_grads(
            not last,
            me,
            layer,
            parts[1],
            parts[2],
            pair,
            mates[0],
            grads,
            grads_mate,
            low,
            low_mate,
            grad_one,
            qkv_weight,
        )
        if last:
            projections[layer] = Shards(*weights)

    half_at = me[:1] % 2
    vis_keep, vis_send, normal_grad, vis_rows = visual_back(
        half_at, gradient, normal_low, centered_hat, vis_weight
    )
    vis_came = flipped(vis_send, "tp", 0)
    seq_ways = [("seq", bit) for bit in range(mesh_bits("seq"))]
    far_ways = [("tp", bit) for bit in range(2, mesh_bits("tp"))]
    vis_ways = far_ways + [("tp", 1)] + seq_ways
    vis_sums = Tree(add_low(vis_keep, vis_came), vis_ways, join=("tp", 0))
    vis_sums.step()
    fold = functools.partial(fold_table, pairs, *score_grads, parts=FOLDS)
    folds = [fold(0, after=vis_sums.lefts)]
    folds[0], *weights = tied(
        (folds[0], *weights),
        ffns[0].underway() + projections[-1].underway() + vis_sums.rights + [ffns[-1].shard],
    )
    ffns[0].second(folds[0])
    projections[-1].scatter(folds[0])
    projections[0] = Shards(*weights)
    vis_sums.step(folds[0])
    folds.append(fold(1, after=folds + vis_sums.lefts))
    (folds[1],) = tied(
        folds[1:], ffns[0].underway() + vis_sums.rights + [projections[-1].shard]
    )
    ffns[0].scatter(folds[1])
    ffns[-1].join(folds[1])
    vis_sums.step(folds[1])
    small = join(norm_sums + projection_rows + bin_grads + [vis_rows, *folds])
    sizes = [part.shape[0] for part in norm_sums + projection_rows]
    sizes += [tp_size * bin_rows(units)] * LAYERS + [vis_rows.shape[0]]
    small_ways = [("tp", 0), ("tp", 1)] + seq_ways + far_ways
    small_sums = Tree(small, small_ways, add=jnp.add)
    small_sums.step()
    small_sums.step(*projections[0].underway())
    behind = small_sums.lefts[0]
    projections[0].second(behind)
    projections[-1].join(behind)
    small_sums.step(*projections[0].underway(), *vis_sums.rights)
    behind = small_sums.lefts[0]
    projections[0].halve(behind)
    vis_sums.step(behind)
    small_sums.step(projections[0].came, *vis_sums.rights)
    behind = small_sums.lefts[0]
    for _ in range(mesh_bits("tp") - 3):
        projections[0].halve_more(behind)
    while vis_sums.steps:
        vis_sums.step(behind)
    ffns[0].join(behind)
    while small_sums.steps:
        small_sums.step(projections[0].came)
    behind = small_sums.lefts[0]
    projections[0].halve_more(behind)
    projections[0].join()
    small, small_came = small_sums.result()
    vis_sum, vis_mate = vis_sums.result()
    vis_weight_grad = jnp.concatenate(
        [
            jnp.where(half == 0, vis_sum, vis_mate),
            jnp.where(half == 0, vis_mate, vis_sum),
        ],
        axis=0,
    ).astype(f32)
    grad_text = gradient[:text_rows]
    attn_total, bout_total, gain_total, shift_total, table_total, visb_total, *rest = split(
        me,
        small,
        small_came,
        sizes,
        count_cells,
        normal_grad,
        centered_hat,
        inverse_std,
        bn_gain,
        units,
        width,
    )
    bn_gain_grad, bn_shift_grad, bin_total, grad_maps = rest
    shard = width // tp_size
    qkv_total, out_total = write_out(
        projection_out_kernel,
        "projections_out",
        me,
        [part for shards in projections for part in (shards.shard, shards.other)],
        [(LAYERS, 3, shard, width), (LAYERS, shard, width)],
    )
    in_total, down_total = write_out(
        ffn_out_kernel,
        "feed_forward_out",
        me,
        [part for shards in ffns for part in (shards.shard, shards.other)],
        [(LAYERS, units, width)] * 2,
    )
    return (
        out_states,
        grad_text,
        grad_maps,
        qkv_total,
        out_total,
        attn_total.transpose(1, 0, 2),
        in_total,
        bin_total,
        down_total,
        bout_total,
        gain_total,
        shift_total,
        table_total.T,
        vis_weight_grad,
        visb_total.reshape(-1),
        bn_gain_grad[0],
        bn_shift_grad[0],
    )


def solution(mesh):
    rows = P(("seq", "tp"), None)
    units = P(None, "tp", None)
    return jax.shard_map(
        body,
        mesh=mesh,
        in_specs=(
            rows,
            rows,
            P(None, ("seq", "tp")),
            P(),
            P(),
            P(),
            P(),
            units,
            P(None, "tp"),
            units,
            P(),
            P(),
            P(),
            P(),
            P(),
            P(),
            P(),
            P(),
            rows,
        ),
        out_specs=(
            rows,
            rows,
            rows,
            P(None, None, "tp", None),
            units,
            P(),
            units,
            P(None, "tp"),
            units,
            P(),
            P(),
            P(),
            P(),
            P(),
            P(),
            P(),
            P(),
        ),
        check_vma=False,
    )
```

```python
import functools

import jax
import jax.numpy as jnp
import numpy as np
from jax import lax
from jax.experimental import pallas as pl
from jax.experimental.pallas import tpu as pltpu
from jax.sharding import PartitionSpec as P

HEADS = 12
HEAD_DIM = 64
VIS_TOK = 49
VIS_SLOTS = 64
POS_BINS = 32
BOX_BINS = 64
LAYERS = 2
BUCKETS = POS_BINS + 2 * BOX_BINS

HALF_TEXT = 256
HALF_SLOTS = VIS_SLOTS // 2
ROWS = HALF_TEXT + HALF_SLOTS
KEYS = 640
PAIRS = HEADS // 2
SLABS = 2
STEPS = PAIRS // SLABS
LANES = 128
FOLDS = 2
FOLD_HEADS = 2
BLOCKS = 4
HALF = BLOCKS // 2
norm_epsilon = 1e-05
NEVER = -1e30
bf16 = jnp.bfloat16
f32 = jnp.float32
MIB = 1 << 20
brief = pl.CostEstimate(flops=1, bytes_accessed=1, transcendentals=0)


def mesh_bits(axis):
    return (lax.axis_size(axis) - 1).bit_length()


def flipped(block, axis, bit):
    count = lax.axis_size(axis)
    return lax.ppermute(block, axis, [(i, i ^ (1 << bit)) for i in range(count)])


def total_over_all(value):
    for axis in ("tp", "seq"):
        for bit in range(mesh_bits(axis)):
            value = value + flipped(value, axis, bit)
    return value


def add_low(left, right):
    return (left.astype(f32) + right.astype(f32)).astype(bf16)


def tied(values, after):
    return lax.optimization_barrier((tuple(values), tuple(after)))[0]


class Shards:
    def __init__(self, near_keep, near_send, seq_keep, seq_send):
        self.near = near_keep
        self.seq = seq_keep
        self.near_came = flipped(near_send, "tp", 1)
        self.seq_came = flipped(seq_send, "seq", 0)

    def underway(self):
        return [self.near_came, self.seq_came]

    def second(self, *after):
        near, near_came, seq, seq_came = tied(
            (self.near, self.near_came, self.seq, self.seq_came), after
        )
        turn = lax.axis_index("seq") % 2
        middle = near.shape[-1] // 2
        pick = lambda block, which: jnp.where(
            turn == which, block[..., :middle], block[..., middle:]
        )
        self.near = add_low(pick(near, 0), pick(near_came, 0))
        self.near_came = flipped(add_low(pick(near, 1), pick(near_came, 1)), "seq", 0)
        far = seq.shape[0] // 2
        self.seq = add_low(seq[:far], seq_came[:far])
        self.seq_came = flipped(add_low(seq[far:], seq_came[far:]), "tp", 1)

    def arrived(self, *after):
        near, near_came, seq, seq_came = tied(
            (self.near, self.near_came, self.seq, self.seq_came), after
        )
        return add_low(near, near_came), add_low(seq, seq_came)

    def halve(self, *after):
        near, near_came, seq, seq_came = tied(
            (self.near, self.near_came, self.seq, self.seq_came), after
        )
        bit = mesh_bits("tp") - (near.shape[0] - 1).bit_length()
        pick = lambda block, which: block.reshape((-1, 2) + block.shape[1:])[:, which]
        add = lambda which: jnp.concatenate(
            [
                add_low(pick(near, which), pick(near_came, which)),
                add_low(pick(seq, which), pick(seq_came, which)),
            ],
            axis=1,
        )
        self.shard, self.came = add(0), flipped(add(1), "tp", bit)
        self.bit = bit + 1

    def halve_more(self, *after):
        shard, came = tied((self.shard, self.came), after)
        if shard.shape[0] == 1:
            self.shard = add_low(shard, came)[0]
            return
        pick = lambda block, which: block.reshape((-1, 2) + block.shape[1:])[:, which]
        self.shard = add_low(pick(shard, 0), pick(came, 0))
        self.came = flipped(add_low(pick(shard, 1), pick(came, 1)), "tp", self.bit)
        self.bit += 1

    def join(self, *after):
        (shard,) = tied((self.shard,), after)
        for bit in range(1, mesh_bits("seq")):
            shard = add_low(shard, flipped(shard, "seq", bit))
        self.shard = shard
        self.other = flipped(shard, "seq", 0)


class Scattered:
    def __init__(self, group, *after):
        parts = [part for shards in group for part in shards.arrived(*after)]
        columns = min(part.shape[-1] for part in parts)
        pieces = [
            part[..., start : start + columns]
            for part in parts
            for start in range(0, part.shape[-1], columns)
        ]
        count = lax.axis_size("tp")
        groups = [list(range(first, count, 4)) for first in range(4)]
        self.shard = lax.psum_scatter(
            jnp.concatenate(pieces, axis=1), "tp", scatter_dimension=0, axis_index_groups=groups
        )

    def join(self, *after):
        (shard,) = tied((self.shard,), after)
        for bit in range(1, mesh_bits("seq")):
            shard = add_low(shard, flipped(shard, "seq", bit))
        self.shard = shard
        self.other = flipped(shard, "seq", 0)


class Tree:
    def __init__(self, value, ways, join=None, add=add_low):
        self.lefts = [value]
        self.rights = []
        self.steps = list(ways) + ([join] if join else [])
        self.add = add

    def step(self, *after):
        if after:
            both = tied(self.lefts + self.rights, after)
            self.lefts, self.rights = list(both[:1]), list(both[1:])
        if self.rights:
            self.lefts = [self.add(self.lefts[0], self.rights[0])]
        self.rights = [flipped(self.lefts[0], *self.steps.pop(0))]

    def result(self):
        return self.lefts[0], self.rights[0]


def page_places(half, length, own_boxes, other_boxes):
    def slots(width, first, second):
        lane = lax.broadcasted_iota(jnp.int32, (1, width), 1)
        place = jnp.where(lane < HALF_SLOTS, first + lane, second + lane - HALF_SLOTS)
        place = jnp.where(lane < VIS_SLOTS, place, VIS_SLOTS - 1)
        row = (place * 37) >> 8
        return place, 71 + 143 * (place - 7 * row), 71 + 143 * row

    text = lax.broadcasted_iota(jnp.int32, (1, HALF_TEXT), 1)
    own_text = half * HALF_TEXT + text
    other_text = (1 - half) * HALF_TEXT + text
    slot = slots(LANES, half * HALF_SLOTS, (1 - half) * HALF_SLOTS)
    lane = lax.broadcasted_iota(jnp.int32, (1, LANES), 1)
    slot_used = jnp.where((slot[0] < VIS_TOK) & (lane < VIS_SLOTS), 1, 0)
    keys = (
        jnp.concatenate([own_text, other_text, slot[0]], axis=1),
        jnp.concatenate([own_boxes[0:1], other_boxes[0:1], slot[1]], axis=1),
        jnp.concatenate([own_boxes[1:2], other_boxes[1:2], slot[2]], axis=1),
        jnp.concatenate(
            [
                jnp.where(own_text < length, 1, 0),
                jnp.where(other_text < length, 1, 0),
                slot_used,
            ],
            axis=1,
        ),
    )
    queries = (
        jnp.concatenate([own_text, slot[0]], axis=1),
        jnp.concatenate([own_boxes[0:1], slot[1]], axis=1),
        jnp.concatenate([own_boxes[1:2], slot[2]], axis=1),
    )
    return keys, queries


def as_columns(rows):
    stacked = jnp.concatenate(list(rows) + [rows[0]] * (8 - len(rows)), axis=0)
    turned = jnp.transpose(stacked.astype(f32), (1, 0)).astype(jnp.int32)
    return [turned[:ROWS, i : i + 1] for i in range(len(rows))]


def bias_kernel(facts, own_boxes, other_boxes, table_a, table_b, out, near_s, across_s, down_s):
    @pl.when(pl.program_id(0) == 0)
    def _():
        keys, queries = page_places(facts[0], facts[1], own_boxes[...], other_boxes[...])
        place, x, y = as_columns(queries)
        near_s[...] = jnp.clip(keys[0] - place, -16, 15) + 16
        across_s[...] = jnp.clip((keys[1] - x) >> 4, -32, 31) + 64
        down_s[...] = jnp.where(
            keys[3] > 0, jnp.clip((keys[2] - y) >> 4, -32, 31) + 32, BOX_BINS
        )

    a = jnp.broadcast_to(table_a[0, 0:1, :], (ROWS, LANES))
    b = jnp.broadcast_to(table_b[0, 0:1, :], (ROWS, LANES))
    for tile in range(KEYS // LANES):
        span = slice(tile * LANES, (tile + 1) * LANES)

        def look(table, codes):
            return jnp.take_along_axis(table, codes, axis=1, mode="promise_in_bounds")

        out[0, :, span] = (
            look(a, near_s[:, span]) + look(a, across_s[:, span]) + look(b, down_s[:, span])
        )


def make_bias(facts, own_boxes, other_boxes, bias_table):
    columns = bias_table.T
    table_a = jnp.pad(columns[:, : POS_BINS + BOX_BINS], ((0, 0), (0, LANES - POS_BINS - BOX_BINS)))
    table_b = jnp.pad(
        columns[:, POS_BINS + BOX_BINS :],
        ((0, 0), (0, LANES - BOX_BINS)),
        constant_values=NEVER,
    )
    spread = lambda t: jnp.broadcast_to(t[:, None, :], (HEADS, 8, LANES))
    whole = lambda h, facts: (0, 0)
    return pl.pallas_call(
        bias_kernel,
        out_shape=jax.ShapeDtypeStruct((HEADS, ROWS, KEYS), f32),
        grid_spec=pltpu.PrefetchScalarGridSpec(
            num_scalar_prefetch=1,
            grid=(HEADS,),
            in_specs=[
                pl.BlockSpec((2, HALF_TEXT), whole),
                pl.BlockSpec((2, HALF_TEXT), whole),
                pl.BlockSpec((1, 8, LANES), lambda h, facts: (h, 0, 0)),
                pl.BlockSpec((1, 8, LANES), lambda h, facts: (h, 0, 0)),
            ],
            out_specs=pl.BlockSpec((1, ROWS, KEYS), lambda h, facts: (h, 0, 0)),
            scratch_shapes=[pltpu.VMEM((ROWS, KEYS), jnp.int32)] * 3,
        ),
        compiler_params=pltpu.CompilerParams(vmem_limit_bytes=50 * MIB),
        cost_estimate=brief,
        name="score_bias",
    )(facts, own_boxes, other_boxes, spread(table_a), spread(table_b))


def pairs_kernel(facts, own_boxes, other_boxes, right, left, masks):
    keys, queries = page_places(facts[0], facts[1], own_boxes[...], other_boxes[...])
    place, x, y = as_columns(queries)
    diff = keys[0] - place
    for index, holds in enumerate(
        (
            (diff >= -16) & (diff <= 15),
            (keys[1] & 15) < (x & 15),
            (keys[2] & 15) < (y & 15),
            diff > 15,
        )
    ):
        masks[index] = jnp.where(holds, 1.0, 0.0).astype(bf16)
    row = lax.broadcasted_iota(jnp.int32, (64, KEYS), 0)
    key_hot = [
        jnp.where((63 - row) == (code & 63), 1.0, 0.0)
        for code in (keys[1] >> 4, keys[2] >> 4, keys[0])
    ]
    key_hot.append(jnp.zeros((64, KEYS), f32))
    right[...] = jnp.transpose(jnp.concatenate(key_hot, axis=0), (1, 0)).astype(bf16)
    row = lax.broadcasted_iota(jnp.int32, (64, 384), 0)
    query_hot = [
        jnp.where(row == queries[1] >> 4, 1.0, 0.0),
        jnp.where(row == queries[2] >> 4, 1.0, 0.0),
        jnp.where(row[:32] + 64 == queries[2] >> 4, 1.0, 0.0),
        jnp.where(row == (queries[0] & 63), 1.0, 0.0),
    ]
    left[...] = jnp.concatenate(query_hot, axis=0)[:, :ROWS].astype(bf16)


def page_pairs(facts, own_boxes, other_boxes):
    vmem = pl.BlockSpec(memory_space=pltpu.VMEM)
    return pl.pallas_call(
        pairs_kernel,
        in_specs=[pl.BlockSpec(memory_space=pltpu.SMEM), vmem, vmem],
        out_specs=[vmem] * 3,
        out_shape=[
            jax.ShapeDtypeStruct((KEYS, 256), bf16),
            jax.ShapeDtypeStruct((224, ROWS), bf16),
            jax.ShapeDtypeStruct((4, ROWS, KEYS), bf16),
        ],
        compiler_params=pltpu.CompilerParams(vmem_limit_bytes=24 * MIB),
        cost_estimate=brief,
        name="page_pairs",
    )(facts, own_boxes, other_boxes)


def table_kernel(right, left, masks, ds_a, ds_b, *rest):
    for head in range(ds_a.shape[0]):
        fold_head(right, left, masks, ds_a[head], ds_b[head], rest[-1].at[head])


def fold_head(right, left, masks, ds_a, ds_b, out):
    total = (ds_a.astype(f32) + ds_b.astype(f32)).astype(bf16)
    hot = right[...]
    query_hot = left[...]

    def fold(values, columns, rows):
        inner = jnp.dot(values, hot[:, columns], preferred_element_type=f32).astype(bf16)
        return jnp.dot(query_hot[rows], inner, preferred_element_type=f32)

    near = fold(total * masks[0], slice(128, 256), slice(160, 224))
    together = jnp.concatenate([total, total * masks[1], total * masks[2]], axis=0)
    inner = jnp.dot(together, hot[:, :128], preferred_element_type=f32).astype(bf16)
    outer = lambda rows, which: jnp.dot(
        query_hot[rows], inner[which * ROWS : (which + 1) * ROWS], preferred_element_type=f32
    )
    plain = outer(slice(0, 160), 0)
    by_x = outer(slice(0, 64), 1)
    by_y = outer(slice(64, 160), 2)

    def diagonals(square):
        lane = lax.broadcasted_iota(jnp.int32, square.shape, 1)
        square = jnp.where(lane < 64, square, 0.0)
        turned = pltpu.roll(square, 0, axis=1, stride=1, stride_axis=0)
        return jnp.sum(turned, axis=0, keepdims=True)

    def second(square):
        return pltpu.roll(square, 64, axis=1)

    above = jnp.sum((total * masks[3]).astype(f32), axis=0, keepdims=True)
    above = sum(above[:, t * LANES : (t + 1) * LANES] for t in range(KEYS // LANES))
    out[...] = jnp.concatenate(
        [
            diagonals(plain[:64]),
            diagonals(by_x),
            diagonals(second(plain[64:128])),
            diagonals(second(by_y[:64])),
            diagonals(near),
            above,
            diagonals(second(plain[128:])),
            diagonals(second(by_y[64:])),
        ],
        axis=0,
    )


def table_bins():
    bins = np.zeros((8, LANES, BUCKETS), np.float32)
    for c in range(127):
        diff = 63 - c
        for kind, base in ((0, POS_BINS), (1, POS_BINS + BOX_BINS)):
            here = base + 32 + min(max(diff, -32), 31)
            below = base + 32 + min(max(diff - 1, -32), 31)
            bins[2 * kind, c, here] += 1
            bins[2 * kind + 1, c, below] += 1
            bins[2 * kind + 1, c, here] -= 1
        far = -1 - c
        bins[6, c, 128 + max(far, -32)] += 1
        bins[7, c, 128 + max(far - 1, -32)] += 1
        bins[7, c, 128 + max(far, -32)] -= 1
        near = (diff + 32) % 64 - 32
        if -16 <= near <= 15:
            bins[4, c, near + 16] += 1
        bins[0, c, 0] += 1
        bins[4, c, 0] -= 1
    bins[5, :, 31] += 1
    bins[5, :, 0] -= 1
    return bins


def fold_table(pairs, ds_a, ds_b, part, parts, after=()):
    count = HEADS // parts
    steps = count // FOLD_HEADS
    head = pl.BlockSpec((FOLD_HEADS, ROWS, KEYS), lambda h: (h + part * steps, 0, 0))
    return pl.pallas_call(
        table_kernel,
        out_shape=jax.ShapeDtypeStruct((count, 8, LANES), f32),
        grid=(steps,),
        in_specs=[full(array) for array in pairs]
        + [head, head]
        + [pl.BlockSpec(memory_space=pl.ANY)] * len(after),
        out_specs=pl.BlockSpec((FOLD_HEADS, 8, LANES), lambda h: (h, 0, 0)),
        compiler_params=pltpu.CompilerParams(vmem_limit_bytes=58 * MIB),
        cost_estimate=brief,
        name="table_grad",
    )(*pairs, ds_a, ds_b, *after)


def visual_kernel(half, grad_ref, normal_low, hat, weight, keep, send, normal_grad, sums):
    rows = normal_low.shape[0]
    column = lambda block: jnp.sum(block, axis=0, keepdims=True)
    token_grad = grad_ref[...].astype(bf16)
    whole = tn_dot(normal_low[...], token_grad)
    mid = whole.shape[0] // 2
    first = half[0] == 0
    keep[...] = jnp.where(first, whole[:mid], whole[mid:]).astype(bf16)
    send[...] = jnp.where(first, whole[mid:], whole[:mid]).astype(bf16)
    place = half[0] * rows + lax.broadcasted_iota(jnp.int32, (rows, 1), 0)
    grad = jnp.where(place < VIS_TOK, nt_dot(token_grad, weight[...]), 0.0)
    normal_grad[...] = grad
    total = column(token_grad.astype(f32))
    put_row(sums, 0, total)
    at = total.shape[1] // LANES
    count = grad.shape[1] // LANES
    put_row(sums.at[at : at + count], 0, column(grad * hat[...]))
    put_row(sums.at[at + count : at + 2 * count], 0, column(grad))


def visual_back(half, gradient, normal_low, hat, weight):
    slots, channels = normal_low.shape
    width = weight.shape[1]
    return pl.pallas_call(
        visual_kernel,
        grid_spec=pltpu.PrefetchScalarGridSpec(
            num_scalar_prefetch=1,
            grid=(1,),
            in_specs=[
                pl.BlockSpec(
                    (slots, width), lambda i, half: (gradient.shape[0] // slots - 1, 0)
                ),
                full(normal_low),
                full(hat),
                full(weight),
            ],
            out_specs=[
                pl.BlockSpec((channels // 2, width), lambda i, half: (0, 0)),
                pl.BlockSpec((channels // 2, width), lambda i, half: (0, 0)),
                pl.BlockSpec((slots, channels), lambda i, half: (0, 0)),
                pl.BlockSpec(((width + 2 * channels) // LANES, LANES), lambda i, half: (0, 0)),
            ],
        ),
        out_shape=[
            jax.ShapeDtypeStruct((channels // 2, width), bf16),
            jax.ShapeDtypeStruct((channels // 2, width), bf16),
            jax.ShapeDtypeStruct((slots, channels), f32),
            jax.ShapeDtypeStruct(((width + 2 * channels) // LANES, LANES), f32),
        ],
        cost_estimate=brief,
        name="visual_back",
    )(half, gradient, normal_low, hat, weight)


def join_kernel(*refs):
    low, out = refs[-2:]
    out[...] = jnp.zeros_like(out)
    at = 0
    for ref in refs[:-2]:
        values = ref[...]
        if len(values.shape) == 3 and values.shape[1] > 1:
            for head in range(values.shape[0]):
                out[at : at + values.shape[1], :] = values[head]
                at += values.shape[1]
        elif len(values.shape) == 3:
            for group in range(values.shape[0]):
                for start in range(0, values.shape[2], LANES):
                    size = min(LANES, values.shape[2] - start)
                    out[at : at + 1, :size] = ref[group, :, start : start + size]
                    at += 1
        else:
            out[at : at + values.shape[0], :] = values
            at += values.shape[0]
    low[...] = out[...].astype(bf16)


def bin_rows(units):
    return -(-units // LANES)


def join(parts):
    rows = 0
    for part in parts:
        if part.ndim == 3 and part.shape[1] == 1:
            rows += part.shape[0] * bin_rows(part.shape[2])
        else:
            rows += part.size // LANES
    rows += -rows % 16
    vmem = pl.BlockSpec(memory_space=pltpu.VMEM)
    return pl.pallas_call(
        join_kernel,
        out_shape=jax.ShapeDtypeStruct((rows, LANES), bf16),
        in_specs=[vmem] * len(parts),
        out_specs=vmem,
        scratch_shapes=[pltpu.VMEM((rows, LANES), f32)],
        cost_estimate=brief,
        name="join",
    )(*parts)


def split_kernel(
    sizes,
    count,
    me,
    left,
    right,
    bins,
    normal_grad,
    hat,
    inverse_std,
    bn_gain,
    attn,
    out_bias,
    gain,
    shift,
    table,
    vis_bias,
    gain_grad,
    shift_grad,
    hidden_bias,
    maps,
    total,
):
    total[...] = left[...].astype(f32) + right[...].astype(f32)
    units = hidden_bias.shape[1]
    width = out_bias.shape[1]
    channels = gain_grad.shape[1]
    starts = [0]
    for size in sizes:
        starts.append(starts[-1] + size)

    def take(start, index, wide):
        per = wide // LANES
        begin = start + index * per
        return jnp.concatenate([total[begin + i : begin + i + 1, :] for i in range(per)], axis=1)

    for layer in range(LAYERS):
        norm = functools.partial(take, starts[layer])
        gain[layer, 1:2, :] = norm(0, width)
        shift[layer, 1:2, :] = norm(1, width)
        out_bias[layer : layer + 1, :] = norm(2, width)
        gain[layer, 0:1, :] = norm(3, width)
        shift[layer, 0:1, :] = norm(4, width)
        attn[2, layer : layer + 1, :] = norm(5, width)
        rows = functools.partial(take, starts[LAYERS + layer])
        attn[0, layer : layer + 1, :] = rows(0, width)
        attn[1, layer : layer + 1, :] = rows(1, width)
        per = bin_rows(units)
        begin = starts[2 * LAYERS + layer] + me[0] * per
        for part in range(per):
            span = min(LANES, units - part * LANES)
            hidden_bias[layer : layer + 1, part * LANES : part * LANES + span] = total[
                pl.ds(begin + part, 1), :span
            ]
    at = starts[3 * LAYERS]
    vis_bias[...] = total[at : at + width // LANES, :]
    at += width // LANES
    by_gain = take(at, 0, channels)
    by_shift = take(at, 1, channels)
    gain_grad[...] = by_gain
    shift_grad[...] = by_shift
    scale = inverse_std[...] * bn_gain[...]
    slots = normal_grad.shape[0]
    place = (me[0] & 1) * slots + lax.broadcasted_iota(jnp.int32, (slots, 1), 0)
    maps[...] = jnp.where(
        place < VIS_TOK,
        scale * (normal_grad[...] - by_shift / count - hat[...] * (by_gain / count)),
        0.0,
    )
    at = starts[3 * LAYERS + 1]
    folded = jnp.zeros((16, BUCKETS), f32)
    for kind in range(8):
        rows = jnp.concatenate(
            [total[at + 8 * head + kind : at + 8 * head + kind + 1, :] for head in range(HEADS)]
            + [jnp.zeros((16 - HEADS, LANES), f32)],
            axis=0,
        )
        high = rows.astype(bf16)
        middle = (rows - high.astype(f32)).astype(bf16)
        low = (rows - high.astype(f32) - middle.astype(f32)).astype(bf16)
        for part in (high, middle, low):
            folded = folded + nt_dot(part, bins[kind])
    table[...] = folded[:HEADS]


def split(me, left, right, sizes, count, normal_grad, hat, inverse_std, bn_gain, units, width):
    slots, channels = normal_grad.shape
    bins = jnp.asarray(table_bins().transpose(0, 2, 1), bf16)
    row = lambda value: value.reshape(1, -1)
    vmem = pl.BlockSpec(memory_space=pltpu.VMEM)
    shape = lambda *size: jax.ShapeDtypeStruct(size, f32)
    return pl.pallas_call(
        functools.partial(split_kernel, sizes, count),
        in_specs=[pl.BlockSpec(memory_space=pltpu.SMEM)] + [vmem] * 7,
        out_specs=[vmem] * 10,
        out_shape=[
            shape(3, LAYERS, width),
            shape(LAYERS, width),
            shape(LAYERS, 2, width),
            shape(LAYERS, 2, width),
            shape(HEADS, BUCKETS),
            shape(width // LANES, LANES),
            shape(1, channels),
            shape(1, channels),
            shape(LAYERS, units),
            shape(slots, channels),
        ],
        scratch_shapes=[pltpu.VMEM(left.shape, f32)],
        cost_estimate=brief,
        name="split",
    )(me, left, right, bins, normal_grad, hat, row(inverse_std), row(bn_gain))


def whole_page(own, other):
    return jnp.concatenate(
        [
            own[:HALF_TEXT],
            other[:HALF_TEXT],
            own[HALF_TEXT:],
            other[HALF_TEXT:],
            jnp.zeros((KEYS - 2 * ROWS, own.shape[1]), own.dtype),
        ],
        axis=0,
    )


def page_split(both):
    mid = 2 * HALF_TEXT
    own = jnp.concatenate([both[:HALF_TEXT], both[mid : mid + HALF_SLOTS]], axis=0)
    other = jnp.concatenate(
        [both[HALF_TEXT:mid], both[mid + HALF_SLOTS : mid + VIS_SLOTS]], axis=0
    )
    return own, other


def nt_dot(left, right):
    return lax.dot_general(left, right, (((1,), (1,)), ((), ())), preferred_element_type=f32)


def tn_dot(left, right):
    return lax.dot_general(left, right, (((0,), (0,)), ((), ())), preferred_element_type=f32)


def put_row(target, index, row):
    count = row.shape[1] // LANES
    for part in range(count):
        at = index * count + part
        target[at : at + 1, :] = row[:, part * LANES : (part + 1) * LANES]


def centred(values):
    center = values - jnp.mean(values, axis=1, keepdims=True)
    spread = jnp.mean(center * center, axis=1, keepdims=True)
    rate = lax.rsqrt(spread + norm_epsilon)
    return center * rate, rate


def norm_back(grad, values, gain_row):
    hat, rate = centred(values)
    scaled = grad * gain_row
    mean = jnp.mean(scaled, axis=1, keepdims=True)
    along = jnp.mean(scaled * hat, axis=1, keepdims=True)
    column = lambda block: jnp.sum(block, axis=0, keepdims=True)
    return rate * (scaled - mean - hat * along), column(grad * hat), column(grad)


def attend_kernel(
    layer,
    q_ref,
    ko,
    kp,
    vo,
    vp,
    bias,
    x_ref,
    weight,
    attn_bias,
    gain,
    shift,
    soft,
    pair,
    residual,
    normed,
    x_s,
    weight_s,
    semaphores,
):
    step = pl.program_id(0)
    later = Later([(x_ref, x_s), (weight.at[layer], weight_s)], semaphores)
    pl.when(step == 0)(later.start)
    first = lax.broadcasted_iota(jnp.int32, (ROWS, LANES), 1) < HEAD_DIM
    for part in range(SLABS):
        lanes = slice(part * LANES, (part + 1) * LANES)
        q = q_ref[:, lanes] * jnp.asarray(HEAD_DIM**-0.5, bf16)
        keys = whole_page(ko[:, lanes], kp[:, lanes])
        values = whole_page(vo[:, lanes], vp[:, lanes])
        found = []
        for head in range(2):
            mine = jnp.where(first if head == 0 else ~first, q, jnp.zeros_like(q))
            scores = nt_dot(mine, keys) + bias[2 * part + head]
            raised = jnp.exp(scores - jnp.max(scores, axis=1, keepdims=True))
            weights = (raised * (1.0 / jnp.sum(raised, axis=1, keepdims=True))).astype(bf16)
            soft[2 * part + head] = weights
            found.append(jnp.dot(weights, values, preferred_element_type=f32))
        slab = pl.ds(pl.multiple_of((step * SLABS + part) * LANES, LANES), LANES)
        pair[0, :, slab] = jnp.where(first, found[0], found[1]).astype(bf16)

    @pl.when(step == STEPS - 1)
    def _():
        later.wait(0, 1)
        attended = jnp.dot(pair[0], weight_s[...], preferred_element_type=f32)
        summed = x_s[...] + (attended + attn_bias[layer, 2:3, :])
        residual[...] = summed
        out = centred(summed)[0] * gain[layer, 0:1, :] + shift[layer, 0:1, :]
        normed[...] = out
        pair[1] = out.astype(bf16)


class Later:
    def __init__(self, pairs, semaphores):
        self.copies = [
            pltpu.make_async_copy(source, target, semaphores.at[index])
            for index, (source, target) in enumerate(pairs)
        ]

    def start(self):
        for copy in self.copies:
            copy.start()

    def wait(self, *indices):
        for index in indices:
            self.copies[index].wait()


anywhere = pl.BlockSpec(memory_space=pl.ANY)


def full(array):
    return pl.BlockSpec(array.shape, lambda *at: (0,) * array.ndim)


def attend(layer, q, kv, other_kv, bias, x, out_weight, attn_bias, gain, shift):
    rows, width = q.shape
    slab = pl.BlockSpec((ROWS, SLABS * LANES), lambda p: (0, p))
    second = pl.BlockSpec((ROWS, SLABS * LANES), lambda p: (0, p + STEPS))
    heads = pl.BlockSpec((2 * SLABS, ROWS, KEYS), lambda p: (p, 0, 0))
    whole = pl.BlockSpec((rows, width), lambda p: (0, 0))
    wide = jax.ShapeDtypeStruct((rows, width), f32)
    low = jax.ShapeDtypeStruct((2, rows, width), bf16)
    return pl.pallas_call(
        functools.partial(attend_kernel, layer),
        grid=(STEPS,),
        in_specs=[
            slab,
            slab,
            slab,
            second,
            second,
            heads,
            anywhere,
            anywhere,
            full(attn_bias),
            full(gain),
            full(shift),
        ],
        out_specs=[
            heads,
            pl.BlockSpec((2, rows, width), lambda p: (0, 0, 0)),
            whole,
            whole,
        ],
        out_shape=[jax.ShapeDtypeStruct((HEADS, ROWS, KEYS), bf16), low, wide, wide],
        scratch_shapes=[
            pltpu.VMEM((rows, width), f32),
            pltpu.VMEM((width, width), bf16),
            pltpu.SemaphoreType.DMA((2,)),
        ],
        compiler_params=pltpu.CompilerParams(vmem_limit_bytes=50 * MIB),
        cost_estimate=brief,
        name="attend",
    )(q, kv, other_kv, kv, other_kv, bias, x, out_weight, attn_bias, gain, shift)


def attend_back_kernel(q_ref, ko, kp, vo, vp, dc_ref, soft, *rest):
    ds, *grads = rest[-6:]
    scale = HEAD_DIM**-0.5
    first = lax.broadcasted_iota(jnp.int32, (ROWS, LANES), 1) < HEAD_DIM
    for part in range(SLABS):
        lanes = slice(part * LANES, (part + 1) * LANES)
        q = q_ref[:, lanes]
        dc = dc_ref[:, lanes]
        keys = whole_page(ko[:, lanes], kp[:, lanes])
        values = whole_page(vo[:, lanes], vp[:, lanes])
        q_turned = jnp.transpose(q.astype(f32), (1, 0)).astype(bf16)
        dc_turned = jnp.transpose(dc.astype(f32), (1, 0)).astype(bf16)
        dq_parts, dk_parts, dv_parts = [], [], []
        for head in range(2):
            span = slice(head * HEAD_DIM, (head + 1) * HEAD_DIM)
            mine = jnp.where(first if head == 0 else ~first, dc, jnp.zeros_like(dc))
            weights = soft[2 * part + head]
            weights_f = weights.astype(f32)
            flow = nt_dot(mine, values)
            share = jnp.sum(weights_f * flow, axis=1, keepdims=True)
            score_grad = (weights_f * (flow - share)).astype(bf16)
            ds[2 * part + head] = score_grad
            dq_parts.append(jnp.dot(score_grad, keys, preferred_element_type=f32))
            dk_parts.append(jnp.dot(q_turned[span], score_grad, preferred_element_type=f32))
            dv_parts.append(jnp.dot(dc_turned[span], weights, preferred_element_type=f32))
        grads[0][:, lanes] = (jnp.where(first, dq_parts[0], dq_parts[1]) * scale).astype(bf16)
        own, other = page_split(jnp.transpose(jnp.concatenate(dk_parts, axis=0) * scale, (1, 0)))
        grads[1][:, lanes] = own.astype(bf16)
        grads[2][:, lanes] = other.astype(bf16)
        own, other = page_split(jnp.transpose(jnp.concatenate(dv_parts, axis=0), (1, 0)))
        grads[3][:, lanes] = own.astype(bf16)
        grads[4][:, lanes] = other.astype(bf16)


def attend_back(q, kv, other_kv, dctx, soft, after=()):
    slab = pl.BlockSpec((ROWS, SLABS * LANES), lambda p: (0, p))
    second = pl.BlockSpec((ROWS, SLABS * LANES), lambda p: (0, p + STEPS))
    heads = pl.BlockSpec((2 * SLABS, ROWS, KEYS), lambda p: (p, 0, 0))
    return pl.pallas_call(
        attend_back_kernel,
        grid=(STEPS,),
        in_specs=[slab, slab, slab, second, second, slab, heads]
        + [pl.BlockSpec(memory_space=pl.ANY)] * len(after),
        out_specs=[heads] + [slab] * 5,
        out_shape=[
            jax.ShapeDtypeStruct((HEADS, ROWS, KEYS), bf16),
        ]
        + [jax.ShapeDtypeStruct(q.shape, bf16)] * 5,
        compiler_params=pltpu.CompilerParams(vmem_limit_bytes=50 * MIB),
        cost_estimate=brief,
        name="attend_back",
    )(q, kv, other_kv, kv, other_kv, dctx, soft, *after)


def ffn_kernel(layer, more, me, x_ref, *refs):
    step = pl.program_id(0)
    width = x_ref.shape[1]
    blocks, (bias, n_ref, out_bias, gain, shift), rest = refs[:BLOCKS], refs[BLOCKS:][:5], refs[BLOCKS + 5 :]
    units = blocks[0].shape[1]
    if more:
        weight, attn_bias, *rest, weight_s, semaphores = rest
        later = Later([(weight.at[layer + 1], weight_s)], semaphores)
        pl.when(step == 0)(later.start)
    own_act, mate_act, slope, residual = rest[:4]
    x = x_ref[...]

    total = None
    for index, block in enumerate(blocks):
        weights = block[0]
        row = bias[pl.ds(me[0] ^ (BLOCKS * step + index), 1), layer, :units]
        hidden = nt_dot(x, weights[:, :width]) + row.astype(f32)
        half_cdf = 0.5 + 0.5 * lax.erf(hidden * 0.5**0.5)
        low = (hidden * half_cdf).astype(bf16)
        (mate_act if index % 2 else own_act)[index // 2] = low
        density = jnp.exp(hidden * hidden * -0.5) * (1.0 / (2.0 * np.pi) ** 0.5)
        slope[index] = (half_cdf + hidden * density).astype(bf16)
        term = jnp.dot(low, weights[:, width:], preferred_element_type=f32)
        total = term if total is None else total + term

    @pl.when(step == 0)
    def _():
        residual[...] = n_ref[...] + out_bias[layer : layer + 1, :] + total

    @pl.when(step > 0)
    def _():
        residual[...] += total

    @pl.when(step == pl.num_programs(0) - 1)
    def _():
        states = centred(residual[...])[0] * gain[layer, 1:2, :] + shift[layer, 1:2, :]
        rounded = states.astype(bf16)
        if more:
            wide, query, shared = rest[-3:]
            wide[...] = states
            later.wait(0)
            project = lambda index: jnp.dot(
                rounded, weight_s[index], preferred_element_type=f32
            )
            query[...] = (project(0) + attn_bias[layer + 1, 0:1, :]).astype(bf16)
            shared[:, :width] = project(1).astype(bf16)
            shared[:, width : 2 * width] = (
                project(2) + attn_bias[layer + 1, 1:2, :]
            ).astype(bf16)
            shared[:, 2 * width :] = rounded
        else:
            rest[-1][...] = rounded


def weight_blocks(layer, units, width):
    pick = lambda which: pl.BlockSpec(
        (1, units, 2 * width), lambda i, me: (me[0] ^ (BLOCKS * i + which), layer, 0)
    )
    return [pick(which) for which in range(BLOCKS)]


def ffn(me, layer, pair, n, gathered, units, out_bias, gain, shift, qkv_weight, attn_bias):
    groups = gathered.shape[0]
    rows, width = n.shape
    more = layer < LAYERS - 1
    whole = pl.BlockSpec((rows, width), lambda i, me: (0, 0))
    kept = pl.BlockSpec((BLOCKS, rows, units), lambda i, me: (i, 0, 0))
    kept_shape = jax.ShapeDtypeStruct((groups, rows, units), bf16)
    wide = jax.ShapeDtypeStruct((rows, width), f32)
    low = jax.ShapeDtypeStruct((rows, width), bf16)
    half_act = pl.BlockSpec((HALF, rows, units), lambda i, me: (i, 0, 0))
    half_shape = jax.ShapeDtypeStruct((groups // 2, rows, units), bf16)
    inputs = [pair] + [gathered] * (BLOCKS + 1) + [n, out_bias, gain, shift]
    in_specs = [
        pl.BlockSpec((None, rows, width), lambda i, me: (1, 0, 0)),
        *weight_blocks(layer, units, width),
        pl.BlockSpec(
            (groups, 16, 2 * width), lambda i, me: (0, LAYERS * units // 16, 0)
        ),
        whole,
        full(out_bias),
        full(gain),
        full(shift),
    ]
    out_specs = [half_act, half_act, kept, whole]
    out_shape = [half_shape, half_shape, kept_shape, wide]
    if more:
        inputs += [qkv_weight, attn_bias]
        in_specs += [
            anywhere,
            full(attn_bias),
        ]
        out_specs += [whole, whole, pl.BlockSpec((rows, 3 * width), lambda i, me: (0, 0))]
        out_shape += [wide, low, jax.ShapeDtypeStruct((rows, 3 * width), bf16)]
    else:
        out_specs += [whole]
        out_shape += [low]
    return pl.pallas_call(
        functools.partial(ffn_kernel, layer, more),
        out_shape=out_shape,
        grid_spec=pltpu.PrefetchScalarGridSpec(
            num_scalar_prefetch=1,
            grid=(groups // BLOCKS,),
            in_specs=in_specs,
            out_specs=out_specs,
            scratch_shapes=[
                pltpu.VMEM((3, width, width), bf16),
                pltpu.SemaphoreType.DMA((1,)),
            ]
            if more
            else [],
        ),
        compiler_params=pltpu.CompilerParams(vmem_limit_bytes=50 * MIB),
        cost_estimate=brief,
        name="feed_forward",
    )(me, *inputs)


def ffn_back_kernel(layer, me, grad_ref, r2_ref, r1_ref, *refs):
    blocks, (slope, gain, out_weight), rest = refs[:BLOCKS], refs[BLOCKS:][:3], refs[BLOCKS + 3 :]
    own_dh, mate_dh, low_grads, bias_grad, sums, dx, dctx, total_s, r1_s, weight_s, semaphores = rest
    later = Later([(r1_ref, r1_s), (out_weight.at[layer], weight_s)], semaphores)
    step = pl.program_id(0)
    width = r2_ref.shape[1]
    column = lambda block: jnp.sum(block, axis=0, keepdims=True)

    @pl.when(step == 0)
    def _():
        later.start()
        grad, gain_grad, shift_grad = norm_back(
            grad_ref[...].astype(f32), r2_ref[...], gain[layer, 1:2, :]
        )
        low = grad.astype(bf16)
        total_s[...] = grad
        low_grads[0] = low
        put_row(sums, 0, gain_grad)
        put_row(sums, 1, shift_grad)
        put_row(sums, 2, column(low.astype(f32)))

    dy = low_grads[0]
    total = None
    for index, block in enumerate(blocks):
        weights = block[0]
        flow = nt_dot(dy, weights[:, width:])
        grad = (flow * slope[index].astype(f32)).astype(bf16)
        (mate_dh if index % 2 else own_dh)[index // 2] = grad
        bias_grad[index ^ (me[0] & (BLOCKS - 1))] = column(grad.astype(f32))
        term = jnp.dot(grad, weights[:, :width], preferred_element_type=f32)
        total = term if total is None else total + term
    total_s[...] += total

    @pl.when(step == pl.num_programs(0) - 1)
    def _():
        later.wait(0, 1)
        grad, gain_grad, shift_grad = norm_back(total_s[...], r1_s[...], gain[layer, 0:1, :])
        low = grad.astype(bf16)
        dx[...] = grad
        low_grads[1] = low
        dctx[...] = nt_dot(low, weight_s[...]).astype(bf16)
        put_row(sums, 3, gain_grad)
        put_row(sums, 4, shift_grad)
        put_row(sums, 5, column(low.astype(f32)))


def ffn_back(me, layer, grad, r2, r1, gathered, slope, gain, out_weight):
    groups, rows, units = slope.shape
    width = r2.shape[1]
    whole = pl.BlockSpec((rows, width), lambda i, me: (0, 0))
    half = pl.BlockSpec((HALF, rows, units), lambda i, me: (i, 0, 0))
    half_shape = jax.ShapeDtypeStruct((groups // 2, rows, units), bf16)
    return pl.pallas_call(
        functools.partial(ffn_back_kernel, layer),
        out_shape=[
            half_shape,
            half_shape,
            jax.ShapeDtypeStruct((2, rows, width), bf16),
            jax.ShapeDtypeStruct((groups, 1, units), f32),
            jax.ShapeDtypeStruct((6 * width // LANES, LANES), f32),
            jax.ShapeDtypeStruct((rows, width), f32),
            jax.ShapeDtypeStruct((rows, width), bf16),
        ],
        grid_spec=pltpu.PrefetchScalarGridSpec(
            num_scalar_prefetch=1,
            grid=(groups // BLOCKS,),
            in_specs=[
                whole,
                whole,
                anywhere,
                *weight_blocks(layer, units, width),
                pl.BlockSpec((BLOCKS, rows, units), lambda i, me: (i, 0, 0)),
                full(gain),
                anywhere,
            ],
            out_specs=[
                half,
                half,
                pl.BlockSpec((2, rows, width), lambda i, me: (0, 0, 0)),
                pl.BlockSpec((BLOCKS, 1, units), lambda i, me: (me[0] // BLOCKS ^ i, 0, 0)),
                pl.BlockSpec((6 * width // LANES, LANES), lambda i, me: (0, 0)),
                whole,
                whole,
            ],
            scratch_shapes=[
                pltpu.VMEM((rows, width), f32),
                pltpu.VMEM((rows, width), f32),
                pltpu.VMEM((width, width), bf16),
                pltpu.SemaphoreType.DMA((2,)),
            ],
        ),
        compiler_params=pltpu.CompilerParams(vmem_limit_bytes=50 * MIB),
        cost_estimate=brief,
        name="feed_forward_back",
    )(me, grad, r2, r1, *[gathered] * BLOCKS, slope, gain, out_weight)


def ffn_grads_kernel(me, n, n_mate, dy, dy_mate, dh, dh_mate, act, act_mate, *rest):
    near_keep, near_send, seq_keep, seq_send, n_s, dy_s = rest[-6:]
    rows, width = n.shape
    far, units = near_keep.shape[:2]
    step = pl.program_id(0)

    @pl.when(step == 0)
    def _():
        for target, own, mate in ((n_s, n, n_mate), (dy_s, dy, dy_mate)):
            target[:rows] = own[...]
            target[rows:] = mate[...]

    def product(own, mate, right):
        turned = [
            jnp.transpose(jnp.concatenate([own[i, 0], mate[i, 0]], axis=0), (1, 0))
            for i in range(far)
        ]
        return jnp.dot(
            jnp.concatenate(turned, axis=0), right[...], preferred_element_type=f32
        ).astype(bf16)

    def put(target, values):
        for i in range(far):
            target[(me[0] >> 2) ^ i] = values[i * units : (i + 1) * units]

    into = product(dh, dh_mate, n_s)
    pl.when(step == 0)(lambda: put(near_keep, into))
    pl.when(step == 1)(lambda: put(near_send, into))
    out = product(act, act_mate, dy_s)
    turn = me[1] % 2 == 0
    put(seq_keep, jnp.where(turn, out[:, : width // 2], out[:, width // 2 :]))
    put(seq_send, jnp.where(turn, out[:, width // 2 :], out[:, : width // 2]))


def ffn_grads(me, pair, pair_mate, low_grads, low_grads_mate, dh, dh_mate, act, act_mate):
    groups, rows, units = dh.shape
    width = pair.shape[2]
    far = groups // 2
    row_block = lambda which: pl.BlockSpec((None, rows, width), lambda i, me: (which, 0, 0))
    hidden = pl.BlockSpec((far, 1, rows, units), lambda i, me: (0, i, 0, 0))
    near_shape = jax.ShapeDtypeStruct((far, units, width), bf16)
    near_block = pl.BlockSpec((far, units, width), lambda i, me: (0, 0, 0))
    seq_shape = jax.ShapeDtypeStruct((groups, units, width // 2), bf16)
    seq_block = pl.BlockSpec((far, units, width // 2), lambda i, me: (i, 0, 0))
    by_far = lambda block: block.reshape(far, 2, rows, units)
    return pl.pallas_call(
        ffn_grads_kernel,
        out_shape=[near_shape, near_shape, seq_shape, seq_shape],
        grid_spec=pltpu.PrefetchScalarGridSpec(
            num_scalar_prefetch=1,
            grid=(2,),
            in_specs=[row_block(1), row_block(1), row_block(0), row_block(0)] + [hidden] * 4,
            out_specs=[near_block, near_block, seq_block, seq_block],
            scratch_shapes=[pltpu.VMEM((2 * rows, width), bf16)] * 2,
        ),
        compiler_params=pltpu.CompilerParams(vmem_limit_bytes=50 * MIB),
        cost_estimate=brief,
        name="feed_forward_grads",
    )(
        me,
        pair,
        pair_mate,
        low_grads,
        low_grads_mate,
        *[by_far(block) for block in (dh, dh_mate, act, act_mate)],
    )


def projection_kernel(by_distance, me, x, x_mate, ctx, ctx_mate, *refs):
    own, mate, refs = refs[:5], refs[5:10], refs[10:]
    da, da_mate, dr_ref, weight = refs[:4]
    near_keep, near_send, seq_keep, seq_send, dx, sums = refs[-11:-5]
    turned_s, picked_s, left_s, right_s, shards_s = refs[-5:]
    step = pl.program_id(0)
    far, shard = near_keep.shape[:2]
    rows, width = x.shape
    column = lambda block: jnp.sum(block.astype(f32), axis=0, keepdims=True)

    def place_of(place, near):
        far_place = (me[0] >> 2) ^ place if by_distance else place
        return far_place * 4 + ((me[0] & 3) ^ (2 * near))

    gap = -rows % LANES
    mate_rows = slice(rows + gap, 2 * rows + gap)

    def pick_left(first, second):
        for block, at_rows in ((first, slice(0, rows)), (second, mate_rows)):
            turned_s[...] = jnp.transpose(block[...].astype(f32), (1, 0))
            for near in range(2):
                for place in range(far):
                    start = pl.multiple_of(place_of(place, near) * shard, 8)
                    at = (near * far + place) * shard
                    picked_s[at : at + shard, at_rows] = turned_s[pl.ds(start, shard), :]
        left_s[...] = picked_s[...].astype(bf16)

    @pl.when(step == 0)
    def _():
        dx[...] = dr_ref[...]
        picked_s[:, rows : rows + gap] = jnp.zeros((width // 2, gap), f32)
        right_s[rows : rows + gap] = jnp.zeros((gap, width), bf16)
        pick_left(x, x_mate)
        right_s[:rows] = own[0][...]
        right_s[mate_rows] = mate[0][...]
        put_row(sums, 0, column(own[0][...]))

    for index in (1, 2):

        @pl.when(step == index)
        def _():
            right_s[:rows] = add_low(own[2 * index - 1][...], mate[2 * index][...])
            right_s[mate_rows] = add_low(mate[2 * index - 1][...], own[2 * index][...])

    @pl.when(step == 2)
    def _():
        put_row(sums, 1, column(right_s[:rows]))

    @pl.when(step < 3)
    def _():
        dx[...] += nt_dot(right_s[:rows], weight[0, 0])

    @pl.when(step == 3)
    def _():
        pick_left(ctx, ctx_mate)
        right_s[:rows] = da[...]
        right_s[mate_rows] = da_mate[...]

    shards_s[...] = jnp.dot(left_s[...], right_s[...], preferred_element_type=f32)

    def put(target, first, near, columns):
        for place in range(far):
            at = (near * far + place) * shard
            target[first + place, :, columns] = shards_s[at : at + shard, :].astype(bf16)

    for index in range(2):

        @pl.when(step == index)
        def _():
            columns = slice(index * width, (index + 1) * width)
            put(near_keep, 0, 0, columns)
            put(near_send, 0, 1, columns)

    def put_seq(target):
        put(target, 0, 0, slice(None))
        put(target, far, 1, slice(None))

    mine = step - 2 == me[1] % 2
    pl.when((step >= 2) & mine)(lambda: put_seq(seq_keep))
    pl.when((step >= 2) & jnp.logical_not(mine))(lambda: put_seq(seq_send))


def projection_grads(
    by_distance,
    me,
    layer,
    shared,
    shared_mate,
    pair,
    pair_mate,
    own,
    mate,
    low,
    low_mate,
    dr,
    weight,
    after=(),
):
    rows, width = dr.shape
    groups = lax.axis_size("tp")
    shard = width // groups
    whole = pl.BlockSpec((rows, width), lambda t, me: (0, 0))
    x_block = pl.BlockSpec((rows, width), lambda t, me: (0, 2))
    layered = lambda which: pl.BlockSpec((None, rows, width), lambda t, me: (which, 0, 0))
    near_shape = jax.ShapeDtypeStruct((groups // 4, shard, 2 * width), bf16)
    near_block = pl.BlockSpec(near_shape.shape, lambda t, me: (0, 0, 0))
    seq_shape = jax.ShapeDtypeStruct((groups // 2, shard, width), bf16)
    seq_block = pl.BlockSpec(seq_shape.shape, lambda t, me: (0, 0, 0))
    return pl.pallas_call(
        functools.partial(projection_kernel, by_distance),
        out_shape=[near_shape, near_shape, seq_shape, seq_shape]
        + [
            jax.ShapeDtypeStruct((rows, width), f32),
            jax.ShapeDtypeStruct((2 * width // LANES, LANES), f32),
        ],
        grid_spec=pltpu.PrefetchScalarGridSpec(
            num_scalar_prefetch=1,
            grid=(4,),
            in_specs=[
                x_block,
                x_block,
                layered(0),
                layered(0),
                *[whole] * 10,
                layered(1),
                layered(1),
                whole,
                pl.BlockSpec(
                    (1, 1, width, width), lambda t, me: (layer, jnp.minimum(t, 2), 0, 0)
                ),
            ]
            + [pl.BlockSpec(memory_space=pl.ANY)] * len(after),
            out_specs=[near_block, near_block, seq_block, seq_block]
            + [
                whole,
                pl.BlockSpec((2 * width // LANES, LANES), lambda t, me: (0, 0)),
            ],
            scratch_shapes=[
                pltpu.VMEM((width, rows), f32),
                pltpu.VMEM((width // 2, 2 * rows + -rows % LANES), f32),
                pltpu.VMEM((width // 2, 2 * rows + -rows % LANES), bf16),
                pltpu.VMEM((2 * rows + -rows % LANES, width), bf16),
                pltpu.VMEM((width // 2, width), f32),
            ],
        ),
        compiler_params=pltpu.CompilerParams(vmem_limit_bytes=50 * MIB),
        cost_estimate=brief,
        name="projection_grads",
    )(
        me,
        shared,
        shared_mate,
        pair,
        pair_mate,
        *own,
        *mate,
        low,
        low_mate,
        dr,
        weight,
        *after,
    )


def ordered(turn, mine, other):
    return jnp.where(turn, mine, other), jnp.where(turn, other, mine)


def stacked_parts(block, start, rows, count):
    return jnp.concatenate(
        [block[start + i * rows : start + (i + 1) * rows] for i in range(count)], axis=1
    )


def projection_out_kernel(starts, me, *refs):
    qkv, out = refs[-2:]
    rows, width = out.shape[1:]
    for layer in range(LAYERS):
        mine, other = refs[2 * layer : 2 * layer + 2]
        count = width // mine.shape[1]
        first, second = ordered(me[1] % 2 == 0, mine[...], other[...])
        take = lambda block, part: stacked_parts(
            block, starts[layer] + part * rows * count, rows, count
        ).astype(f32)
        qkv[layer, 0] = take(first, 0)
        qkv[layer, 1] = take(second, 0)
        qkv[layer, 2] = take(first, 1)
        out[layer] = take(second, 1)


def ffn_out_kernel(me, *refs):
    into, out = refs[-2:]
    units, width = out.shape[1:]
    for layer in range(LAYERS):
        mine, other = refs[2 * layer : 2 * layer + 2]
        for index, part in enumerate(ordered(me[1] % 2 == 0, mine[...], other[...])):
            columns = slice(index * (width // 2), (index + 1) * (width // 2))
            into[layer, :, columns] = part[:units].astype(f32)
            out[layer, :, columns] = part[units : 2 * units].astype(f32)


def write_out(kernel, name, me, parts, shapes):
    vmem = pl.BlockSpec(memory_space=pltpu.VMEM)
    return pl.pallas_call(
        kernel,
        in_specs=[pl.BlockSpec(memory_space=pltpu.SMEM)] + [vmem] * len(parts),
        out_specs=[vmem] * len(shapes),
        out_shape=[jax.ShapeDtypeStruct(shape, f32) for shape in shapes],
        compiler_params=pltpu.CompilerParams(vmem_limit_bytes=24 * MIB),
        cost_estimate=brief,
        name=name,
    )(me, *parts)


def body(
    text_states,
    visual_maps,
    text_boxes,
    text_lengths,
    qkv_weight,
    out_weight,
    attn_bias,
    ffn_in,
    ffn_in_bias,
    ffn_out,
    ffn_out_bias,
    norm_gain,
    norm_shift,
    bias_table,
    vis_weight,
    vis_bias,
    bn_gain,
    bn_shift,
    cotangent,
):
    tp_index = lax.axis_index("tp")
    tp_size = lax.axis_size("tp")
    half = tp_index % 2
    page = (lax.axis_index("seq") * tp_size + tp_index) // 2
    me = jnp.stack([tp_index, lax.axis_index("seq")]).astype(jnp.int32)
    units = ffn_in.shape[1]
    width = text_states.shape[1]
    text_rows = text_states.shape[0]

    bias_rows = jnp.pad(ffn_in_bias, ((0, 16 - LAYERS), (0, 2 * width - units)))
    packed = jnp.concatenate(
        [
            jnp.concatenate([ffn_in, ffn_out], axis=2).reshape(LAYERS * units, 2 * width),
            bias_rows,
        ],
        axis=0,
    )
    gathered = lax.all_gather(packed, "tp", axis=0)

    other_boxes = flipped(text_boxes, "tp", 0)
    length = lax.dynamic_index_in_dim(text_lengths, page, 0, keepdims=False)
    facts = jnp.stack([half.astype(jnp.int32), length])
    score_bias = make_bias(facts, text_boxes, other_boxes, bias_table)

    count_cells = text_lengths.shape[0] * VIS_TOK
    maps_float = visual_maps.astype(f32)
    slot_place = half * HALF_SLOTS + jnp.arange(HALF_SLOTS, dtype=jnp.int32)
    slot_mask = (slot_place < VIS_TOK)[:, None]
    masked_maps = jnp.where(slot_mask, maps_float, 0.0)
    sums = total_over_all(
        jnp.stack([jnp.sum(masked_maps, axis=0), jnp.sum(masked_maps * masked_maps, axis=0)])
    )
    channel_mean = sums[0] / count_cells
    inverse_std = lax.rsqrt(sums[1] / count_cells - channel_mean * channel_mean + norm_epsilon)
    centered_hat = jnp.where(slot_mask, (maps_float - channel_mean) * inverse_std, 0.0)
    normal_low = jnp.where(slot_mask, centered_hat * bn_gain + bn_shift, 0.0).astype(bf16)
    visual_tokens = jnp.dot(normal_low, vis_weight, preferred_element_type=f32) + vis_bias
    states = jnp.concatenate([text_states.astype(f32), visual_tokens], axis=0)

    rounded = states.astype(bf16)
    project = lambda index: jnp.dot(rounded, qkv_weight[0, index], preferred_element_type=f32)
    shared = jnp.concatenate(
        [project(1).astype(bf16), (project(2) + attn_bias[0, 1]).astype(bf16), rounded], axis=1
    )
    query = (project(0) + attn_bias[0, 0]).astype(bf16)
    saved = []
    for layer in range(LAYERS):
        shared_mate = flipped(shared, "tp", 0)
        parts = (query, shared, shared_mate)
        soft, pair, residual_one, normed = attend(
            layer, *parts, score_bias, states, out_weight, attn_bias, norm_gain, norm_shift
        )
        if layer == 0:
            pairs = page_pairs(facts, text_boxes, other_boxes)
            normed, *pairs = tied((normed, *pairs), ())
        act, act_send, slope, residual_two, *onwards = ffn(
            me,
            layer,
            pair,
            normed,
            gathered,
            units,
            ffn_out_bias,
            norm_gain,
            norm_shift,
            qkv_weight,
            attn_bias,
        )
        mates = (flipped(pair, "tp", 0), flipped(act_send, "tp", 0))
        saved.append((parts, soft, pair, residual_one, residual_two, act, slope, mates))
        if layer < LAYERS - 1:
            states, query, shared = onwards
    out_states = onwards[0]

    gradient = cotangent
    norm_sums = [None] * LAYERS
    projection_rows = [None] * LAYERS
    bin_grads = [None] * LAYERS
    score_grads = [None] * LAYERS
    projections = [None] * LAYERS
    ffns = [None] * LAYERS
    for layer in reversed(range(LAYERS)):
        last = layer == LAYERS - 1
        parts, soft, pair, residual_one, residual_two, act, slope, mates = saved[layer]
        dh, dh_send, low, bin_grads[layer], norm_sums[layer], grad_one, context_grad = ffn_back(
            me, layer, gradient, residual_two, residual_one, gathered, slope, norm_gain, out_weight
        )
        if not last:
            context_grad, dh_send = tied((context_grad, dh_send), ffns[-1].underway())
            ffns[-1].second(context_grad)
        dh_mate, low_mate = flipped(dh_send, "tp", 0), flipped(low, "tp", 0)
        score_grads[layer], *grads = attend_back(*parts, context_grad, soft)
        (dh, dh_mate, low_mate, pair_mate, act_mate), grads = (
            tied((dh, dh_mate, low_mate, *mates), grads[:1]),
            tied(grads, (dh_mate, low_mate, *mates)),
        )
        grads_mate = [flipped(part, "tp", 0) for part in grads]
        weights = ffn_grads(me, pair, pair_mate, low, low_mate, dh, dh_mate, act, act_mate)
        if not last:
            weights = tied(weights, projections[-1].underway() + ffns[-1].underway())
            projections[-1].second(weights[0])
            upper = Scattered([ffns[-1]], weights[0])
        ffns[layer] = Shards(*weights)
        *weights, gradient, projection_rows[layer] = projection_grads(
            not last,
            me,
            layer,
            parts[1],
            parts[2],
            pair,
            mates[0],
            grads,
            grads_mate,
            low,
            low_mate,
            grad_one,
            qkv_weight,
        )
        if last:
            projections[layer] = Shards(*weights)

    half_at = me[:1] % 2
    vis_keep, vis_send, normal_grad, vis_rows = visual_back(
        half_at, gradient, normal_low, centered_hat, vis_weight
    )
    vis_came = flipped(vis_send, "tp", 0)
    seq_ways = [("seq", bit) for bit in range(mesh_bits("seq"))]
    far_ways = [("tp", bit) for bit in range(2, mesh_bits("tp"))]
    vis_ways = far_ways + [("tp", 1)] + seq_ways
    vis_sums = Tree(add_low(vis_keep, vis_came), vis_ways, join=("tp", 0))
    vis_sums.step()
    fold = functools.partial(fold_table, pairs, *score_grads, parts=FOLDS)
    folds = [fold(0, after=vis_sums.lefts)]
    folds[0], *weights = tied(
        (folds[0], *weights),
        ffns[0].underway() + projections[-1].underway() + vis_sums.rights + [upper.shard],
    )
    ffns[0].second(folds[0])
    projections[0] = Shards(*weights)
    vis_sums.step(folds[0])
    folds.append(fold(1, after=folds + vis_sums.lefts))
    (folds[1],) = tied(folds[1:], ffns[0].underway() + vis_sums.rights)
    lower = Scattered([ffns[0], projections[-1]], folds[1])
    vis_sums.step(folds[1])
    small = join(norm_sums + projection_rows + bin_grads + [vis_rows, *folds])
    sizes = [part.shape[0] for part in norm_sums + projection_rows]
    sizes += [tp_size * bin_rows(units)] * LAYERS + [vis_rows.shape[0]]
    small_ways = [("tp", 0), ("tp", 1)] + seq_ways + far_ways
    small_sums = Tree(small, small_ways)
    small_sums.step()
    small_sums.step(*projections[0].underway())
    behind = small_sums.lefts[0]
    projections[0].second(behind)
    small_sums.step(*projections[0].underway(), *vis_sums.rights)
    behind = small_sums.lefts[0]
    projections[0].halve(behind)
    vis_sums.step(behind)
    upper.join(behind)
    small_sums.step(*vis_sums.rights, upper.other)
    behind = small_sums.lefts[0]
    for _ in range(mesh_bits("tp") - 3):
        projections[0].halve_more(behind)
    while vis_sums.steps:
        vis_sums.step(behind)
    lower.join(behind)
    while small_sums.steps:
        small_sums.step(lower.shard)
    behind = small_sums.lefts[0]
    projections[0].halve_more(behind)
    projections[0].join()
    small, small_came = small_sums.result()
    vis_sum, vis_mate = vis_sums.result()
    vis_weight_grad = jnp.concatenate(
        [
            jnp.where(half == 0, vis_sum, vis_mate),
            jnp.where(half == 0, vis_mate, vis_sum),
        ],
        axis=0,
    ).astype(f32)
    grad_text = gradient[:text_rows]
    attn_total, bout_total, gain_total, shift_total, table_total, visb_total, *rest = split(
        me,
        small,
        small_came,
        sizes,
        count_cells,
        normal_grad,
        centered_hat,
        inverse_std,
        bn_gain,
        units,
        width,
    )
    bn_gain_grad, bn_shift_grad, bin_total, grad_maps = rest
    shard = width // tp_size
    qkv_total, out_total = write_out(
        functools.partial(projection_out_kernel, (0, 2 * units)),
        "projections_out",
        me,
        [part for sums in (projections[0], lower) for part in (sums.shard, sums.other)],
        [(LAYERS, 3, shard, width), (LAYERS, shard, width)],
    )
    in_total, down_total = write_out(
        ffn_out_kernel,
        "feed_forward_out",
        me,
        [part for sums in (lower, upper) for part in (sums.shard, sums.other)],
        [(LAYERS, units, width)] * 2,
    )
    return (
        out_states,
        grad_text,
        grad_maps,
        qkv_total,
        out_total,
        attn_total.transpose(1, 0, 2),
        in_total,
        bin_total,
        down_total,
        bout_total,
        gain_total,
        shift_total,
        table_total.T,
        vis_weight_grad,
        visb_total.reshape(-1),
        bn_gain_grad[0],
        bn_shift_grad[0],
    )


def solution(mesh):
    rows = P(("seq", "tp"), None)
    units = P(None, "tp", None)
    return jax.shard_map(
        body,
        mesh=mesh,
        in_specs=(
            rows,
            rows,
            P(None, ("seq", "tp")),
            P(),
            P(),
            P(),
            P(),
            units,
            P(None, "tp"),
            units,
            P(),
            P(),
            P(),
            P(),
            P(),
            P(),
            P(),
            P(),
            rows,
        ),
        out_specs=(
            rows,
            rows,
            rows,
            P(None, None, "tp", None),
            units,
            P(),
            units,
            P(None, "tp"),
            units,
            P(),
            P(),
            P(),
            P(),
            P(),
            P(),
            P(),
            P(),
        ),
        check_vma=False,
    )
```

```python
import functools

import jax
import jax.numpy as jnp
import numpy as np
from jax import lax
from jax.experimental import pallas as pl
from jax.experimental.pallas import tpu as pltpu
from jax.sharding import PartitionSpec as P

HEADS = 12
HEAD_DIM = 64
VIS_TOK = 49
VIS_SLOTS = 64
POS_BINS = 32
BOX_BINS = 64
LAYERS = 2
BUCKETS = POS_BINS + 2 * BOX_BINS

HALF_TEXT = 256
HALF_SLOTS = VIS_SLOTS // 2
ROWS = HALF_TEXT + HALF_SLOTS
KEYS = 640
PAIRS = HEADS // 2
SLABS = 2
STEPS = PAIRS // SLABS
LANES = 128
FOLDS = 2
FOLD_HEADS = 2
BLOCKS = 4
HALF = BLOCKS // 2
norm_epsilon = 1e-05
NEVER = -1e30
bf16 = jnp.bfloat16
f32 = jnp.float32
MIB = 1 << 20
brief = pl.CostEstimate(flops=1, bytes_accessed=1, transcendentals=0)


def mesh_bits(axis):
    return (lax.axis_size(axis) - 1).bit_length()


def flipped(block, axis, bit):
    count = lax.axis_size(axis)
    return lax.ppermute(block, axis, [(i, i ^ (1 << bit)) for i in range(count)])


def total_over_all(value):
    for axis in ("tp", "seq"):
        for bit in range(mesh_bits(axis)):
            value = value + flipped(value, axis, bit)
    return value


def add_low(left, right):
    return (left.astype(f32) + right.astype(f32)).astype(bf16)


def tied(values, after):
    return lax.optimization_barrier((tuple(values), tuple(after)))[0]


class Shards:
    def __init__(self, near_keep, near_send, seq_keep, seq_send):
        self.near = near_keep
        self.seq = seq_keep
        self.near_came = flipped(near_send, "tp", 1)
        self.seq_came = flipped(seq_send, "seq", 0)

    def underway(self):
        return [self.near_came, self.seq_came]

    def second(self, *after):
        near, near_came, seq, seq_came = tied(
            (self.near, self.near_came, self.seq, self.seq_came), after
        )
        turn = lax.axis_index("seq") % 2
        middle = near.shape[-1] // 2
        pick = lambda block, which: jnp.where(
            turn == which, block[..., :middle], block[..., middle:]
        )
        self.near = add_low(pick(near, 0), pick(near_came, 0))
        self.near_came = flipped(add_low(pick(near, 1), pick(near_came, 1)), "seq", 0)
        far = seq.shape[0] // 2
        self.seq = add_low(seq[:far], seq_came[:far])
        self.seq_came = flipped(add_low(seq[far:], seq_came[far:]), "tp", 1)

    def arrived(self, *after):
        near, near_came, seq, seq_came = tied(
            (self.near, self.near_came, self.seq, self.seq_came), after
        )
        return add_low(near, near_came), add_low(seq, seq_came)

    def halve(self, *after):
        near, near_came, seq, seq_came = tied(
            (self.near, self.near_came, self.seq, self.seq_came), after
        )
        bit = mesh_bits("tp") - (near.shape[0] - 1).bit_length()
        pick = lambda block, which: block.reshape((-1, 2) + block.shape[1:])[:, which]
        add = lambda which: jnp.concatenate(
            [
                add_low(pick(near, which), pick(near_came, which)),
                add_low(pick(seq, which), pick(seq_came, which)),
            ],
            axis=1,
        )
        self.shard, self.came = add(0), flipped(add(1), "tp", bit)
        self.bit = bit + 1

    def halve_more(self, *after):
        shard, came = tied((self.shard, self.came), after)
        if shard.shape[0] == 1:
            self.shard = add_low(shard, came)[0]
            return
        pick = lambda block, which: block.reshape((-1, 2) + block.shape[1:])[:, which]
        self.shard = add_low(pick(shard, 0), pick(came, 0))
        self.came = flipped(add_low(pick(shard, 1), pick(came, 1)), "tp", self.bit)
        self.bit += 1

    def join(self, *after):
        (shard,) = tied((self.shard,), after)
        for bit in range(1, mesh_bits("seq")):
            shard = add_low(shard, flipped(shard, "seq", bit))
        self.shard = shard
        self.other = flipped(shard, "seq", 0)


class Scattered:
    def __init__(self, group, *after):
        parts = [part for shards in group for part in shards.arrived(*after)]
        columns = min(part.shape[-1] for part in parts)
        pieces = [
            part[..., start : start + columns]
            for part in parts
            for start in range(0, part.shape[-1], columns)
        ]
        count = lax.axis_size("tp")
        groups = [list(range(first, count, 4)) for first in range(4)]
        self.shard = lax.psum_scatter(
            jnp.concatenate(pieces, axis=1), "tp", scatter_dimension=0, axis_index_groups=groups
        )

    def join(self, *after):
        (shard,) = tied((self.shard,), after)
        for bit in range(1, mesh_bits("seq")):
            shard = add_low(shard, flipped(shard, "seq", bit))
        self.shard = shard
        self.other = flipped(shard, "seq", 0)


class Tree:
    def __init__(self, value, ways, join=None, add=add_low):
        self.lefts = [value]
        self.rights = []
        self.steps = list(ways) + ([join] if join else [])
        self.add = add

    def step(self, *after):
        if after:
            both = tied(self.lefts + self.rights, after)
            self.lefts, self.rights = list(both[:1]), list(both[1:])
        if self.rights:
            self.lefts = [self.add(self.lefts[0], self.rights[0])]
        self.rights = [flipped(self.lefts[0], *self.steps.pop(0))]

    def result(self):
        return self.lefts[0], self.rights[0]


def page_places(half, length, own_boxes, other_boxes):
    def slots(width, first, second):
        lane = lax.broadcasted_iota(jnp.int32, (1, width), 1)
        place = jnp.where(lane < HALF_SLOTS, first + lane, second + lane - HALF_SLOTS)
        place = jnp.where(lane < VIS_SLOTS, place, VIS_SLOTS - 1)
        row = (place * 37) >> 8
        return place, 71 + 143 * (place - 7 * row), 71 + 143 * row

    text = lax.broadcasted_iota(jnp.int32, (1, HALF_TEXT), 1)
    own_text = half * HALF_TEXT + text
    other_text = (1 - half) * HALF_TEXT + text
    slot = slots(LANES, half * HALF_SLOTS, (1 - half) * HALF_SLOTS)
    lane = lax.broadcasted_iota(jnp.int32, (1, LANES), 1)
    slot_used = jnp.where((slot[0] < VIS_TOK) & (lane < VIS_SLOTS), 1, 0)
    keys = (
        jnp.concatenate([own_text, other_text, slot[0]], axis=1),
        jnp.concatenate([own_boxes[0:1], other_boxes[0:1], slot[1]], axis=1),
        jnp.concatenate([own_boxes[1:2], other_boxes[1:2], slot[2]], axis=1),
        jnp.concatenate(
            [
                jnp.where(own_text < length, 1, 0),
                jnp.where(other_text < length, 1, 0),
                slot_used,
            ],
            axis=1,
        ),
    )
    queries = (
        jnp.concatenate([own_text, slot[0]], axis=1),
        jnp.concatenate([own_boxes[0:1], slot[1]], axis=1),
        jnp.concatenate([own_boxes[1:2], slot[2]], axis=1),
    )
    return keys, queries


def as_columns(rows):
    stacked = jnp.concatenate(list(rows) + [rows[0]] * (8 - len(rows)), axis=0)
    turned = jnp.transpose(stacked.astype(f32), (1, 0)).astype(jnp.int32)
    return [turned[:ROWS, i : i + 1] for i in range(len(rows))]


def bias_kernel(facts, own_boxes, other_boxes, table_a, table_b, out, near_s, across_s, down_s):
    @pl.when(pl.program_id(0) == 0)
    def _():
        keys, queries = page_places(facts[0], facts[1], own_boxes[...], other_boxes[...])
        place, x, y = as_columns(queries)
        near_s[...] = jnp.clip(keys[0] - place, -16, 15) + 16
        across_s[...] = jnp.clip((keys[1] - x) >> 4, -32, 31) + 64
        down_s[...] = jnp.where(
            keys[3] > 0, jnp.clip((keys[2] - y) >> 4, -32, 31) + 32, BOX_BINS
        )

    a = jnp.broadcast_to(table_a[0, 0:1, :], (ROWS, LANES))
    b = jnp.broadcast_to(table_b[0, 0:1, :], (ROWS, LANES))
    for tile in range(KEYS // LANES):
        span = slice(tile * LANES, (tile + 1) * LANES)

        def look(table, codes):
            return jnp.take_along_axis(table, codes, axis=1, mode="promise_in_bounds")

        out[0, :, span] = (
            look(a, near_s[:, span]) + look(a, across_s[:, span]) + look(b, down_s[:, span])
        )


def make_bias(facts, own_boxes, other_boxes, bias_table):
    columns = bias_table.T
    table_a = jnp.pad(columns[:, : POS_BINS + BOX_BINS], ((0, 0), (0, LANES - POS_BINS - BOX_BINS)))
    table_b = jnp.pad(
        columns[:, POS_BINS + BOX_BINS :],
        ((0, 0), (0, LANES - BOX_BINS)),
        constant_values=NEVER,
    )
    spread = lambda t: jnp.broadcast_to(t[:, None, :], (HEADS, 8, LANES))
    whole = lambda h, facts: (0, 0)
    return pl.pallas_call(
        bias_kernel,
        out_shape=jax.ShapeDtypeStruct((HEADS, ROWS, KEYS), f32),
        grid_spec=pltpu.PrefetchScalarGridSpec(
            num_scalar_prefetch=1,
            grid=(HEADS,),
            in_specs=[
                pl.BlockSpec((2, HALF_TEXT), whole),
                pl.BlockSpec((2, HALF_TEXT), whole),
                pl.BlockSpec((1, 8, LANES), lambda h, facts: (h, 0, 0)),
                pl.BlockSpec((1, 8, LANES), lambda h, facts: (h, 0, 0)),
            ],
            out_specs=pl.BlockSpec((1, ROWS, KEYS), lambda h, facts: (h, 0, 0)),
            scratch_shapes=[pltpu.VMEM((ROWS, KEYS), jnp.int32)] * 3,
        ),
        compiler_params=pltpu.CompilerParams(vmem_limit_bytes=50 * MIB),
        cost_estimate=brief,
        name="score_bias",
    )(facts, own_boxes, other_boxes, spread(table_a), spread(table_b))


def pairs_kernel(facts, own_boxes, other_boxes, right, left, masks):
    keys, queries = page_places(facts[0], facts[1], own_boxes[...], other_boxes[...])
    place, x, y = as_columns(queries)
    diff = keys[0] - place
    for index, holds in enumerate(
        (
            (diff >= -16) & (diff <= 15),
            (keys[1] & 15) < (x & 15),
            (keys[2] & 15) < (y & 15),
            diff > 15,
        )
    ):
        masks[index] = jnp.where(holds, 1.0, 0.0).astype(bf16)
    row = lax.broadcasted_iota(jnp.int32, (64, KEYS), 0)
    key_hot = [
        jnp.where((63 - row) == (code & 63), 1.0, 0.0)
        for code in (keys[1] >> 4, keys[2] >> 4, keys[0])
    ]
    key_hot.append(jnp.zeros((64, KEYS), f32))
    right[...] = jnp.transpose(jnp.concatenate(key_hot, axis=0), (1, 0)).astype(bf16)
    row = lax.broadcasted_iota(jnp.int32, (64, 384), 0)
    query_hot = [
        jnp.where(row == queries[1] >> 4, 1.0, 0.0),
        jnp.where(row == queries[2] >> 4, 1.0, 0.0),
        jnp.where(row[:32] + 64 == queries[2] >> 4, 1.0, 0.0),
        jnp.where(row == (queries[0] & 63), 1.0, 0.0),
    ]
    left[...] = jnp.concatenate(query_hot, axis=0)[:, :ROWS].astype(bf16)


def page_pairs(facts, own_boxes, other_boxes):
    vmem = pl.BlockSpec(memory_space=pltpu.VMEM)
    return pl.pallas_call(
        pairs_kernel,
        in_specs=[pl.BlockSpec(memory_space=pltpu.SMEM), vmem, vmem],
        out_specs=[vmem] * 3,
        out_shape=[
            jax.ShapeDtypeStruct((KEYS, 256), bf16),
            jax.ShapeDtypeStruct((224, ROWS), bf16),
            jax.ShapeDtypeStruct((4, ROWS, KEYS), bf16),
        ],
        compiler_params=pltpu.CompilerParams(vmem_limit_bytes=24 * MIB),
        cost_estimate=brief,
        name="page_pairs",
    )(facts, own_boxes, other_boxes)


def table_kernel(right, left, masks, ds_a, ds_b, *rest):
    for head in range(ds_a.shape[0]):
        fold_head(right, left, masks, ds_a[head], ds_b[head], rest[-1].at[head])


def fold_head(right, left, masks, ds_a, ds_b, out):
    total = (ds_a.astype(f32) + ds_b.astype(f32)).astype(bf16)
    hot = right[...]
    query_hot = left[...]

    def fold(values, columns, rows):
        inner = jnp.dot(values, hot[:, columns], preferred_element_type=f32).astype(bf16)
        return jnp.dot(query_hot[rows], inner, preferred_element_type=f32)

    near = fold(total * masks[0], slice(128, 256), slice(160, 224))
    together = jnp.concatenate([total, total * masks[1], total * masks[2]], axis=0)
    inner = jnp.dot(together, hot[:, :128], preferred_element_type=f32).astype(bf16)
    outer = lambda rows, which: jnp.dot(
        query_hot[rows], inner[which * ROWS : (which + 1) * ROWS], preferred_element_type=f32
    )
    plain = outer(slice(0, 160), 0)
    by_x = outer(slice(0, 64), 1)
    by_y = outer(slice(64, 160), 2)

    def diagonals(square):
        lane = lax.broadcasted_iota(jnp.int32, square.shape, 1)
        square = jnp.where(lane < 64, square, 0.0)
        turned = pltpu.roll(square, 0, axis=1, stride=1, stride_axis=0)
        return jnp.sum(turned, axis=0, keepdims=True)

    def second(square):
        return pltpu.roll(square, 64, axis=1)

    above = jnp.sum((total * masks[3]).astype(f32), axis=0, keepdims=True)
    above = sum(above[:, t * LANES : (t + 1) * LANES] for t in range(KEYS // LANES))
    out[...] = jnp.concatenate(
        [
            diagonals(plain[:64]),
            diagonals(by_x),
            diagonals(second(plain[64:128])),
            diagonals(second(by_y[:64])),
            diagonals(near),
            above,
            diagonals(second(plain[128:])),
            diagonals(second(by_y[64:])),
        ],
        axis=0,
    )


def table_bins():
    bins = np.zeros((8, LANES, BUCKETS), np.float32)
    for c in range(127):
        diff = 63 - c
        for kind, base in ((0, POS_BINS), (1, POS_BINS + BOX_BINS)):
            here = base + 32 + min(max(diff, -32), 31)
            below = base + 32 + min(max(diff - 1, -32), 31)
            bins[2 * kind, c, here] += 1
            bins[2 * kind + 1, c, below] += 1
            bins[2 * kind + 1, c, here] -= 1
        far = -1 - c
        bins[6, c, 128 + max(far, -32)] += 1
        bins[7, c, 128 + max(far - 1, -32)] += 1
        bins[7, c, 128 + max(far, -32)] -= 1
        near = (diff + 32) % 64 - 32
        if -16 <= near <= 15:
            bins[4, c, near + 16] += 1
        bins[0, c, 0] += 1
        bins[4, c, 0] -= 1
    bins[5, :, 31] += 1
    bins[5, :, 0] -= 1
    return bins


def fold_table(pairs, ds_a, ds_b, part, parts, after=()):
    count = HEADS // parts
    steps = count // FOLD_HEADS
    head = pl.BlockSpec((FOLD_HEADS, ROWS, KEYS), lambda h: (h + part * steps, 0, 0))
    return pl.pallas_call(
        table_kernel,
        out_shape=jax.ShapeDtypeStruct((count, 8, LANES), f32),
        grid=(steps,),
        in_specs=[full(array) for array in pairs]
        + [head, head]
        + [pl.BlockSpec(memory_space=pl.ANY)] * len(after),
        out_specs=pl.BlockSpec((FOLD_HEADS, 8, LANES), lambda h: (h, 0, 0)),
        compiler_params=pltpu.CompilerParams(vmem_limit_bytes=58 * MIB),
        cost_estimate=brief,
        name="table_grad",
    )(*pairs, ds_a, ds_b, *after)


def visual_kernel(half, grad_ref, normal_low, hat, weight, keep, send, normal_grad, sums):
    rows = normal_low.shape[0]
    column = lambda block: jnp.sum(block, axis=0, keepdims=True)
    token_grad = grad_ref[...].astype(bf16)
    whole = tn_dot(normal_low[...], token_grad)
    mid = whole.shape[0] // 2
    first = half[0] == 0
    keep[...] = jnp.where(first, whole[:mid], whole[mid:]).astype(bf16)
    send[...] = jnp.where(first, whole[mid:], whole[:mid]).astype(bf16)
    place = half[0] * rows + lax.broadcasted_iota(jnp.int32, (rows, 1), 0)
    grad = jnp.where(place < VIS_TOK, nt_dot(token_grad, weight[...]), 0.0)
    normal_grad[...] = grad
    total = column(token_grad.astype(f32))
    put_row(sums, 0, total)
    at = total.shape[1] // LANES
    count = grad.shape[1] // LANES
    put_row(sums.at[at : at + count], 0, column(grad * hat[...]))
    put_row(sums.at[at + count : at + 2 * count], 0, column(grad))


def visual_back(half, gradient, normal_low, hat, weight):
    slots, channels = normal_low.shape
    width = weight.shape[1]
    return pl.pallas_call(
        visual_kernel,
        grid_spec=pltpu.PrefetchScalarGridSpec(
            num_scalar_prefetch=1,
            grid=(1,),
            in_specs=[
                pl.BlockSpec(
                    (slots, width), lambda i, half: (gradient.shape[0] // slots - 1, 0)
                ),
                full(normal_low),
                full(hat),
                full(weight),
            ],
            out_specs=[
                pl.BlockSpec((channels // 2, width), lambda i, half: (0, 0)),
                pl.BlockSpec((channels // 2, width), lambda i, half: (0, 0)),
                pl.BlockSpec((slots, channels), lambda i, half: (0, 0)),
                pl.BlockSpec(((width + 2 * channels) // LANES, LANES), lambda i, half: (0, 0)),
            ],
        ),
        out_shape=[
            jax.ShapeDtypeStruct((channels // 2, width), bf16),
            jax.ShapeDtypeStruct((channels // 2, width), bf16),
            jax.ShapeDtypeStruct((slots, channels), f32),
            jax.ShapeDtypeStruct(((width + 2 * channels) // LANES, LANES), f32),
        ],
        cost_estimate=brief,
        name="visual_back",
    )(half, gradient, normal_low, hat, weight)


def join_kernel(*refs):
    low, out = refs[-2:]
    out[...] = jnp.zeros_like(out)
    at = 0
    for ref in refs[:-2]:
        values = ref[...]
        if len(values.shape) == 3 and values.shape[1] > 1:
            for head in range(values.shape[0]):
                out[at : at + values.shape[1], :] = values[head]
                at += values.shape[1]
        elif len(values.shape) == 3:
            for group in range(values.shape[0]):
                for start in range(0, values.shape[2], LANES):
                    size = min(LANES, values.shape[2] - start)
                    out[at : at + 1, :size] = ref[group, :, start : start + size]
                    at += 1
        else:
            out[at : at + values.shape[0], :] = values
            at += values.shape[0]
    low[...] = out[...].astype(bf16)


def bin_rows(units):
    return -(-units // LANES)


def join(parts):
    rows = 0
    for part in parts:
        if part.ndim == 3 and part.shape[1] == 1:
            rows += part.shape[0] * bin_rows(part.shape[2])
        else:
            rows += part.size // LANES
    rows += -rows % 16
    vmem = pl.BlockSpec(memory_space=pltpu.VMEM)
    return pl.pallas_call(
        join_kernel,
        out_shape=jax.ShapeDtypeStruct((rows, LANES), bf16),
        in_specs=[vmem] * len(parts),
        out_specs=vmem,
        scratch_shapes=[pltpu.VMEM((rows, LANES), f32)],
        cost_estimate=brief,
        name="join",
    )(*parts)


def split_kernel(
    sizes,
    count,
    me,
    left,
    right,
    bins,
    normal_grad,
    hat,
    inverse_std,
    bn_gain,
    attn,
    out_bias,
    gain,
    shift,
    table,
    vis_bias,
    gain_grad,
    shift_grad,
    hidden_bias,
    maps,
    total,
):
    total[...] = left[...].astype(f32) + right[...].astype(f32)
    units = hidden_bias.shape[1]
    width = out_bias.shape[1]
    channels = gain_grad.shape[1]
    starts = [0]
    for size in sizes:
        starts.append(starts[-1] + size)

    def take(start, index, wide):
        per = wide // LANES
        begin = start + index * per
        return jnp.concatenate([total[begin + i : begin + i + 1, :] for i in range(per)], axis=1)

    for layer in range(LAYERS):
        norm = functools.partial(take, starts[layer])
        gain[layer, 1:2, :] = norm(0, width)
        shift[layer, 1:2, :] = norm(1, width)
        out_bias[layer : layer + 1, :] = norm(2, width)
        gain[layer, 0:1, :] = norm(3, width)
        shift[layer, 0:1, :] = norm(4, width)
        attn[2, layer : layer + 1, :] = norm(5, width)
        rows = functools.partial(take, starts[LAYERS + layer])
        attn[0, layer : layer + 1, :] = rows(0, width)
        attn[1, layer : layer + 1, :] = rows(1, width)
        per = bin_rows(units)
        begin = starts[2 * LAYERS + layer] + me[0] * per
        for part in range(per):
            span = min(LANES, units - part * LANES)
            hidden_bias[layer : layer + 1, part * LANES : part * LANES + span] = total[
                pl.ds(begin + part, 1), :span
            ]
    at = starts[3 * LAYERS]
    vis_bias[...] = total[at : at + width // LANES, :]
    at += width // LANES
    by_gain = take(at, 0, channels)
    by_shift = take(at, 1, channels)
    gain_grad[...] = by_gain
    shift_grad[...] = by_shift
    scale = inverse_std[...] * bn_gain[...]
    slots = normal_grad.shape[0]
    place = (me[0] & 1) * slots + lax.broadcasted_iota(jnp.int32, (slots, 1), 0)
    maps[...] = jnp.where(
        place < VIS_TOK,
        scale * (normal_grad[...] - by_shift / count - hat[...] * (by_gain / count)),
        0.0,
    )
    at = starts[3 * LAYERS + 1]
    folded = jnp.zeros((16, BUCKETS), f32)
    for kind in range(8):
        rows = jnp.concatenate(
            [total[at + 8 * head + kind : at + 8 * head + kind + 1, :] for head in range(HEADS)]
            + [jnp.zeros((16 - HEADS, LANES), f32)],
            axis=0,
        )
        high = rows.astype(bf16)
        middle = (rows - high.astype(f32)).astype(bf16)
        low = (rows - high.astype(f32) - middle.astype(f32)).astype(bf16)
        for part in (high, middle, low):
            folded = folded + nt_dot(part, bins[kind])
    table[...] = folded[:HEADS]


def split(me, left, right, sizes, count, normal_grad, hat, inverse_std, bn_gain, units, width):
    slots, channels = normal_grad.shape
    bins = jnp.asarray(table_bins().transpose(0, 2, 1), bf16)
    row = lambda value: value.reshape(1, -1)
    vmem = pl.BlockSpec(memory_space=pltpu.VMEM)
    shape = lambda *size: jax.ShapeDtypeStruct(size, f32)
    return pl.pallas_call(
        functools.partial(split_kernel, sizes, count),
        in_specs=[pl.BlockSpec(memory_space=pltpu.SMEM)] + [vmem] * 7,
        out_specs=[vmem] * 10,
        out_shape=[
            shape(3, LAYERS, width),
            shape(LAYERS, width),
            shape(LAYERS, 2, width),
            shape(LAYERS, 2, width),
            shape(HEADS, BUCKETS),
            shape(width // LANES, LANES),
            shape(1, channels),
            shape(1, channels),
            shape(LAYERS, units),
            shape(slots, channels),
        ],
        scratch_shapes=[pltpu.VMEM(left.shape, f32)],
        cost_estimate=brief,
        name="split",
    )(me, left, right, bins, normal_grad, hat, row(inverse_std), row(bn_gain))


def whole_page(own, other):
    return jnp.concatenate(
        [
            own[:HALF_TEXT],
            other[:HALF_TEXT],
            own[HALF_TEXT:],
            other[HALF_TEXT:],
            jnp.zeros((KEYS - 2 * ROWS, own.shape[1]), own.dtype),
        ],
        axis=0,
    )


def page_split(both):
    mid = 2 * HALF_TEXT
    own = jnp.concatenate([both[:HALF_TEXT], both[mid : mid + HALF_SLOTS]], axis=0)
    other = jnp.concatenate(
        [both[HALF_TEXT:mid], both[mid + HALF_SLOTS : mid + VIS_SLOTS]], axis=0
    )
    return own, other


def nt_dot(left, right):
    return lax.dot_general(left, right, (((1,), (1,)), ((), ())), preferred_element_type=f32)


def tn_dot(left, right):
    return lax.dot_general(left, right, (((0,), (0,)), ((), ())), preferred_element_type=f32)


def put_row(target, index, row):
    count = row.shape[1] // LANES
    for part in range(count):
        at = index * count + part
        target[at : at + 1, :] = row[:, part * LANES : (part + 1) * LANES]


def centred(values):
    center = values - jnp.mean(values, axis=1, keepdims=True)
    spread = jnp.mean(center * center, axis=1, keepdims=True)
    rate = lax.rsqrt(spread + norm_epsilon)
    return center * rate, rate


def norm_back(grad, values, gain_row):
    hat, rate = centred(values)
    scaled = grad * gain_row
    mean = jnp.mean(scaled, axis=1, keepdims=True)
    along = jnp.mean(scaled * hat, axis=1, keepdims=True)
    column = lambda block: jnp.sum(block, axis=0, keepdims=True)
    return rate * (scaled - mean - hat * along), column(grad * hat), column(grad)


def attend_kernel(
    layer,
    q_ref,
    ko,
    kp,
    vo,
    vp,
    bias,
    x_ref,
    weight,
    attn_bias,
    gain,
    shift,
    soft,
    pair,
    residual,
    normed,
    x_s,
    weight_s,
    semaphores,
):
    step = pl.program_id(0)
    later = Later([(x_ref, x_s), (weight.at[layer], weight_s)], semaphores)
    pl.when(step == 0)(later.start)
    first = lax.broadcasted_iota(jnp.int32, (ROWS, LANES), 1) < HEAD_DIM
    for part in range(SLABS):
        lanes = slice(part * LANES, (part + 1) * LANES)
        q = q_ref[:, lanes] * jnp.asarray(HEAD_DIM**-0.5, bf16)
        keys = whole_page(ko[:, lanes], kp[:, lanes])
        values = whole_page(vo[:, lanes], vp[:, lanes])
        found = []
        for head in range(2):
            mine = jnp.where(first if head == 0 else ~first, q, jnp.zeros_like(q))
            scores = nt_dot(mine, keys) + bias[2 * part + head]
            raised = jnp.exp(scores - jnp.max(scores, axis=1, keepdims=True))
            weights = (raised * (1.0 / jnp.sum(raised, axis=1, keepdims=True))).astype(bf16)
            soft[2 * part + head] = weights
            found.append(jnp.dot(weights, values, preferred_element_type=f32))
        slab = pl.ds(pl.multiple_of((step * SLABS + part) * LANES, LANES), LANES)
        pair[0, :, slab] = jnp.where(first, found[0], found[1]).astype(bf16)

    @pl.when(step == STEPS - 1)
    def _():
        later.wait(0, 1)
        attended = jnp.dot(pair[0], weight_s[...], preferred_element_type=f32)
        summed = x_s[...] + (attended + attn_bias[layer, 2:3, :])
        residual[...] = summed
        out = centred(summed)[0] * gain[layer, 0:1, :] + shift[layer, 0:1, :]
        normed[...] = out
        pair[1] = out.astype(bf16)


class Later:
    def __init__(self, pairs, semaphores):
        self.copies = [
            pltpu.make_async_copy(source, target, semaphores.at[index])
            for index, (source, target) in enumerate(pairs)
        ]

    def start(self):
        for copy in self.copies:
            copy.start()

    def wait(self, *indices):
        for index in indices:
            self.copies[index].wait()


anywhere = pl.BlockSpec(memory_space=pl.ANY)


def full(array):
    return pl.BlockSpec(array.shape, lambda *at: (0,) * array.ndim)


def attend(layer, q, kv, other_kv, bias, x, out_weight, attn_bias, gain, shift):
    rows, width = q.shape
    slab = pl.BlockSpec((ROWS, SLABS * LANES), lambda p: (0, p))
    second = pl.BlockSpec((ROWS, SLABS * LANES), lambda p: (0, p + STEPS))
    heads = pl.BlockSpec((2 * SLABS, ROWS, KEYS), lambda p: (p, 0, 0))
    whole = pl.BlockSpec((rows, width), lambda p: (0, 0))
    wide = jax.ShapeDtypeStruct((rows, width), f32)
    low = jax.ShapeDtypeStruct((2, rows, width), bf16)
    return pl.pallas_call(
        functools.partial(attend_kernel, layer),
        grid=(STEPS,),
        in_specs=[
            slab,
            slab,
            slab,
            second,
            second,
            heads,
            anywhere,
            anywhere,
            full(attn_bias),
            full(gain),
            full(shift),
        ],
        out_specs=[
            heads,
            pl.BlockSpec((2, rows, width), lambda p: (0, 0, 0)),
            whole,
            whole,
        ],
        out_shape=[jax.ShapeDtypeStruct((HEADS, ROWS, KEYS), bf16), low, wide, wide],
        scratch_shapes=[
            pltpu.VMEM((rows, width), f32),
            pltpu.VMEM((width, width), bf16),
            pltpu.SemaphoreType.DMA((2,)),
        ],
        compiler_params=pltpu.CompilerParams(vmem_limit_bytes=50 * MIB),
        cost_estimate=brief,
        name="attend",
    )(q, kv, other_kv, kv, other_kv, bias, x, out_weight, attn_bias, gain, shift)


def attend_back_kernel(q_ref, ko, kp, vo, vp, dc_ref, soft, *rest):
    ds, *grads = rest[-6:]
    scale = HEAD_DIM**-0.5
    first = lax.broadcasted_iota(jnp.int32, (ROWS, LANES), 1) < HEAD_DIM
    for part in range(SLABS):
        lanes = slice(part * LANES, (part + 1) * LANES)
        q = q_ref[:, lanes]
        dc = dc_ref[:, lanes]
        keys = whole_page(ko[:, lanes], kp[:, lanes])
        values = whole_page(vo[:, lanes], vp[:, lanes])
        q_turned = jnp.transpose(q.astype(f32), (1, 0)).astype(bf16)
        dc_turned = jnp.transpose(dc.astype(f32), (1, 0)).astype(bf16)
        dq_parts, dk_parts, dv_parts = [], [], []
        for head in range(2):
            span = slice(head * HEAD_DIM, (head + 1) * HEAD_DIM)
            mine = jnp.where(first if head == 0 else ~first, dc, jnp.zeros_like(dc))
            weights = soft[2 * part + head]
            weights_f = weights.astype(f32)
            flow = nt_dot(mine, values)
            share = jnp.sum(weights_f * flow, axis=1, keepdims=True)
            score_grad = (weights_f * (flow - share)).astype(bf16)
            ds[2 * part + head] = score_grad
            dq_parts.append(jnp.dot(score_grad, keys, preferred_element_type=f32))
            dk_parts.append(jnp.dot(q_turned[span], score_grad, preferred_element_type=f32))
            dv_parts.append(jnp.dot(dc_turned[span], weights, preferred_element_type=f32))
        grads[0][:, lanes] = (jnp.where(first, dq_parts[0], dq_parts[1]) * scale).astype(bf16)
        own, other = page_split(jnp.transpose(jnp.concatenate(dk_parts, axis=0) * scale, (1, 0)))
        grads[1][:, lanes] = own.astype(bf16)
        grads[2][:, lanes] = other.astype(bf16)
        own, other = page_split(jnp.transpose(jnp.concatenate(dv_parts, axis=0), (1, 0)))
        grads[3][:, lanes] = own.astype(bf16)
        grads[4][:, lanes] = other.astype(bf16)


def attend_back(q, kv, other_kv, dctx, soft, after=()):
    slab = pl.BlockSpec((ROWS, SLABS * LANES), lambda p: (0, p))
    second = pl.BlockSpec((ROWS, SLABS * LANES), lambda p: (0, p + STEPS))
    heads = pl.BlockSpec((2 * SLABS, ROWS, KEYS), lambda p: (p, 0, 0))
    return pl.pallas_call(
        attend_back_kernel,
        grid=(STEPS,),
        in_specs=[slab, slab, slab, second, second, slab, heads]
        + [pl.BlockSpec(memory_space=pl.ANY)] * len(after),
        out_specs=[heads] + [slab] * 5,
        out_shape=[
            jax.ShapeDtypeStruct((HEADS, ROWS, KEYS), bf16),
        ]
        + [jax.ShapeDtypeStruct(q.shape, bf16)] * 5,
        compiler_params=pltpu.CompilerParams(vmem_limit_bytes=50 * MIB),
        cost_estimate=brief,
        name="attend_back",
    )(q, kv, other_kv, kv, other_kv, dctx, soft, *after)


def ffn_kernel(layer, more, me, x_ref, *refs):
    step = pl.program_id(0)
    width = x_ref.shape[1]
    blocks, (bias, n_ref, out_bias, gain, shift), rest = refs[:BLOCKS], refs[BLOCKS:][:5], refs[BLOCKS + 5 :]
    units = blocks[0].shape[1]
    if more:
        weight, attn_bias, *rest, weight_s, semaphores = rest
        later = Later([(weight.at[layer + 1], weight_s)], semaphores)
        pl.when(step == 0)(later.start)
    own_act, mate_act, slope, residual = rest[:4]
    x = x_ref[...]

    total = None
    for index, block in enumerate(blocks):
        weights = block[0]
        row = bias[pl.ds(BLOCKS * step + index, 1), layer, :]
        hidden = nt_dot(x, weights[:, :width]) + row
        half_cdf = 0.5 + 0.5 * lax.erf(hidden * 0.5**0.5)
        low = (hidden * half_cdf).astype(bf16)
        (mate_act if index % 2 else own_act)[index // 2] = low
        density = jnp.exp(hidden * hidden * -0.5) * (1.0 / (2.0 * np.pi) ** 0.5)
        slope[index] = (half_cdf + hidden * density).astype(bf16)
        term = jnp.dot(low, weights[:, width:], preferred_element_type=f32)
        total = term if total is None else total + term

    @pl.when(step == 0)
    def _():
        residual[...] = n_ref[...] + out_bias[layer : layer + 1, :] + total

    @pl.when(step > 0)
    def _():
        residual[...] += total

    @pl.when(step == pl.num_programs(0) - 1)
    def _():
        states = centred(residual[...])[0] * gain[layer, 1:2, :] + shift[layer, 1:2, :]
        rounded = states.astype(bf16)
        if more:
            wide, query, shared = rest[-3:]
            wide[...] = states
            later.wait(0)
            project = lambda index: jnp.dot(
                rounded, weight_s[index], preferred_element_type=f32
            )
            query[...] = (project(0) + attn_bias[layer + 1, 0:1, :]).astype(bf16)
            shared[:, :width] = project(1).astype(bf16)
            shared[:, width : 2 * width] = (
                project(2) + attn_bias[layer + 1, 1:2, :]
            ).astype(bf16)
            shared[:, 2 * width :] = rounded
        else:
            rest[-1][...] = rounded


def weight_blocks(layer, units, width):
    pick = lambda which: pl.BlockSpec(
        (1, units, 2 * width), lambda i, me: (me[0] ^ (BLOCKS * i + which), layer, 0)
    )
    return [pick(which) for which in range(BLOCKS)]


def ffn(me, layer, pair, n, gathered, bias, out_bias, gain, shift, qkv_weight, attn_bias):
    groups, _, units = bias.shape
    rows, width = n.shape
    more = layer < LAYERS - 1
    whole = pl.BlockSpec((rows, width), lambda i, me: (0, 0))
    kept = pl.BlockSpec((BLOCKS, rows, units), lambda i, me: (i, 0, 0))
    kept_shape = jax.ShapeDtypeStruct((groups, rows, units), bf16)
    wide = jax.ShapeDtypeStruct((rows, width), f32)
    low = jax.ShapeDtypeStruct((rows, width), bf16)
    half_act = pl.BlockSpec((HALF, rows, units), lambda i, me: (i, 0, 0))
    half_shape = jax.ShapeDtypeStruct((groups // 2, rows, units), bf16)
    inputs = [pair] + [gathered] * BLOCKS + [bias, n, out_bias, gain, shift]
    in_specs = [
        pl.BlockSpec((None, rows, width), lambda i, me: (1, 0, 0)),
        *weight_blocks(layer, units, width),
        full(bias),
        whole,
        full(out_bias),
        full(gain),
        full(shift),
    ]
    out_specs = [half_act, half_act, kept, whole]
    out_shape = [half_shape, half_shape, kept_shape, wide]
    if more:
        inputs += [qkv_weight, attn_bias]
        in_specs += [
            anywhere,
            full(attn_bias),
        ]
        out_specs += [whole, whole, pl.BlockSpec((rows, 3 * width), lambda i, me: (0, 0))]
        out_shape += [wide, low, jax.ShapeDtypeStruct((rows, 3 * width), bf16)]
    else:
        out_specs += [whole]
        out_shape += [low]
    return pl.pallas_call(
        functools.partial(ffn_kernel, layer, more),
        out_shape=out_shape,
        grid_spec=pltpu.PrefetchScalarGridSpec(
            num_scalar_prefetch=1,
            grid=(groups // BLOCKS,),
            in_specs=in_specs,
            out_specs=out_specs,
            scratch_shapes=[
                pltpu.VMEM((3, width, width), bf16),
                pltpu.SemaphoreType.DMA((1,)),
            ]
            if more
            else [],
        ),
        compiler_params=pltpu.CompilerParams(vmem_limit_bytes=50 * MIB),
        cost_estimate=brief,
        name="feed_forward",
    )(me, *inputs)


def ffn_back_kernel(layer, me, grad_ref, r2_ref, r1_ref, *refs):
    blocks, (slope, gain, out_weight), rest = refs[:BLOCKS], refs[BLOCKS:][:3], refs[BLOCKS + 3 :]
    own_dh, mate_dh, low_grads, bias_grad, sums, dx, dctx, total_s, r1_s, weight_s, semaphores = rest
    later = Later([(r1_ref, r1_s), (out_weight.at[layer], weight_s)], semaphores)
    step = pl.program_id(0)
    width = r2_ref.shape[1]
    column = lambda block: jnp.sum(block, axis=0, keepdims=True)

    @pl.when(step == 0)
    def _():
        later.start()
        grad, gain_grad, shift_grad = norm_back(
            grad_ref[...].astype(f32), r2_ref[...], gain[layer, 1:2, :]
        )
        low = grad.astype(bf16)
        total_s[...] = grad
        low_grads[0] = low
        put_row(sums, 0, gain_grad)
        put_row(sums, 1, shift_grad)
        put_row(sums, 2, column(low.astype(f32)))

    dy = low_grads[0]
    total = None
    for index, block in enumerate(blocks):
        weights = block[0]
        flow = nt_dot(dy, weights[:, width:])
        grad = (flow * slope[index].astype(f32)).astype(bf16)
        (mate_dh if index % 2 else own_dh)[index // 2] = grad
        bias_grad[index ^ (me[0] & (BLOCKS - 1))] = column(grad.astype(f32))
        term = jnp.dot(grad, weights[:, :width], preferred_element_type=f32)
        total = term if total is None else total + term
    total_s[...] += total

    @pl.when(step == pl.num_programs(0) - 1)
    def _():
        later.wait(0, 1)
        grad, gain_grad, shift_grad = norm_back(total_s[...], r1_s[...], gain[layer, 0:1, :])
        low = grad.astype(bf16)
        dx[...] = grad
        low_grads[1] = low
        dctx[...] = nt_dot(low, weight_s[...]).astype(bf16)
        put_row(sums, 3, gain_grad)
        put_row(sums, 4, shift_grad)
        put_row(sums, 5, column(low.astype(f32)))


def ffn_back(me, layer, grad, r2, r1, gathered, slope, gain, out_weight):
    groups, rows, units = slope.shape
    width = r2.shape[1]
    whole = pl.BlockSpec((rows, width), lambda i, me: (0, 0))
    half = pl.BlockSpec((HALF, rows, units), lambda i, me: (i, 0, 0))
    half_shape = jax.ShapeDtypeStruct((groups // 2, rows, units), bf16)
    return pl.pallas_call(
        functools.partial(ffn_back_kernel, layer),
        out_shape=[
            half_shape,
            half_shape,
            jax.ShapeDtypeStruct((2, rows, width), bf16),
            jax.ShapeDtypeStruct((groups, 1, units), f32),
            jax.ShapeDtypeStruct((6 * width // LANES, LANES), f32),
            jax.ShapeDtypeStruct((rows, width), f32),
            jax.ShapeDtypeStruct((rows, width), bf16),
        ],
        grid_spec=pltpu.PrefetchScalarGridSpec(
            num_scalar_prefetch=1,
            grid=(groups // BLOCKS,),
            in_specs=[
                whole,
                whole,
                anywhere,
                *weight_blocks(layer, units, width),
                pl.BlockSpec((BLOCKS, rows, units), lambda i, me: (i, 0, 0)),
                full(gain),
                anywhere,
            ],
            out_specs=[
                half,
                half,
                pl.BlockSpec((2, rows, width), lambda i, me: (0, 0, 0)),
                pl.BlockSpec((BLOCKS, 1, units), lambda i, me: (me[0] // BLOCKS ^ i, 0, 0)),
                pl.BlockSpec((6 * width // LANES, LANES), lambda i, me: (0, 0)),
                whole,
                whole,
            ],
            scratch_shapes=[
                pltpu.VMEM((rows, width), f32),
                pltpu.VMEM((rows, width), f32),
                pltpu.VMEM((width, width), bf16),
                pltpu.SemaphoreType.DMA((2,)),
            ],
        ),
        compiler_params=pltpu.CompilerParams(vmem_limit_bytes=50 * MIB),
        cost_estimate=brief,
        name="feed_forward_back",
    )(me, grad, r2, r1, *[gathered] * BLOCKS, slope, gain, out_weight)


def ffn_grads_kernel(me, n, n_mate, dy, dy_mate, dh, dh_mate, act, act_mate, *rest):
    near_keep, near_send, seq_keep, seq_send, n_s, dy_s = rest[-6:]
    rows, width = n.shape
    far, units = near_keep.shape[:2]
    step = pl.program_id(0)

    @pl.when(step == 0)
    def _():
        for target, own, mate in ((n_s, n, n_mate), (dy_s, dy, dy_mate)):
            target[:rows] = own[...]
            target[rows:] = mate[...]

    def product(own, mate, right):
        turned = [
            jnp.transpose(jnp.concatenate([own[i, 0], mate[i, 0]], axis=0), (1, 0))
            for i in range(far)
        ]
        return jnp.dot(
            jnp.concatenate(turned, axis=0), right[...], preferred_element_type=f32
        ).astype(bf16)

    def put(target, values):
        for i in range(far):
            target[(me[0] >> 2) ^ i] = values[i * units : (i + 1) * units]

    into = product(dh, dh_mate, n_s)
    pl.when(step == 0)(lambda: put(near_keep, into))
    pl.when(step == 1)(lambda: put(near_send, into))
    out = product(act, act_mate, dy_s)
    turn = me[1] % 2 == 0
    put(seq_keep, jnp.where(turn, out[:, : width // 2], out[:, width // 2 :]))
    put(seq_send, jnp.where(turn, out[:, width // 2 :], out[:, : width // 2]))


def ffn_grads(me, pair, pair_mate, low_grads, low_grads_mate, dh, dh_mate, act, act_mate):
    groups, rows, units = dh.shape
    width = pair.shape[2]
    far = groups // 2
    row_block = lambda which: pl.BlockSpec((None, rows, width), lambda i, me: (which, 0, 0))
    hidden = pl.BlockSpec((far, 1, rows, units), lambda i, me: (0, i, 0, 0))
    near_shape = jax.ShapeDtypeStruct((far, units, width), bf16)
    near_block = pl.BlockSpec((far, units, width), lambda i, me: (0, 0, 0))
    seq_shape = jax.ShapeDtypeStruct((groups, units, width // 2), bf16)
    seq_block = pl.BlockSpec((far, units, width // 2), lambda i, me: (i, 0, 0))
    by_far = lambda block: block.reshape(far, 2, rows, units)
    return pl.pallas_call(
        ffn_grads_kernel,
        out_shape=[near_shape, near_shape, seq_shape, seq_shape],
        grid_spec=pltpu.PrefetchScalarGridSpec(
            num_scalar_prefetch=1,
            grid=(2,),
            in_specs=[row_block(1), row_block(1), row_block(0), row_block(0)] + [hidden] * 4,
            out_specs=[near_block, near_block, seq_block, seq_block],
            scratch_shapes=[pltpu.VMEM((2 * rows, width), bf16)] * 2,
        ),
        compiler_params=pltpu.CompilerParams(vmem_limit_bytes=50 * MIB),
        cost_estimate=brief,
        name="feed_forward_grads",
    )(
        me,
        pair,
        pair_mate,
        low_grads,
        low_grads_mate,
        *[by_far(block) for block in (dh, dh_mate, act, act_mate)],
    )


def projection_kernel(by_distance, me, x, x_mate, ctx, ctx_mate, *refs):
    own, mate, refs = refs[:5], refs[5:10], refs[10:]
    da, da_mate, dr_ref, weight = refs[:4]
    near_keep, near_send, seq_keep, seq_send, dx, sums = refs[-11:-5]
    turned_s, picked_s, left_s, right_s, shards_s = refs[-5:]
    step = pl.program_id(0)
    far, shard = near_keep.shape[:2]
    rows, width = x.shape
    column = lambda block: jnp.sum(block.astype(f32), axis=0, keepdims=True)

    def place_of(place, near):
        far_place = (me[0] >> 2) ^ place if by_distance else place
        return far_place * 4 + ((me[0] & 3) ^ (2 * near))

    gap = -rows % LANES
    mate_rows = slice(rows + gap, 2 * rows + gap)

    def pick_left(first, second):
        for block, at_rows in ((first, slice(0, rows)), (second, mate_rows)):
            turned_s[...] = jnp.transpose(block[...].astype(f32), (1, 0))
            for near in range(2):
                for place in range(far):
                    start = pl.multiple_of(place_of(place, near) * shard, 8)
                    at = (near * far + place) * shard
                    picked_s[at : at + shard, at_rows] = turned_s[pl.ds(start, shard), :]
        left_s[...] = picked_s[...].astype(bf16)

    @pl.when(step == 0)
    def _():
        dx[...] = dr_ref[...]
        picked_s[:, rows : rows + gap] = jnp.zeros((width // 2, gap), f32)
        right_s[rows : rows + gap] = jnp.zeros((gap, width), bf16)
        pick_left(x, x_mate)
        right_s[:rows] = own[0][...]
        right_s[mate_rows] = mate[0][...]
        put_row(sums, 0, column(own[0][...]))

    for index in (1, 2):

        @pl.when(step == index)
        def _():
            right_s[:rows] = add_low(own[2 * index - 1][...], mate[2 * index][...])
            right_s[mate_rows] = add_low(mate[2 * index - 1][...], own[2 * index][...])

    @pl.when(step == 2)
    def _():
        put_row(sums, 1, column(right_s[:rows]))

    @pl.when(step < 3)
    def _():
        dx[...] += nt_dot(right_s[:rows], weight[0, 0])

    @pl.when(step == 3)
    def _():
        pick_left(ctx, ctx_mate)
        right_s[:rows] = da[...]
        right_s[mate_rows] = da_mate[...]

    shards_s[...] = jnp.dot(left_s[...], right_s[...], preferred_element_type=f32)

    def put(target, first, near, columns):
        for place in range(far):
            at = (near * far + place) * shard
            target[first + place, :, columns] = shards_s[at : at + shard, :].astype(bf16)

    for index in range(2):

        @pl.when(step == index)
        def _():
            columns = slice(index * width, (index + 1) * width)
            put(near_keep, 0, 0, columns)
            put(near_send, 0, 1, columns)

    def put_seq(target):
        put(target, 0, 0, slice(None))
        put(target, far, 1, slice(None))

    mine = step - 2 == me[1] % 2
    pl.when((step >= 2) & mine)(lambda: put_seq(seq_keep))
    pl.when((step >= 2) & jnp.logical_not(mine))(lambda: put_seq(seq_send))


def projection_grads(
    by_distance,
    me,
    layer,
    shared,
    shared_mate,
    pair,
    pair_mate,
    own,
    mate,
    low,
    low_mate,
    dr,
    weight,
    after=(),
):
    rows, width = dr.shape
    groups = lax.axis_size("tp")
    shard = width // groups
    whole = pl.BlockSpec((rows, width), lambda t, me: (0, 0))
    x_block = pl.BlockSpec((rows, width), lambda t, me: (0, 2))
    layered = lambda which: pl.BlockSpec((None, rows, width), lambda t, me: (which, 0, 0))
    near_shape = jax.ShapeDtypeStruct((groups // 4, shard, 2 * width), bf16)
    near_block = pl.BlockSpec(near_shape.shape, lambda t, me: (0, 0, 0))
    seq_shape = jax.ShapeDtypeStruct((groups // 2, shard, width), bf16)
    seq_block = pl.BlockSpec(seq_shape.shape, lambda t, me: (0, 0, 0))
    return pl.pallas_call(
        functools.partial(projection_kernel, by_distance),
        out_shape=[near_shape, near_shape, seq_shape, seq_shape]
        + [
            jax.ShapeDtypeStruct((rows, width), f32),
            jax.ShapeDtypeStruct((2 * width // LANES, LANES), f32),
        ],
        grid_spec=pltpu.PrefetchScalarGridSpec(
            num_scalar_prefetch=1,
            grid=(4,),
            in_specs=[
                x_block,
                x_block,
                layered(0),
                layered(0),
                *[whole] * 10,
                layered(1),
                layered(1),
                whole,
                pl.BlockSpec(
                    (1, 1, width, width), lambda t, me: (layer, jnp.minimum(t, 2), 0, 0)
                ),
            ]
            + [pl.BlockSpec(memory_space=pl.ANY)] * len(after),
            out_specs=[near_block, near_block, seq_block, seq_block]
            + [
                whole,
                pl.BlockSpec((2 * width // LANES, LANES), lambda t, me: (0, 0)),
            ],
            scratch_shapes=[
                pltpu.VMEM((width, rows), f32),
                pltpu.VMEM((width // 2, 2 * rows + -rows % LANES), f32),
                pltpu.VMEM((width // 2, 2 * rows + -rows % LANES), bf16),
                pltpu.VMEM((2 * rows + -rows % LANES, width), bf16),
                pltpu.VMEM((width // 2, width), f32),
            ],
        ),
        compiler_params=pltpu.CompilerParams(vmem_limit_bytes=50 * MIB),
        cost_estimate=brief,
        name="projection_grads",
    )(
        me,
        shared,
        shared_mate,
        pair,
        pair_mate,
        *own,
        *mate,
        low,
        low_mate,
        dr,
        weight,
        *after,
    )


def ordered(turn, mine, other):
    return jnp.where(turn, mine, other), jnp.where(turn, other, mine)


def stacked_parts(block, start, rows, count):
    return jnp.concatenate(
        [block[start + i * rows : start + (i + 1) * rows] for i in range(count)], axis=1
    )


def projection_out_kernel(starts, me, *refs):
    qkv, out = refs[-2:]
    rows, width = out.shape[1:]
    for layer in range(LAYERS):
        mine, other = refs[2 * layer : 2 * layer + 2]
        count = width // mine.shape[1]
        first, second = ordered(me[1] % 2 == 0, mine[...], other[...])
        take = lambda block, part: stacked_parts(
            block, starts[layer] + part * rows * count, rows, count
        ).astype(f32)
        qkv[layer, 0] = take(first, 0)
        qkv[layer, 1] = take(second, 0)
        qkv[layer, 2] = take(first, 1)
        out[layer] = take(second, 1)


def ffn_out_kernel(me, *refs):
    into, out = refs[-2:]
    units, width = out.shape[1:]
    for layer in range(LAYERS):
        mine, other = refs[2 * layer : 2 * layer + 2]
        for index, part in enumerate(ordered(me[1] % 2 == 0, mine[...], other[...])):
            columns = slice(index * (width // 2), (index + 1) * (width // 2))
            into[layer, :, columns] = part[:units].astype(f32)
            out[layer, :, columns] = part[units : 2 * units].astype(f32)


def write_out(kernel, name, me, parts, shapes):
    vmem = pl.BlockSpec(memory_space=pltpu.VMEM)
    return pl.pallas_call(
        kernel,
        in_specs=[pl.BlockSpec(memory_space=pltpu.SMEM)] + [vmem] * len(parts),
        out_specs=[vmem] * len(shapes),
        out_shape=[jax.ShapeDtypeStruct(shape, f32) for shape in shapes],
        compiler_params=pltpu.CompilerParams(vmem_limit_bytes=24 * MIB),
        cost_estimate=brief,
        name=name,
    )(me, *parts)


def body(
    text_states,
    visual_maps,
    text_boxes,
    text_lengths,
    qkv_weight,
    out_weight,
    attn_bias,
    ffn_in,
    ffn_in_bias,
    ffn_out,
    ffn_out_bias,
    norm_gain,
    norm_shift,
    bias_table,
    vis_weight,
    vis_bias,
    bn_gain,
    bn_shift,
    cotangent,
):
    tp_index = lax.axis_index("tp")
    tp_size = lax.axis_size("tp")
    half = tp_index % 2
    page = (lax.axis_index("seq") * tp_size + tp_index) // 2
    me = jnp.stack([tp_index, lax.axis_index("seq")]).astype(jnp.int32)
    units = ffn_in.shape[1]
    width = text_states.shape[1]
    text_rows = text_states.shape[0]

    packed = jnp.concatenate([ffn_in, ffn_out], axis=2).reshape(LAYERS * units, 2 * width)
    gathered = lax.all_gather(packed, "tp", axis=0)
    hidden_bias = ffn_in_bias.astype(f32)[None]
    for bit in range(mesh_bits("tp")):
        hidden_bias = jnp.concatenate([hidden_bias, flipped(hidden_bias, "tp", bit)], axis=0)

    other_boxes = flipped(text_boxes, "tp", 0)
    length = lax.dynamic_index_in_dim(text_lengths, page, 0, keepdims=False)
    facts = jnp.stack([half.astype(jnp.int32), length])
    score_bias = make_bias(facts, text_boxes, other_boxes, bias_table)

    count_cells = text_lengths.shape[0] * VIS_TOK
    maps_float = visual_maps.astype(f32)
    slot_place = half * HALF_SLOTS + jnp.arange(HALF_SLOTS, dtype=jnp.int32)
    slot_mask = (slot_place < VIS_TOK)[:, None]
    masked_maps = jnp.where(slot_mask, maps_float, 0.0)
    sums = total_over_all(
        jnp.stack([jnp.sum(masked_maps, axis=0), jnp.sum(masked_maps * masked_maps, axis=0)])
    )
    channel_mean = sums[0] / count_cells
    inverse_std = lax.rsqrt(sums[1] / count_cells - channel_mean * channel_mean + norm_epsilon)
    centered_hat = jnp.where(slot_mask, (maps_float - channel_mean) * inverse_std, 0.0)
    normal_low = jnp.where(slot_mask, centered_hat * bn_gain + bn_shift, 0.0).astype(bf16)
    visual_tokens = jnp.dot(normal_low, vis_weight, preferred_element_type=f32) + vis_bias
    states = jnp.concatenate([text_states.astype(f32), visual_tokens], axis=0)

    rounded = states.astype(bf16)
    project = lambda index: jnp.dot(rounded, qkv_weight[0, index], preferred_element_type=f32)
    shared = jnp.concatenate(
        [project(1).astype(bf16), (project(2) + attn_bias[0, 1]).astype(bf16), rounded], axis=1
    )
    query = (project(0) + attn_bias[0, 0]).astype(bf16)
    saved = []
    for layer in range(LAYERS):
        shared_mate = flipped(shared, "tp", 0)
        parts = (query, shared, shared_mate)
        soft, pair, residual_one, normed = attend(
            layer, *parts, score_bias, states, out_weight, attn_bias, norm_gain, norm_shift
        )
        if layer == 0:
            pairs = page_pairs(facts, text_boxes, other_boxes)
            normed, *pairs = tied((normed, *pairs), ())
        act, act_send, slope, residual_two, *onwards = ffn(
            me,
            layer,
            pair,
            normed,
            gathered,
            hidden_bias,
            ffn_out_bias,
            norm_gain,
            norm_shift,
            qkv_weight,
            attn_bias,
        )
        mates = (flipped(pair, "tp", 0), flipped(act_send, "tp", 0))
        saved.append((parts, soft, pair, residual_one, residual_two, act, slope, mates))
        if layer < LAYERS - 1:
            states, query, shared = onwards
    out_states = onwards[0]

    gradient = cotangent
    norm_sums = [None] * LAYERS
    projection_rows = [None] * LAYERS
    bin_grads = [None] * LAYERS
    score_grads = [None] * LAYERS
    projections = [None] * LAYERS
    ffns = [None] * LAYERS
    for layer in reversed(range(LAYERS)):
        last = layer == LAYERS - 1
        parts, soft, pair, residual_one, residual_two, act, slope, mates = saved[layer]
        dh, dh_send, low, bin_grads[layer], norm_sums[layer], grad_one, context_grad = ffn_back(
            me, layer, gradient, residual_two, residual_one, gathered, slope, norm_gain, out_weight
        )
        if not last:
            context_grad, dh_send = tied((context_grad, dh_send), ffns[-1].underway())
            ffns[-1].second(context_grad)
        dh_mate, low_mate = flipped(dh_send, "tp", 0), flipped(low, "tp", 0)
        score_grads[layer], *grads = attend_back(*parts, context_grad, soft)
        (dh, dh_mate, low_mate, pair_mate, act_mate), grads = (
            tied((dh, dh_mate, low_mate, *mates), grads[:1]),
            tied(grads, (dh_mate, low_mate, *mates)),
        )
        grads_mate = [flipped(part, "tp", 0) for part in grads]
        weights = ffn_grads(me, pair, pair_mate, low, low_mate, dh, dh_mate, act, act_mate)
        if not last:
            weights = tied(weights, projections[-1].underway() + ffns[-1].underway())
            projections[-1].second(weights[0])
            upper = Scattered([ffns[-1]], weights[0])
        ffns[layer] = Shards(*weights)
        *weights, gradient, projection_rows[layer] = projection_grads(
            not last,
            me,
            layer,
            parts[1],
            parts[2],
            pair,
            mates[0],
            grads,
            grads_mate,
            low,
            low_mate,
            grad_one,
            qkv_weight,
        )
        if last:
            projections[layer] = Shards(*weights)

    half_at = me[:1] % 2
    vis_keep, vis_send, normal_grad, vis_rows = visual_back(
        half_at, gradient, normal_low, centered_hat, vis_weight
    )
    vis_came = flipped(vis_send, "tp", 0)
    seq_ways = [("seq", bit) for bit in range(mesh_bits("seq"))]
    far_ways = [("tp", bit) for bit in range(2, mesh_bits("tp"))]
    vis_ways = far_ways + [("tp", 1)] + seq_ways
    vis_sums = Tree(add_low(vis_keep, vis_came), vis_ways, join=("tp", 0))
    vis_sums.step()
    fold = functools.partial(fold_table, pairs, *score_grads, parts=FOLDS)
    folds = [fold(0, after=vis_sums.lefts)]
    folds[0], *weights = tied(
        (folds[0], *weights),
        ffns[0].underway() + projections[-1].underway() + vis_sums.rights + [upper.shard],
    )
    ffns[0].second(folds[0])
    projections[0] = Shards(*weights)
    vis_sums.step(folds[0])
    folds.append(fold(1, after=folds + vis_sums.lefts))
    (folds[1],) = tied(folds[1:], ffns[0].underway() + vis_sums.rights)
    lower = Scattered([ffns[0], projections[-1]], folds[1])
    vis_sums.step(folds[1])
    small = join(norm_sums + projection_rows + bin_grads + [vis_rows, *folds])
    sizes = [part.shape[0] for part in norm_sums + projection_rows]
    sizes += [tp_size * bin_rows(units)] * LAYERS + [vis_rows.shape[0]]
    small_ways = [("tp", 0), ("tp", 1)] + seq_ways + far_ways
    small_sums = Tree(small, small_ways)
    small_sums.step()
    small_sums.step(*projections[0].underway())
    behind = small_sums.lefts[0]
    projections[0].second(behind)
    small_sums.step(*projections[0].underway(), *vis_sums.rights)
    behind = small_sums.lefts[0]
    projections[0].halve(behind)
    vis_sums.step(behind)
    upper.join(behind)
    small_sums.step(*vis_sums.rights, upper.other)
    behind = small_sums.lefts[0]
    for _ in range(mesh_bits("tp") - 3):
        projections[0].halve_more(behind)
    while vis_sums.steps:
        vis_sums.step(behind)
    lower.join(behind)
    while small_sums.steps:
        small_sums.step(lower.shard)
    behind = small_sums.lefts[0]
    projections[0].halve_more(behind)
    projections[0].join()
    small, small_came = small_sums.result()
    vis_sum, vis_mate = vis_sums.result()
    vis_weight_grad = jnp.concatenate(
        [
            jnp.where(half == 0, vis_sum, vis_mate),
            jnp.where(half == 0, vis_mate, vis_sum),
        ],
        axis=0,
    ).astype(f32)
    grad_text = gradient[:text_rows]
    attn_total, bout_total, gain_total, shift_total, table_total, visb_total, *rest = split(
        me,
        small,
        small_came,
        sizes,
        count_cells,
        normal_grad,
        centered_hat,
        inverse_std,
        bn_gain,
        units,
        width,
    )
    bn_gain_grad, bn_shift_grad, bin_total, grad_maps = rest
    shard = width // tp_size
    qkv_total, out_total = write_out(
        functools.partial(projection_out_kernel, (0, 2 * units)),
        "projections_out",
        me,
        [part for sums in (projections[0], lower) for part in (sums.shard, sums.other)],
        [(LAYERS, 3, shard, width), (LAYERS, shard, width)],
    )
    in_total, down_total = write_out(
        ffn_out_kernel,
        "feed_forward_out",
        me,
        [part for sums in (lower, upper) for part in (sums.shard, sums.other)],
        [(LAYERS, units, width)] * 2,
    )
    return (
        out_states,
        grad_text,
        grad_maps,
        qkv_total,
        out_total,
        attn_total.transpose(1, 0, 2),
        in_total,
        bin_total,
        down_total,
        bout_total,
        gain_total,
        shift_total,
        table_total.T,
        vis_weight_grad,
        visb_total.reshape(-1),
        bn_gain_grad[0],
        bn_shift_grad[0],
    )


def solution(mesh):
    rows = P(("seq", "tp"), None)
    units = P(None, "tp", None)
    return jax.shard_map(
        body,
        mesh=mesh,
        in_specs=(
            rows,
            rows,
            P(None, ("seq", "tp")),
            P(),
            P(),
            P(),
            P(),
            units,
            P(None, "tp"),
            units,
            P(),
            P(),
            P(),
            P(),
            P(),
            P(),
            P(),
            P(),
            rows,
        ),
        out_specs=(
            rows,
            rows,
            rows,
            P(None, None, "tp", None),
            units,
            P(),
            units,
            P(None, "tp"),
            units,
            P(),
            P(),
            P(),
            P(),
            P(),
            P(),
            P(),
            P(),
        ),
        check_vma=False,
    )
```

```python
import functools

import jax
import jax.numpy as jnp
import numpy as np
from jax import lax
from jax.experimental import pallas as pl
from jax.experimental.pallas import tpu as pltpu
from jax.sharding import PartitionSpec as P

HEADS = 12
HEAD_DIM = 64
VIS_TOK = 49
VIS_SLOTS = 64
POS_BINS = 32
BOX_BINS = 64
LAYERS = 2
BUCKETS = POS_BINS + 2 * BOX_BINS

HALF_TEXT = 256
HALF_SLOTS = VIS_SLOTS // 2
ROWS = HALF_TEXT + HALF_SLOTS
KEYS = 640
PAIRS = HEADS // 2
SLABS = 2
STEPS = PAIRS // SLABS
LANES = 128
FOLDS = 2
FOLD_HEADS = 2
BLOCKS = 4
HALF = BLOCKS // 2
norm_epsilon = 1e-05
NEVER = -1e30
bf16 = jnp.bfloat16
f32 = jnp.float32
MIB = 1 << 20
brief = pl.CostEstimate(flops=1, bytes_accessed=1, transcendentals=0)


def mesh_bits(axis):
    return (lax.axis_size(axis) - 1).bit_length()


def flipped(block, axis, bit):
    count = lax.axis_size(axis)
    return lax.ppermute(block, axis, [(i, i ^ (1 << bit)) for i in range(count)])


def total_over_all(value):
    for axis in ("tp", "seq"):
        for bit in range(mesh_bits(axis)):
            value = value + flipped(value, axis, bit)
    return value


def add_low(left, right):
    return (left.astype(f32) + right.astype(f32)).astype(bf16)


def tied(values, after):
    return lax.optimization_barrier((tuple(values), tuple(after)))[0]


class Shards:
    def __init__(self, near_keep, near_send, seq_keep, seq_send):
        self.near = near_keep
        self.seq = seq_keep
        self.near_came = flipped(near_send, "tp", 1)
        self.seq_came = flipped(seq_send, "seq", 0)

    def underway(self):
        return [self.near_came, self.seq_came]

    def second(self, *after):
        near, near_came, seq, seq_came = tied(
            (self.near, self.near_came, self.seq, self.seq_came), after
        )
        turn = lax.axis_index("seq") % 2
        middle = near.shape[-1] // 2
        pick = lambda block, which: jnp.where(
            turn == which, block[..., :middle], block[..., middle:]
        )
        self.near = add_low(pick(near, 0), pick(near_came, 0))
        self.near_came = flipped(add_low(pick(near, 1), pick(near_came, 1)), "seq", 0)
        far = seq.shape[0] // 2
        self.seq = add_low(seq[:far], seq_came[:far])
        self.seq_came = flipped(add_low(seq[far:], seq_came[far:]), "tp", 1)

    def arrived(self, *after):
        near, near_came, seq, seq_came = tied(
            (self.near, self.near_came, self.seq, self.seq_came), after
        )
        return add_low(near, near_came), add_low(seq, seq_came)

    def halve(self, *after):
        near, near_came, seq, seq_came = tied(
            (self.near, self.near_came, self.seq, self.seq_came), after
        )
        bit = mesh_bits("tp") - (near.shape[0] - 1).bit_length()
        pick = lambda block, which: block.reshape((-1, 2) + block.shape[1:])[:, which]
        add = lambda which: jnp.concatenate(
            [
                add_low(pick(near, which), pick(near_came, which)),
                add_low(pick(seq, which), pick(seq_came, which)),
            ],
            axis=1,
        )
        self.shard, self.came = add(0), flipped(add(1), "tp", bit)
        self.bit = bit + 1

    def halve_more(self, *after):
        shard, came = tied((self.shard, self.came), after)
        if shard.shape[0] == 1:
            self.shard = add_low(shard, came)[0]
            return
        pick = lambda block, which: block.reshape((-1, 2) + block.shape[1:])[:, which]
        self.shard = add_low(pick(shard, 0), pick(came, 0))
        self.came = flipped(add_low(pick(shard, 1), pick(came, 1)), "tp", self.bit)
        self.bit += 1

    def join(self, *after):
        (shard,) = tied((self.shard,), after)
        for bit in range(1, mesh_bits("seq")):
            shard = add_low(shard, flipped(shard, "seq", bit))
        self.shard = shard
        self.other = flipped(shard, "seq", 0)


class Scattered:
    def __init__(self, group, *after):
        parts = [part for shards in group for part in shards.arrived(*after)]
        columns = min(part.shape[-1] for part in parts)
        pieces = [
            part[..., start : start + columns]
            for part in parts
            for start in range(0, part.shape[-1], columns)
        ]
        count = lax.axis_size("tp")
        groups = [list(range(first, count, 4)) for first in range(4)]
        self.shard = lax.psum_scatter(
            jnp.concatenate(pieces, axis=1), "tp", scatter_dimension=0, axis_index_groups=groups
        )

    def join(self, *after):
        (shard,) = tied((self.shard,), after)
        for bit in range(1, mesh_bits("seq")):
            shard = add_low(shard, flipped(shard, "seq", bit))
        self.shard = shard
        self.other = flipped(shard, "seq", 0)


class Tree:
    def __init__(self, value, ways, join=None, add=add_low):
        self.lefts = [value]
        self.rights = []
        self.steps = list(ways) + ([join] if join else [])
        self.add = add

    def step(self, *after):
        if after:
            both = tied(self.lefts + self.rights, after)
            self.lefts, self.rights = list(both[:1]), list(both[1:])
        if self.rights:
            self.lefts = [self.add(self.lefts[0], self.rights[0])]
        self.rights = [flipped(self.lefts[0], *self.steps.pop(0))]

    def result(self):
        return self.lefts[0], self.rights[0]


def page_places(half, length, own_boxes, other_boxes):
    def slots(width, first, second):
        lane = lax.broadcasted_iota(jnp.int32, (1, width), 1)
        place = jnp.where(lane < HALF_SLOTS, first + lane, second + lane - HALF_SLOTS)
        place = jnp.where(lane < VIS_SLOTS, place, VIS_SLOTS - 1)
        row = (place * 37) >> 8
        return place, 71 + 143 * (place - 7 * row), 71 + 143 * row

    text = lax.broadcasted_iota(jnp.int32, (1, HALF_TEXT), 1)
    own_text = half * HALF_TEXT + text
    other_text = (1 - half) * HALF_TEXT + text
    slot = slots(LANES, half * HALF_SLOTS, (1 - half) * HALF_SLOTS)
    lane = lax.broadcasted_iota(jnp.int32, (1, LANES), 1)
    slot_used = jnp.where((slot[0] < VIS_TOK) & (lane < VIS_SLOTS), 1, 0)
    keys = (
        jnp.concatenate([own_text, other_text, slot[0]], axis=1),
        jnp.concatenate([own_boxes[0:1], other_boxes[0:1], slot[1]], axis=1),
        jnp.concatenate([own_boxes[1:2], other_boxes[1:2], slot[2]], axis=1),
        jnp.concatenate(
            [
                jnp.where(own_text < length, 1, 0),
                jnp.where(other_text < length, 1, 0),
                slot_used,
            ],
            axis=1,
        ),
    )
    queries = (
        jnp.concatenate([own_text, slot[0]], axis=1),
        jnp.concatenate([own_boxes[0:1], slot[1]], axis=1),
        jnp.concatenate([own_boxes[1:2], slot[2]], axis=1),
    )
    return keys, queries


def as_columns(rows):
    stacked = jnp.concatenate(list(rows) + [rows[0]] * (8 - len(rows)), axis=0)
    turned = jnp.transpose(stacked.astype(f32), (1, 0)).astype(jnp.int32)
    return [turned[:ROWS, i : i + 1] for i in range(len(rows))]


def bias_kernel(facts, own_boxes, other_boxes, table_a, table_b, out, near_s, across_s, down_s):
    @pl.when(pl.program_id(0) == 0)
    def _():
        keys, queries = page_places(facts[0], facts[1], own_boxes[...], other_boxes[...])
        place, x, y = as_columns(queries)
        near_s[...] = jnp.clip(keys[0] - place, -16, 15) + 16
        across_s[...] = jnp.clip((keys[1] - x) >> 4, -32, 31) + 64
        down_s[...] = jnp.where(
            keys[3] > 0, jnp.clip((keys[2] - y) >> 4, -32, 31) + 32, BOX_BINS
        )

    a = jnp.broadcast_to(table_a[0, 0:1, :], (ROWS, LANES))
    b = jnp.broadcast_to(table_b[0, 0:1, :], (ROWS, LANES))
    for tile in range(KEYS // LANES):
        span = slice(tile * LANES, (tile + 1) * LANES)

        def look(table, codes):
            return jnp.take_along_axis(table, codes, axis=1, mode="promise_in_bounds")

        out[0, :, span] = (
            look(a, near_s[:, span]) + look(a, across_s[:, span]) + look(b, down_s[:, span])
        )


def make_bias(facts, own_boxes, other_boxes, bias_table):
    columns = bias_table.T
    table_a = jnp.pad(columns[:, : POS_BINS + BOX_BINS], ((0, 0), (0, LANES - POS_BINS - BOX_BINS)))
    table_b = jnp.pad(
        columns[:, POS_BINS + BOX_BINS :],
        ((0, 0), (0, LANES - BOX_BINS)),
        constant_values=NEVER,
    )
    spread = lambda t: jnp.broadcast_to(t[:, None, :], (HEADS, 8, LANES))
    whole = lambda h, facts: (0, 0)
    return pl.pallas_call(
        bias_kernel,
        out_shape=jax.ShapeDtypeStruct((HEADS, ROWS, KEYS), f32),
        grid_spec=pltpu.PrefetchScalarGridSpec(
            num_scalar_prefetch=1,
            grid=(HEADS,),
            in_specs=[
                pl.BlockSpec((2, HALF_TEXT), whole),
                pl.BlockSpec((2, HALF_TEXT), whole),
                pl.BlockSpec((1, 8, LANES), lambda h, facts: (h, 0, 0)),
                pl.BlockSpec((1, 8, LANES), lambda h, facts: (h, 0, 0)),
            ],
            out_specs=pl.BlockSpec((1, ROWS, KEYS), lambda h, facts: (h, 0, 0)),
            scratch_shapes=[pltpu.VMEM((ROWS, KEYS), jnp.int32)] * 3,
        ),
        compiler_params=pltpu.CompilerParams(vmem_limit_bytes=50 * MIB),
        cost_estimate=brief,
        name="score_bias",
    )(facts, own_boxes, other_boxes, spread(table_a), spread(table_b))


def pairs_kernel(facts, own_boxes, other_boxes, right, left, masks):
    keys, queries = page_places(facts[0], facts[1], own_boxes[...], other_boxes[...])
    place, x, y = as_columns(queries)
    diff = keys[0] - place
    for index, holds in enumerate(
        (
            (diff >= -16) & (diff <= 15),
            (keys[1] & 15) < (x & 15),
            (keys[2] & 15) < (y & 15),
            diff > 15,
        )
    ):
        masks[index] = jnp.where(holds, 1.0, 0.0).astype(bf16)
    row = lax.broadcasted_iota(jnp.int32, (64, KEYS), 0)
    key_hot = [
        jnp.where((63 - row) == (code & 63), 1.0, 0.0)
        for code in (keys[1] >> 4, keys[2] >> 4, keys[0])
    ]
    key_hot.append(jnp.zeros((64, KEYS), f32))
    right[...] = jnp.transpose(jnp.concatenate(key_hot, axis=0), (1, 0)).astype(bf16)
    row = lax.broadcasted_iota(jnp.int32, (64, 384), 0)
    query_hot = [
        jnp.where(row == queries[1] >> 4, 1.0, 0.0),
        jnp.where(row == queries[2] >> 4, 1.0, 0.0),
        jnp.where(row[:32] + 64 == queries[2] >> 4, 1.0, 0.0),
        jnp.where(row == (queries[0] & 63), 1.0, 0.0),
    ]
    left[...] = jnp.concatenate(query_hot, axis=0)[:, :ROWS].astype(bf16)


def page_pairs(facts, own_boxes, other_boxes):
    vmem = pl.BlockSpec(memory_space=pltpu.VMEM)
    return pl.pallas_call(
        pairs_kernel,
        in_specs=[pl.BlockSpec(memory_space=pltpu.SMEM), vmem, vmem],
        out_specs=[vmem] * 3,
        out_shape=[
            jax.ShapeDtypeStruct((KEYS, 256), bf16),
            jax.ShapeDtypeStruct((224, ROWS), bf16),
            jax.ShapeDtypeStruct((4, ROWS, KEYS), bf16),
        ],
        compiler_params=pltpu.CompilerParams(vmem_limit_bytes=24 * MIB),
        cost_estimate=brief,
        name="page_pairs",
    )(facts, own_boxes, other_boxes)


def table_kernel(right, left, masks, ds_a, ds_b, *rest):
    for head in range(ds_a.shape[0]):
        fold_head(right, left, masks, ds_a[head], ds_b[head], rest[-1].at[head])


def fold_head(right, left, masks, ds_a, ds_b, out):
    total = (ds_a.astype(f32) + ds_b.astype(f32)).astype(bf16)
    hot = right[...]
    query_hot = left[...]

    def fold(values, columns, rows):
        inner = jnp.dot(values, hot[:, columns], preferred_element_type=f32).astype(bf16)
        return jnp.dot(query_hot[rows], inner, preferred_element_type=f32)

    near = fold(total * masks[0], slice(128, 256), slice(160, 224))
    together = jnp.concatenate([total, total * masks[1], total * masks[2]], axis=0)
    inner = jnp.dot(together, hot[:, :128], preferred_element_type=f32).astype(bf16)
    outer = lambda rows, which: jnp.dot(
        query_hot[rows], inner[which * ROWS : (which + 1) * ROWS], preferred_element_type=f32
    )
    plain = outer(slice(0, 160), 0)
    by_x = outer(slice(0, 64), 1)
    by_y = outer(slice(64, 160), 2)

    def diagonals(square):
        lane = lax.broadcasted_iota(jnp.int32, square.shape, 1)
        square = jnp.where(lane < 64, square, 0.0)
        turned = pltpu.roll(square, 0, axis=1, stride=1, stride_axis=0)
        return jnp.sum(turned, axis=0, keepdims=True)

    def second(square):
        return pltpu.roll(square, 64, axis=1)

    above = jnp.sum((total * masks[3]).astype(f32), axis=0, keepdims=True)
    above = sum(above[:, t * LANES : (t + 1) * LANES] for t in range(KEYS // LANES))
    out[...] = jnp.concatenate(
        [
            diagonals(plain[:64]),
            diagonals(by_x),
            diagonals(second(plain[64:128])),
            diagonals(second(by_y[:64])),
            diagonals(near),
            above,
            diagonals(second(plain[128:])),
            diagonals(second(by_y[64:])),
        ],
        axis=0,
    )


def table_bins():
    bins = np.zeros((8, LANES, BUCKETS), np.float32)
    for c in range(127):
        diff = 63 - c
        for kind, base in ((0, POS_BINS), (1, POS_BINS + BOX_BINS)):
            here = base + 32 + min(max(diff, -32), 31)
            below = base + 32 + min(max(diff - 1, -32), 31)
            bins[2 * kind, c, here] += 1
            bins[2 * kind + 1, c, below] += 1
            bins[2 * kind + 1, c, here] -= 1
        far = -1 - c
        bins[6, c, 128 + max(far, -32)] += 1
        bins[7, c, 128 + max(far - 1, -32)] += 1
        bins[7, c, 128 + max(far, -32)] -= 1
        near = (diff + 32) % 64 - 32
        if -16 <= near <= 15:
            bins[4, c, near + 16] += 1
        bins[0, c, 0] += 1
        bins[4, c, 0] -= 1
    bins[5, :, 31] += 1
    bins[5, :, 0] -= 1
    return bins


def fold_table(pairs, ds_a, ds_b, part, parts, after=()):
    count = HEADS // parts
    steps = count // FOLD_HEADS
    head = pl.BlockSpec((FOLD_HEADS, ROWS, KEYS), lambda h: (h + part * steps, 0, 0))
    return pl.pallas_call(
        table_kernel,
        out_shape=jax.ShapeDtypeStruct((count, 8, LANES), f32),
        grid=(steps,),
        in_specs=[full(array) for array in pairs]
        + [head, head]
        + [pl.BlockSpec(memory_space=pl.ANY)] * len(after),
        out_specs=pl.BlockSpec((FOLD_HEADS, 8, LANES), lambda h: (h, 0, 0)),
        compiler_params=pltpu.CompilerParams(vmem_limit_bytes=58 * MIB),
        cost_estimate=brief,
        name="table_grad",
    )(*pairs, ds_a, ds_b, *after)


def visual_kernel(half, grad_ref, normal_low, hat, weight, keep, send, normal_grad, sums):
    rows = normal_low.shape[0]
    column = lambda block: jnp.sum(block, axis=0, keepdims=True)
    token_grad = grad_ref[...].astype(bf16)
    whole = tn_dot(normal_low[...], token_grad)
    mid = whole.shape[0] // 2
    first = half[0] == 0
    keep[...] = jnp.where(first, whole[:mid], whole[mid:]).astype(bf16)
    send[...] = jnp.where(first, whole[mid:], whole[:mid]).astype(bf16)
    place = half[0] * rows + lax.broadcasted_iota(jnp.int32, (rows, 1), 0)
    grad = jnp.where(place < VIS_TOK, nt_dot(token_grad, weight[...]), 0.0)
    normal_grad[...] = grad
    total = column(token_grad.astype(f32))
    put_row(sums, 0, total)
    at = total.shape[1] // LANES
    count = grad.shape[1] // LANES
    put_row(sums.at[at : at + count], 0, column(grad * hat[...]))
    put_row(sums.at[at + count : at + 2 * count], 0, column(grad))


def visual_back(half, gradient, normal_low, hat, weight):
    slots, channels = normal_low.shape
    width = weight.shape[1]
    return pl.pallas_call(
        visual_kernel,
        grid_spec=pltpu.PrefetchScalarGridSpec(
            num_scalar_prefetch=1,
            grid=(1,),
            in_specs=[
                pl.BlockSpec(
                    (slots, width), lambda i, half: (gradient.shape[0] // slots - 1, 0)
                ),
                full(normal_low),
                full(hat),
                full(weight),
            ],
            out_specs=[
                pl.BlockSpec((channels // 2, width), lambda i, half: (0, 0)),
                pl.BlockSpec((channels // 2, width), lambda i, half: (0, 0)),
                pl.BlockSpec((slots, channels), lambda i, half: (0, 0)),
                pl.BlockSpec(((width + 2 * channels) // LANES, LANES), lambda i, half: (0, 0)),
            ],
        ),
        out_shape=[
            jax.ShapeDtypeStruct((channels // 2, width), bf16),
            jax.ShapeDtypeStruct((channels // 2, width), bf16),
            jax.ShapeDtypeStruct((slots, channels), f32),
            jax.ShapeDtypeStruct(((width + 2 * channels) // LANES, LANES), f32),
        ],
        cost_estimate=brief,
        name="visual_back",
    )(half, gradient, normal_low, hat, weight)


def join_kernel(*refs):
    low, out = refs[-2:]
    out[...] = jnp.zeros_like(out)
    at = 0
    for ref in refs[:-2]:
        values = ref[...]
        if len(values.shape) == 3 and values.shape[1] > 1:
            for head in range(values.shape[0]):
                out[at : at + values.shape[1], :] = values[head]
                at += values.shape[1]
        elif len(values.shape) == 3:
            for group in range(values.shape[0]):
                for start in range(0, values.shape[2], LANES):
                    size = min(LANES, values.shape[2] - start)
                    out[at : at + 1, :size] = ref[group, :, start : start + size]
                    at += 1
        else:
            out[at : at + values.shape[0], :] = values
            at += values.shape[0]
    low[...] = out[...].astype(bf16)


def bin_rows(units):
    return -(-units // LANES)


def join(parts):
    rows = 0
    for part in parts:
        if part.ndim == 3 and part.shape[1] == 1:
            rows += part.shape[0] * bin_rows(part.shape[2])
        else:
            rows += part.size // LANES
    rows += -rows % 16
    vmem = pl.BlockSpec(memory_space=pltpu.VMEM)
    return pl.pallas_call(
        join_kernel,
        out_shape=jax.ShapeDtypeStruct((rows, LANES), bf16),
        in_specs=[vmem] * len(parts),
        out_specs=vmem,
        scratch_shapes=[pltpu.VMEM((rows, LANES), f32)],
        cost_estimate=brief,
        name="join",
    )(*parts)


def split_kernel(
    sizes,
    count,
    me,
    left,
    right,
    bins,
    normal_grad,
    hat,
    inverse_std,
    bn_gain,
    attn,
    out_bias,
    gain,
    shift,
    table,
    vis_bias,
    gain_grad,
    shift_grad,
    hidden_bias,
    maps,
    total,
):
    total[...] = left[...].astype(f32) + right[...].astype(f32)
    units = hidden_bias.shape[1]
    width = out_bias.shape[1]
    channels = gain_grad.shape[1]
    starts = [0]
    for size in sizes:
        starts.append(starts[-1] + size)

    def take(start, index, wide):
        per = wide // LANES
        begin = start + index * per
        return jnp.concatenate([total[begin + i : begin + i + 1, :] for i in range(per)], axis=1)

    for layer in range(LAYERS):
        norm = functools.partial(take, starts[layer])
        gain[layer, 1:2, :] = norm(0, width)
        shift[layer, 1:2, :] = norm(1, width)
        out_bias[layer : layer + 1, :] = norm(2, width)
        gain[layer, 0:1, :] = norm(3, width)
        shift[layer, 0:1, :] = norm(4, width)
        attn[2, layer : layer + 1, :] = norm(5, width)
        rows = functools.partial(take, starts[LAYERS + layer])
        attn[0, layer : layer + 1, :] = rows(0, width)
        attn[1, layer : layer + 1, :] = rows(1, width)
        per = bin_rows(units)
        begin = starts[2 * LAYERS + layer] + me[0] * per
        for part in range(per):
            span = min(LANES, units - part * LANES)
            hidden_bias[layer : layer + 1, part * LANES : part * LANES + span] = total[
                pl.ds(begin + part, 1), :span
            ]
    at = starts[3 * LAYERS]
    vis_bias[...] = total[at : at + width // LANES, :]
    at += width // LANES
    by_gain = take(at, 0, channels)
    by_shift = take(at, 1, channels)
    gain_grad[...] = by_gain
    shift_grad[...] = by_shift
    scale = inverse_std[...] * bn_gain[...]
    slots = normal_grad.shape[0]
    place = (me[0] & 1) * slots + lax.broadcasted_iota(jnp.int32, (slots, 1), 0)
    maps[...] = jnp.where(
        place < VIS_TOK,
        scale * (normal_grad[...] - by_shift / count - hat[...] * (by_gain / count)),
        0.0,
    )
    at = starts[3 * LAYERS + 1]
    folded = jnp.zeros((16, BUCKETS), f32)
    for kind in range(8):
        rows = jnp.concatenate(
            [total[at + 8 * head + kind : at + 8 * head + kind + 1, :] for head in range(HEADS)]
            + [jnp.zeros((16 - HEADS, LANES), f32)],
            axis=0,
        )
        high = rows.astype(bf16)
        middle = (rows - high.astype(f32)).astype(bf16)
        low = (rows - high.astype(f32) - middle.astype(f32)).astype(bf16)
        for part in (high, middle, low):
            folded = folded + nt_dot(part, bins[kind])
    table[...] = folded[:HEADS]


def split(me, left, right, sizes, count, normal_grad, hat, inverse_std, bn_gain, units, width):
    slots, channels = normal_grad.shape
    bins = jnp.asarray(table_bins().transpose(0, 2, 1), bf16)
    row = lambda value: value.reshape(1, -1)
    vmem = pl.BlockSpec(memory_space=pltpu.VMEM)
    shape = lambda *size: jax.ShapeDtypeStruct(size, f32)
    return pl.pallas_call(
        functools.partial(split_kernel, sizes, count),
        in_specs=[pl.BlockSpec(memory_space=pltpu.SMEM)] + [vmem] * 7,
        out_specs=[vmem] * 10,
        out_shape=[
            shape(3, LAYERS, width),
            shape(LAYERS, width),
            shape(LAYERS, 2, width),
            shape(LAYERS, 2, width),
            shape(HEADS, BUCKETS),
            shape(width // LANES, LANES),
            shape(1, channels),
            shape(1, channels),
            shape(LAYERS, units),
            shape(slots, channels),
        ],
        scratch_shapes=[pltpu.VMEM(left.shape, f32)],
        cost_estimate=brief,
        name="split",
    )(me, left, right, bins, normal_grad, hat, row(inverse_std), row(bn_gain))


def whole_page(own, other):
    return jnp.concatenate(
        [
            own[:HALF_TEXT],
            other[:HALF_TEXT],
            own[HALF_TEXT:],
            other[HALF_TEXT:],
            jnp.zeros((KEYS - 2 * ROWS, own.shape[1]), own.dtype),
        ],
        axis=0,
    )


def page_split(both):
    mid = 2 * HALF_TEXT
    own = jnp.concatenate([both[:HALF_TEXT], both[mid : mid + HALF_SLOTS]], axis=0)
    other = jnp.concatenate(
        [both[HALF_TEXT:mid], both[mid + HALF_SLOTS : mid + VIS_SLOTS]], axis=0
    )
    return own, other


def nt_dot(left, right):
    return lax.dot_general(left, right, (((1,), (1,)), ((), ())), preferred_element_type=f32)


def tn_dot(left, right):
    return lax.dot_general(left, right, (((0,), (0,)), ((), ())), preferred_element_type=f32)


def put_row(target, index, row):
    count = row.shape[1] // LANES
    for part in range(count):
        at = index * count + part
        target[at : at + 1, :] = row[:, part * LANES : (part + 1) * LANES]


def centred(values):
    center = values - jnp.mean(values, axis=1, keepdims=True)
    spread = jnp.mean(center * center, axis=1, keepdims=True)
    rate = lax.rsqrt(spread + norm_epsilon)
    return center * rate, rate


def norm_back(grad, values, gain_row):
    hat, rate = centred(values)
    scaled = grad * gain_row
    mean = jnp.mean(scaled, axis=1, keepdims=True)
    along = jnp.mean(scaled * hat, axis=1, keepdims=True)
    column = lambda block: jnp.sum(block, axis=0, keepdims=True)
    return rate * (scaled - mean - hat * along), column(grad * hat), column(grad)


def attend_kernel(
    layer,
    q_ref,
    ko,
    kp,
    vo,
    vp,
    bias,
    x_ref,
    weight,
    attn_bias,
    gain,
    shift,
    soft,
    pair,
    residual,
    normed,
    x_s,
    weight_s,
    semaphores,
):
    step = pl.program_id(0)
    later = Later([(x_ref, x_s), (weight.at[layer], weight_s)], semaphores)
    pl.when(step == 0)(later.start)
    first = lax.broadcasted_iota(jnp.int32, (ROWS, LANES), 1) < HEAD_DIM
    for part in range(SLABS):
        lanes = slice(part * LANES, (part + 1) * LANES)
        q = q_ref[:, lanes] * jnp.asarray(HEAD_DIM**-0.5, bf16)
        keys = whole_page(ko[:, lanes], kp[:, lanes])
        values = whole_page(vo[:, lanes], vp[:, lanes])
        found = []
        for head in range(2):
            mine = jnp.where(first if head == 0 else ~first, q, jnp.zeros_like(q))
            scores = nt_dot(mine, keys) + bias[2 * part + head]
            raised = jnp.exp(scores - jnp.max(scores, axis=1, keepdims=True))
            weights = (raised * (1.0 / jnp.sum(raised, axis=1, keepdims=True))).astype(bf16)
            soft[2 * part + head] = weights
            found.append(jnp.dot(weights, values, preferred_element_type=f32))
        slab = pl.ds(pl.multiple_of((step * SLABS + part) * LANES, LANES), LANES)
        pair[0, :, slab] = jnp.where(first, found[0], found[1]).astype(bf16)

    @pl.when(step == STEPS - 1)
    def _():
        later.wait(0, 1)
        attended = jnp.dot(pair[0], weight_s[...], preferred_element_type=f32)
        summed = x_s[...] + (attended + attn_bias[layer, 2:3, :])
        residual[...] = summed
        out = centred(summed)[0] * gain[layer, 0:1, :] + shift[layer, 0:1, :]
        normed[...] = out
        pair[1] = out.astype(bf16)


class Later:
    def __init__(self, pairs, semaphores):
        self.copies = [
            pltpu.make_async_copy(source, target, semaphores.at[index])
            for index, (source, target) in enumerate(pairs)
        ]

    def start(self):
        for copy in self.copies:
            copy.start()

    def wait(self, *indices):
        for index in indices:
            self.copies[index].wait()


anywhere = pl.BlockSpec(memory_space=pl.ANY)


def full(array):
    return pl.BlockSpec(array.shape, lambda *at: (0,) * array.ndim)


def attend(layer, q, kv, other_kv, bias, x, out_weight, attn_bias, gain, shift):
    rows, width = q.shape
    slab = pl.BlockSpec((ROWS, SLABS * LANES), lambda p: (0, p))
    second = pl.BlockSpec((ROWS, SLABS * LANES), lambda p: (0, p + STEPS))
    heads = pl.BlockSpec((2 * SLABS, ROWS, KEYS), lambda p: (p, 0, 0))
    whole = pl.BlockSpec((rows, width), lambda p: (0, 0))
    wide = jax.ShapeDtypeStruct((rows, width), f32)
    low = jax.ShapeDtypeStruct((2, rows, width), bf16)
    return pl.pallas_call(
        functools.partial(attend_kernel, layer),
        grid=(STEPS,),
        in_specs=[
            slab,
            slab,
            slab,
            second,
            second,
            heads,
            anywhere,
            anywhere,
            full(attn_bias),
            full(gain),
            full(shift),
        ],
        out_specs=[
            heads,
            pl.BlockSpec((2, rows, width), lambda p: (0, 0, 0)),
            whole,
            whole,
        ],
        out_shape=[jax.ShapeDtypeStruct((HEADS, ROWS, KEYS), bf16), low, wide, wide],
        scratch_shapes=[
            pltpu.VMEM((rows, width), f32),
            pltpu.VMEM((width, width), bf16),
            pltpu.SemaphoreType.DMA((2,)),
        ],
        compiler_params=pltpu.CompilerParams(vmem_limit_bytes=50 * MIB),
        cost_estimate=brief,
        name="attend",
    )(q, kv, other_kv, kv, other_kv, bias, x, out_weight, attn_bias, gain, shift)


def attend_back_kernel(q_ref, ko, kp, vo, vp, dc_ref, soft, *rest):
    ds, *grads = rest[-6:]
    scale = HEAD_DIM**-0.5
    first = lax.broadcasted_iota(jnp.int32, (ROWS, LANES), 1) < HEAD_DIM
    for part in range(SLABS):
        lanes = slice(part * LANES, (part + 1) * LANES)
        q = q_ref[:, lanes]
        dc = dc_ref[:, lanes]
        keys = whole_page(ko[:, lanes], kp[:, lanes])
        values = whole_page(vo[:, lanes], vp[:, lanes])
        q_turned = jnp.transpose(q.astype(f32), (1, 0)).astype(bf16)
        dc_turned = jnp.transpose(dc.astype(f32), (1, 0)).astype(bf16)
        dq_parts, dk_parts, dv_parts = [], [], []
        for head in range(2):
            span = slice(head * HEAD_DIM, (head + 1) * HEAD_DIM)
            mine = jnp.where(first if head == 0 else ~first, dc, jnp.zeros_like(dc))
            weights = soft[2 * part + head]
            weights_f = weights.astype(f32)
            flow = nt_dot(mine, values)
            share = jnp.sum(weights_f * flow, axis=1, keepdims=True)
            score_grad = (weights_f * (flow - share)).astype(bf16)
            ds[2 * part + head] = score_grad
            dq_parts.append(jnp.dot(score_grad, keys, preferred_element_type=f32))
            dk_parts.append(jnp.dot(q_turned[span], score_grad, preferred_element_type=f32))
            dv_parts.append(jnp.dot(dc_turned[span], weights, preferred_element_type=f32))
        grads[0][:, lanes] = (jnp.where(first, dq_parts[0], dq_parts[1]) * scale).astype(bf16)
        own, other = page_split(jnp.transpose(jnp.concatenate(dk_parts, axis=0) * scale, (1, 0)))
        grads[1][:, lanes] = own.astype(bf16)
        grads[2][:, lanes] = other.astype(bf16)
        own, other = page_split(jnp.transpose(jnp.concatenate(dv_parts, axis=0), (1, 0)))
        grads[3][:, lanes] = own.astype(bf16)
        grads[4][:, lanes] = other.astype(bf16)


def attend_back(q, kv, other_kv, dctx, soft, after=()):
    slab = pl.BlockSpec((ROWS, SLABS * LANES), lambda p: (0, p))
    second = pl.BlockSpec((ROWS, SLABS * LANES), lambda p: (0, p + STEPS))
    heads = pl.BlockSpec((2 * SLABS, ROWS, KEYS), lambda p: (p, 0, 0))
    return pl.pallas_call(
        attend_back_kernel,
        grid=(STEPS,),
        in_specs=[slab, slab, slab, second, second, slab, heads]
        + [pl.BlockSpec(memory_space=pl.ANY)] * len(after),
        out_specs=[heads] + [slab] * 5,
        out_shape=[
            jax.ShapeDtypeStruct((HEADS, ROWS, KEYS), bf16),
        ]
        + [jax.ShapeDtypeStruct(q.shape, bf16)] * 5,
        compiler_params=pltpu.CompilerParams(vmem_limit_bytes=50 * MIB),
        cost_estimate=brief,
        name="attend_back",
    )(q, kv, other_kv, kv, other_kv, dctx, soft, *after)


def ffn_kernel(layer, more, me, x_ref, *refs):
    step = pl.program_id(0)
    width = x_ref.shape[1]
    blocks, (bias, n_ref, out_bias, gain, shift), rest = refs[:BLOCKS], refs[BLOCKS:][:5], refs[BLOCKS + 5 :]
    units = blocks[0].shape[1]
    if more:
        weight, attn_bias, *rest, weight_s, semaphores = rest
        later = Later([(weight.at[layer + 1], weight_s)], semaphores)
        pl.when(step == 0)(later.start)
    own_act, mate_act, slope, residual = rest[:4]
    x = x_ref[...]

    total = None
    for index, block in enumerate(blocks):
        weights = block[0]
        row = bias[pl.ds(BLOCKS * step + index, 1), layer, :]
        hidden = nt_dot(x, weights[:, :width]) + row
        half_cdf = 0.5 + 0.5 * lax.erf(hidden * 0.5**0.5)
        low = (hidden * half_cdf).astype(bf16)
        (mate_act if index % 2 else own_act)[index // 2] = low
        density = jnp.exp(hidden * hidden * -0.5) * (1.0 / (2.0 * np.pi) ** 0.5)
        slope[index] = (half_cdf + hidden * density).astype(bf16)
        term = jnp.dot(low, weights[:, width:], preferred_element_type=f32)
        total = term if total is None else total + term

    @pl.when(step == 0)
    def _():
        residual[...] = n_ref[...] + out_bias[layer : layer + 1, :] + total

    @pl.when(step > 0)
    def _():
        residual[...] += total

    @pl.when(step == pl.num_programs(0) - 1)
    def _():
        states = centred(residual[...])[0] * gain[layer, 1:2, :] + shift[layer, 1:2, :]
        rounded = states.astype(bf16)
        if more:
            wide, query, shared = rest[-3:]
            wide[...] = states
            later.wait(0)
            project = lambda index: jnp.dot(
                rounded, weight_s[index], preferred_element_type=f32
            )
            query[...] = (project(0) + attn_bias[layer + 1, 0:1, :]).astype(bf16)
            shared[:, :width] = project(1).astype(bf16)
            shared[:, width : 2 * width] = (
                project(2) + attn_bias[layer + 1, 1:2, :]
            ).astype(bf16)
            shared[:, 2 * width :] = rounded
        else:
            rest[-1][...] = rounded


def weight_blocks(layer, units, width):
    pick = lambda which: pl.BlockSpec(
        (1, units, 2 * width), lambda i, me: (me[0] ^ (BLOCKS * i + which), layer, 0)
    )
    return [pick(which) for which in range(BLOCKS)]


def ffn(me, layer, pair, n, gathered, bias, out_bias, gain, shift, qkv_weight, attn_bias):
    groups, _, units = bias.shape
    rows, width = n.shape
    more = layer < LAYERS - 1
    whole = pl.BlockSpec((rows, width), lambda i, me: (0, 0))
    kept = pl.BlockSpec((BLOCKS, rows, units), lambda i, me: (i, 0, 0))
    kept_shape = jax.ShapeDtypeStruct((groups, rows, units), bf16)
    wide = jax.ShapeDtypeStruct((rows, width), f32)
    low = jax.ShapeDtypeStruct((rows, width), bf16)
    half_act = pl.BlockSpec((HALF, rows, units), lambda i, me: (i, 0, 0))
    half_shape = jax.ShapeDtypeStruct((groups // 2, rows, units), bf16)
    inputs = [pair] + [gathered] * BLOCKS + [bias, n, out_bias, gain, shift]
    in_specs = [
        pl.BlockSpec((None, rows, width), lambda i, me: (1, 0, 0)),
        *weight_blocks(layer, units, width),
        full(bias),
        whole,
        full(out_bias),
        full(gain),
        full(shift),
    ]
    out_specs = [half_act, half_act, kept, whole]
    out_shape = [half_shape, half_shape, kept_shape, wide]
    if more:
        inputs += [qkv_weight, attn_bias]
        in_specs += [
            anywhere,
            full(attn_bias),
        ]
        out_specs += [whole, whole, pl.BlockSpec((rows, 3 * width), lambda i, me: (0, 0))]
        out_shape += [wide, low, jax.ShapeDtypeStruct((rows, 3 * width), bf16)]
    else:
        out_specs += [whole]
        out_shape += [low]
    return pl.pallas_call(
        functools.partial(ffn_kernel, layer, more),
        out_shape=out_shape,
        grid_spec=pltpu.PrefetchScalarGridSpec(
            num_scalar_prefetch=1,
            grid=(groups // BLOCKS,),
            in_specs=in_specs,
            out_specs=out_specs,
            scratch_shapes=[
                pltpu.VMEM((3, width, width), bf16),
                pltpu.SemaphoreType.DMA((1,)),
            ]
            if more
            else [],
        ),
        compiler_params=pltpu.CompilerParams(vmem_limit_bytes=50 * MIB),
        cost_estimate=brief,
        name="feed_forward",
    )(me, *inputs)


def ffn_back_kernel(layer, me, grad_ref, r2_ref, r1_ref, *refs):
    blocks, (slope, gain, out_weight), rest = refs[:BLOCKS], refs[BLOCKS:][:3], refs[BLOCKS + 3 :]
    own_dh, mate_dh, low_grads, bias_grad, sums, dx, dctx, total_s, r1_s, weight_s, semaphores = rest
    later = Later([(r1_ref, r1_s), (out_weight.at[layer], weight_s)], semaphores)
    step = pl.program_id(0)
    width = r2_ref.shape[1]
    column = lambda block: jnp.sum(block, axis=0, keepdims=True)

    @pl.when(step == 0)
    def _():
        later.start()
        grad, gain_grad, shift_grad = norm_back(
            grad_ref[...].astype(f32), r2_ref[...], gain[layer, 1:2, :]
        )
        low = grad.astype(bf16)
        total_s[...] = grad
        low_grads[0] = low
        put_row(sums, 0, gain_grad)
        put_row(sums, 1, shift_grad)
        put_row(sums, 2, column(low.astype(f32)))

    dy = low_grads[0]
    total = None
    for index, block in enumerate(blocks):
        weights = block[0]
        flow = nt_dot(dy, weights[:, width:])
        grad = (flow * slope[index].astype(f32)).astype(bf16)
        (mate_dh if index % 2 else own_dh)[index // 2] = grad
        bias_grad[index ^ (me[0] & (BLOCKS - 1))] = column(grad.astype(f32))
        term = jnp.dot(grad, weights[:, :width], preferred_element_type=f32)
        total = term if total is None else total + term
    total_s[...] += total

    @pl.when(step == pl.num_programs(0) - 1)
    def _():
        later.wait(0, 1)
        grad, gain_grad, shift_grad = norm_back(total_s[...], r1_s[...], gain[layer, 0:1, :])
        low = grad.astype(bf16)
        dx[...] = grad
        low_grads[1] = low
        dctx[...] = nt_dot(low, weight_s[...]).astype(bf16)
        put_row(sums, 3, gain_grad)
        put_row(sums, 4, shift_grad)
        put_row(sums, 5, column(low.astype(f32)))


def ffn_back(me, layer, grad, r2, r1, gathered, slope, gain, out_weight):
    groups, rows, units = slope.shape
    width = r2.shape[1]
    whole = pl.BlockSpec((rows, width), lambda i, me: (0, 0))
    half = pl.BlockSpec((HALF, rows, units), lambda i, me: (i, 0, 0))
    half_shape = jax.ShapeDtypeStruct((groups // 2, rows, units), bf16)
    return pl.pallas_call(
        functools.partial(ffn_back_kernel, layer),
        out_shape=[
            half_shape,
            half_shape,
            jax.ShapeDtypeStruct((2, rows, width), bf16),
            jax.ShapeDtypeStruct((groups, 1, units), f32),
            jax.ShapeDtypeStruct((6 * width // LANES, LANES), f32),
            jax.ShapeDtypeStruct((rows, width), f32),
            jax.ShapeDtypeStruct((rows, width), bf16),
        ],
        grid_spec=pltpu.PrefetchScalarGridSpec(
            num_scalar_prefetch=1,
            grid=(groups // BLOCKS,),
            in_specs=[
                whole,
                whole,
                anywhere,
                *weight_blocks(layer, units, width),
                pl.BlockSpec((BLOCKS, rows, units), lambda i, me: (i, 0, 0)),
                full(gain),
                anywhere,
            ],
            out_specs=[
                half,
                half,
                pl.BlockSpec((2, rows, width), lambda i, me: (0, 0, 0)),
                pl.BlockSpec((BLOCKS, 1, units), lambda i, me: (me[0] // BLOCKS ^ i, 0, 0)),
                pl.BlockSpec((6 * width // LANES, LANES), lambda i, me: (0, 0)),
                whole,
                whole,
            ],
            scratch_shapes=[
                pltpu.VMEM((rows, width), f32),
                pltpu.VMEM((rows, width), f32),
                pltpu.VMEM((width, width), bf16),
                pltpu.SemaphoreType.DMA((2,)),
            ],
        ),
        compiler_params=pltpu.CompilerParams(vmem_limit_bytes=50 * MIB),
        cost_estimate=brief,
        name="feed_forward_back",
    )(me, grad, r2, r1, *[gathered] * BLOCKS, slope, gain, out_weight)


def ffn_grads_kernel(me, n, n_mate, dy, dy_mate, dh, dh_mate, act, act_mate, *rest):
    near_keep, near_send, seq_keep, seq_send, n_s, dy_s = rest[-6:]
    rows, width = n.shape
    far, units = near_keep.shape[:2]
    step = pl.program_id(0)

    @pl.when(step == 0)
    def _():
        for target, own, mate in ((n_s, n, n_mate), (dy_s, dy, dy_mate)):
            target[:rows] = own[...]
            target[rows:] = mate[...]

    def product(own, mate, right):
        turned = [
            jnp.transpose(jnp.concatenate([own[i, 0], mate[i, 0]], axis=0), (1, 0))
            for i in range(far)
        ]
        return jnp.dot(
            jnp.concatenate(turned, axis=0), right[...], preferred_element_type=f32
        ).astype(bf16)

    def put(target, values):
        for i in range(far):
            target[(me[0] >> 2) ^ i] = values[i * units : (i + 1) * units]

    into = product(dh, dh_mate, n_s)
    pl.when(step == 0)(lambda: put(near_keep, into))
    pl.when(step == 1)(lambda: put(near_send, into))
    out = product(act, act_mate, dy_s)
    turn = me[1] % 2 == 0
    put(seq_keep, jnp.where(turn, out[:, : width // 2], out[:, width // 2 :]))
    put(seq_send, jnp.where(turn, out[:, width // 2 :], out[:, : width // 2]))


def ffn_grads(me, pair, pair_mate, low_grads, low_grads_mate, dh, dh_mate, act, act_mate):
    groups, rows, units = dh.shape
    width = pair.shape[2]
    far = groups // 2
    row_block = lambda which: pl.BlockSpec((None, rows, width), lambda i, me: (which, 0, 0))
    hidden = pl.BlockSpec((far, 1, rows, units), lambda i, me: (0, i, 0, 0))
    near_shape = jax.ShapeDtypeStruct((far, units, width), bf16)
    near_block = pl.BlockSpec((far, units, width), lambda i, me: (0, 0, 0))
    seq_shape = jax.ShapeDtypeStruct((groups, units, width // 2), bf16)
    seq_block = pl.BlockSpec((far, units, width // 2), lambda i, me: (i, 0, 0))
    by_far = lambda block: block.reshape(far, 2, rows, units)
    return pl.pallas_call(
        ffn_grads_kernel,
        out_shape=[near_shape, near_shape, seq_shape, seq_shape],
        grid_spec=pltpu.PrefetchScalarGridSpec(
            num_scalar_prefetch=1,
            grid=(2,),
            in_specs=[row_block(1), row_block(1), row_block(0), row_block(0)] + [hidden] * 4,
            out_specs=[near_block, near_block, seq_block, seq_block],
            scratch_shapes=[pltpu.VMEM((2 * rows, width), bf16)] * 2,
        ),
        compiler_params=pltpu.CompilerParams(vmem_limit_bytes=50 * MIB),
        cost_estimate=brief,
        name="feed_forward_grads",
    )(
        me,
        pair,
        pair_mate,
        low_grads,
        low_grads_mate,
        *[by_far(block) for block in (dh, dh_mate, act, act_mate)],
    )


def projection_kernel(by_distance, me, x, x_mate, ctx, ctx_mate, *refs):
    own, mate, refs = refs[:5], refs[5:10], refs[10:]
    da, da_mate, dr_ref, weight = refs[:4]
    near_keep, near_send, seq_keep, seq_send, dx, sums = refs[-11:-5]
    turned_s, picked_s, left_s, right_s, shards_s = refs[-5:]
    step = pl.program_id(0)
    far, shard = near_keep.shape[:2]
    rows, width = x.shape
    column = lambda block: jnp.sum(block.astype(f32), axis=0, keepdims=True)

    def place_of(place, near):
        far_place = (me[0] >> 2) ^ place if by_distance else place
        return far_place * 4 + ((me[0] & 3) ^ (2 * near))

    gap = -rows % LANES
    mate_rows = slice(rows + gap, 2 * rows + gap)

    def pick_left(first, second):
        for block, at_rows in ((first, slice(0, rows)), (second, mate_rows)):
            turned_s[...] = jnp.transpose(block[...].astype(f32), (1, 0))
            for near in range(2):
                for place in range(far):
                    start = pl.multiple_of(place_of(place, near) * shard, 8)
                    at = (near * far + place) * shard
                    picked_s[at : at + shard, at_rows] = turned_s[pl.ds(start, shard), :]
        left_s[...] = picked_s[...].astype(bf16)

    @pl.when(step == 0)
    def _():
        dx[...] = dr_ref[...]
        picked_s[:, rows : rows + gap] = jnp.zeros((width // 2, gap), f32)
        right_s[rows : rows + gap] = jnp.zeros((gap, width), bf16)
        pick_left(x, x_mate)
        right_s[:rows] = own[0][...]
        right_s[mate_rows] = mate[0][...]
        put_row(sums, 0, column(own[0][...]))

    for index in (1, 2):

        @pl.when(step == index)
        def _():
            right_s[:rows] = add_low(own[2 * index - 1][...], mate[2 * index][...])
            right_s[mate_rows] = add_low(mate[2 * index - 1][...], own[2 * index][...])

    @pl.when(step == 2)
    def _():
        put_row(sums, 1, column(right_s[:rows]))

    @pl.when(step < 3)
    def _():
        dx[...] += nt_dot(right_s[:rows], weight[0, 0])

    @pl.when(step == 3)
    def _():
        pick_left(ctx, ctx_mate)
        right_s[:rows] = da[...]
        right_s[mate_rows] = da_mate[...]

    shards_s[...] = jnp.dot(left_s[...], right_s[...], preferred_element_type=f32)

    def put(target, first, near, columns):
        for place in range(far):
            at = (near * far + place) * shard
            target[first + place, :, columns] = shards_s[at : at + shard, :].astype(bf16)

    for index in range(2):

        @pl.when(step == index)
        def _():
            columns = slice(index * width, (index + 1) * width)
            put(near_keep, 0, 0, columns)
            put(near_send, 0, 1, columns)

    def put_seq(target):
        put(target, 0, 0, slice(None))
        put(target, far, 1, slice(None))

    mine = step - 2 == me[1] % 2
    pl.when((step >= 2) & mine)(lambda: put_seq(seq_keep))
    pl.when((step >= 2) & jnp.logical_not(mine))(lambda: put_seq(seq_send))


def projection_grads(
    by_distance,
    me,
    layer,
    shared,
    shared_mate,
    pair,
    pair_mate,
    own,
    mate,
    low,
    low_mate,
    dr,
    weight,
    after=(),
):
    rows, width = dr.shape
    groups = lax.axis_size("tp")
    shard = width // groups
    whole = pl.BlockSpec((rows, width), lambda t, me: (0, 0))
    x_block = pl.BlockSpec((rows, width), lambda t, me: (0, 2))
    layered = lambda which: pl.BlockSpec((None, rows, width), lambda t, me: (which, 0, 0))
    near_shape = jax.ShapeDtypeStruct((groups // 4, shard, 2 * width), bf16)
    near_block = pl.BlockSpec(near_shape.shape, lambda t, me: (0, 0, 0))
    seq_shape = jax.ShapeDtypeStruct((groups // 2, shard, width), bf16)
    seq_block = pl.BlockSpec(seq_shape.shape, lambda t, me: (0, 0, 0))
    return pl.pallas_call(
        functools.partial(projection_kernel, by_distance),
        out_shape=[near_shape, near_shape, seq_shape, seq_shape]
        + [
            jax.ShapeDtypeStruct((rows, width), f32),
            jax.ShapeDtypeStruct((2 * width // LANES, LANES), f32),
        ],
        grid_spec=pltpu.PrefetchScalarGridSpec(
            num_scalar_prefetch=1,
            grid=(4,),
            in_specs=[
                x_block,
                x_block,
                layered(0),
                layered(0),
                *[whole] * 10,
                layered(1),
                layered(1),
                whole,
                pl.BlockSpec(
                    (1, 1, width, width), lambda t, me: (layer, jnp.minimum(t, 2), 0, 0)
                ),
            ]
            + [pl.BlockSpec(memory_space=pl.ANY)] * len(after),
            out_specs=[near_block, near_block, seq_block, seq_block]
            + [
                whole,
                pl.BlockSpec((2 * width // LANES, LANES), lambda t, me: (0, 0)),
            ],
            scratch_shapes=[
                pltpu.VMEM((width, rows), f32),
                pltpu.VMEM((width // 2, 2 * rows + -rows % LANES), f32),
                pltpu.VMEM((width // 2, 2 * rows + -rows % LANES), bf16),
                pltpu.VMEM((2 * rows + -rows % LANES, width), bf16),
                pltpu.VMEM((width // 2, width), f32),
            ],
        ),
        compiler_params=pltpu.CompilerParams(vmem_limit_bytes=50 * MIB),
        cost_estimate=brief,
        name="projection_grads",
    )(
        me,
        shared,
        shared_mate,
        pair,
        pair_mate,
        *own,
        *mate,
        low,
        low_mate,
        dr,
        weight,
        *after,
    )


def ordered(turn, mine, other):
    return jnp.where(turn, mine, other), jnp.where(turn, other, mine)


def stacked_parts(block, start, rows, count):
    return jnp.concatenate(
        [block[start + i * rows : start + (i + 1) * rows] for i in range(count)], axis=1
    )


def projection_out_kernel(starts, me, *refs):
    qkv, out = refs[-2:]
    rows, width = out.shape[1:]
    for layer in range(LAYERS):
        mine, other = refs[2 * layer : 2 * layer + 2]
        count = width // mine.shape[1]
        first, second = ordered(me[1] % 2 == 0, mine[...], other[...])
        take = lambda block, part: stacked_parts(
            block, starts[layer] + part * rows * count, rows, count
        ).astype(f32)
        qkv[layer, 0] = take(first, 0)
        qkv[layer, 1] = take(second, 0)
        qkv[layer, 2] = take(first, 1)
        out[layer] = take(second, 1)


def ffn_out_kernel(me, *refs):
    into, out = refs[-2:]
    units, width = out.shape[1:]
    for layer in range(LAYERS):
        mine, other = refs[2 * layer : 2 * layer + 2]
        for index, part in enumerate(ordered(me[1] % 2 == 0, mine[...], other[...])):
            columns = slice(index * (width // 2), (index + 1) * (width // 2))
            into[layer, :, columns] = part[:units].astype(f32)
            out[layer, :, columns] = part[units : 2 * units].astype(f32)


def write_out(kernel, name, me, parts, shapes):
    vmem = pl.BlockSpec(memory_space=pltpu.VMEM)
    return pl.pallas_call(
        kernel,
        in_specs=[pl.BlockSpec(memory_space=pltpu.SMEM)] + [vmem] * len(parts),
        out_specs=[vmem] * len(shapes),
        out_shape=[jax.ShapeDtypeStruct(shape, f32) for shape in shapes],
        compiler_params=pltpu.CompilerParams(vmem_limit_bytes=24 * MIB),
        cost_estimate=brief,
        name=name,
    )(me, *parts)


def body(
    text_states,
    visual_maps,
    text_boxes,
    text_lengths,
    qkv_weight,
    out_weight,
    attn_bias,
    ffn_in,
    ffn_in_bias,
    ffn_out,
    ffn_out_bias,
    norm_gain,
    norm_shift,
    bias_table,
    vis_weight,
    vis_bias,
    bn_gain,
    bn_shift,
    cotangent,
):
    tp_index = lax.axis_index("tp")
    tp_size = lax.axis_size("tp")
    half = tp_index % 2
    page = (lax.axis_index("seq") * tp_size + tp_index) // 2
    me = jnp.stack([tp_index, lax.axis_index("seq")]).astype(jnp.int32)
    units = ffn_in.shape[1]
    width = text_states.shape[1]
    text_rows = text_states.shape[0]

    packed = jnp.concatenate([ffn_in, ffn_out], axis=2).reshape(LAYERS * units, 2 * width)
    gathered = lax.all_gather(packed, "tp", axis=0)
    hidden_bias = ffn_in_bias.astype(f32)[None]
    for bit in range(mesh_bits("tp")):
        hidden_bias = jnp.concatenate([hidden_bias, flipped(hidden_bias, "tp", bit)], axis=0)

    other_boxes = flipped(text_boxes, "tp", 0)
    length = lax.dynamic_index_in_dim(text_lengths, page, 0, keepdims=False)
    facts = jnp.stack([half.astype(jnp.int32), length])
    score_bias = make_bias(facts, text_boxes, other_boxes, bias_table)

    count_cells = text_lengths.shape[0] * VIS_TOK
    maps_float = visual_maps.astype(f32)
    slot_place = half * HALF_SLOTS + jnp.arange(HALF_SLOTS, dtype=jnp.int32)
    slot_mask = (slot_place < VIS_TOK)[:, None]
    masked_maps = jnp.where(slot_mask, maps_float, 0.0)
    sums = total_over_all(
        jnp.stack([jnp.sum(masked_maps, axis=0), jnp.sum(masked_maps * masked_maps, axis=0)])
    )
    channel_mean = sums[0] / count_cells
    inverse_std = lax.rsqrt(sums[1] / count_cells - channel_mean * channel_mean + norm_epsilon)
    centered_hat = jnp.where(slot_mask, (maps_float - channel_mean) * inverse_std, 0.0)
    normal_low = jnp.where(slot_mask, centered_hat * bn_gain + bn_shift, 0.0).astype(bf16)
    visual_tokens = jnp.dot(normal_low, vis_weight, preferred_element_type=f32) + vis_bias
    states = jnp.concatenate([text_states.astype(f32), visual_tokens], axis=0)

    rounded = states.astype(bf16)
    project = lambda index: jnp.dot(rounded, qkv_weight[0, index], preferred_element_type=f32)
    shared = jnp.concatenate(
        [project(1).astype(bf16), (project(2) + attn_bias[0, 1]).astype(bf16), rounded], axis=1
    )
    query = (project(0) + attn_bias[0, 0]).astype(bf16)
    saved = []
    for layer in range(LAYERS):
        shared_mate = flipped(shared, "tp", 0)
        parts = (query, shared, shared_mate)
        soft, pair, residual_one, normed = attend(
            layer, *parts, score_bias, states, out_weight, attn_bias, norm_gain, norm_shift
        )
        if layer == 0:
            pairs = page_pairs(facts, text_boxes, other_boxes)
            normed, *pairs = tied((normed, *pairs), ())
        act, act_send, slope, residual_two, *onwards = ffn(
            me,
            layer,
            pair,
            normed,
            gathered,
            hidden_bias,
            ffn_out_bias,
            norm_gain,
            norm_shift,
            qkv_weight,
            attn_bias,
        )
        mates = (flipped(pair, "tp", 0), flipped(act_send, "tp", 0))
        saved.append((parts, soft, pair, residual_one, residual_two, act, slope, mates))
        if layer < LAYERS - 1:
            states, query, shared = onwards
    out_states = onwards[0]

    gradient = cotangent
    norm_sums = [None] * LAYERS
    projection_rows = [None] * LAYERS
    bin_grads = [None] * LAYERS
    score_grads = [None] * LAYERS
    projections = [None] * LAYERS
    ffns = [None] * LAYERS
    for layer in reversed(range(LAYERS)):
        last = layer == LAYERS - 1
        parts, soft, pair, residual_one, residual_two, act, slope, mates = saved[layer]
        dh, dh_send, low, bin_grads[layer], norm_sums[layer], grad_one, context_grad = ffn_back(
            me, layer, gradient, residual_two, residual_one, gathered, slope, norm_gain, out_weight
        )
        if not last:
            context_grad, dh_send = tied((context_grad, dh_send), ffns[-1].underway())
            ffns[-1].second(context_grad)
        dh_mate, low_mate = flipped(dh_send, "tp", 0), flipped(low, "tp", 0)
        score_grads[layer], *grads = attend_back(*parts, context_grad, soft)
        (dh, dh_mate, low_mate, pair_mate, act_mate), grads = (
            tied((dh, dh_mate, low_mate, *mates), grads[:1]),
            tied(grads, (dh_mate, low_mate, *mates)),
        )
        grads_mate = [flipped(part, "tp", 0) for part in grads]
        weights = ffn_grads(me, pair, pair_mate, low, low_mate, dh, dh_mate, act, act_mate)
        if last:
            *weights, grads_mate = (lambda out: (*out[:4], list(out[4:])))(
                tied((*weights, *grads_mate), ())
            )
        else:
            weights = tied(weights, projections[-1].underway() + ffns[-1].underway())
            projections[-1].second(weights[0])
            upper = Scattered([ffns[-1]], weights[0])
        ffns[layer] = Shards(*weights)
        *weights, gradient, projection_rows[layer] = projection_grads(
            not last,
            me,
            layer,
            parts[1],
            parts[2],
            pair,
            mates[0],
            grads,
            grads_mate,
            low,
            low_mate,
            grad_one,
            qkv_weight,
        )
        if last:
            projections[layer] = Shards(*weights)

    half_at = me[:1] % 2
    vis_keep, vis_send, normal_grad, vis_rows = visual_back(
        half_at, gradient, normal_low, centered_hat, vis_weight
    )
    vis_came = flipped(vis_send, "tp", 0)
    seq_ways = [("seq", bit) for bit in range(mesh_bits("seq"))]
    far_ways = [("tp", bit) for bit in range(2, mesh_bits("tp"))]
    vis_ways = far_ways + [("tp", 1)] + seq_ways
    vis_sums = Tree(add_low(vis_keep, vis_came), vis_ways, join=("tp", 0))
    vis_sums.step()
    fold = functools.partial(fold_table, pairs, *score_grads, parts=FOLDS)
    folds = [fold(0, after=vis_sums.lefts)]
    folds[0], *weights = tied(
        (folds[0], *weights),
        ffns[0].underway() + projections[-1].underway() + vis_sums.rights + [upper.shard],
    )
    ffns[0].second(folds[0])
    projections[0] = Shards(*weights)
    vis_sums.step(folds[0])
    folds.append(fold(1, after=folds + vis_sums.lefts))
    (folds[1],) = tied(folds[1:], ffns[0].underway() + vis_sums.rights)
    lower = Scattered([ffns[0], projections[-1]], folds[1])
    vis_sums.step(folds[1])
    small = join(norm_sums + projection_rows + bin_grads + [vis_rows, *folds])
    sizes = [part.shape[0] for part in norm_sums + projection_rows]
    sizes += [tp_size * bin_rows(units)] * LAYERS + [vis_rows.shape[0]]
    small_ways = [("tp", 0), ("tp", 1)] + seq_ways + far_ways
    small_sums = Tree(small, small_ways)
    small_sums.step()
    small_sums.step(*projections[0].underway())
    behind = small_sums.lefts[0]
    projections[0].second(behind)
    small_sums.step(*projections[0].underway(), *vis_sums.rights)
    behind = small_sums.lefts[0]
    projections[0].halve(behind)
    vis_sums.step(behind)
    upper.join(behind)
    small_sums.step(*vis_sums.rights, upper.other)
    behind = small_sums.lefts[0]
    for _ in range(mesh_bits("tp") - 3):
        projections[0].halve_more(behind)
    while vis_sums.steps:
        vis_sums.step(behind)
    lower.join(behind)
    while small_sums.steps:
        small_sums.step(lower.shard)
    behind = small_sums.lefts[0]
    projections[0].halve_more(behind)
    projections[0].join()
    small, small_came = small_sums.result()
    vis_sum, vis_mate = vis_sums.result()
    vis_weight_grad = jnp.concatenate(
        [
            jnp.where(half == 0, vis_sum, vis_mate),
            jnp.where(half == 0, vis_mate, vis_sum),
        ],
        axis=0,
    ).astype(f32)
    grad_text = gradient[:text_rows]
    attn_total, bout_total, gain_total, shift_total, table_total, visb_total, *rest = split(
        me,
        small,
        small_came,
        sizes,
        count_cells,
        normal_grad,
        centered_hat,
        inverse_std,
        bn_gain,
        units,
        width,
    )
    bn_gain_grad, bn_shift_grad, bin_total, grad_maps = rest
    shard = width // tp_size
    qkv_total, out_total = write_out(
        functools.partial(projection_out_kernel, (0, 2 * units)),
        "projections_out",
        me,
        [part for sums in (projections[0], lower) for part in (sums.shard, sums.other)],
        [(LAYERS, 3, shard, width), (LAYERS, shard, width)],
    )
    in_total, down_total = write_out(
        ffn_out_kernel,
        "feed_forward_out",
        me,
        [part for sums in (lower, upper) for part in (sums.shard, sums.other)],
        [(LAYERS, units, width)] * 2,
    )
    return (
        out_states,
        grad_text,
        grad_maps,
        qkv_total,
        out_total,
        attn_total.transpose(1, 0, 2),
        in_total,
        bin_total,
        down_total,
        bout_total,
        gain_total,
        shift_total,
        table_total.T,
        vis_weight_grad,
        visb_total.reshape(-1),
        bn_gain_grad[0],
        bn_shift_grad[0],
    )


def solution(mesh):
    rows = P(("seq", "tp"), None)
    units = P(None, "tp", None)
    return jax.shard_map(
        body,
        mesh=mesh,
        in_specs=(
            rows,
            rows,
            P(None, ("seq", "tp")),
            P(),
            P(),
            P(),
            P(),
            units,
            P(None, "tp"),
            units,
            P(),
            P(),
            P(),
            P(),
            P(),
            P(),
            P(),
            P(),
            rows,
        ),
        out_specs=(
            rows,
            rows,
            rows,
            P(None, None, "tp", None),
            units,
            P(),
            units,
            P(None, "tp"),
            units,
            P(),
            P(),
            P(),
            P(),
            P(),
            P(),
            P(),
            P(),
        ),
        check_vma=False,
    )
```

```python
import functools

import jax
import jax.numpy as jnp
import numpy as np
from jax import lax
from jax.experimental import pallas as pl
from jax.experimental.pallas import tpu as pltpu
from jax.sharding import PartitionSpec as P

HEADS = 12
HEAD_DIM = 64
VIS_TOK = 49
VIS_SLOTS = 64
POS_BINS = 32
BOX_BINS = 64
LAYERS = 2
BUCKETS = POS_BINS + 2 * BOX_BINS

HALF_TEXT = 256
HALF_SLOTS = VIS_SLOTS // 2
ROWS = HALF_TEXT + HALF_SLOTS
KEYS = 640
PAIRS = HEADS // 2
SLABS = 2
STEPS = PAIRS // SLABS
LANES = 128
FOLDS = 2
FOLD_HEADS = 2
BLOCKS = 4
HALF = BLOCKS // 2
norm_epsilon = 1e-05
NEVER = -1e30
bf16 = jnp.bfloat16
f32 = jnp.float32
MIB = 1 << 20
brief = pl.CostEstimate(flops=1, bytes_accessed=1, transcendentals=0)


def mesh_bits(axis):
    return (lax.axis_size(axis) - 1).bit_length()


def flipped(block, axis, bit):
    count = lax.axis_size(axis)
    return lax.ppermute(block, axis, [(i, i ^ (1 << bit)) for i in range(count)])


def total_over_all(value):
    for axis in ("tp", "seq"):
        for bit in range(mesh_bits(axis)):
            value = value + flipped(value, axis, bit)
    return value


def add_low(left, right):
    return (left.astype(f32) + right.astype(f32)).astype(bf16)


def tied(values, after):
    return lax.optimization_barrier((tuple(values), tuple(after)))[0]


class Shards:
    def __init__(self, near_keep, near_send, seq_keep, seq_send):
        self.near = near_keep
        self.seq = seq_keep
        self.near_came = flipped(near_send, "tp", 1)
        self.seq_came = flipped(seq_send, "seq", 0)

    def underway(self):
        return [self.near_came, self.seq_came]

    def second(self, *after):
        near, near_came, seq, seq_came = tied(
            (self.near, self.near_came, self.seq, self.seq_came), after
        )
        turn = lax.axis_index("seq") % 2
        middle = near.shape[-1] // 2
        pick = lambda block, which: jnp.where(
            turn == which, block[..., :middle], block[..., middle:]
        )
        self.near = add_low(pick(near, 0), pick(near_came, 0))
        self.near_came = flipped(add_low(pick(near, 1), pick(near_came, 1)), "seq", 0)
        far = seq.shape[0] // 2
        self.seq = add_low(seq[:far], seq_came[:far])
        self.seq_came = flipped(add_low(seq[far:], seq_came[far:]), "tp", 1)

    def arrived(self, *after):
        near, near_came, seq, seq_came = tied(
            (self.near, self.near_came, self.seq, self.seq_came), after
        )
        return add_low(near, near_came), add_low(seq, seq_came)

    def halve(self, *after):
        near, near_came, seq, seq_came = tied(
            (self.near, self.near_came, self.seq, self.seq_came), after
        )
        bit = mesh_bits("tp") - (near.shape[0] - 1).bit_length()
        pick = lambda block, which: block.reshape((-1, 2) + block.shape[1:])[:, which]
        add = lambda which: jnp.concatenate(
            [
                add_low(pick(near, which), pick(near_came, which)),
                add_low(pick(seq, which), pick(seq_came, which)),
            ],
            axis=1,
        )
        self.shard, self.came = add(0), flipped(add(1), "tp", bit)
        self.bit = bit + 1

    def halve_more(self, *after):
        shard, came = tied((self.shard, self.came), after)
        if shard.shape[0] == 1:
            self.shard = add_low(shard, came)[0]
            return
        pick = lambda block, which: block.reshape((-1, 2) + block.shape[1:])[:, which]
        self.shard = add_low(pick(shard, 0), pick(came, 0))
        self.came = flipped(add_low(pick(shard, 1), pick(came, 1)), "tp", self.bit)
        self.bit += 1

    def join(self, *after):
        (shard,) = tied((self.shard,), after)
        for bit in range(1, mesh_bits("seq")):
            shard = add_low(shard, flipped(shard, "seq", bit))
        self.shard = shard
        self.other = flipped(shard, "seq", 0)


class Scattered:
    def __init__(self, group, *after):
        parts = [part for shards in group for part in shards.arrived(*after)]
        columns = min(part.shape[-1] for part in parts)
        pieces = [
            part[..., start : start + columns]
            for part in parts
            for start in range(0, part.shape[-1], columns)
        ]
        count = lax.axis_size("tp")
        groups = [list(range(first, count, 4)) for first in range(4)]
        self.shard = lax.psum_scatter(
            jnp.concatenate(pieces, axis=1), "tp", scatter_dimension=0, axis_index_groups=groups
        )

    def join(self, *after):
        (shard,) = tied((self.shard,), after)
        for bit in range(1, mesh_bits("seq")):
            shard = add_low(shard, flipped(shard, "seq", bit))
        self.shard = shard
        self.other = flipped(shard, "seq", 0)


class Tree:
    def __init__(self, value, ways, join=None, add=add_low):
        self.lefts = [value]
        self.rights = []
        self.steps = list(ways) + ([join] if join else [])
        self.add = add

    def step(self, *after):
        if after:
            both = tied(self.lefts + self.rights, after)
            self.lefts, self.rights = list(both[:1]), list(both[1:])
        if self.rights:
            self.lefts = [self.add(self.lefts[0], self.rights[0])]
        self.rights = [flipped(self.lefts[0], *self.steps.pop(0))]

    def result(self):
        return self.lefts[0], self.rights[0]


def page_places(half, length, own_boxes, other_boxes):
    def slots(width, first, second):
        lane = lax.broadcasted_iota(jnp.int32, (1, width), 1)
        place = jnp.where(lane < HALF_SLOTS, first + lane, second + lane - HALF_SLOTS)
        place = jnp.where(lane < VIS_SLOTS, place, VIS_SLOTS - 1)
        row = (place * 37) >> 8
        return place, 71 + 143 * (place - 7 * row), 71 + 143 * row

    text = lax.broadcasted_iota(jnp.int32, (1, HALF_TEXT), 1)
    own_text = half * HALF_TEXT + text
    other_text = (1 - half) * HALF_TEXT + text
    slot = slots(LANES, half * HALF_SLOTS, (1 - half) * HALF_SLOTS)
    lane = lax.broadcasted_iota(jnp.int32, (1, LANES), 1)
    slot_used = jnp.where((slot[0] < VIS_TOK) & (lane < VIS_SLOTS), 1, 0)
    keys = (
        jnp.concatenate([own_text, other_text, slot[0]], axis=1),
        jnp.concatenate([own_boxes[0:1], other_boxes[0:1], slot[1]], axis=1),
        jnp.concatenate([own_boxes[1:2], other_boxes[1:2], slot[2]], axis=1),
        jnp.concatenate(
            [
                jnp.where(own_text < length, 1, 0),
                jnp.where(other_text < length, 1, 0),
                slot_used,
            ],
            axis=1,
        ),
    )
    queries = (
        jnp.concatenate([own_text, slot[0]], axis=1),
        jnp.concatenate([own_boxes[0:1], slot[1]], axis=1),
        jnp.concatenate([own_boxes[1:2], slot[2]], axis=1),
    )
    return keys, queries


def as_columns(rows):
    stacked = jnp.concatenate(list(rows) + [rows[0]] * (8 - len(rows)), axis=0)
    turned = jnp.transpose(stacked.astype(f32), (1, 0)).astype(jnp.int32)
    return [turned[:ROWS, i : i + 1] for i in range(len(rows))]


def bias_kernel(facts, own_boxes, other_boxes, table_a, table_b, out, near_s, across_s, down_s):
    @pl.when(pl.program_id(0) == 0)
    def _():
        keys, queries = page_places(facts[0], facts[1], own_boxes[...], other_boxes[...])
        place, x, y = as_columns(queries)
        near_s[...] = jnp.clip(keys[0] - place, -16, 15) + 16
        across_s[...] = jnp.clip((keys[1] - x) >> 4, -32, 31) + 64
        down_s[...] = jnp.where(
            keys[3] > 0, jnp.clip((keys[2] - y) >> 4, -32, 31) + 32, BOX_BINS
        )

    a = jnp.broadcast_to(table_a[0, 0:1, :], (ROWS, LANES))
    b = jnp.broadcast_to(table_b[0, 0:1, :], (ROWS, LANES))
    for tile in range(KEYS // LANES):
        span = slice(tile * LANES, (tile + 1) * LANES)

        def look(table, codes):
            return jnp.take_along_axis(table, codes, axis=1, mode="promise_in_bounds")

        out[0, :, span] = (
            look(a, near_s[:, span]) + look(a, across_s[:, span]) + look(b, down_s[:, span])
        )


def make_bias(facts, own_boxes, other_boxes, bias_table):
    columns = bias_table.T
    table_a = jnp.pad(columns[:, : POS_BINS + BOX_BINS], ((0, 0), (0, LANES - POS_BINS - BOX_BINS)))
    table_b = jnp.pad(
        columns[:, POS_BINS + BOX_BINS :],
        ((0, 0), (0, LANES - BOX_BINS)),
        constant_values=NEVER,
    )
    spread = lambda t: jnp.broadcast_to(t[:, None, :], (HEADS, 8, LANES))
    whole = lambda h, facts: (0, 0)
    return pl.pallas_call(
        bias_kernel,
        out_shape=jax.ShapeDtypeStruct((HEADS, ROWS, KEYS), f32),
        grid_spec=pltpu.PrefetchScalarGridSpec(
            num_scalar_prefetch=1,
            grid=(HEADS,),
            in_specs=[
                pl.BlockSpec((2, HALF_TEXT), whole),
                pl.BlockSpec((2, HALF_TEXT), whole),
                pl.BlockSpec((1, 8, LANES), lambda h, facts: (h, 0, 0)),
                pl.BlockSpec((1, 8, LANES), lambda h, facts: (h, 0, 0)),
            ],
            out_specs=pl.BlockSpec((1, ROWS, KEYS), lambda h, facts: (h, 0, 0)),
            scratch_shapes=[pltpu.VMEM((ROWS, KEYS), jnp.int32)] * 3,
        ),
        compiler_params=pltpu.CompilerParams(vmem_limit_bytes=50 * MIB),
        cost_estimate=brief,
        name="score_bias",
    )(facts, own_boxes, other_boxes, spread(table_a), spread(table_b))


def pairs_kernel(facts, own_boxes, other_boxes, right, left, masks):
    keys, queries = page_places(facts[0], facts[1], own_boxes[...], other_boxes[...])
    place, x, y = as_columns(queries)
    diff = keys[0] - place
    for index, holds in enumerate(
        (
            (diff >= -16) & (diff <= 15),
            (keys[1] & 15) < (x & 15),
            (keys[2] & 15) < (y & 15),
            diff > 15,
        )
    ):
        masks[index] = jnp.where(holds, 1.0, 0.0).astype(bf16)
    row = lax.broadcasted_iota(jnp.int32, (64, KEYS), 0)
    key_hot = [
        jnp.where((63 - row) == (code & 63), 1.0, 0.0)
        for code in (keys[1] >> 4, keys[2] >> 4, keys[0])
    ]
    key_hot.append(jnp.zeros((64, KEYS), f32))
    right[...] = jnp.transpose(jnp.concatenate(key_hot, axis=0), (1, 0)).astype(bf16)
    row = lax.broadcasted_iota(jnp.int32, (64, 384), 0)
    query_hot = [
        jnp.where(row == queries[1] >> 4, 1.0, 0.0),
        jnp.where(row == queries[2] >> 4, 1.0, 0.0),
        jnp.where(row[:32] + 64 == queries[2] >> 4, 1.0, 0.0),
        jnp.where(row == (queries[0] & 63), 1.0, 0.0),
    ]
    left[...] = jnp.concatenate(query_hot, axis=0)[:, :ROWS].astype(bf16)


def page_pairs(facts, own_boxes, other_boxes):
    vmem = pl.BlockSpec(memory_space=pltpu.VMEM)
    return pl.pallas_call(
        pairs_kernel,
        in_specs=[pl.BlockSpec(memory_space=pltpu.SMEM), vmem, vmem],
        out_specs=[vmem] * 3,
        out_shape=[
            jax.ShapeDtypeStruct((KEYS, 256), bf16),
            jax.ShapeDtypeStruct((224, ROWS), bf16),
            jax.ShapeDtypeStruct((4, ROWS, KEYS), bf16),
        ],
        compiler_params=pltpu.CompilerParams(vmem_limit_bytes=24 * MIB),
        cost_estimate=brief,
        name="page_pairs",
    )(facts, own_boxes, other_boxes)


def table_kernel(right, left, masks, ds_a, ds_b, *rest):
    for head in range(ds_a.shape[0]):
        fold_head(right, left, masks, ds_a[head], ds_b[head], rest[-1].at[head])


def fold_head(right, left, masks, ds_a, ds_b, out):
    total = (ds_a.astype(f32) + ds_b.astype(f32)).astype(bf16)
    hot = right[...]
    query_hot = left[...]

    def fold(values, columns, rows):
        inner = jnp.dot(values, hot[:, columns], preferred_element_type=f32).astype(bf16)
        return jnp.dot(query_hot[rows], inner, preferred_element_type=f32)

    near = fold(total * masks[0], slice(128, 256), slice(160, 224))
    together = jnp.concatenate([total, total * masks[1], total * masks[2]], axis=0)
    inner = jnp.dot(together, hot[:, :128], preferred_element_type=f32).astype(bf16)
    outer = lambda rows, which: jnp.dot(
        query_hot[rows], inner[which * ROWS : (which + 1) * ROWS], preferred_element_type=f32
    )
    plain = outer(slice(0, 160), 0)
    by_x = outer(slice(0, 64), 1)
    by_y = outer(slice(64, 160), 2)

    def diagonals(square):
        lane = lax.broadcasted_iota(jnp.int32, square.shape, 1)
        square = jnp.where(lane < 64, square, 0.0)
        turned = pltpu.roll(square, 0, axis=1, stride=1, stride_axis=0)
        return jnp.sum(turned, axis=0, keepdims=True)

    def second(square):
        return pltpu.roll(square, 64, axis=1)

    above = jnp.sum((total * masks[3]).astype(f32), axis=0, keepdims=True)
    above = sum(above[:, t * LANES : (t + 1) * LANES] for t in range(KEYS // LANES))
    out[...] = jnp.concatenate(
        [
            diagonals(plain[:64]),
            diagonals(by_x),
            diagonals(second(plain[64:128])),
            diagonals(second(by_y[:64])),
            diagonals(near),
            above,
            diagonals(second(plain[128:])),
            diagonals(second(by_y[64:])),
        ],
        axis=0,
    )


def table_bins():
    bins = np.zeros((8, LANES, BUCKETS), np.float32)
    for c in range(127):
        diff = 63 - c
        for kind, base in ((0, POS_BINS), (1, POS_BINS + BOX_BINS)):
            here = base + 32 + min(max(diff, -32), 31)
            below = base + 32 + min(max(diff - 1, -32), 31)
            bins[2 * kind, c, here] += 1
            bins[2 * kind + 1, c, below] += 1
            bins[2 * kind + 1, c, here] -= 1
        far = -1 - c
        bins[6, c, 128 + max(far, -32)] += 1
        bins[7, c, 128 + max(far - 1, -32)] += 1
        bins[7, c, 128 + max(far, -32)] -= 1
        near = (diff + 32) % 64 - 32
        if -16 <= near <= 15:
            bins[4, c, near + 16] += 1
        bins[0, c, 0] += 1
        bins[4, c, 0] -= 1
    bins[5, :, 31] += 1
    bins[5, :, 0] -= 1
    return bins


def fold_table(pairs, ds_a, ds_b, part, parts, after=()):
    count = HEADS // parts
    steps = count // FOLD_HEADS
    head = pl.BlockSpec((FOLD_HEADS, ROWS, KEYS), lambda h: (h + part * steps, 0, 0))
    return pl.pallas_call(
        table_kernel,
        out_shape=jax.ShapeDtypeStruct((count, 8, LANES), f32),
        grid=(steps,),
        in_specs=[full(array) for array in pairs]
        + [head, head]
        + [pl.BlockSpec(memory_space=pl.ANY)] * len(after),
        out_specs=pl.BlockSpec((FOLD_HEADS, 8, LANES), lambda h: (h, 0, 0)),
        compiler_params=pltpu.CompilerParams(vmem_limit_bytes=58 * MIB),
        cost_estimate=brief,
        name="table_grad",
    )(*pairs, ds_a, ds_b, *after)


def visual_kernel(half, grad_ref, normal_low, hat, weight, keep, send, normal_grad, sums):
    rows = normal_low.shape[0]
    column = lambda block: jnp.sum(block, axis=0, keepdims=True)
    token_grad = grad_ref[...].astype(bf16)
    whole = tn_dot(normal_low[...], token_grad)
    mid = whole.shape[0] // 2
    first = half[0] == 0
    keep[...] = jnp.where(first, whole[:mid], whole[mid:]).astype(bf16)
    send[...] = jnp.where(first, whole[mid:], whole[:mid]).astype(bf16)
    place = half[0] * rows + lax.broadcasted_iota(jnp.int32, (rows, 1), 0)
    grad = jnp.where(place < VIS_TOK, nt_dot(token_grad, weight[...]), 0.0)
    normal_grad[...] = grad
    total = column(token_grad.astype(f32))
    put_row(sums, 0, total)
    at = total.shape[1] // LANES
    count = grad.shape[1] // LANES
    put_row(sums.at[at : at + count], 0, column(grad * hat[...]))
    put_row(sums.at[at + count : at + 2 * count], 0, column(grad))


def visual_back(half, gradient, normal_low, hat, weight):
    slots, channels = normal_low.shape
    width = weight.shape[1]
    return pl.pallas_call(
        visual_kernel,
        grid_spec=pltpu.PrefetchScalarGridSpec(
            num_scalar_prefetch=1,
            grid=(1,),
            in_specs=[
                pl.BlockSpec(
                    (slots, width), lambda i, half: (gradient.shape[0] // slots - 1, 0)
                ),
                full(normal_low),
                full(hat),
                full(weight),
            ],
            out_specs=[
                pl.BlockSpec((channels // 2, width), lambda i, half: (0, 0)),
                pl.BlockSpec((channels // 2, width), lambda i, half: (0, 0)),
                pl.BlockSpec((slots, channels), lambda i, half: (0, 0)),
                pl.BlockSpec(((width + 2 * channels) // LANES, LANES), lambda i, half: (0, 0)),
            ],
        ),
        out_shape=[
            jax.ShapeDtypeStruct((channels // 2, width), bf16),
            jax.ShapeDtypeStruct((channels // 2, width), bf16),
            jax.ShapeDtypeStruct((slots, channels), f32),
            jax.ShapeDtypeStruct(((width + 2 * channels) // LANES, LANES), f32),
        ],
        cost_estimate=brief,
        name="visual_back",
    )(half, gradient, normal_low, hat, weight)


def join_kernel(*refs):
    low, out = refs[-2:]
    out[...] = jnp.zeros_like(out)
    at = 0
    for ref in refs[:-2]:
        values = ref[...]
        if len(values.shape) == 3 and values.shape[1] > 1:
            for head in range(values.shape[0]):
                out[at : at + values.shape[1], :] = values[head]
                at += values.shape[1]
        elif len(values.shape) == 3:
            for group in range(values.shape[0]):
                for start in range(0, values.shape[2], LANES):
                    size = min(LANES, values.shape[2] - start)
                    out[at : at + 1, :size] = ref[group, :, start : start + size]
                    at += 1
        else:
            out[at : at + values.shape[0], :] = values
            at += values.shape[0]
    low[...] = out[...].astype(bf16)


def bin_rows(units):
    return -(-units // LANES)


def join(parts):
    rows = 0
    for part in parts:
        if part.ndim == 3 and part.shape[1] == 1:
            rows += part.shape[0] * bin_rows(part.shape[2])
        else:
            rows += part.size // LANES
    rows += -rows % 16
    vmem = pl.BlockSpec(memory_space=pltpu.VMEM)
    return pl.pallas_call(
        join_kernel,
        out_shape=jax.ShapeDtypeStruct((rows, LANES), bf16),
        in_specs=[vmem] * len(parts),
        out_specs=vmem,
        scratch_shapes=[pltpu.VMEM((rows, LANES), f32)],
        cost_estimate=brief,
        name="join",
    )(*parts)


def split_kernel(
    sizes,
    count,
    me,
    left,
    right,
    bins,
    normal_grad,
    hat,
    inverse_std,
    bn_gain,
    attn,
    out_bias,
    gain,
    shift,
    table,
    vis_bias,
    gain_grad,
    shift_grad,
    hidden_bias,
    maps,
    total,
):
    total[...] = left[...].astype(f32) + right[...].astype(f32)
    units = hidden_bias.shape[1]
    width = out_bias.shape[1]
    channels = gain_grad.shape[1]
    starts = [0]
    for size in sizes:
        starts.append(starts[-1] + size)

    def take(start, index, wide):
        per = wide // LANES
        begin = start + index * per
        return jnp.concatenate([total[begin + i : begin + i + 1, :] for i in range(per)], axis=1)

    for layer in range(LAYERS):
        norm = functools.partial(take, starts[layer])
        gain[layer, 1:2, :] = norm(0, width)
        shift[layer, 1:2, :] = norm(1, width)
        out_bias[layer : layer + 1, :] = norm(2, width)
        gain[layer, 0:1, :] = norm(3, width)
        shift[layer, 0:1, :] = norm(4, width)
        attn[2, layer : layer + 1, :] = norm(5, width)
        rows = functools.partial(take, starts[LAYERS + layer])
        attn[0, layer : layer + 1, :] = rows(0, width)
        attn[1, layer : layer + 1, :] = rows(1, width)
        per = bin_rows(units)
        begin = starts[2 * LAYERS + layer] + me[0] * per
        for part in range(per):
            span = min(LANES, units - part * LANES)
            hidden_bias[layer : layer + 1, part * LANES : part * LANES + span] = total[
                pl.ds(begin + part, 1), :span
            ]
    at = starts[3 * LAYERS]
    vis_bias[...] = total[at : at + width // LANES, :]
    at += width // LANES
    by_gain = take(at, 0, channels)
    by_shift = take(at, 1, channels)
    gain_grad[...] = by_gain
    shift_grad[...] = by_shift
    scale = inverse_std[...] * bn_gain[...]
    slots = normal_grad.shape[0]
    place = (me[0] & 1) * slots + lax.broadcasted_iota(jnp.int32, (slots, 1), 0)
    maps[...] = jnp.where(
        place < VIS_TOK,
        scale * (normal_grad[...] - by_shift / count - hat[...] * (by_gain / count)),
        0.0,
    )
    at = starts[3 * LAYERS + 1]
    folded = jnp.zeros((16, BUCKETS), f32)
    for kind in range(8):
        rows = jnp.concatenate(
            [total[at + 8 * head + kind : at + 8 * head + kind + 1, :] for head in range(HEADS)]
            + [jnp.zeros((16 - HEADS, LANES), f32)],
            axis=0,
        )
        high = rows.astype(bf16)
        middle = (rows - high.astype(f32)).astype(bf16)
        low = (rows - high.astype(f32) - middle.astype(f32)).astype(bf16)
        for part in (high, middle, low):
            folded = folded + nt_dot(part, bins[kind])
    table[...] = folded[:HEADS]


def split(me, left, right, sizes, count, normal_grad, hat, inverse_std, bn_gain, units, width):
    slots, channels = normal_grad.shape
    bins = jnp.asarray(table_bins().transpose(0, 2, 1), bf16)
    row = lambda value: value.reshape(1, -1)
    vmem = pl.BlockSpec(memory_space=pltpu.VMEM)
    shape = lambda *size: jax.ShapeDtypeStruct(size, f32)
    return pl.pallas_call(
        functools.partial(split_kernel, sizes, count),
        in_specs=[pl.BlockSpec(memory_space=pltpu.SMEM)] + [vmem] * 7,
        out_specs=[vmem] * 10,
        out_shape=[
            shape(3, LAYERS, width),
            shape(LAYERS, width),
            shape(LAYERS, 2, width),
            shape(LAYERS, 2, width),
            shape(HEADS, BUCKETS),
            shape(width // LANES, LANES),
            shape(1, channels),
            shape(1, channels),
            shape(LAYERS, units),
            shape(slots, channels),
        ],
        scratch_shapes=[pltpu.VMEM(left.shape, f32)],
        cost_estimate=brief,
        name="split",
    )(me, left, right, bins, normal_grad, hat, row(inverse_std), row(bn_gain))


def whole_page(own, other):
    return jnp.concatenate(
        [
            own[:HALF_TEXT],
            other[:HALF_TEXT],
            own[HALF_TEXT:],
            other[HALF_TEXT:],
            jnp.zeros((KEYS - 2 * ROWS, own.shape[1]), own.dtype),
        ],
        axis=0,
    )


def page_split(both):
    mid = 2 * HALF_TEXT
    own = jnp.concatenate([both[:HALF_TEXT], both[mid : mid + HALF_SLOTS]], axis=0)
    other = jnp.concatenate(
        [both[HALF_TEXT:mid], both[mid + HALF_SLOTS : mid + VIS_SLOTS]], axis=0
    )
    return own, other


def nt_dot(left, right):
    return lax.dot_general(left, right, (((1,), (1,)), ((), ())), preferred_element_type=f32)


def tn_dot(left, right):
    return lax.dot_general(left, right, (((0,), (0,)), ((), ())), preferred_element_type=f32)


def put_row(target, index, row):
    count = row.shape[1] // LANES
    for part in range(count):
        at = index * count + part
        target[at : at + 1, :] = row[:, part * LANES : (part + 1) * LANES]


def centred(values):
    center = values - jnp.mean(values, axis=1, keepdims=True)
    spread = jnp.mean(center * center, axis=1, keepdims=True)
    rate = lax.rsqrt(spread + norm_epsilon)
    return center * rate, rate


def norm_back(grad, values, gain_row):
    hat, rate = centred(values)
    scaled = grad * gain_row
    mean = jnp.mean(scaled, axis=1, keepdims=True)
    along = jnp.mean(scaled * hat, axis=1, keepdims=True)
    column = lambda block: jnp.sum(block, axis=0, keepdims=True)
    return rate * (scaled - mean - hat * along), column(grad * hat), column(grad)


def attend_kernel(
    layer,
    q_ref,
    ko,
    kp,
    vo,
    vp,
    bias,
    x_ref,
    weight,
    attn_bias,
    gain,
    shift,
    soft,
    pair,
    residual,
    normed,
    x_s,
    weight_s,
    semaphores,
):
    step = pl.program_id(0)
    later = Later([(x_ref, x_s), (weight.at[layer], weight_s)], semaphores)
    pl.when(step == 0)(later.start)
    first = lax.broadcasted_iota(jnp.int32, (ROWS, LANES), 1) < HEAD_DIM
    for part in range(SLABS):
        lanes = slice(part * LANES, (part + 1) * LANES)
        q = q_ref[:, lanes] * jnp.asarray(HEAD_DIM**-0.5, bf16)
        keys = whole_page(ko[:, lanes], kp[:, lanes])
        values = whole_page(vo[:, lanes], vp[:, lanes])
        found = []
        for head in range(2):
            mine = jnp.where(first if head == 0 else ~first, q, jnp.zeros_like(q))
            scores = nt_dot(mine, keys) + bias[2 * part + head]
            raised = jnp.exp(scores - jnp.max(scores, axis=1, keepdims=True))
            weights = (raised * (1.0 / jnp.sum(raised, axis=1, keepdims=True))).astype(bf16)
            soft[2 * part + head] = weights
            found.append(jnp.dot(weights, values, preferred_element_type=f32))
        slab = pl.ds(pl.multiple_of((step * SLABS + part) * LANES, LANES), LANES)
        pair[0, :, slab] = jnp.where(first, found[0], found[1]).astype(bf16)

    @pl.when(step == STEPS - 1)
    def _():
        later.wait(0, 1)
        attended = jnp.dot(pair[0], weight_s[...], preferred_element_type=f32)
        summed = x_s[...] + (attended + attn_bias[layer, 2:3, :])
        residual[...] = summed
        out = centred(summed)[0] * gain[layer, 0:1, :] + shift[layer, 0:1, :]
        normed[...] = out
        pair[1] = out.astype(bf16)
        pair[2] = x_s[...].astype(bf16)


class Later:
    def __init__(self, pairs, semaphores):
        self.copies = [
            pltpu.make_async_copy(source, target, semaphores.at[index])
            for index, (source, target) in enumerate(pairs)
        ]

    def start(self):
        for copy in self.copies:
            copy.start()

    def wait(self, *indices):
        for index in indices:
            self.copies[index].wait()


anywhere = pl.BlockSpec(memory_space=pl.ANY)


def full(array):
    return pl.BlockSpec(array.shape, lambda *at: (0,) * array.ndim)


def attend(layer, q, kv, other_kv, bias, x, out_weight, attn_bias, gain, shift):
    rows, width = q.shape
    slab = pl.BlockSpec((ROWS, SLABS * LANES), lambda p: (0, p))
    second = pl.BlockSpec((ROWS, SLABS * LANES), lambda p: (0, p + STEPS))
    heads = pl.BlockSpec((2 * SLABS, ROWS, KEYS), lambda p: (p, 0, 0))
    whole = pl.BlockSpec((rows, width), lambda p: (0, 0))
    wide = jax.ShapeDtypeStruct((rows, width), f32)
    low = jax.ShapeDtypeStruct((3, rows, width), bf16)
    return pl.pallas_call(
        functools.partial(attend_kernel, layer),
        grid=(STEPS,),
        in_specs=[
            slab,
            slab,
            slab,
            second,
            second,
            heads,
            anywhere,
            anywhere,
            full(attn_bias),
            full(gain),
            full(shift),
        ],
        out_specs=[
            heads,
            pl.BlockSpec((3, rows, width), lambda p: (0, 0, 0)),
            whole,
            whole,
        ],
        out_shape=[jax.ShapeDtypeStruct((HEADS, ROWS, KEYS), bf16), low, wide, wide],
        scratch_shapes=[
            pltpu.VMEM((rows, width), f32),
            pltpu.VMEM((width, width), bf16),
            pltpu.SemaphoreType.DMA((2,)),
        ],
        compiler_params=pltpu.CompilerParams(vmem_limit_bytes=50 * MIB),
        cost_estimate=brief,
        name="attend",
    )(q, kv, other_kv, kv, other_kv, bias, x, out_weight, attn_bias, gain, shift)


def attend_back_kernel(q_ref, ko, kp, vo, vp, dc_ref, soft, *rest):
    ds, *grads = rest[-6:]
    scale = HEAD_DIM**-0.5
    first = lax.broadcasted_iota(jnp.int32, (ROWS, LANES), 1) < HEAD_DIM
    for part in range(SLABS):
        lanes = slice(part * LANES, (part + 1) * LANES)
        q = q_ref[:, lanes]
        dc = dc_ref[:, lanes]
        keys = whole_page(ko[:, lanes], kp[:, lanes])
        values = whole_page(vo[:, lanes], vp[:, lanes])
        q_turned = jnp.transpose(q.astype(f32), (1, 0)).astype(bf16)
        dc_turned = jnp.transpose(dc.astype(f32), (1, 0)).astype(bf16)
        dq_parts, dk_parts, dv_parts = [], [], []
        for head in range(2):
            span = slice(head * HEAD_DIM, (head + 1) * HEAD_DIM)
            mine = jnp.where(first if head == 0 else ~first, dc, jnp.zeros_like(dc))
            weights = soft[2 * part + head]
            weights_f = weights.astype(f32)
            flow = nt_dot(mine, values)
            share = jnp.sum(weights_f * flow, axis=1, keepdims=True)
            score_grad = (weights_f * (flow - share)).astype(bf16)
            ds[2 * part + head] = score_grad
            dq_parts.append(jnp.dot(score_grad, keys, preferred_element_type=f32))
            dk_parts.append(jnp.dot(q_turned[span], score_grad, preferred_element_type=f32))
            dv_parts.append(jnp.dot(dc_turned[span], weights, preferred_element_type=f32))
        grads[0][:, lanes] = (jnp.where(first, dq_parts[0], dq_parts[1]) * scale).astype(bf16)
        own, other = page_split(jnp.transpose(jnp.concatenate(dk_parts, axis=0) * scale, (1, 0)))
        grads[1][:, lanes] = own.astype(bf16)
        grads[2][:, lanes] = other.astype(bf16)
        own, other = page_split(jnp.transpose(jnp.concatenate(dv_parts, axis=0), (1, 0)))
        grads[3][:, lanes] = own.astype(bf16)
        grads[4][:, lanes] = other.astype(bf16)


def attend_back(q, kv, other_kv, dctx, soft, after=()):
    slab = pl.BlockSpec((ROWS, SLABS * LANES), lambda p: (0, p))
    second = pl.BlockSpec((ROWS, SLABS * LANES), lambda p: (0, p + STEPS))
    heads = pl.BlockSpec((2 * SLABS, ROWS, KEYS), lambda p: (p, 0, 0))
    return pl.pallas_call(
        attend_back_kernel,
        grid=(STEPS,),
        in_specs=[slab, slab, slab, second, second, slab, heads]
        + [pl.BlockSpec(memory_space=pl.ANY)] * len(after),
        out_specs=[heads] + [slab] * 5,
        out_shape=[
            jax.ShapeDtypeStruct((HEADS, ROWS, KEYS), bf16),
        ]
        + [jax.ShapeDtypeStruct(q.shape, bf16)] * 5,
        compiler_params=pltpu.CompilerParams(vmem_limit_bytes=50 * MIB),
        cost_estimate=brief,
        name="attend_back",
    )(q, kv, other_kv, kv, other_kv, dctx, soft, *after)


def ffn_kernel(layer, more, me, x_ref, *refs):
    step = pl.program_id(0)
    width = x_ref.shape[1]
    blocks, (bias, n_ref, out_bias, gain, shift), rest = refs[:BLOCKS], refs[BLOCKS:][:5], refs[BLOCKS + 5 :]
    units = blocks[0].shape[1]
    if more:
        weight, attn_bias, *rest, weight_s, semaphores = rest
        later = Later([(weight.at[layer + 1], weight_s)], semaphores)
        pl.when(step == 0)(later.start)
    own_act, mate_act, slope, residual = rest[:4]
    x = x_ref[...]

    total = None
    for index, block in enumerate(blocks):
        weights = block[0]
        row = bias[pl.ds(BLOCKS * step + index, 1), layer, :]
        hidden = nt_dot(x, weights[:, :width]) + row
        half_cdf = 0.5 + 0.5 * lax.erf(hidden * 0.5**0.5)
        low = (hidden * half_cdf).astype(bf16)
        (mate_act if index % 2 else own_act)[index // 2] = low
        density = jnp.exp(hidden * hidden * -0.5) * (1.0 / (2.0 * np.pi) ** 0.5)
        slope[index] = (half_cdf + hidden * density).astype(bf16)
        term = jnp.dot(low, weights[:, width:], preferred_element_type=f32)
        total = term if total is None else total + term

    @pl.when(step == 0)
    def _():
        residual[...] = n_ref[...] + out_bias[layer : layer + 1, :] + total

    @pl.when(step > 0)
    def _():
        residual[...] += total

    @pl.when(step == pl.num_programs(0) - 1)
    def _():
        states = centred(residual[...])[0] * gain[layer, 1:2, :] + shift[layer, 1:2, :]
        rounded = states.astype(bf16)
        if more:
            wide, query, shared = rest[-3:]
            wide[...] = states
            later.wait(0)
            project = lambda index: jnp.dot(
                rounded, weight_s[index], preferred_element_type=f32
            )
            query[...] = (project(0) + attn_bias[layer + 1, 0:1, :]).astype(bf16)
            shared[:, :width] = project(1).astype(bf16)
            shared[:, width : 2 * width] = (
                project(2) + attn_bias[layer + 1, 1:2, :]
            ).astype(bf16)
        else:
            rest[-1][...] = rounded


def weight_blocks(layer, units, width):
    pick = lambda which: pl.BlockSpec(
        (1, units, 2 * width), lambda i, me: (me[0] ^ (BLOCKS * i + which), layer, 0)
    )
    return [pick(which) for which in range(BLOCKS)]


def ffn(me, layer, pair, n, gathered, bias, out_bias, gain, shift, qkv_weight, attn_bias):
    groups, _, units = bias.shape
    rows, width = n.shape
    more = layer < LAYERS - 1
    whole = pl.BlockSpec((rows, width), lambda i, me: (0, 0))
    kept = pl.BlockSpec((BLOCKS, rows, units), lambda i, me: (i, 0, 0))
    kept_shape = jax.ShapeDtypeStruct((groups, rows, units), bf16)
    wide = jax.ShapeDtypeStruct((rows, width), f32)
    low = jax.ShapeDtypeStruct((rows, width), bf16)
    half_act = pl.BlockSpec((HALF, rows, units), lambda i, me: (i, 0, 0))
    half_shape = jax.ShapeDtypeStruct((groups // 2, rows, units), bf16)
    inputs = [pair] + [gathered] * BLOCKS + [bias, n, out_bias, gain, shift]
    in_specs = [
        pl.BlockSpec((None, rows, width), lambda i, me: (1, 0, 0)),
        *weight_blocks(layer, units, width),
        full(bias),
        whole,
        full(out_bias),
        full(gain),
        full(shift),
    ]
    out_specs = [half_act, half_act, kept, whole]
    out_shape = [half_shape, half_shape, kept_shape, wide]
    if more:
        inputs += [qkv_weight, attn_bias]
        in_specs += [
            anywhere,
            full(attn_bias),
        ]
        out_specs += [whole, whole, pl.BlockSpec((rows, 2 * width), lambda i, me: (0, 0))]
        out_shape += [wide, low, jax.ShapeDtypeStruct((rows, 2 * width), bf16)]
    else:
        out_specs += [whole]
        out_shape += [low]
    return pl.pallas_call(
        functools.partial(ffn_kernel, layer, more),
        out_shape=out_shape,
        grid_spec=pltpu.PrefetchScalarGridSpec(
            num_scalar_prefetch=1,
            grid=(groups // BLOCKS,),
            in_specs=in_specs,
            out_specs=out_specs,
            scratch_shapes=[
                pltpu.VMEM((3, width, width), bf16),
                pltpu.SemaphoreType.DMA((1,)),
            ]
            if more
            else [],
        ),
        compiler_params=pltpu.CompilerParams(vmem_limit_bytes=50 * MIB),
        cost_estimate=brief,
        name="feed_forward",
    )(me, *inputs)


def ffn_back_kernel(layer, me, grad_ref, r2_ref, r1_ref, *refs):
    blocks, (slope, gain, out_weight), rest = refs[:BLOCKS], refs[BLOCKS:][:3], refs[BLOCKS + 3 :]
    own_dh, mate_dh, low_grads, bias_grad, sums, dx, dctx, total_s, r1_s, weight_s, semaphores = rest
    later = Later([(r1_ref, r1_s), (out_weight.at[layer], weight_s)], semaphores)
    step = pl.program_id(0)
    width = r2_ref.shape[1]
    column = lambda block: jnp.sum(block, axis=0, keepdims=True)

    @pl.when(step == 0)
    def _():
        later.start()
        grad, gain_grad, shift_grad = norm_back(
            grad_ref[...].astype(f32), r2_ref[...], gain[layer, 1:2, :]
        )
        low = grad.astype(bf16)
        total_s[...] = grad
        low_grads[0] = low
        put_row(sums, 0, gain_grad)
        put_row(sums, 1, shift_grad)
        put_row(sums, 2, column(low.astype(f32)))

    dy = low_grads[0]
    total = None
    for index, block in enumerate(blocks):
        weights = block[0]
        flow = nt_dot(dy, weights[:, width:])
        grad = (flow * slope[index].astype(f32)).astype(bf16)
        (mate_dh if index % 2 else own_dh)[index // 2] = grad
        bias_grad[index ^ (me[0] & (BLOCKS - 1))] = column(grad.astype(f32))
        term = jnp.dot(grad, weights[:, :width], preferred_element_type=f32)
        total = term if total is None else total + term
    total_s[...] += total

    @pl.when(step == pl.num_programs(0) - 1)
    def _():
        later.wait(0, 1)
        grad, gain_grad, shift_grad = norm_back(total_s[...], r1_s[...], gain[layer, 0:1, :])
        low = grad.astype(bf16)
        dx[...] = grad
        low_grads[1] = low
        dctx[...] = nt_dot(low, weight_s[...]).astype(bf16)
        put_row(sums, 3, gain_grad)
        put_row(sums, 4, shift_grad)
        put_row(sums, 5, column(low.astype(f32)))


def ffn_back(me, layer, grad, r2, r1, gathered, slope, gain, out_weight):
    groups, rows, units = slope.shape
    width = r2.shape[1]
    whole = pl.BlockSpec((rows, width), lambda i, me: (0, 0))
    half = pl.BlockSpec((HALF, rows, units), lambda i, me: (i, 0, 0))
    half_shape = jax.ShapeDtypeStruct((groups // 2, rows, units), bf16)
    return pl.pallas_call(
        functools.partial(ffn_back_kernel, layer),
        out_shape=[
            half_shape,
            half_shape,
            jax.ShapeDtypeStruct((2, rows, width), bf16),
            jax.ShapeDtypeStruct((groups, 1, units), f32),
            jax.ShapeDtypeStruct((6 * width // LANES, LANES), f32),
            jax.ShapeDtypeStruct((rows, width), f32),
            jax.ShapeDtypeStruct((rows, width), bf16),
        ],
        grid_spec=pltpu.PrefetchScalarGridSpec(
            num_scalar_prefetch=1,
            grid=(groups // BLOCKS,),
            in_specs=[
                whole,
                whole,
                anywhere,
                *weight_blocks(layer, units, width),
                pl.BlockSpec((BLOCKS, rows, units), lambda i, me: (i, 0, 0)),
                full(gain),
                anywhere,
            ],
            out_specs=[
                half,
                half,
                pl.BlockSpec((2, rows, width), lambda i, me: (0, 0, 0)),
                pl.BlockSpec((BLOCKS, 1, units), lambda i, me: (me[0] // BLOCKS ^ i, 0, 0)),
                pl.BlockSpec((6 * width // LANES, LANES), lambda i, me: (0, 0)),
                whole,
                whole,
            ],
            scratch_shapes=[
                pltpu.VMEM((rows, width), f32),
                pltpu.VMEM((rows, width), f32),
                pltpu.VMEM((width, width), bf16),
                pltpu.SemaphoreType.DMA((2,)),
            ],
        ),
        compiler_params=pltpu.CompilerParams(vmem_limit_bytes=50 * MIB),
        cost_estimate=brief,
        name="feed_forward_back",
    )(me, grad, r2, r1, *[gathered] * BLOCKS, slope, gain, out_weight)


def ffn_grads_kernel(me, n, n_mate, dy, dy_mate, dh, dh_mate, act, act_mate, *rest):
    near_keep, near_send, seq_keep, seq_send, n_s, dy_s = rest[-6:]
    rows, width = n.shape
    far, units = near_keep.shape[:2]
    step = pl.program_id(0)

    @pl.when(step == 0)
    def _():
        for target, own, mate in ((n_s, n, n_mate), (dy_s, dy, dy_mate)):
            target[:rows] = own[...]
            target[rows:] = mate[...]

    def product(own, mate, right):
        turned = [
            jnp.transpose(jnp.concatenate([own[i, 0], mate[i, 0]], axis=0), (1, 0))
            for i in range(far)
        ]
        return jnp.dot(
            jnp.concatenate(turned, axis=0), right[...], preferred_element_type=f32
        ).astype(bf16)

    def put(target, values):
        for i in range(far):
            target[(me[0] >> 2) ^ i] = values[i * units : (i + 1) * units]

    into = product(dh, dh_mate, n_s)
    pl.when(step == 0)(lambda: put(near_keep, into))
    pl.when(step == 1)(lambda: put(near_send, into))
    out = product(act, act_mate, dy_s)
    turn = me[1] % 2 == 0
    put(seq_keep, jnp.where(turn, out[:, : width // 2], out[:, width // 2 :]))
    put(seq_send, jnp.where(turn, out[:, width // 2 :], out[:, : width // 2]))


def ffn_grads(me, pair, pair_mate, low_grads, low_grads_mate, dh, dh_mate, act, act_mate):
    groups, rows, units = dh.shape
    width = pair.shape[2]
    far = groups // 2
    row_block = lambda which: pl.BlockSpec((None, rows, width), lambda i, me: (which, 0, 0))
    hidden = pl.BlockSpec((far, 1, rows, units), lambda i, me: (0, i, 0, 0))
    near_shape = jax.ShapeDtypeStruct((far, units, width), bf16)
    near_block = pl.BlockSpec((far, units, width), lambda i, me: (0, 0, 0))
    seq_shape = jax.ShapeDtypeStruct((groups, units, width // 2), bf16)
    seq_block = pl.BlockSpec((far, units, width // 2), lambda i, me: (i, 0, 0))
    by_far = lambda block: block.reshape(far, 2, rows, units)
    return pl.pallas_call(
        ffn_grads_kernel,
        out_shape=[near_shape, near_shape, seq_shape, seq_shape],
        grid_spec=pltpu.PrefetchScalarGridSpec(
            num_scalar_prefetch=1,
            grid=(2,),
            in_specs=[row_block(1), row_block(1), row_block(0), row_block(0)] + [hidden] * 4,
            out_specs=[near_block, near_block, seq_block, seq_block],
            scratch_shapes=[pltpu.VMEM((2 * rows, width), bf16)] * 2,
        ),
        compiler_params=pltpu.CompilerParams(vmem_limit_bytes=50 * MIB),
        cost_estimate=brief,
        name="feed_forward_grads",
    )(
        me,
        pair,
        pair_mate,
        low_grads,
        low_grads_mate,
        *[by_far(block) for block in (dh, dh_mate, act, act_mate)],
    )


def projection_kernel(by_distance, me, x, x_mate, ctx, ctx_mate, *refs):
    own, mate, refs = refs[:5], refs[5:10], refs[10:]
    da, da_mate, dr_ref, weight = refs[:4]
    near_keep, near_send, seq_keep, seq_send, dx, sums = refs[-11:-5]
    turned_s, picked_s, left_s, right_s, shards_s = refs[-5:]
    step = pl.program_id(0)
    far, shard = near_keep.shape[:2]
    rows, width = x.shape
    column = lambda block: jnp.sum(block.astype(f32), axis=0, keepdims=True)

    def place_of(place, near):
        far_place = (me[0] >> 2) ^ place if by_distance else place
        return far_place * 4 + ((me[0] & 3) ^ (2 * near))

    gap = -rows % LANES
    mate_rows = slice(rows + gap, 2 * rows + gap)

    def pick_left(first, second):
        for block, at_rows in ((first, slice(0, rows)), (second, mate_rows)):
            turned_s[...] = jnp.transpose(block[...].astype(f32), (1, 0))
            for near in range(2):
                for place in range(far):
                    start = pl.multiple_of(place_of(place, near) * shard, 8)
                    at = (near * far + place) * shard
                    picked_s[at : at + shard, at_rows] = turned_s[pl.ds(start, shard), :]
        left_s[...] = picked_s[...].astype(bf16)

    @pl.when(step == 0)
    def _():
        dx[...] = dr_ref[...]
        picked_s[:, rows : rows + gap] = jnp.zeros((width // 2, gap), f32)
        right_s[rows : rows + gap] = jnp.zeros((gap, width), bf16)
        pick_left(x, x_mate)
        right_s[:rows] = own[0][...]
        right_s[mate_rows] = mate[0][...]
        put_row(sums, 0, column(own[0][...]))

    for index in (1, 2):

        @pl.when(step == index)
        def _():
            right_s[:rows] = add_low(own[2 * index - 1][...], mate[2 * index][...])
            right_s[mate_rows] = add_low(mate[2 * index - 1][...], own[2 * index][...])

    @pl.when(step == 2)
    def _():
        put_row(sums, 1, column(right_s[:rows]))

    @pl.when(step < 3)
    def _():
        dx[...] += nt_dot(right_s[:rows], weight[0, 0])

    @pl.when(step == 3)
    def _():
        pick_left(ctx, ctx_mate)
        right_s[:rows] = da[...]
        right_s[mate_rows] = da_mate[...]

    shards_s[...] = jnp.dot(left_s[...], right_s[...], preferred_element_type=f32)

    def put(target, first, near, columns):
        for place in range(far):
            at = (near * far + place) * shard
            target[first + place, :, columns] = shards_s[at : at + shard, :].astype(bf16)

    for index in range(2):

        @pl.when(step == index)
        def _():
            columns = slice(index * width, (index + 1) * width)
            put(near_keep, 0, 0, columns)
            put(near_send, 0, 1, columns)

    def put_seq(target):
        put(target, 0, 0, slice(None))
        put(target, far, 1, slice(None))

    mine = step - 2 == me[1] % 2
    pl.when((step >= 2) & mine)(lambda: put_seq(seq_keep))
    pl.when((step >= 2) & jnp.logical_not(mine))(lambda: put_seq(seq_send))


def projection_grads(
    by_distance,
    me,
    layer,
    pair,
    pair_mate,
    own,
    mate,
    low,
    low_mate,
    dr,
    weight,
    after=(),
):
    rows, width = dr.shape
    groups = lax.axis_size("tp")
    shard = width // groups
    whole = pl.BlockSpec((rows, width), lambda t, me: (0, 0))
    layered = lambda which: pl.BlockSpec((None, rows, width), lambda t, me: (which, 0, 0))
    near_shape = jax.ShapeDtypeStruct((groups // 4, shard, 2 * width), bf16)
    near_block = pl.BlockSpec(near_shape.shape, lambda t, me: (0, 0, 0))
    seq_shape = jax.ShapeDtypeStruct((groups // 2, shard, width), bf16)
    seq_block = pl.BlockSpec(seq_shape.shape, lambda t, me: (0, 0, 0))
    return pl.pallas_call(
        functools.partial(projection_kernel, by_distance),
        out_shape=[near_shape, near_shape, seq_shape, seq_shape]
        + [
            jax.ShapeDtypeStruct((rows, width), f32),
            jax.ShapeDtypeStruct((2 * width // LANES, LANES), f32),
        ],
        grid_spec=pltpu.PrefetchScalarGridSpec(
            num_scalar_prefetch=1,
            grid=(4,),
            in_specs=[
                layered(2),
                layered(2),
                layered(0),
                layered(0),
                *[whole] * 10,
                layered(1),
                layered(1),
                whole,
                pl.BlockSpec(
                    (1, 1, width, width), lambda t, me: (layer, jnp.minimum(t, 2), 0, 0)
                ),
            ]
            + [pl.BlockSpec(memory_space=pl.ANY)] * len(after),
            out_specs=[near_block, near_block, seq_block, seq_block]
            + [
                whole,
                pl.BlockSpec((2 * width // LANES, LANES), lambda t, me: (0, 0)),
            ],
            scratch_shapes=[
                pltpu.VMEM((width, rows), f32),
                pltpu.VMEM((width // 2, 2 * rows + -rows % LANES), f32),
                pltpu.VMEM((width // 2, 2 * rows + -rows % LANES), bf16),
                pltpu.VMEM((2 * rows + -rows % LANES, width), bf16),
                pltpu.VMEM((width // 2, width), f32),
            ],
        ),
        compiler_params=pltpu.CompilerParams(vmem_limit_bytes=50 * MIB),
        cost_estimate=brief,
        name="projection_grads",
    )(
        me,
        pair,
        pair_mate,
        pair,
        pair_mate,
        *own,
        *mate,
        low,
        low_mate,
        dr,
        weight,
        *after,
    )


def ordered(turn, mine, other):
    return jnp.where(turn, mine, other), jnp.where(turn, other, mine)


def stacked_parts(block, start, rows, count):
    return jnp.concatenate(
        [block[start + i * rows : start + (i + 1) * rows] for i in range(count)], axis=1
    )


def projection_out_kernel(starts, me, *refs):
    qkv, out = refs[-2:]
    rows, width = out.shape[1:]
    for layer in range(LAYERS):
        mine, other = refs[2 * layer : 2 * layer + 2]
        count = width // mine.shape[1]
        first, second = ordered(me[1] % 2 == 0, mine[...], other[...])
        take = lambda block, part: stacked_parts(
            block, starts[layer] + part * rows * count, rows, count
        ).astype(f32)
        qkv[layer, 0] = take(first, 0)
        qkv[layer, 1] = take(second, 0)
        qkv[layer, 2] = take(first, 1)
        out[layer] = take(second, 1)


def ffn_out_kernel(me, *refs):
    into, out = refs[-2:]
    units, width = out.shape[1:]
    for layer in range(LAYERS):
        mine, other = refs[2 * layer : 2 * layer + 2]
        for index, part in enumerate(ordered(me[1] % 2 == 0, mine[...], other[...])):
            columns = slice(index * (width // 2), (index + 1) * (width // 2))
            into[layer, :, columns] = part[:units].astype(f32)
            out[layer, :, columns] = part[units : 2 * units].astype(f32)


def write_out(kernel, name, me, parts, shapes):
    vmem = pl.BlockSpec(memory_space=pltpu.VMEM)
    return pl.pallas_call(
        kernel,
        in_specs=[pl.BlockSpec(memory_space=pltpu.SMEM)] + [vmem] * len(parts),
        out_specs=[vmem] * len(shapes),
        out_shape=[jax.ShapeDtypeStruct(shape, f32) for shape in shapes],
        compiler_params=pltpu.CompilerParams(vmem_limit_bytes=24 * MIB),
        cost_estimate=brief,
        name=name,
    )(me, *parts)


def body(
    text_states,
    visual_maps,
    text_boxes,
    text_lengths,
    qkv_weight,
    out_weight,
    attn_bias,
    ffn_in,
    ffn_in_bias,
    ffn_out,
    ffn_out_bias,
    norm_gain,
    norm_shift,
    bias_table,
    vis_weight,
    vis_bias,
    bn_gain,
    bn_shift,
    cotangent,
):
    tp_index = lax.axis_index("tp")
    tp_size = lax.axis_size("tp")
    half = tp_index % 2
    page = (lax.axis_index("seq") * tp_size + tp_index) // 2
    me = jnp.stack([tp_index, lax.axis_index("seq")]).astype(jnp.int32)
    units = ffn_in.shape[1]
    width = text_states.shape[1]
    text_rows = text_states.shape[0]

    packed = jnp.concatenate([ffn_in, ffn_out], axis=2).reshape(LAYERS * units, 2 * width)
    gathered = lax.all_gather(packed, "tp", axis=0)
    hidden_bias = ffn_in_bias.astype(f32)[None]
    for bit in range(mesh_bits("tp")):
        hidden_bias = jnp.concatenate([hidden_bias, flipped(hidden_bias, "tp", bit)], axis=0)

    other_boxes = flipped(text_boxes, "tp", 0)
    length = lax.dynamic_index_in_dim(text_lengths, page, 0, keepdims=False)
    facts = jnp.stack([half.astype(jnp.int32), length])
    score_bias = make_bias(facts, text_boxes, other_boxes, bias_table)

    count_cells = text_lengths.shape[0] * VIS_TOK
    maps_float = visual_maps.astype(f32)
    slot_place = half * HALF_SLOTS + jnp.arange(HALF_SLOTS, dtype=jnp.int32)
    slot_mask = (slot_place < VIS_TOK)[:, None]
    masked_maps = jnp.where(slot_mask, maps_float, 0.0)
    sums = total_over_all(
        jnp.stack([jnp.sum(masked_maps, axis=0), jnp.sum(masked_maps * masked_maps, axis=0)])
    )
    channel_mean = sums[0] / count_cells
    inverse_std = lax.rsqrt(sums[1] / count_cells - channel_mean * channel_mean + norm_epsilon)
    centered_hat = jnp.where(slot_mask, (maps_float - channel_mean) * inverse_std, 0.0)
    normal_low = jnp.where(slot_mask, centered_hat * bn_gain + bn_shift, 0.0).astype(bf16)
    visual_tokens = jnp.dot(normal_low, vis_weight, preferred_element_type=f32) + vis_bias
    states = jnp.concatenate([text_states.astype(f32), visual_tokens], axis=0)

    rounded = states.astype(bf16)
    project = lambda index: jnp.dot(rounded, qkv_weight[0, index], preferred_element_type=f32)
    shared = jnp.concatenate(
        [project(1).astype(bf16), (project(2) + attn_bias[0, 1]).astype(bf16)], axis=1
    )
    query = (project(0) + attn_bias[0, 0]).astype(bf16)
    saved = []
    for layer in range(LAYERS):
        shared_mate = flipped(shared, "tp", 0)
        parts = (query, shared, shared_mate)
        soft, pair, residual_one, normed = attend(
            layer, *parts, score_bias, states, out_weight, attn_bias, norm_gain, norm_shift
        )
        if layer == 0:
            pairs = page_pairs(facts, text_boxes, other_boxes)
            normed, *pairs = tied((normed, *pairs), ())
        act, act_send, slope, residual_two, *onwards = ffn(
            me,
            layer,
            pair,
            normed,
            gathered,
            hidden_bias,
            ffn_out_bias,
            norm_gain,
            norm_shift,
            qkv_weight,
            attn_bias,
        )
        mates = (flipped(pair, "tp", 0), flipped(act_send, "tp", 0))
        saved.append((parts, soft, pair, residual_one, residual_two, act, slope, mates))
        if layer < LAYERS - 1:
            states, query, shared = onwards
    out_states = onwards[0]

    gradient = cotangent
    norm_sums = [None] * LAYERS
    projection_rows = [None] * LAYERS
    bin_grads = [None] * LAYERS
    score_grads = [None] * LAYERS
    projections = [None] * LAYERS
    ffns = [None] * LAYERS
    for layer in reversed(range(LAYERS)):
        last = layer == LAYERS - 1
        parts, soft, pair, residual_one, residual_two, act, slope, mates = saved[layer]
        dh, dh_send, low, bin_grads[layer], norm_sums[layer], grad_one, context_grad = ffn_back(
            me, layer, gradient, residual_two, residual_one, gathered, slope, norm_gain, out_weight
        )
        if not last:
            context_grad, dh_send = tied((context_grad, dh_send), ffns[-1].underway())
            ffns[-1].second(context_grad)
        dh_mate, low_mate = flipped(dh_send, "tp", 0), flipped(low, "tp", 0)
        score_grads[layer], *grads = attend_back(*parts, context_grad, soft)
        (dh, dh_mate, low_mate, pair_mate, act_mate), grads = (
            tied((dh, dh_mate, low_mate, *mates), grads[:1]),
            tied(grads, (dh_mate, low_mate, *mates)),
        )
        grads_mate = [flipped(part, "tp", 0) for part in grads]
        weights = ffn_grads(me, pair, pair_mate, low, low_mate, dh, dh_mate, act, act_mate)
        if last:
            *weights, grads_mate = (lambda out: (*out[:4], list(out[4:])))(
                tied((*weights, *grads_mate), ())
            )
        else:
            weights = tied(weights, projections[-1].underway() + ffns[-1].underway())
            projections[-1].second(weights[0])
            upper = Scattered([ffns[-1]], weights[0])
        ffns[layer] = Shards(*weights)
        *weights, gradient, projection_rows[layer] = projection_grads(
            not last,
            me,
            layer,
            pair,
            mates[0],
            grads,
            grads_mate,
            low,
            low_mate,
            grad_one,
            qkv_weight,
        )
        if last:
            projections[layer] = Shards(*weights)

    half_at = me[:1] % 2
    vis_keep, vis_send, normal_grad, vis_rows = visual_back(
        half_at, gradient, normal_low, centered_hat, vis_weight
    )
    vis_came = flipped(vis_send, "tp", 0)
    seq_ways = [("seq", bit) for bit in range(mesh_bits("seq"))]
    far_ways = [("tp", bit) for bit in range(2, mesh_bits("tp"))]
    vis_ways = far_ways + [("tp", 1)] + seq_ways
    vis_sums = Tree(add_low(vis_keep, vis_came), vis_ways, join=("tp", 0))
    vis_sums.step()
    fold = functools.partial(fold_table, pairs, *score_grads, parts=FOLDS)
    folds = [fold(0, after=vis_sums.lefts)]
    folds[0], *weights = tied(
        (folds[0], *weights),
        ffns[0].underway() + projections[-1].underway() + vis_sums.rights + [upper.shard],
    )
    ffns[0].second(folds[0])
    projections[0] = Shards(*weights)
    vis_sums.step(folds[0])
    folds.append(fold(1, after=folds + vis_sums.lefts))
    (folds[1],) = tied(folds[1:], ffns[0].underway() + vis_sums.rights)
    lower = Scattered([ffns[0], projections[-1]], folds[1])
    vis_sums.step(folds[1])
    small = join(norm_sums + projection_rows + bin_grads + [vis_rows, *folds])
    sizes = [part.shape[0] for part in norm_sums + projection_rows]
    sizes += [tp_size * bin_rows(units)] * LAYERS + [vis_rows.shape[0]]
    small_ways = [("tp", 0), ("tp", 1)] + seq_ways + far_ways
    small_sums = Tree(small, small_ways)
    small_sums.step()
    small_sums.step(*projections[0].underway())
    behind = small_sums.lefts[0]
    projections[0].second(behind)
    small_sums.step(*projections[0].underway(), *vis_sums.rights)
    behind = small_sums.lefts[0]
    projections[0].halve(behind)
    vis_sums.step(behind)
    upper.join(behind)
    small_sums.step(*vis_sums.rights, upper.other)
    behind = small_sums.lefts[0]
    for _ in range(mesh_bits("tp") - 3):
        projections[0].halve_more(behind)
    while vis_sums.steps:
        vis_sums.step(behind)
    lower.join(behind)
    while small_sums.steps:
        small_sums.step(lower.shard)
    behind = small_sums.lefts[0]
    projections[0].halve_more(behind)
    projections[0].join()
    small, small_came = small_sums.result()
    vis_sum, vis_mate = vis_sums.result()
    vis_weight_grad = jnp.concatenate(
        [
            jnp.where(half == 0, vis_sum, vis_mate),
            jnp.where(half == 0, vis_mate, vis_sum),
        ],
        axis=0,
    ).astype(f32)
    grad_text = gradient[:text_rows]
    attn_total, bout_total, gain_total, shift_total, table_total, visb_total, *rest = split(
        me,
        small,
        small_came,
        sizes,
        count_cells,
        normal_grad,
        centered_hat,
        inverse_std,
        bn_gain,
        units,
        width,
    )
    bn_gain_grad, bn_shift_grad, bin_total, grad_maps = rest
    shard = width // tp_size
    qkv_total, out_total = write_out(
        functools.partial(projection_out_kernel, (0, 2 * units)),
        "projections_out",
        me,
        [part for sums in (projections[0], lower) for part in (sums.shard, sums.other)],
        [(LAYERS, 3, shard, width), (LAYERS, shard, width)],
    )
    in_total, down_total = write_out(
        ffn_out_kernel,
        "feed_forward_out",
        me,
        [part for sums in (lower, upper) for part in (sums.shard, sums.other)],
        [(LAYERS, units, width)] * 2,
    )
    return (
        out_states,
        grad_text,
        grad_maps,
        qkv_total,
        out_total,
        attn_total.transpose(1, 0, 2),
        in_total,
        bin_total,
        down_total,
        bout_total,
        gain_total,
        shift_total,
        table_total.T,
        vis_weight_grad,
        visb_total.reshape(-1),
        bn_gain_grad[0],
        bn_shift_grad[0],
    )


def solution(mesh):
    rows = P(("seq", "tp"), None)
    units = P(None, "tp", None)
    return jax.shard_map(
        body,
        mesh=mesh,
        in_specs=(
            rows,
            rows,
            P(None, ("seq", "tp")),
            P(),
            P(),
            P(),
            P(),
            units,
            P(None, "tp"),
            units,
            P(),
            P(),
            P(),
            P(),
            P(),
            P(),
            P(),
            P(),
            rows,
        ),
        out_specs=(
            rows,
            rows,
            rows,
            P(None, None, "tp", None),
            units,
            P(),
            units,
            P(None, "tp"),
            units,
            P(),
            P(),
            P(),
            P(),
            P(),
            P(),
            P(),
            P(),
        ),
        check_vma=False,
    )
```
